32 devices in a mesh: gx: 8 (over z, core), gy: 4 (over y, x).
Axes of the slice: x: 2, y: 2, z: 4, core: 2. Of those that a mesh axis runs over, the one named last changes fastest.
Arguments:
- right_side: float32 [128, 128, 128], P('gx', 'gy'), may hold values from -1 to 2
- screening: float32 [128, 128, 128], P('gx', 'gy'), may hold values from 0.5 to 5
- active_blocks: int32 [8, 4, 12], P('gx', 'gy'), may hold values from -1 to 15, as said below
- visible_bricks: int32 [8, 4, 8], P('gx', 'gy'), may hold values from -1 to 15, as said below
Outputs:
- indicator: float32 [128, 128, 128], P('gx', 'gy')
- crossing: float32 [64, 4, 3, 4096], P('gx', 'gy')
The draws below stay inside these ranges and needn't reach their ends.
Inputs may be any that keep to these rules, and one draw needn't show every extreme that they name: `active_blocks`: each device's row lists distinct block numbers of that device's 16 blocks first, then -1 in the unused slots; at least one entry is a block number; some device fills all 12 slots and some leaves slots unused. `visible_bricks`: each device's row lists distinct block numbers of that device's 16 blocks first, then -1 in the unused slots; at least one entry is a block number; some device fills all 8 slots.
All inputs are finite; a program needn't handle non-finite values.
Results may differ from the reference program's by a relative error of at most 0.0003.
Values sent between devices are 32-bit elements; how exact they have to be, the bound alone decides.
No kernel may reach another device: no remote copies, remote signals or barrier semaphores. Data moves between devices by JAX's collectives and lax.ppermute only.
A program may use at most 64 MiB of HBM per device.

```python
import math
import jax
import jax.numpy as jnp
from jax import lax

BLK = 16
CX = 16
CY = 32
CZ = 128
ITERS = 3
ACT = 12
VIS = 8
NX = 128
NY = 128
N_GX = 8
N_GY = 4


def slot_lists(key, slots, salt):
    blocks = CX // BLK * (CY // BLK) * (CZ // BLK)
    devices = N_GX * N_GY

    def one_row(row_key, forced, sparse):
        perm_key, count_key = jax.random.split(row_key)
        order = jax.random.permutation(perm_key, blocks).astype(jnp.int32)
        place = jnp.argmax(order == blocks - 1)
        order = order.at[place].set(order[0]).at[0].set(blocks - 1)
        count = jax.random.randint(count_key, (), 1, slots + 1)
        count = jnp.where(sparse, max(1, slots // 4), count)
        count = jnp.where(forced, slots, count)
        taken = order[:slots]
        return jnp.where(jnp.arange(slots) < count, taken, -1).astype(jnp.int32)
    keys = jax.random.split(jax.random.fold_in(key, salt), devices)
    chosen = jax.random.randint(jax.random.fold_in(key, salt + 1), (), 0, devices)
    forced = jnp.arange(devices) == chosen
    sparse = jnp.arange(devices) == (chosen + 1) % devices
    return jax.vmap(one_row)(keys, forced, sparse).reshape(N_GX, N_GY, slots)


def draw_active_blocks(key, part):
    return slot_lists(key, ACT, 11)


def draw_visible_bricks(key, part):
    return slot_lists(key, VIS, 23)


def block_scale(stream_key, dims, shards, smallest, high):
    def one(dim, shards_of):
        heights = jax.random.uniform(jax.random.fold_in(jax.random.fold_in(stream_key, 6), dim), (shards_of,), jnp.float32, smallest / len(shards), high / len(shards))
        return jnp.repeat(jnp.exp(heights), dims[dim] // shards_of).reshape((-1,) + (1,) * (len(dims) - dim - 1))

    factor_of = one(*shards[0])
    for cut in shards[1:]:
        factor_of = factor_of * one(*cut)
    return factor_of


def setup_inputs(seed: int = 0) -> dict:
    arg_keys = jax.random.split(jax.random.key(seed), 5)
    right_side = jnp.clip(-1.0 + 3.0 * jax.random.uniform(arg_keys[0], (NX, NY, CZ), jnp.float32) ** block_scale(arg_keys[0], (NX, NY, CZ), ((0, 8), (1, 4)), -0.2, 0.2), -1.0, 2.0)
    screening = jnp.clip(jnp.exp(math.log(5.0) - 2.3025851 * jax.random.uniform(arg_keys[1], (NX, NY, CZ), jnp.float32) ** block_scale(arg_keys[1], (NX, NY, CZ), ((0, 8), (1, 4)), -0.2, 0.2)), 0.5, 5.0)
    active_blocks = draw_active_blocks(jax.random.fold_in(arg_keys[4], 71), 0)
    visible_bricks = draw_visible_bricks(jax.random.fold_in(arg_keys[4], 71), 0)
    return {"right_side": right_side, "screening": screening, "active_blocks": active_blocks, "visible_bricks": visible_bricks}


MASS = (11.0 / 20.0, 13.0 / 60.0, 1.0 / 120.0)
STIFF = (1.0, -1.0 / 3.0, -1.0 / 6.0)
SHARP = 4.0


def apply_axis(padded, axis, coef):
    count = padded.shape[axis] - 4

    def part(start):
        return lax.slice_in_dim(padded, start, start + count, axis=axis)

    return coef[0] * part(2) + coef[1] * (part(1) + part(3)) + coef[2] * (part(0) + part(4))


def pad_axis(field, axis):
    widths = [(0, 0)] * field.ndim
    widths[axis] = (2, 2)
    return jnp.pad(field, widths)


def operate(field, screening, mask):
    zpadded = pad_axis(field, 2)
    mass_z = pad_axis(apply_axis(zpadded, 2, MASS), 1)
    stiff_z = pad_axis(apply_axis(zpadded, 2, STIFF), 1)
    inner = pad_axis(apply_axis(stiff_z, 1, MASS) + apply_axis(mass_z, 1, STIFF), 0)
    outer = pad_axis(apply_axis(mass_z, 1, MASS), 0)
    return mask * (apply_axis(inner, 0, MASS) + apply_axis(outer, 0, STIFF) + screening * field)


def crossing_weight(low, high):
    lower = jax.nn.sigmoid(SHARP * low)
    upper = jax.nn.sigmoid(SHARP * high)
    return lower * (1.0 - upper) + (1.0 - lower) * upper


def reference(right_side, screening, active_blocks, visible_bricks):
    n_gx, n_gy = active_blocks.shape[0], active_blocks.shape[1]
    bx_dev, by_dev, bz_dev = CX // BLK, CY // BLK, CZ // BLK
    numbers = jnp.arange(bx_dev * by_dev * bz_dev, dtype=jnp.int32)
    block_mask = jnp.any(numbers[None, None, :, None] == active_blocks[:, :, None, :], axis=-1).astype(jnp.float32)
    block_mask = block_mask.reshape(n_gx, n_gy, bx_dev, by_dev, bz_dev).transpose(0, 2, 1, 3, 4)
    block_mask = block_mask.reshape(n_gx, bx_dev, 1, n_gy, by_dev, 1, bz_dev, 1)
    mask = jnp.broadcast_to(block_mask, (n_gx, bx_dev, BLK, n_gy, by_dev, BLK, bz_dev, BLK)).reshape(right_side.shape)
    indicator = jnp.zeros_like(right_side)
    residual = mask * right_side
    direction = residual
    norm_now = jnp.sum(residual * residual)
    for step in range(ITERS):
        image = operate(direction, screening, mask)
        alpha = norm_now / jnp.sum(direction * image)
        indicator = indicator + alpha * direction
        residual = residual - alpha * image
        if step + 1 < ITERS:
            norm_next = jnp.sum(residual * residual)
            direction = residual + (norm_next / norm_now) * direction
            norm_now = norm_next
    total = jnp.sum(indicator)
    count = jnp.sum((active_blocks >= 0).astype(jnp.float32)) * float(BLK ** 3)
    iso = total / count
    extended = jnp.pad(indicator, ((0, 1), (0, 1), (0, 1)))
    flat = visible_bricks.reshape(-1)
    slots = visible_bricks.shape[2]
    owner_x = jnp.arange(flat.shape[0], dtype=jnp.int32) // (n_gy * slots)
    owner_y = (jnp.arange(flat.shape[0], dtype=jnp.int32) // slots) % n_gy

    def brick_weights(entry):
        number, dev_x, dev_y = entry
        safe = jnp.maximum(number, 0)
        block_x = safe // (by_dev * bz_dev)
        block_y = (safe // bz_dev) % by_dev
        block_z = safe % bz_dev
        start = (dev_x * CX + block_x * BLK, dev_y * CY + block_y * BLK, block_z * BLK)
        region = lax.dynamic_slice(extended, [s.astype(jnp.int32) for s in start], (BLK + 1, BLK + 1, BLK + 1)) - iso
        base = region[:-1, :-1, :-1]
        result = jnp.stack([crossing_weight(base, region[1:, :-1, :-1]),
                            crossing_weight(base, region[:-1, 1:, :-1]),
                            crossing_weight(base, region[:-1, :-1, 1:])]).reshape(3, BLK * BLK * BLK)
        return jnp.where(number >= 0, result, jnp.zeros_like(result))

    weights = lax.map(brick_weights, (flat, owner_x, owner_y))
    weights = weights.reshape(n_gx, n_gy, slots, 3, BLK * BLK * BLK).transpose(0, 2, 1, 3, 4)
    crossing = weights.reshape(n_gx * slots, n_gy, 3, BLK * BLK * BLK)
    return indicator, crossing
```

```python
import functools
import math

import jax
import jax.numpy as jnp
from jax import lax
from jax.experimental import pallas as pl
from jax.experimental.pallas import tpu as pltpu
from jax.sharding import PartitionSpec as P

BLK = 16
WIDE = 6
NEAR = 4
EDGE = 8
SHARP = 4.0
SCALE = 1.0 / 86400.0
SHIFT = 2.25
LOW, HIGH = 0.5, 7.0
SUMS = 16
F32 = jnp.float32


def mass(mid, one, two):
    return 66.0 * mid + (26.0 * one + two)


def stiff(mid, one, two):
    return 6.0 * mid - (2.0 * one + two)


def block_mask(active, slots, rows, columns):
    y = lax.broadcasted_iota(jnp.int32, (rows, columns), 0)
    z = lax.broadcasted_iota(jnp.int32, (rows, columns), 1)
    number = (y // BLK) * (columns // BLK) + z // BLK
    mask = jnp.zeros((rows, columns), F32)
    for slot in range(slots):
        mask = jnp.where(number == active[slot], 1.0, mask)
    return mask


def pack_kernel(active, right, screen, x_low, x_high, y_low, y_high):
    nx, ny, nz = right.shape
    mask = block_mask(active, active.shape[0], ny, nz)
    for x in range(nx):
        field = right[x] * mask
        weight = screen[x] * mask
        if x < WIDE:
            x_low[x] = field
        if x < NEAR:
            x_low[WIDE + x] = weight
        if x >= nx - WIDE:
            x_high[x - (nx - WIDE)] = field
        if x >= nx - NEAR:
            x_high[WIDE + x - (nx - NEAR)] = weight
        y_low[x] = field[:EDGE]
        y_low[nx + x] = weight[:EDGE]
        y_high[x] = field[ny - EDGE :]
        y_high[nx + x] = weight[ny - EDGE :]


def along_z(value):
    lane = lax.broadcasted_iota(jnp.int32, value.shape, 1)
    last = value.shape[1]

    def shifted(step):
        before = jnp.where(lane >= step, pltpu.roll(value, step, 1), 0.0)
        after = jnp.where(lane < last - step, pltpu.roll(value, last - step, 1), 0.0)
        return before + after

    one, two = shifted(1), shifted(2)
    return mass(value, one, two), stiff(value, one, two)


def powers_kernel(
    active, right, screen, x_low, x_high, y_low, y_high, c_low, c_high,
    out0, out1, out2, sums,
    field, keep, shifted, first, second, za, zb, yp, yq,
):
    nx, ny, nz = right.shape
    wide = ny + 2 * EDGE
    rows = ny + 2 * NEAR
    mask = block_mask(active, active.shape[0], ny, nz)

    def set_weight(at, span, weight):
        on = weight > 0.0
        keep[at, span] = jnp.where(on, SCALE, 0.0)
        shifted[at, span] = jnp.where(on, weight - SHIFT, 0.0)

    mid = pl.ds(EDGE, ny)
    low = pl.ds(0, EDGE)
    high = pl.ds(EDGE + ny, EDGE)
    for x in range(nx):
        field[WIDE + x, mid] = right[x] * mask
        set_weight(NEAR + x, mid, screen[x] * mask)
        for span, source in ((low, y_low), (high, y_high)):
            field[WIDE + x, span] = source[x]
            set_weight(NEAR + x, span, source[nx + x])
    for base, near, source, skip in ((0, 0, x_low, 0), (WIDE + nx, NEAR + nx, x_high, WIDE + NEAR)):
        for x in range(WIDE):
            field[base + x, mid] = source[x]
            field[base + x, low] = c_low[skip + x]
            field[base + x, high] = c_high[skip + x]
        for x in range(NEAR):
            set_weight(near + x, mid, source[WIDE + x])
            set_weight(near + x, low, c_low[skip + WIDE + x])
            set_weight(near + x, high, c_high[skip + WIDE + x])

    def spread(source, planes, size, start, count):
        @pl.loop(0, planes)
        def _(x):
            a, b = along_z(source[x])
            za[x, pl.ds(EDGE, size)] = a
            zb[x, pl.ds(EDGE, size)] = b

        @pl.loop(0, planes)
        def _(x):
            def part(ref, step):
                return ref[x, pl.ds(EDGE + start + step, count)]

            a0, a1, a2 = part(za, 0), part(za, -1) + part(za, 1), part(za, -2) + part(za, 2)
            b0, b1, b2 = part(zb, 0), part(zb, -1) + part(zb, 1), part(zb, -2) + part(zb, 2)
            yp[x, pl.ds(0, count)] = mass(a0, a1, a2)
            yq[x, pl.ds(0, count)] = mass(b0, b1, b2) + stiff(a0, a1, a2)

    def across(x, count):
        def part(ref, step):
            return ref[x + 2 + step, pl.ds(0, count)]

        q0, q1, q2 = part(yq, 0), part(yq, -1) + part(yq, 1), part(yq, -2) + part(yq, 2)
        p0, p1, p2 = part(yp, 0), part(yp, -1) + part(yp, 1), part(yp, -2) + part(yp, 2)
        return mass(q0, q1, q2) + stiff(p0, p1, p2)

    outer = pl.ds(EDGE - NEAR, rows)
    spread(field, nx + 2 * WIDE, wide, EDGE - NEAR, rows)

    @pl.loop(0, nx + 2 * NEAR)
    def _(x):
        first[x] = keep[x, outer] * across(x, rows) + shifted[x, outer] * field[x + 2, outer]

    spread(first, nx + 2 * NEAR, rows, 0, rows)

    @pl.loop(0, nx + NEAR)
    def _(x):
        second[x] = keep[x + 2, outer] * across(x, rows) + shifted[x + 2, outer] * first[x + 2]

    spread(second, nx + NEAR, rows, NEAR, ny)

    def fold(value):
        return jnp.sum(value.reshape(ny // 8, 8, nz), axis=0)

    own = pl.ds(NEAR, ny)

    def add(x, totals):
        v0 = field[x + WIDE, mid]
        v1 = first[x + NEAR, own]
        v2 = second[x + 2, own]
        v3 = keep[x + NEAR, mid] * across(x, ny) + shifted[x + NEAR, mid] * v2
        new = (v0 * v0, v0 * v1, v1 * v1, v1 * v2, v2 * v2, v2 * v3, v0, v1, v2)
        return tuple(total + fold(value) for total, value in zip(totals, new))

    totals = lax.fori_loop(0, nx, add, (jnp.zeros((8, nz), F32),) * 9)
    for place, total in enumerate(totals):
        sums[place : place + 1] = jnp.sum(total, axis=0, keepdims=True)
    count = jnp.int32(0)
    for slot in range(active.shape[0]):
        count += (active[slot] >= 0).astype(jnp.int32)
    lane = lax.broadcasted_iota(jnp.int32, (1, nz), 1)
    sums[9:10] = jnp.where(lane == 0, count.astype(F32), 0.0)
    sums[10:SUMS] = jnp.zeros((SUMS - 10, nz), F32)

    @pl.loop(0, nx + 1)
    def _(x):
        out0[x] = field[x + WIDE, pl.ds(EDGE, ny + EDGE)]
        out1[x, pl.ds(0, ny + NEAR)] = first[x + NEAR, pl.ds(NEAR, ny + NEAR)]
        out2[x, pl.ds(0, ny + NEAR)] = second[x + 2, pl.ds(NEAR, ny + NEAR)]


def two_sum(a, b):
    total = a + b
    part = total - a
    return total, (a - (total - part)) + (b - part)


def pair_add(a, b):
    total, rest = two_sum(a[0], b[0])
    return total, rest + (a[1] + b[1])


def halves(a):
    wide = 4097.0 * a
    top = wide - (wide - a)
    return top, a - top


def pair_mul(a, b):
    product = a[0] * b[0]
    a_top, a_rest = halves(a[0])
    b_top, b_rest = halves(b[0])
    rest = ((a_top * b_top - product) + a_top * b_rest + a_rest * b_top) + a_rest * b_rest
    rest = rest + (a[0] * b[1] + a[1] * b[0])
    total = product + rest
    return total, rest - (total - product)


def pair_sub(a, b):
    total, rest = two_sum(a[0], -b[0])
    rest = rest + (a[1] - b[1])
    out = total + rest
    return out, rest - (out - total)


def ratio(over, under, low, high):
    good = under > 0.0
    value = jnp.where(good, over / jnp.where(good, under, 1.0), 0.5 * (low + high))
    return jnp.minimum(jnp.maximum(value, low), high)


def coefficients(total):
    scale = 1.0 / total[0][0]
    zero = jnp.zeros_like(scale)
    g = [pair_mul(item, (scale, zero)) for item in total[:6]]
    shift = (jnp.full_like(scale, SHIFT), zero)
    h = [pair_add(g[k + 1], pair_mul(g[k], shift)) for k in range(5)]

    def minor(a, b, c, d):
        return pair_sub(pair_mul(a, b), pair_mul(c, d))

    s11 = minor(h[2], h[0], h[1], h[1])
    s12 = minor(h[3], h[0], h[1], h[2])
    s22 = minor(h[4], h[0], h[2], h[2])
    y1 = minor(g[1], h[0], h[1], g[0])
    y2 = minor(g[2], h[0], h[2], g[0])
    last = minor(s22, s11, s12, s12)
    side = minor(y2, s11, s12, y1)
    alpha = g[0][0] / h[0][0]
    l10 = h[1][0] / h[0][0]
    l20 = h[2][0] / h[0][0]
    l21 = ratio(s12[0], s11[0], l10 + (LOW - SHIFT), l10 + (HIGH - SHIFT))
    gamma1 = ratio(y1[0], s11[0], -alpha / LOW, -alpha / HIGH)
    gamma2 = ratio(side[0], last[0], -gamma1 / HIGH, -gamma1 / LOW)
    c1 = gamma1 - gamma2 * l21
    return alpha - c1 * l10 - gamma2 * l20, c1, gamma2


def sigmoid(value):
    return 1.0 / (1.0 + jnp.exp(-SHARP * value))


def finish_kernel(visible, parts, v0, v1, v2, indicator, crossing, level, weight):
    nx, ny, nz = indicator.shape
    devices = parts.shape[0]
    group = math.gcd(devices, 32)

    def gather(step, carry):
        items = [(parts[step * group + k], None) for k in range(group)]
        pairs = [two_sum(a[0], b[0]) for a, b in zip(items[::2], items[1::2])]
        while len(pairs) > 1:
            pairs = [pair_add(a, b) for a, b in zip(pairs[::2], pairs[1::2])]
        return pair_add(carry, pairs[0])

    start = (jnp.zeros((SUMS, nz), F32), jnp.zeros((SUMS, nz), F32))
    total = lax.fori_loop(0, devices // group, gather, start)
    step = nz // 2
    while step:
        total = pair_add(total, (pltpu.roll(total[0], step, 1), pltpu.roll(total[1], step, 1)))
        step //= 2
    item = [(total[0][k : k + 1], total[1][k : k + 1]) for k in range(10)]
    c0, c1, c2 = coefficients(item)
    over = c0 * (item[6][0] + item[6][1]) + c1 * (item[7][0] + item[7][1]) + c2 * (item[8][0] + item[8][1])
    iso = over / (item[9][0] * float(BLK**3))

    @pl.loop(0, nx + 1)
    def _(x):
        value = c0 * v0[x] + c1 * v1[x] + c2 * v2[x]
        level[x] = sigmoid(value - iso)

        @pl.when(x < nx)
        def _():
            indicator[x] = value[:ny]

    outside = sigmoid(-iso)
    lane = lax.broadcasted_iota(jnp.int32, (ny, nz), 1)

    @pl.loop(0, nx)
    def _(x):
        here = level[x, pl.ds(0, ny)]
        above = jnp.where(lane < nz - 1, pltpu.roll(here, nz - 1, 1), outside)
        for edge, there in enumerate((level[x + 1, pl.ds(0, ny)], level[x, pl.ds(1, ny)], above)):
            weight[edge, pl.ds(x * ny, ny)] = here * (1.0 - there) + (1.0 - here) * there

    chunk = lax.broadcasted_iota(jnp.int32, (8, nz), 1) // BLK
    bricks_z = nz // BLK
    per_row = nz // BLK

    @pl.loop(0, visible.shape[0])
    def _(slot):
        number = visible[slot]
        safe = jnp.maximum(number, 0)
        begin = (safe // bricks_z) * BLK
        column = safe % bricks_z
        used = jnp.where(number >= 0, 1.0, 0.0)
        for edge in range(3):
            for half in range(2):
                for part in range(BLK // per_row):
                    tile = jnp.zeros((8, nz), F32)
                    for row in range(per_row):
                        at = half * 8 * ny + begin + part * per_row + row
                        lines = weight[edge, pl.ds(at, 8, stride=ny)]
                        turn = lax.rem((row - column) * BLK + nz, nz)
                        tile = jnp.where(chunk == row, pltpu.roll(lines, turn, 1), tile)
                    crossing[slot, edge, pl.ds(half * 16 + part, 8, stride=2)] = tile * used


def whole(*shape):
    return jax.ShapeDtypeStruct(shape, F32)


VMEM = pl.BlockSpec(memory_space=pltpu.VMEM)
SMEM = pl.BlockSpec(memory_space=pltpu.SMEM)


def kernel(body, inputs, outputs, scratch=()):
    return pl.pallas_call(
        body,
        in_specs=[SMEM] + [VMEM] * (inputs - 1),
        out_specs=[VMEM] * len(outputs),
        out_shape=list(outputs),
        scratch_shapes=list(scratch),
        compiler_params=pltpu.CompilerParams(vmem_limit_bytes=32 * 1024 * 1024),
    )


def shift(value, axis, step):
    count = lax.axis_size(axis)
    pairs = [(k, k + step) for k in range(count) if 0 <= k + step < count]
    return lax.ppermute(value, axis, pairs)


def gather_sums(part):
    return lax.all_gather(part, ("gx", "gy"))


def body(right_side, screening, active_blocks, visible_bricks):
    nx, ny, nz = right_side.shape
    active = active_blocks.reshape(-1)
    visible = visible_bricks.reshape(-1)
    side = whole(WIDE + NEAR, ny, nz)
    edge = whole(2 * nx, EDGE, nz)
    x_low, x_high, y_low, y_high = kernel(pack_kernel, 3, (side, side, edge, edge))(
        active, right_side, screening
    )
    x_from_low = shift(x_high, "gx", 1)
    x_from_high = shift(x_low, "gx", -1)
    y_from_low = shift(y_high, "gy", 1)
    y_from_high = shift(y_low, "gy", -1)

    def corner(rows):
        return jnp.concatenate([x_from_low[:, rows], x_from_high[:, rows]], axis=0)

    c_from_low = shift(corner(slice(ny - EDGE, ny)), "gy", 1)
    c_from_high = shift(corner(slice(0, EDGE)), "gy", -1)

    wide, rows = ny + 2 * EDGE, ny + 2 * NEAR
    reach = whole(nx + 1, ny + EDGE, nz)
    v0, v1, v2, sums = kernel(
        powers_kernel,
        9,
        (reach, reach, reach, whole(SUMS, nz)),
        (
            pltpu.VMEM((nx + 2 * WIDE, wide, nz), F32),
            pltpu.VMEM((nx + 2 * NEAR, wide, nz), F32),
            pltpu.VMEM((nx + 2 * NEAR, wide, nz), F32),
            pltpu.VMEM((nx + 2 * NEAR, rows, nz), F32),
            pltpu.VMEM((nx + NEAR, rows, nz), F32),
            pltpu.VMEM((nx + 2 * WIDE, wide + EDGE, nz), F32),
            pltpu.VMEM((nx + 2 * WIDE, wide + EDGE, nz), F32),
            pltpu.VMEM((nx + 2 * WIDE, rows, nz), F32),
            pltpu.VMEM((nx + 2 * WIDE, rows, nz), F32),
        ),
    )(active, right_side, screening, x_from_low, x_from_high, y_from_low, y_from_high, c_from_low, c_from_high)
    parts = gather_sums(sums)
    slots = visible.shape[0]
    indicator, crossing = kernel(
        finish_kernel,
        5,
        (whole(nx, ny, nz), whole(slots, 3, BLK**3 // nz, nz)),
        (pltpu.VMEM((nx + 1, ny + EDGE, nz), F32), pltpu.VMEM((3, nx * ny, nz), F32)),
    )(visible, parts, v0, v1, v2)
    return indicator, crossing.reshape(slots, 1, 3, BLK**3)


def solution(mesh):
    return jax.shard_map(
        body,
        mesh=mesh,
        in_specs=(
            P("gx", "gy", None),
            P("gx", "gy", None),
            P("gx", "gy", None),
            P("gx", "gy", None),
        ),
        out_specs=(P("gx", "gy", None), P("gx", "gy", None, None)),
        check_vma=False,
    )
```

```python
import functools
import math

import jax
import jax.numpy as jnp
from jax import lax
from jax.experimental import pallas as pl
from jax.experimental.pallas import tpu as pltpu
from jax.sharding import PartitionSpec as P

BLK = 16
WIDE = 6
NEAR = 4
EDGE = 8
SHARP = 4.0
SCALE = 1.0 / 86400.0
SHIFT = 2.25
LOW, HIGH = 0.5, 7.0
SUMS = 16
F32 = jnp.float32


def mass(mid, one, two):
    return 66.0 * mid + (26.0 * one + two)


def stiff(mid, one, two):
    return 6.0 * mid - (2.0 * one + two)


def block_mask(active, slots, rows, columns):
    y = lax.broadcasted_iota(jnp.int32, (rows, columns), 0)
    z = lax.broadcasted_iota(jnp.int32, (rows, columns), 1)
    number = (y // BLK) * (columns // BLK) + z // BLK
    mask = jnp.zeros((rows, columns), F32)
    for slot in range(slots):
        mask = jnp.where(number == active[slot], 1.0, mask)
    return mask


def pack_kernel(active, right, screen, x_low, x_high, y_low, y_high):
    nx, ny, nz = right.shape
    mask = block_mask(active, active.shape[0], ny, nz)
    for x in range(nx):
        field = right[x] * mask
        weight = screen[x] * mask
        if x < WIDE:
            x_low[x] = field
        if x < NEAR:
            x_low[WIDE + x] = weight
        if x >= nx - WIDE:
            x_high[x - (nx - WIDE)] = field
        if x >= nx - NEAR:
            x_high[WIDE + x - (nx - NEAR)] = weight
        y_low[x] = field[:EDGE]
        y_low[nx + x] = weight[:EDGE]
        y_high[x] = field[ny - EDGE :]
        y_high[nx + x] = weight[ny - EDGE :]


def along_z(value):
    lane = lax.broadcasted_iota(jnp.int32, value.shape, 1)
    last = value.shape[1]

    def shifted(step):
        before = jnp.where(lane >= step, pltpu.roll(value, step, 1), 0.0)
        after = jnp.where(lane < last - step, pltpu.roll(value, last - step, 1), 0.0)
        return before + after

    one, two = shifted(1), shifted(2)
    return mass(value, one, two), stiff(value, one, two)


def powers_kernel(
    active, right, screen, x_low, x_high, y_low, y_high, c_low, c_high,
    out0, out1, out2, sums,
    field, keep, shifted, first, second, za, zb, yp, yq,
):
    nx, ny, nz = right.shape
    wide = ny + 2 * EDGE
    rows = ny + 2 * NEAR
    mask = block_mask(active, active.shape[0], ny, nz)

    def set_weight(at, span, weight):
        on = weight > 0.0
        keep[at, span] = jnp.where(on, SCALE, 0.0)
        shifted[at, span] = jnp.where(on, weight - SHIFT, 0.0)

    mid = pl.ds(EDGE, ny)
    low = pl.ds(0, EDGE)
    high = pl.ds(EDGE + ny, EDGE)
    for x in range(nx):
        field[WIDE + x, mid] = right[x] * mask
        set_weight(NEAR + x, mid, screen[x] * mask)
        for span, source in ((low, y_low), (high, y_high)):
            field[WIDE + x, span] = source[x]
            set_weight(NEAR + x, span, source[nx + x])
    for base, near, source, skip in ((0, 0, x_low, 0), (WIDE + nx, NEAR + nx, x_high, WIDE + NEAR)):
        for x in range(WIDE):
            field[base + x, mid] = source[x]
            field[base + x, low] = c_low[skip + x]
            field[base + x, high] = c_high[skip + x]
        for x in range(NEAR):
            set_weight(near + x, mid, source[WIDE + x])
            set_weight(near + x, low, c_low[skip + WIDE + x])
            set_weight(near + x, high, c_high[skip + WIDE + x])

    def spread(source, planes, size, start, count):
        @pl.loop(0, planes)
        def _(x):
            a, b = along_z(source[x])
            za[x, pl.ds(EDGE, size)] = a
            zb[x, pl.ds(EDGE, size)] = b

        @pl.loop(0, planes)
        def _(x):
            def part(ref, step):
                return ref[x, pl.ds(EDGE + start + step, count)]

            a0, a1, a2 = part(za, 0), part(za, -1) + part(za, 1), part(za, -2) + part(za, 2)
            b0, b1, b2 = part(zb, 0), part(zb, -1) + part(zb, 1), part(zb, -2) + part(zb, 2)
            yp[x, pl.ds(0, count)] = mass(a0, a1, a2)
            yq[x, pl.ds(0, count)] = mass(b0, b1, b2) + stiff(a0, a1, a2)

    def across(x, count):
        def part(ref, step):
            return ref[x + 2 + step, pl.ds(0, count)]

        q0, q1, q2 = part(yq, 0), part(yq, -1) + part(yq, 1), part(yq, -2) + part(yq, 2)
        p0, p1, p2 = part(yp, 0), part(yp, -1) + part(yp, 1), part(yp, -2) + part(yp, 2)
        return mass(q0, q1, q2) + stiff(p0, p1, p2)

    outer = pl.ds(EDGE - NEAR, rows)
    spread(field, nx + 2 * WIDE, wide, EDGE - NEAR, rows)

    @pl.loop(0, nx + 2 * NEAR)
    def _(x):
        first[x] = keep[x, outer] * across(x, rows) + shifted[x, outer] * field[x + 2, outer]

    spread(first, nx + 2 * NEAR, rows, 0, rows)

    @pl.loop(0, nx + NEAR)
    def _(x):
        second[x] = keep[x + 2, outer] * across(x, rows) + shifted[x + 2, outer] * first[x + 2]

    spread(second, nx + NEAR, rows, NEAR, ny)

    def fold(value):
        return jnp.sum(value.reshape(ny // 8, 8, nz), axis=0)

    own = pl.ds(NEAR, ny)

    def add(x, totals):
        v0 = field[x + WIDE, mid]
        v1 = first[x + NEAR, own]
        v2 = second[x + 2, own]
        v3 = keep[x + NEAR, mid] * across(x, ny) + shifted[x + NEAR, mid] * v2
        new = (v0 * v0, v0 * v1, v1 * v1, v1 * v2, v2 * v2, v2 * v3, v0, v1, v2)
        return tuple(total + fold(value) for total, value in zip(totals, new))

    totals = lax.fori_loop(0, nx, add, (jnp.zeros((8, nz), F32),) * 9)
    for place, total in enumerate(totals):
        sums[place : place + 1] = jnp.sum(total, axis=0, keepdims=True)
    count = jnp.int32(0)
    for slot in range(active.shape[0]):
        count += (active[slot] >= 0).astype(jnp.int32)
    lane = lax.broadcasted_iota(jnp.int32, (1, nz), 1)
    sums[9:10] = jnp.where(lane == 0, count.astype(F32), 0.0)
    sums[10:SUMS] = jnp.zeros((SUMS - 10, nz), F32)

    @pl.loop(0, nx + 1)
    def _(x):
        out0[x] = field[x + WIDE, pl.ds(EDGE, ny + EDGE)]
        out1[x, pl.ds(0, ny + NEAR)] = first[x + NEAR, pl.ds(NEAR, ny + NEAR)]
        out2[x, pl.ds(0, ny + NEAR)] = second[x + 2, pl.ds(NEAR, ny + NEAR)]


def two_sum(a, b):
    total = a + b
    part = total - a
    return total, (a - (total - part)) + (b - part)


def pair_add(a, b):
    total, rest = two_sum(a[0], b[0])
    return total, rest + (a[1] + b[1])


def halves(a):
    wide = 4097.0 * a
    top = wide - (wide - a)
    return top, a - top


def pair_mul(a, b):
    product = a[0] * b[0]
    a_top, a_rest = halves(a[0])
    b_top, b_rest = halves(b[0])
    rest = ((a_top * b_top - product) + a_top * b_rest + a_rest * b_top) + a_rest * b_rest
    rest = rest + (a[0] * b[1] + a[1] * b[0])
    total = product + rest
    return total, rest - (total - product)


def pair_sub(a, b):
    total, rest = two_sum(a[0], -b[0])
    rest = rest + (a[1] - b[1])
    out = total + rest
    return out, rest - (out - total)


def ratio(over, under, low, high):
    good = under > 0.0
    value = jnp.where(good, over / jnp.where(good, under, 1.0), 0.5 * (low + high))
    return jnp.minimum(jnp.maximum(value, low), high)


def coefficients(total):
    scale = 1.0 / total[0][0]
    zero = jnp.zeros_like(scale)
    g = [pair_mul(item, (scale, zero)) for item in total[:6]]
    shift = (jnp.full_like(scale, SHIFT), zero)
    h = [pair_add(g[k + 1], pair_mul(g[k], shift)) for k in range(5)]

    def minor(a, b, c, d):
        return pair_sub(pair_mul(a, b), pair_mul(c, d))

    s11 = minor(h[2], h[0], h[1], h[1])
    s12 = minor(h[3], h[0], h[1], h[2])
    s22 = minor(h[4], h[0], h[2], h[2])
    y1 = minor(g[1], h[0], h[1], g[0])
    y2 = minor(g[2], h[0], h[2], g[0])
    last = minor(s22, s11, s12, s12)
    side = minor(y2, s11, s12, y1)
    alpha = g[0][0] / h[0][0]
    l10 = h[1][0] / h[0][0]
    l20 = h[2][0] / h[0][0]
    l21 = ratio(s12[0], s11[0], l10 + (LOW - SHIFT), l10 + (HIGH - SHIFT))
    gamma1 = ratio(y1[0], s11[0], -alpha / LOW, -alpha / HIGH)
    gamma2 = ratio(side[0], last[0], -gamma1 / HIGH, -gamma1 / LOW)
    c1 = gamma1 - gamma2 * l21
    return alpha - c1 * l10 - gamma2 * l20, c1, gamma2


def sigmoid(value):
    return 1.0 / (1.0 + jnp.exp(-SHARP * value))


def finish_kernel(visible, parts, v0, v1, v2, indicator, crossing, level, weight):
    nx, ny, nz = indicator.shape
    devices = parts.shape[0]
    group = math.gcd(devices, 32)

    def gather(step, carry):
        items = [(parts[step * group + k], None) for k in range(group)]
        pairs = [two_sum(a[0], b[0]) for a, b in zip(items[::2], items[1::2])]
        while len(pairs) > 1:
            pairs = [pair_add(a, b) for a, b in zip(pairs[::2], pairs[1::2])]
        return pair_add(carry, pairs[0])

    start = (jnp.zeros((SUMS, nz), F32), jnp.zeros((SUMS, nz), F32))
    total = lax.fori_loop(0, devices // group, gather, start)
    step = nz // 2
    while step:
        total = pair_add(total, (pltpu.roll(total[0], step, 1), pltpu.roll(total[1], step, 1)))
        step //= 2
    item = [(total[0][k : k + 1], total[1][k : k + 1]) for k in range(10)]
    c0, c1, c2 = coefficients(item)
    over = c0 * (item[6][0] + item[6][1]) + c1 * (item[7][0] + item[7][1]) + c2 * (item[8][0] + item[8][1])
    iso = over / (item[9][0] * float(BLK**3))

    @pl.loop(0, nx + 1)
    def _(x):
        value = c0 * v0[x] + c1 * v1[x] + c2 * v2[x]
        level[x] = sigmoid(value - iso)

        @pl.when(x < nx)
        def _():
            indicator[x] = value[:ny]

    outside = sigmoid(-iso)
    lane = lax.broadcasted_iota(jnp.int32, (ny, nz), 1)

    @pl.loop(0, nx)
    def _(x):
        here = level[x, pl.ds(0, ny)]
        above = jnp.where(lane < nz - 1, pltpu.roll(here, nz - 1, 1), outside)
        for edge, there in enumerate((level[x + 1, pl.ds(0, ny)], level[x, pl.ds(1, ny)], above)):
            weight[edge, pl.ds(x * ny, ny)] = here * (1.0 - there) + (1.0 - here) * there

    chunk = lax.broadcasted_iota(jnp.int32, (8, nz), 1) // BLK
    bricks_z = nz // BLK
    per_row = nz // BLK

    @pl.loop(0, visible.shape[0])
    def _(slot):
        number = visible[slot]
        safe = jnp.maximum(number, 0)
        begin = (safe // bricks_z) * BLK
        column = safe % bricks_z
        used = jnp.where(number >= 0, 1.0, 0.0)
        for edge in range(3):
            for half in range(2):
                for part in range(BLK // per_row):
                    tile = jnp.zeros((8, nz), F32)
                    for row in range(per_row):
                        at = half * 8 * ny + begin + part * per_row + row
                        lines = weight[edge, pl.ds(at, 8, stride=ny)]
                        turn = lax.rem((row - column) * BLK + nz, nz)
                        tile = jnp.where(chunk == row, pltpu.roll(lines, turn, 1), tile)
                    crossing[slot, edge, pl.ds(half * 16 + part, 8, stride=2)] = tile * used


def whole(*shape):
    return jax.ShapeDtypeStruct(shape, F32)


VMEM = pl.BlockSpec(memory_space=pltpu.VMEM)
SMEM = pl.BlockSpec(memory_space=pltpu.SMEM)


def kernel(body, inputs, outputs, scratch=()):
    return pl.pallas_call(
        body,
        in_specs=[SMEM] + [VMEM] * (inputs - 1),
        out_specs=[VMEM] * len(outputs),
        out_shape=list(outputs),
        scratch_shapes=list(scratch),
        compiler_params=pltpu.CompilerParams(vmem_limit_bytes=32 * 1024 * 1024),
    )


def shift(value, axis, step):
    count = lax.axis_size(axis)
    pairs = [(k, k + step) for k in range(count) if 0 <= k + step < count]
    return lax.ppermute(value, axis, pairs)


def gather_sums(part):
    count = lax.axis_size("gx") * lax.axis_size("gy")
    return lax.all_to_all(jnp.broadcast_to(part, (count,) + part.shape), ("gx", "gy"), 0, 0)


def body(right_side, screening, active_blocks, visible_bricks):
    nx, ny, nz = right_side.shape
    active = active_blocks.reshape(-1)
    visible = visible_bricks.reshape(-1)
    side = whole(WIDE + NEAR, ny, nz)
    edge = whole(2 * nx, EDGE, nz)
    x_low, x_high, y_low, y_high = kernel(pack_kernel, 3, (side, side, edge, edge))(
        active, right_side, screening
    )
    x_from_low = shift(x_high, "gx", 1)
    x_from_high = shift(x_low, "gx", -1)
    y_from_low = shift(y_high, "gy", 1)
    y_from_high = shift(y_low, "gy", -1)

    def corner(rows):
        return jnp.concatenate([x_from_low[:, rows], x_from_high[:, rows]], axis=0)

    c_from_low = shift(corner(slice(ny - EDGE, ny)), "gy", 1)
    c_from_high = shift(corner(slice(0, EDGE)), "gy", -1)

    wide, rows = ny + 2 * EDGE, ny + 2 * NEAR
    reach = whole(nx + 1, ny + EDGE, nz)
    v0, v1, v2, sums = kernel(
        powers_kernel,
        9,
        (reach, reach, reach, whole(SUMS, nz)),
        (
            pltpu.VMEM((nx + 2 * WIDE, wide, nz), F32),
            pltpu.VMEM((nx + 2 * NEAR, wide, nz), F32),
            pltpu.VMEM((nx + 2 * NEAR, wide, nz), F32),
            pltpu.VMEM((nx + 2 * NEAR, rows, nz), F32),
            pltpu.VMEM((nx + NEAR, rows, nz), F32),
            pltpu.VMEM((nx + 2 * WIDE, wide + EDGE, nz), F32),
            pltpu.VMEM((nx + 2 * WIDE, wide + EDGE, nz), F32),
            pltpu.VMEM((nx + 2 * WIDE, rows, nz), F32),
            pltpu.VMEM((nx + 2 * WIDE, rows, nz), F32),
        ),
    )(active, right_side, screening, x_from_low, x_from_high, y_from_low, y_from_high, c_from_low, c_from_high)
    parts = gather_sums(sums)
    slots = visible.shape[0]
    indicator, crossing = kernel(
        finish_kernel,
        5,
        (whole(nx, ny, nz), whole(slots, 3, BLK**3 // nz, nz)),
        (pltpu.VMEM((nx + 1, ny + EDGE, nz), F32), pltpu.VMEM((3, nx * ny, nz), F32)),
    )(visible, parts, v0, v1, v2)
    return indicator, crossing.reshape(slots, 1, 3, BLK**3)


def solution(mesh):
    return jax.shard_map(
        body,
        mesh=mesh,
        in_specs=(
            P("gx", "gy", None),
            P("gx", "gy", None),
            P("gx", "gy", None),
            P("gx", "gy", None),
        ),
        out_specs=(P("gx", "gy", None), P("gx", "gy", None, None)),
        check_vma=False,
    )
```

```python
import functools

import jax
import jax.numpy as jnp
from jax import lax
from jax.experimental import pallas as pl
from jax.experimental.pallas import tpu as pltpu
from jax.sharding import PartitionSpec as P

BLK = 16
WIDE = 6
NEAR = 4
EDGE = 8
SHARP = 4.0
SCALE = 1.0 / 86400.0
SHIFT = 2.25
LOW, HIGH = 0.5, 7.0
SUMS = 16
F32 = jnp.float32


def mass(mid, one, two):
    return 66.0 * mid + (26.0 * one + two)


def stiff(mid, one, two):
    return 6.0 * mid - (2.0 * one + two)


def block_mask(active, slots, rows, columns):
    y = lax.broadcasted_iota(jnp.int32, (rows, columns), 0)
    z = lax.broadcasted_iota(jnp.int32, (rows, columns), 1)
    number = (y // BLK) * (columns // BLK) + z // BLK
    mask = jnp.zeros((rows, columns), F32)
    for slot in range(slots):
        mask = jnp.where(number == active[slot], 1.0, mask)
    return mask


def on_odd():
    return lax.rem(lax.axis_index("gx"), 2)


def pack_kernel(active_hbm, right_hbm, screen_hbm, field, weight, cross, chip, active, right, screen, sems):
    copies = [
        pltpu.make_async_copy(source, target, sems.at[k])
        for k, (source, target) in enumerate(((active_hbm, active), (right_hbm, right), (screen_hbm, screen)))
    ]
    for copy in copies:
        copy.start()
    nx, ny, nz = right.shape
    copies[0].wait()
    mask = block_mask(active, active.shape[0], ny, nz)
    odd = on_odd()
    for copy, source, target, wide, base in (
        (copies[1], right, field, WIDE, 0),
        (copies[2], screen, weight, NEAR, WIDE),
    ):
        copy.wait()
        for x in range(nx):
            target[x] = source[x] * mask
        upper = nx - wide
        for x in range(wide):
            cross[base + x] = source[odd * upper + x] * mask
            chip[base + x] = source[(1 - odd) * upper + x] * mask


def rim_kernel(field, weight, cross, chip, out):
    nx, ny, nz = field.shape
    odd = on_odd()
    me = lax.axis_index("gy")

    def write(place, top_field, top_weight):
        def put(row, value, wide, top):
            out[place, pl.ds(row, wide)] = value[top : top + wide]

        for x in range(nx):
            put((WIDE + x) * WIDE, field[x], WIDE, top_field)
            put((nx + 2 * WIDE) * WIDE + (NEAR + x) * NEAR, weight[x], NEAR, top_weight)
        for source, side in ((cross, odd), (chip, 1 - odd)):
            for x in range(WIDE):
                put((side * (nx + WIDE) + x) * WIDE, source[x], WIDE, top_field)
            for x in range(NEAR):
                put((nx + 2 * WIDE) * WIDE + (side * (nx + NEAR) + x) * NEAR, source[WIDE + x], NEAR, top_weight)

    @pl.when(me > 0)
    def _():
        write(me - 1, 0, 0)

    @pl.when(me < out.shape[0] - 1)
    def _():
        write(me + 1, ny - WIDE, ny - NEAR)


def along_z(value):
    lane = lax.broadcasted_iota(jnp.int32, value.shape, 1)
    last = value.shape[1]

    def shifted(step):
        before = jnp.where(lane >= step, pltpu.roll(value, step, 1), 0.0)
        after = jnp.where(lane < last - step, pltpu.roll(value, last - step, 1), 0.0)
        return before + after

    one, two = shifted(1), shifted(2)
    return mass(value, one, two), stiff(value, one, two)


def powers_kernel(
    own_field, own_weight, cross, chip, rim,
    out0, out1, out2, sums,
    field, keep, shifted, first, second, za, zb, yp, yq,
):
    nx, ny, nz = own_field.shape
    wide = ny + 2 * EDGE
    rows = ny + 2 * NEAR
    odd = on_odd()
    me = lax.axis_index("gy")

    def set_weight(at, span, weight):
        on = weight > 0.0
        keep[at, span] = jnp.where(on, SCALE, 0.0)
        shifted[at, span] = jnp.where(on, weight - SHIFT, 0.0)

    mid = pl.ds(EDGE, ny)
    for x in range(nx):
        field[WIDE + x, mid] = own_field[x]
        set_weight(NEAR + x, mid, own_weight[x])
    for source, side in ((cross, odd), (chip, 1 - odd)):
        for x in range(WIDE):
            field[side * (nx + WIDE) + x, mid] = source[x]
        for x in range(NEAR):
            set_weight(side * (nx + NEAR) + x, mid, source[WIDE + x])

    def read(place, there, top_field, top_weight):
        block = jnp.where(there, place, 0)

        def part(row, count):
            return jnp.where(there, rim[block, pl.ds(row, count)], 0.0)

        @pl.loop(0, nx + 2 * WIDE)
        def _(x):
            field[x, pl.ds(top_field, WIDE)] = part(x * WIDE, WIDE)

        @pl.loop(0, nx + 2 * NEAR)
        def _(x):
            set_weight(x, pl.ds(top_weight, NEAR), part((nx + 2 * WIDE) * WIDE + x * NEAR, NEAR))

    read(me - 1, me > 0, EDGE - WIDE, EDGE - NEAR)
    read(me + 1, me < rim.shape[0] - 1, EDGE + ny, EDGE + ny)

    def spread(source, planes, size, start, count):
        @pl.loop(0, planes)
        def _(x):
            a, b = along_z(source[x])
            za[x, pl.ds(EDGE, size)] = a
            zb[x, pl.ds(EDGE, size)] = b

        @pl.loop(0, planes)
        def _(x):
            def part(ref, step):
                return ref[x, pl.ds(EDGE + start + step, count)]

            a0, a1, a2 = part(za, 0), part(za, -1) + part(za, 1), part(za, -2) + part(za, 2)
            b0, b1, b2 = part(zb, 0), part(zb, -1) + part(zb, 1), part(zb, -2) + part(zb, 2)
            yp[x, pl.ds(0, count)] = mass(a0, a1, a2)
            yq[x, pl.ds(0, count)] = mass(b0, b1, b2) + stiff(a0, a1, a2)

    def across(x, count):
        def part(ref, step):
            return ref[x + 2 + step, pl.ds(0, count)]

        q0, q1, q2 = part(yq, 0), part(yq, -1) + part(yq, 1), part(yq, -2) + part(yq, 2)
        p0, p1, p2 = part(yp, 0), part(yp, -1) + part(yp, 1), part(yp, -2) + part(yp, 2)
        return mass(q0, q1, q2) + stiff(p0, p1, p2)

    outer = pl.ds(EDGE - NEAR, rows)
    spread(field, nx + 2 * WIDE, wide, EDGE - NEAR, rows)

    @pl.loop(0, nx + 2 * NEAR)
    def _(x):
        first[x] = keep[x, outer] * across(x, rows) + shifted[x, outer] * field[x + 2, outer]

    spread(first, nx + 2 * NEAR, rows, 0, rows)

    @pl.loop(0, nx + NEAR)
    def _(x):
        second[x] = keep[x + 2, outer] * across(x, rows) + shifted[x + 2, outer] * first[x + 2]

    spread(second, nx + NEAR, rows, NEAR, ny)

    def fold(value):
        return jnp.sum(value.reshape(ny // 8, 8, nz), axis=0)

    own = pl.ds(NEAR, ny)

    def add(x, totals):
        v0 = field[x + WIDE, mid]
        v1 = first[x + NEAR, own]
        v2 = second[x + 2, own]
        v3 = keep[x + NEAR, mid] * across(x, ny) + shifted[x + NEAR, mid] * v2
        on = jnp.where(keep[x + NEAR, mid] > 0.0, 1.0, 0.0)
        new = (v0 * v0, v0 * v1, v1 * v1, v1 * v2, v2 * v2, v2 * v3, v0, v1, v2, on)
        return tuple(total + fold(value) for total, value in zip(totals, new))

    totals = lax.fori_loop(0, nx, add, (jnp.zeros((8, nz), F32),) * 10)
    row = lax.broadcasted_iota(jnp.int32, (SUMS, nz), 0)
    lane = lax.broadcasted_iota(jnp.int32, (SUMS, nz), 1)
    lines = jnp.zeros((SUMS, nz), F32)
    for place, total in enumerate(totals):
        lines = jnp.where(row == place, jnp.sum(total, axis=0, keepdims=True), lines)
    pair = (lines, jnp.zeros_like(lines))
    step = nz // 2
    while step:
        pair = pair_add(pair, (pltpu.roll(pair[0], step, 1), pltpu.roll(pair[1], step, 1)))
        step //= 2
    spot = jnp.where(lane == row, pair[0], jnp.where(lane == row + SUMS, pair[1], 0.0))
    sums[...] = jnp.sum(spot, axis=0, keepdims=True)

    @pl.loop(0, nx + 1)
    def _(x):
        out0[x] = field[x + WIDE, pl.ds(EDGE, ny + EDGE)]
        out1[x, pl.ds(0, ny + NEAR)] = first[x + NEAR, pl.ds(NEAR, ny + NEAR)]
        out2[x, pl.ds(0, ny + NEAR)] = second[x + 2, pl.ds(NEAR, ny + NEAR)]


def two_sum(a, b):
    total = a + b
    part = total - a
    return total, (a - (total - part)) + (b - part)


def pair_add(a, b):
    total, rest = two_sum(a[0], b[0])
    return total, rest + (a[1] + b[1])


def halves(a):
    wide = 4097.0 * a
    top = wide - (wide - a)
    return top, a - top


def pair_mul(a, b):
    product = a[0] * b[0]
    a_top, a_rest = halves(a[0])
    b_top, b_rest = halves(b[0])
    rest = ((a_top * b_top - product) + a_top * b_rest + a_rest * b_top) + a_rest * b_rest
    rest = rest + (a[0] * b[1] + a[1] * b[0])
    total = product + rest
    return total, rest - (total - product)


def pair_sub(a, b):
    total, rest = two_sum(a[0], -b[0])
    rest = rest + (a[1] - b[1])
    out = total + rest
    return out, rest - (out - total)


def ratio(over, under, low, high):
    good = under > 0.0
    value = jnp.where(good, over / jnp.where(good, under, 1.0), 0.5 * (low + high))
    return jnp.minimum(jnp.maximum(value, low), high)


def coefficients(total):
    scale = 1.0 / total[0][0]
    zero = jnp.zeros_like(scale)
    g = [pair_mul(item, (scale, zero)) for item in total[:6]]
    shift = (jnp.full_like(scale, SHIFT), zero)
    h = [pair_add(g[k + 1], pair_mul(g[k], shift)) for k in range(5)]

    def minor(a, b, c, d):
        return pair_sub(pair_mul(a, b), pair_mul(c, d))

    s11 = minor(h[2], h[0], h[1], h[1])
    s12 = minor(h[3], h[0], h[1], h[2])
    s22 = minor(h[4], h[0], h[2], h[2])
    y1 = minor(g[1], h[0], h[1], g[0])
    y2 = minor(g[2], h[0], h[2], g[0])
    last = minor(s22, s11, s12, s12)
    side = minor(y2, s11, s12, y1)
    alpha = g[0][0] / h[0][0]
    l10 = h[1][0] / h[0][0]
    l20 = h[2][0] / h[0][0]
    l21 = ratio(s12[0], s11[0], l10 + (LOW - SHIFT), l10 + (HIGH - SHIFT))
    gamma1 = ratio(y1[0], s11[0], -alpha / LOW, -alpha / HIGH)
    gamma2 = ratio(side[0], last[0], -gamma1 / HIGH, -gamma1 / LOW)
    c1 = gamma1 - gamma2 * l21
    return alpha - c1 * l10 - gamma2 * l20, c1, gamma2


def sigmoid(value):
    return 1.0 / (1.0 + jnp.exp(-SHARP * value))


def finish_kernel(visible_hbm, parts, v0, v1, v2, indicator, crossing, visible, level, weight, sem):
    nx, ny, nz = indicator.shape
    copy = pltpu.make_async_copy(visible_hbm, visible, sem)
    copy.start()
    devices = parts.shape[0]
    tiles = [parts[pl.ds(8 * k, 8)] for k in range(devices // 8)]
    pairs = [(tile, pltpu.roll(tile, nz - SUMS, 1)) for tile in tiles]
    while len(pairs) > 1:
        pairs = [pair_add(a, b) for a, b in zip(pairs[::2], pairs[1::2])]
    total = pairs[0]
    for step in (4, 2, 1):
        total = pair_add(total, (pltpu.roll(total[0], step, 0), pltpu.roll(total[1], step, 0)))

    def spread(value, k):
        return jnp.broadcast_to(value[0:1, k : k + 1], (1, nz))

    item = [(spread(total[0], k), spread(total[1], k)) for k in range(10)]
    c0, c1, c2 = coefficients(item)
    over = c0 * (item[6][0] + item[6][1]) + c1 * (item[7][0] + item[7][1]) + c2 * (item[8][0] + item[8][1])
    iso = over / item[9][0]

    @pl.loop(0, nx + 1)
    def _(x):
        value = c0 * v0[x] + c1 * v1[x] + c2 * v2[x]
        level[x] = sigmoid(value - iso)

        @pl.when(x < nx)
        def _():
            indicator[x] = value[:ny]

    outside = sigmoid(-iso)
    lane = lax.broadcasted_iota(jnp.int32, (ny, nz), 1)

    @pl.loop(0, nx)
    def _(x):
        here = level[x, pl.ds(0, ny)]
        above = jnp.where(lane < nz - 1, pltpu.roll(here, nz - 1, 1), outside)
        for edge, there in enumerate((level[x + 1, pl.ds(0, ny)], level[x, pl.ds(1, ny)], above)):
            weight[edge, pl.ds(x * ny, ny)] = here * (1.0 - there) + (1.0 - here) * there

    chunk = lax.broadcasted_iota(jnp.int32, (8, nz), 1) // BLK
    bricks_z = nz // BLK
    per_row = nz // BLK

    copy.wait()

    @pl.loop(0, visible.shape[0])
    def _(slot):
        number = visible[slot]
        safe = jnp.maximum(number, 0)
        begin = (safe // bricks_z) * BLK
        column = safe % bricks_z
        used = jnp.where(number >= 0, 1.0, 0.0)
        for edge in range(3):
            for half in range(2):
                for part in range(BLK // per_row):
                    tile = jnp.zeros((8, nz), F32)
                    for row in range(per_row):
                        at = half * 8 * ny + begin + part * per_row + row
                        lines = weight[edge, pl.ds(at, 8, stride=ny)]
                        turn = lax.rem((row - column) * BLK + nz, nz)
                        tile = jnp.where(chunk == row, pltpu.roll(lines, turn, 1), tile)
                    crossing[slot, edge, pl.ds(half * 16 + part, 8, stride=2)] = tile * used


def whole(*shape):
    return jax.ShapeDtypeStruct(shape, F32)


VMEM = pl.BlockSpec(memory_space=pltpu.VMEM)


HBM = pl.BlockSpec(memory_space=pltpu.HBM)


def kernel(body, inputs, outputs, scratch=()):
    return pl.pallas_call(
        body,
        in_specs=list(inputs),
        out_specs=[VMEM] * len(outputs),
        out_shape=list(outputs),
        scratch_shapes=list(scratch),
        compiler_params=pltpu.CompilerParams(vmem_limit_bytes=32 * 1024 * 1024),
    )


def swap(value, axis, first):
    count = lax.axis_size(axis)
    pairs = [(k, k + 1) for k in range(first, count - 1, 2)]
    return lax.ppermute(value, axis, pairs + [(b, a) for a, b in pairs])


def body(right_side, screening, active_blocks, visible_bricks):
    nx, ny, nz = right_side.shape
    active = active_blocks.reshape(-1)
    visible = visible_bricks.reshape(-1)
    devices = lax.axis_size("gx") * lax.axis_size("gy")
    slab, side = whole(nx, ny, nz), whole(WIDE + NEAR, ny, nz)
    field, weight, cross, chip = kernel(
        pack_kernel,
        (HBM, HBM, HBM),
        (slab, slab, side, side),
        (
            pltpu.SMEM(active.shape, jnp.int32),
            pltpu.VMEM(slab.shape, F32),
            pltpu.VMEM(slab.shape, F32),
            pltpu.SemaphoreType.DMA((3,)),
        ),
    )(active, right_side, screening)
    cross = swap(cross, "gx", 1)
    chip = swap(chip, "gx", 0)
    planes, near = nx + 2 * WIDE, nx + 2 * NEAR
    wide, rows = ny + 2 * EDGE, ny + 2 * NEAR
    (rim,) = kernel(
        rim_kernel, (VMEM,) * 4, (whole(lax.axis_size("gy"), planes * WIDE + near * NEAR, nz),)
    )(field, weight, cross, chip)
    rim = lax.all_to_all(rim, "gy", 0, 0)
    reach = whole(nx + 1, ny + EDGE, nz)
    v0, v1, v2, sums = kernel(
        powers_kernel,
        (VMEM,) * 5,
        (reach, reach, reach, whole(1, nz)),
        (
            pltpu.VMEM((planes, wide, nz), F32),
            pltpu.VMEM((near, wide, nz), F32),
            pltpu.VMEM((near, wide, nz), F32),
            pltpu.VMEM((near, rows, nz), F32),
            pltpu.VMEM((nx + NEAR, rows, nz), F32),
            pltpu.VMEM((planes, wide + EDGE, nz), F32),
            pltpu.VMEM((planes, wide + EDGE, nz), F32),
            pltpu.VMEM((planes, rows, nz), F32),
            pltpu.VMEM((planes, rows, nz), F32),
        ),
    )(field, weight, cross, chip, rim)
    parts = lax.all_to_all(jnp.broadcast_to(sums, (devices, 1, nz)), ("gx", "gy"), 0, 0)
    slots = visible.shape[0]
    indicator, crossing = kernel(
        finish_kernel,
        (HBM,) + (VMEM,) * 4,
        (slab, whole(slots, 3, BLK**3 // nz, nz)),
        (
            pltpu.SMEM(visible.shape, jnp.int32),
            pltpu.VMEM((nx + 1, ny + EDGE, nz), F32),
            pltpu.VMEM((3, nx * ny, nz), F32),
            pltpu.SemaphoreType.DMA,
        ),
    )(visible, parts.reshape(devices, nz), v0, v1, v2)
    return indicator, crossing.reshape(slots, 1, 3, BLK**3)


def solution(mesh):
    return jax.shard_map(
        body,
        mesh=mesh,
        in_specs=(
            P("gx", "gy", None),
            P("gx", "gy", None),
            P("gx", "gy", None),
            P("gx", "gy", None),
        ),
        out_specs=(P("gx", "gy", None), P("gx", "gy", None, None)),
        check_vma=False,
    )
```

```python
import functools

import jax
import jax.numpy as jnp
from jax import lax
from jax.experimental import pallas as pl
from jax.experimental.pallas import tpu as pltpu
from jax.sharding import PartitionSpec as P

BLK = 16
WIDE = 6
NEAR = 4
EDGE = 8
SHARP = 4.0
SCALE = 1.0 / 86400.0
SHIFT = 2.25
LOW, HIGH = 0.5, 7.0
SUMS = 16
GRANT = 58
F32 = jnp.float32


def mass(mid, one, two):
    return 66.0 * mid + (26.0 * one + two)


def stiff(mid, one, two):
    return 6.0 * mid - (2.0 * one + two)


def block_mask(active, slots, rows, columns):
    y = lax.broadcasted_iota(jnp.int32, (rows, columns), 0)
    z = lax.broadcasted_iota(jnp.int32, (rows, columns), 1)
    number = (y // BLK) * (columns // BLK) + z // BLK
    mask = jnp.zeros((rows, columns), F32)
    for slot in range(slots):
        mask = jnp.where(number == active[slot], 1.0, mask)
    return mask


def on_odd():
    return lax.rem(lax.axis_index("gx"), 2)


def pack_kernel(active_hbm, right_hbm, screen_hbm, rim, active, right, screen, sems):
    nx, ny, nz = right_hbm.shape
    arrays = ((right_hbm, right, WIDE, 0), (screen_hbm, screen, NEAR, nx * WIDE))
    copies = [pltpu.make_async_copy(active_hbm, active, sems.at[0])]
    for k, (source, target, _, _) in enumerate(arrays):
        for high in range(2):
            rows = pl.ds(high * (ny - EDGE), EDGE)
            copies.append(pltpu.make_async_copy(source.at[:, rows], target.at[high], sems.at[1 + 2 * k + high]))
    for copy in copies:
        copy.start()
    me, last = lax.axis_index("gy"), rim.shape[0] - 1
    copies[0].wait()
    mask = block_mask(active, active.shape[0], ny, nz)
    for copy in copies[1:]:
        copy.wait()
    for _, source, wide, base in arrays:

        def write(place, high, top):
            part = mask[high * (ny - EDGE) :][:EDGE]
            for x in range(nx):
                value = source[high, x] * part
                rim[place, base + x * wide : base + (x + 1) * wide] = value[top : top + wide]

        pl.when(me > 0)(functools.partial(write, me - 1, 0, 0))
        pl.when(me < last)(functools.partial(write, me + 1, 1, EDGE - wide))


def widen_kernel(active_in, visible, right, screen, rim, field, weight, cross, chip, plan, active, sem):
    copy = pltpu.make_async_copy(active_in, active, sem)
    copy.start()
    nx, ny, nz = right.shape
    me, last = lax.axis_index("gy"), rim.shape[0] - 1
    arrays = ((field, WIDE, 0), (weight, NEAR, nx * WIDE))

    def read(place, there, low):
        block = jnp.where(there, place, 0)
        for target, wide, base in arrays:
            top = EDGE - wide if low else EDGE + ny
            for x in range(nx):
                value = rim[block, base + x * wide : base + (x + 1) * wide]
                target[x, top : top + wide] = jnp.where(there, value, 0.0)

    read(me - 1, me > 0, True)
    read(me + 1, me < last, False)
    plan[...] = visible[...]
    copy.wait()
    mask = block_mask(active, active.shape[0], ny, nz)
    for x in range(nx):
        field[x, EDGE : EDGE + ny] = right[x] * mask
        weight[x, EDGE : EDGE + ny] = screen[x] * mask
    odd = lax.rem(lax.axis_index("gx"), 2)
    for target, high in ((cross, odd), (chip, 1 - odd)):
        for x in range(WIDE):
            target[x] = field[high * (nx - WIDE) + x]
        for x in range(NEAR):
            target[WIDE + x] = weight[high * (nx - NEAR) + x]


def along_z(value):
    lane = lax.broadcasted_iota(jnp.int32, value.shape, 1)
    last = value.shape[1]

    def shifted(step):
        before = jnp.where(lane >= step, pltpu.roll(value, step, 1), 0.0)
        after = jnp.where(lane < last - step, pltpu.roll(value, last - step, 1), 0.0)
        return before + after

    one, two = shifted(1), shifted(2)
    return mass(value, one, two), stiff(value, one, two)


def powers_kernel(
    own_field, own_weight, cross, chip,
    out0, out1, out2, sums,
    field, keep, shifted, first, second, za, zb, yp, yq,
):
    nx, wide, nz = own_field.shape
    ny = wide - 2 * EDGE
    rows = ny + 2 * NEAR
    odd = lax.rem(lax.axis_index("gx"), 2)

    def set_weight(at, weight):
        on = weight > 0.0
        keep[at] = jnp.where(on, SCALE, 0.0)
        shifted[at] = jnp.where(on, weight - SHIFT, 0.0)

    mid = pl.ds(EDGE, ny)
    for x in range(nx):
        field[WIDE + x] = own_field[x]
        set_weight(NEAR + x, own_weight[x])
    for source, high in ((cross, odd), (chip, 1 - odd)):
        for x in range(WIDE):
            field[high * (nx + WIDE) + x] = source[x]
        for x in range(NEAR):
            set_weight(high * (nx + NEAR) + x, source[WIDE + x])

    def spread(source, planes, size, start, count):
        @pl.loop(0, planes, unroll=4)
        def _(x):
            a, b = along_z(source[x])
            za[x, pl.ds(EDGE, size)] = a
            zb[x, pl.ds(EDGE, size)] = b

        @pl.loop(0, planes, unroll=4)
        def _(x):
            def part(ref, step):
                return ref[x, pl.ds(EDGE + start + step, count)]

            a0, a1, a2 = part(za, 0), part(za, -1) + part(za, 1), part(za, -2) + part(za, 2)
            b0, b1, b2 = part(zb, 0), part(zb, -1) + part(zb, 1), part(zb, -2) + part(zb, 2)
            yp[x, pl.ds(0, count)] = mass(a0, a1, a2)
            yq[x, pl.ds(0, count)] = mass(b0, b1, b2) + stiff(a0, a1, a2)

    def across(x, count):
        def part(ref, step):
            return ref[x + 2 + step, pl.ds(0, count)]

        q0, q1, q2 = part(yq, 0), part(yq, -1) + part(yq, 1), part(yq, -2) + part(yq, 2)
        p0, p1, p2 = part(yp, 0), part(yp, -1) + part(yp, 1), part(yp, -2) + part(yp, 2)
        return mass(q0, q1, q2) + stiff(p0, p1, p2)

    outer = pl.ds(EDGE - NEAR, rows)
    spread(field, nx + 2 * WIDE, wide, EDGE - NEAR, rows)

    @pl.loop(0, nx + 2 * NEAR, unroll=4)
    def _(x):
        first[x] = keep[x, outer] * across(x, rows) + shifted[x, outer] * field[x + 2, outer]

    spread(first, nx + 2 * NEAR, rows, 0, rows)

    @pl.loop(0, nx + NEAR, unroll=4)
    def _(x):
        second[x] = keep[x + 2, outer] * across(x, rows) + shifted[x + 2, outer] * first[x + 2]

    spread(second, nx + NEAR, rows, NEAR, ny)

    def fold(value):
        return jnp.sum(value.reshape(ny // 8, 8, nz), axis=0)

    own = pl.ds(NEAR, ny)

    def add(x, totals):
        v0 = field[x + WIDE, mid]
        v1 = first[x + NEAR, own]
        v2 = second[x + 2, own]
        v3 = keep[x + NEAR, mid] * across(x, ny) + shifted[x + NEAR, mid] * v2
        on = jnp.where(keep[x + NEAR, mid] > 0.0, 1.0, 0.0)
        new = (v0 * v0, v0 * v1, v1 * v1, v1 * v2, v2 * v2, v2 * v3, v0, v1, v2, on)
        return tuple(total + fold(value) for total, value in zip(totals, new))

    totals = lax.fori_loop(0, nx, add, (jnp.zeros((8, nz), F32),) * 10, unroll=4)
    row = lax.broadcasted_iota(jnp.int32, (SUMS, nz), 0)
    lane = lax.broadcasted_iota(jnp.int32, (SUMS, nz), 1)
    lines = jnp.zeros((SUMS, nz), F32)
    for place, total in enumerate(totals):
        lines = jnp.where(row == place, jnp.sum(total, axis=0, keepdims=True), lines)
    pair = (lines, jnp.zeros_like(lines))
    step = nz // 2
    while step:
        pair = pair_add(pair, (pltpu.roll(pair[0], step, 1), pltpu.roll(pair[1], step, 1)))
        step //= 2
    spot = jnp.where(lane == row, pair[0], jnp.where(lane == row + SUMS, pair[1], 0.0))
    sums[...] = jnp.sum(spot, axis=0, keepdims=True)

    @pl.loop(0, nx + 1)
    def _(x):
        out0[x] = field[x + WIDE, pl.ds(EDGE, ny + EDGE)]
        out1[x, pl.ds(0, ny + NEAR)] = first[x + NEAR, pl.ds(NEAR, ny + NEAR)]
        out2[x, pl.ds(0, ny + NEAR)] = second[x + 2, pl.ds(NEAR, ny + NEAR)]


def two_sum(a, b):
    total = a + b
    part = total - a
    return total, (a - (total - part)) + (b - part)


def pair_add(a, b):
    total, rest = two_sum(a[0], b[0])
    return total, rest + (a[1] + b[1])


def halves(a):
    wide = 4097.0 * a
    top = wide - (wide - a)
    return top, a - top


def pair_mul(a, b):
    product = a[0] * b[0]
    a_top, a_rest = halves(a[0])
    b_top, b_rest = halves(b[0])
    rest = ((a_top * b_top - product) + a_top * b_rest + a_rest * b_top) + a_rest * b_rest
    rest = rest + (a[0] * b[1] + a[1] * b[0])
    total = product + rest
    return total, rest - (total - product)


def pair_sub(a, b):
    total, rest = two_sum(a[0], -b[0])
    rest = rest + (a[1] - b[1])
    out = total + rest
    return out, rest - (out - total)


def ratio(over, under, low, high):
    good = under > 0.0
    value = jnp.where(good, over / jnp.where(good, under, 1.0), 0.5 * (low + high))
    return jnp.minimum(jnp.maximum(value, low), high)


def coefficients(total):
    scale = 1.0 / total[0][0]
    zero = jnp.zeros_like(scale)
    g = [pair_mul(item, (scale, zero)) for item in total[:6]]
    shift = (jnp.full_like(scale, SHIFT), zero)
    h = [pair_add(g[k + 1], pair_mul(g[k], shift)) for k in range(5)]

    def minor(a, b, c, d):
        return pair_sub(pair_mul(a, b), pair_mul(c, d))

    s11 = minor(h[2], h[0], h[1], h[1])
    s12 = minor(h[3], h[0], h[1], h[2])
    s22 = minor(h[4], h[0], h[2], h[2])
    y1 = minor(g[1], h[0], h[1], g[0])
    y2 = minor(g[2], h[0], h[2], g[0])
    last = minor(s22, s11, s12, s12)
    side = minor(y2, s11, s12, y1)
    alpha = g[0][0] / h[0][0]
    l10 = h[1][0] / h[0][0]
    l20 = h[2][0] / h[0][0]
    l21 = ratio(s12[0], s11[0], l10 + (LOW - SHIFT), l10 + (HIGH - SHIFT))
    gamma1 = ratio(y1[0], s11[0], -alpha / LOW, -alpha / HIGH)
    gamma2 = ratio(side[0], last[0], -gamma1 / HIGH, -gamma1 / LOW)
    c1 = gamma1 - gamma2 * l21
    return alpha - c1 * l10 - gamma2 * l20, c1, gamma2


def sigmoid(value):
    return 1.0 / (1.0 + jnp.exp(-SHARP * value))


def finish_kernel(plan, parts, v0, v1, v2, indicator, crossing, visible, level, weight, sem):
    nx, ny, nz = indicator.shape
    copy = pltpu.make_async_copy(plan, visible, sem)
    copy.start()
    devices = parts.shape[0]
    tiles = [parts[pl.ds(8 * k, 8)] for k in range(devices // 8)]
    pairs = [(tile, pltpu.roll(tile, nz - SUMS, 1)) for tile in tiles]
    while len(pairs) > 1:
        pairs = [pair_add(a, b) for a, b in zip(pairs[::2], pairs[1::2])]
    total = pairs[0]
    for step in (4, 2, 1):
        total = pair_add(total, (pltpu.roll(total[0], step, 0), pltpu.roll(total[1], step, 0)))

    def spread(value, k):
        return jnp.broadcast_to(value[0:1, k : k + 1], (1, nz))

    item = [(spread(total[0], k), spread(total[1], k)) for k in range(10)]
    c0, c1, c2 = coefficients(item)
    over = c0 * (item[6][0] + item[6][1]) + c1 * (item[7][0] + item[7][1]) + c2 * (item[8][0] + item[8][1])
    iso = over / item[9][0]

    def set_level(x):
        value = c0 * v0[x] + c1 * v1[x] + c2 * v2[x]
        level[x] = sigmoid(value - iso)
        return value

    @pl.loop(0, nx, unroll=4)
    def _(x):
        indicator[x] = set_level(x)[:ny]

    set_level(nx)
    outside = sigmoid(-iso)
    lane = lax.broadcasted_iota(jnp.int32, (ny, nz), 1)

    @pl.loop(0, nx, unroll=4)
    def _(x):
        here = level[x, pl.ds(0, ny)]
        above = jnp.where(lane < nz - 1, pltpu.roll(here, nz - 1, 1), outside)
        for edge, there in enumerate((level[x + 1, pl.ds(0, ny)], level[x, pl.ds(1, ny)], above)):
            weight[edge, pl.ds(x * ny, ny)] = here * (1.0 - there) + (1.0 - here) * there

    chunk = lax.broadcasted_iota(jnp.int32, (8, nz), 1) // BLK
    bricks_z = nz // BLK
    per_row = nz // BLK

    copy.wait()

    @pl.loop(0, visible.shape[0], unroll=2)
    def _(slot):
        number = visible[slot]
        safe = jnp.maximum(number, 0)
        begin = (safe // bricks_z) * BLK
        column = safe % bricks_z
        used = jnp.where(number >= 0, 1.0, 0.0)
        for edge in range(3):
            for half in range(2):
                for part in range(BLK // per_row):
                    tile = jnp.zeros((8, nz), F32)
                    for row in range(per_row):
                        at = half * 8 * ny + begin + part * per_row + row
                        lines = weight[edge, pl.ds(at, 8, stride=ny)]
                        turn = lax.rem((row - column) * BLK + nz, nz)
                        tile = jnp.where(chunk == row, pltpu.roll(lines, turn, 1), tile)
                    crossing[slot, edge, pl.ds(half * 16 + part, 8, stride=2)] = tile * used


def whole(*shape):
    return jax.ShapeDtypeStruct(shape, F32)


VMEM = pl.BlockSpec(memory_space=pltpu.VMEM)


HBM = pl.BlockSpec(memory_space=pltpu.HBM)


def kernel(body, inputs, outputs, scratch=(), grant=32):
    return pl.pallas_call(
        body,
        in_specs=list(inputs),
        out_specs=[VMEM] * len(outputs),
        out_shape=list(outputs),
        scratch_shapes=list(scratch),
        compiler_params=pltpu.CompilerParams(vmem_limit_bytes=int(grant * 1024 * 1024)),
    )


def swap(value, axis, first):
    count = lax.axis_size(axis)
    pairs = [(k, k + 1) for k in range(first, count - 1, 2)]
    return lax.ppermute(value, axis, pairs + [(b, a) for a, b in pairs])


def body(right_side, screening, active_blocks, visible_bricks):
    nx, ny, nz = right_side.shape
    active = active_blocks.reshape(-1)
    visible = visible_bricks.reshape(-1)
    devices = lax.axis_size("gx") * lax.axis_size("gy")
    slab = whole(nx, ny, nz)
    planes, near = nx + 2 * WIDE, nx + 2 * NEAR
    wide, rows = ny + 2 * EDGE, ny + 2 * NEAR
    side = whole(WIDE + NEAR, wide, nz)
    (rim,) = kernel(
        pack_kernel,
        (HBM, HBM, HBM),
        (whole(lax.axis_size("gy"), nx * (WIDE + NEAR), nz),),
        (
            pltpu.SMEM(active.shape, jnp.int32),
            pltpu.VMEM((2, nx, EDGE, nz), F32),
            pltpu.VMEM((2, nx, EDGE, nz), F32),
            pltpu.SemaphoreType.DMA((5,)),
        ),
        grant=GRANT,
    )(active, right_side, screening)
    rim = lax.all_to_all(rim, "gy", 0, 0)
    field, weight, cross, chip, plan = kernel(
        widen_kernel,
        (VMEM,) * 5,
        (whole(nx, wide, nz), whole(nx, wide, nz), side, side, jax.ShapeDtypeStruct(visible.shape, jnp.int32)),
        (pltpu.SMEM(active.shape, jnp.int32), pltpu.SemaphoreType.DMA),
    )(active, visible, right_side, screening, rim)
    cross = swap(cross, "gx", 1)
    chip = swap(chip, "gx", 0)
    reach = whole(nx + 1, ny + EDGE, nz)
    v0, v1, v2, sums = kernel(
        powers_kernel,
        (VMEM,) * 4,
        (reach, reach, reach, whole(1, nz)),
        (
            pltpu.VMEM((planes, wide, nz), F32),
            pltpu.VMEM((near, wide, nz), F32),
            pltpu.VMEM((near, wide, nz), F32),
            pltpu.VMEM((near, rows, nz), F32),
            pltpu.VMEM((nx + NEAR, rows, nz), F32),
            pltpu.VMEM((planes, wide + EDGE, nz), F32),
            pltpu.VMEM((planes, wide + EDGE, nz), F32),
            pltpu.VMEM((planes, rows, nz), F32),
            pltpu.VMEM((planes, rows, nz), F32),
        ),
    )(field, weight, cross, chip)
    parts = lax.all_to_all(jnp.broadcast_to(sums, (devices, 1, nz)), ("gx", "gy"), 0, 0)
    slots = visible.shape[0]
    indicator, crossing = kernel(
        finish_kernel,
        (VMEM,) * 5,
        (slab, whole(slots, 3, BLK**3 // nz, nz)),
        (
            pltpu.SMEM(visible.shape, jnp.int32),
            pltpu.VMEM((nx + 1, ny + EDGE, nz), F32),
            pltpu.VMEM((3, nx * ny, nz), F32),
            pltpu.SemaphoreType.DMA,
        ),
    )(plan, parts.reshape(devices, nz), v0, v1, v2)
    return indicator, crossing.reshape(slots, 1, 3, BLK**3)


def solution(mesh):
    return jax.shard_map(
        body,
        mesh=mesh,
        in_specs=(
            P("gx", "gy", None),
            P("gx", "gy", None),
            P("gx", "gy", None),
            P("gx", "gy", None),
        ),
        out_specs=(P("gx", "gy", None), P("gx", "gy", None, None)),
        check_vma=False,
    )
```

```python
import functools

import jax
import jax.numpy as jnp
from jax import lax
from jax.experimental import pallas as pl
from jax.experimental.pallas import tpu as pltpu
from jax.sharding import PartitionSpec as P

BLK = 16
WIDE = 6
NEAR = 4
EDGE = 8
SHARP = 4.0
SCALE = 1.0 / 86400.0
SHIFT = 2.25
LOW, HIGH = 0.5, 7.0
SUMS = 16
F32 = jnp.float32


def mass(mid, one, two):
    return 66.0 * mid + (26.0 * one + two)


def stiff(mid, one, two):
    return 6.0 * mid - (2.0 * one + two)


def block_mask(active, slots, rows, columns):
    y = lax.broadcasted_iota(jnp.int32, (rows, columns), 0)
    z = lax.broadcasted_iota(jnp.int32, (rows, columns), 1)
    number = (y // BLK) * (columns // BLK) + z // BLK
    mask = jnp.zeros((rows, columns), F32)
    for slot in range(slots):
        mask = jnp.where(number == active[slot], 1.0, mask)
    return mask


def on_odd():
    return lax.rem(lax.axis_index("gx"), 2)


def pack_kernel(active_hbm, right_hbm, screen_hbm, rim, active, right, screen, sems):
    nx, ny, nz = right_hbm.shape
    arrays = ((right_hbm, right, WIDE, 0), (screen_hbm, screen, NEAR, nx * WIDE))
    copies = [pltpu.make_async_copy(active_hbm, active, sems.at[0])]
    for k, (source, target, _, _) in enumerate(arrays):
        for high in range(2):
            rows = pl.ds(high * (ny - EDGE), EDGE)
            copies.append(pltpu.make_async_copy(source.at[:, rows], target.at[high], sems.at[1 + 2 * k + high]))
    for copy in copies:
        copy.start()
    me, last = lax.axis_index("gy"), rim.shape[0] - 1
    copies[0].wait()
    mask = block_mask(active, active.shape[0], ny, nz)
    for copy in copies[1:]:
        copy.wait()
    for _, source, wide, base in arrays:

        def write(place, high, top):
            part = mask[high * (ny - EDGE) :][:EDGE]
            for x in range(nx):
                value = source[high, x] * part
                rim[place, base + x * wide : base + (x + 1) * wide] = value[top : top + wide]

        pl.when(me > 0)(functools.partial(write, me - 1, 0, 0))
        pl.when(me < last)(functools.partial(write, me + 1, 1, EDGE - wide))


def widen_kernel(active_hbm, right, screen, rim, field, weight, cross, chip, active, sem):
    copy = pltpu.make_async_copy(active_hbm, active, sem)
    copy.start()
    nx, ny, nz = right.shape
    me, last = lax.axis_index("gy"), rim.shape[0] - 1
    arrays = ((field, WIDE, 0, WIDE), (weight, NEAR, nx * WIDE, 0))

    def read(place, there, low):
        block = jnp.where(there, place, 0)
        for target, wide, base, first in arrays:
            top = EDGE - wide if low else EDGE + ny
            for x in range(nx):
                value = rim[block, base + x * wide : base + (x + 1) * wide]
                target[first + x, top : top + wide] = jnp.where(there, value, 0.0)

    read(me - 1, me > 0, True)
    read(me + 1, me < last, False)
    copy.wait()
    mask = block_mask(active, active.shape[0], ny, nz)
    for x in range(nx):
        field[WIDE + x, EDGE : EDGE + ny] = right[x] * mask
        weight[x, EDGE : EDGE + ny] = screen[x] * mask
    odd = lax.rem(lax.axis_index("gx"), 2)
    for target, high in ((cross, odd), (chip, 1 - odd)):
        row = 0
        for source, wide, _, first in arrays:
            size = ny + 2 * wide
            for x in range(wide):
                target[row : row + size] = source[first + high * (nx - wide) + x, EDGE - wide : EDGE + ny + wide]
                row += size


def along_z(value):
    lane = lax.broadcasted_iota(jnp.int32, value.shape, 1)
    last = value.shape[1]

    def shifted(step):
        before = jnp.where(lane >= step, pltpu.roll(value, step, 1), 0.0)
        after = jnp.where(lane < last - step, pltpu.roll(value, last - step, 1), 0.0)
        return before + after

    one, two = shifted(1), shifted(2)
    return mass(value, one, two), stiff(value, one, two)


def set_weight(keep, shifted, at, rows, weight):
    on = weight > 0.0
    keep[at, rows] = jnp.where(on, SCALE, 0.0)
    shifted[at, rows] = jnp.where(on, weight - SHIFT, 0.0)


def spread(source, za, zb, yp, yq, count, plane, start, rows):
    size = source.shape[1]

    @pl.loop(0, count, unroll=4)
    def _(k):
        x = plane(k)
        a, b = along_z(source[x])
        za[x, pl.ds(EDGE, size)] = a
        zb[x, pl.ds(EDGE, size)] = b

    @pl.loop(0, count, unroll=4)
    def _(k):
        x = plane(k)

        def part(ref, step):
            return ref[x, pl.ds(EDGE + start + step, rows)]

        a0, a1, a2 = part(za, 0), part(za, -1) + part(za, 1), part(za, -2) + part(za, 2)
        b0, b1, b2 = part(zb, 0), part(zb, -1) + part(zb, 1), part(zb, -2) + part(zb, 2)
        yp[x] = mass(a0, a1, a2)
        yq[x] = mass(b0, b1, b2) + stiff(a0, a1, a2)


def across(yp, yq, x):
    q0, q1, q2 = yq[x + 2], yq[x + 1] + yq[x + 3], yq[x] + yq[x + 4]
    p0, p1, p2 = yp[x + 2], yp[x + 1] + yp[x + 3], yp[x] + yp[x + 4]
    return mass(q0, q1, q2) + stiff(p0, p1, p2)


def step_up(target, source, keep, shifted, yp, yq, skip, rows, source_rows, count, plane):
    @pl.loop(0, count, unroll=4)
    def _(k):
        x = plane(k)
        target[x] = keep[x + skip, rows] * across(yp, yq, x) + shifted[x + skip, rows] * source[x + 2, source_rows]


def inner_kernel(field, weight, keep, shifted, first, second, yp1, yq1, yp2, yq2, yp3, yq3, za, zb):
    nx, wide = weight.shape[0], weight.shape[1]
    ny = wide - 2 * EDGE
    rows = ny + 2 * NEAR
    outer, every = pl.ds(EDGE - NEAR, rows), pl.ds(0, rows)
    for x in range(nx):
        set_weight(keep, shifted, NEAR + x, pl.ds(0, wide), weight[x])

    def plane(k):
        return WIDE + k

    spread(field, za, zb, yp1, yq1, nx, plane, EDGE - NEAR, rows)
    step_up(first, field, keep, shifted, yp1, yq1, 0, outer, outer, nx - 4, plane)
    spread(first, za, zb, yp2, yq2, nx - 4, plane, 0, rows)
    step_up(second, first, keep, shifted, yp2, yq2, 2, outer, every, nx - 8, plane)
    spread(second, za, zb, yp3, yq3, nx - 8, plane, NEAR, ny)


def outer_kernel(
    cross, chip, field_in, keep_in, shifted_in, first_in, second_in, p1, q1, p2, q2, p3, q3,
    field, keep, shifted, first, second, yp1, yq1, yp2, yq2, yp3, yq3, sums, za, zb,
):
    planes, wide, nz = field.shape
    nx, ny = planes - 2 * WIDE, wide - 2 * EDGE
    rows = ny + 2 * NEAR
    outer, every = pl.ds(EDGE - NEAR, rows), pl.ds(0, rows)
    odd = lax.rem(lax.axis_index("gx"), 2)
    for source, high in ((cross, odd), (chip, 1 - odd)):
        row = 0
        for x in range(WIDE):
            size = ny + 2 * WIDE
            field[high * (nx + WIDE) + x, EDGE - WIDE : EDGE + ny + WIDE] = source[row : row + size]
            row += size
        for x in range(NEAR):
            set_weight(keep, shifted, high * (nx + NEAR) + x, outer, source[row : row + rows])
            row += rows

    def side(total):
        return lambda k: k + jnp.where(k < WIDE, 0, total - 2 * WIDE)

    count = 2 * WIDE
    plane = side(nx + 2 * WIDE)
    spread(field, za, zb, yp1, yq1, count, plane, EDGE - NEAR, rows)
    plane = side(nx + 2 * NEAR)
    step_up(first, field, keep, shifted, yp1, yq1, 0, outer, outer, count, plane)
    spread(first, za, zb, yp2, yq2, count, plane, 0, rows)
    plane = side(nx + NEAR)
    step_up(second, first, keep, shifted, yp2, yq2, 2, outer, every, count, plane)
    spread(second, za, zb, yp3, yq3, count, plane, NEAR, ny)

    def fold(value):
        return jnp.sum(value.reshape(ny // 8, 8, nz), axis=0)

    mid, own = pl.ds(EDGE, ny), pl.ds(NEAR, ny)

    def add(x, totals):
        v0 = field[x + WIDE, mid]
        v1 = first[x + NEAR, own]
        v2 = second[x + 2, own]
        stay = keep[x + NEAR, mid]
        v3 = stay * across(yp3, yq3, x) + shifted[x + NEAR, mid] * v2
        on = jnp.where(stay > 0.0, 1.0, 0.0)
        new = (v0 * v0, v0 * v1, v1 * v1, v1 * v2, v2 * v2, v2 * v3, v0, v1, v2, on)
        return tuple(total + fold(value) for total, value in zip(totals, new))

    totals = lax.fori_loop(0, nx, add, (jnp.zeros((8, nz), F32),) * 10, unroll=4)
    row = lax.broadcasted_iota(jnp.int32, (SUMS, nz), 0)
    lane = lax.broadcasted_iota(jnp.int32, (SUMS, nz), 1)
    lines = jnp.zeros((SUMS, nz), F32)
    for place, total in enumerate(totals):
        lines = jnp.where(row == place, jnp.sum(total, axis=0, keepdims=True), lines)
    pair = (lines, jnp.zeros_like(lines))
    step = nz // 2
    while step:
        pair = pair_add(pair, (pltpu.roll(pair[0], step, 1), pltpu.roll(pair[1], step, 1)))
        step //= 2
    spot = jnp.where(lane == row, pair[0], jnp.where(lane == row + SUMS, pair[1], 0.0))
    sums[...] = jnp.sum(spot, axis=0, keepdims=True)


def two_sum(a, b):
    total = a + b
    part = total - a
    return total, (a - (total - part)) + (b - part)


def pair_add(a, b):
    total, rest = two_sum(a[0], b[0])
    return total, rest + (a[1] + b[1])


def halves(a):
    wide = 4097.0 * a
    top = wide - (wide - a)
    return top, a - top


def pair_mul(a, b):
    product = a[0] * b[0]
    a_top, a_rest = halves(a[0])
    b_top, b_rest = halves(b[0])
    rest = ((a_top * b_top - product) + a_top * b_rest + a_rest * b_top) + a_rest * b_rest
    rest = rest + (a[0] * b[1] + a[1] * b[0])
    total = product + rest
    return total, rest - (total - product)


def pair_sub(a, b):
    total, rest = two_sum(a[0], -b[0])
    rest = rest + (a[1] - b[1])
    out = total + rest
    return out, rest - (out - total)


def ratio(over, under, low, high):
    good = under > 0.0
    value = jnp.where(good, over / jnp.where(good, under, 1.0), 0.5 * (low + high))
    return jnp.minimum(jnp.maximum(value, low), high)


def coefficients(total):
    scale = 1.0 / total[0][0]
    zero = jnp.zeros_like(scale)
    g = [pair_mul(item, (scale, zero)) for item in total[:6]]
    shift = (jnp.full_like(scale, SHIFT), zero)
    h = [pair_add(g[k + 1], pair_mul(g[k], shift)) for k in range(5)]

    def minor(a, b, c, d):
        return pair_sub(pair_mul(a, b), pair_mul(c, d))

    s11 = minor(h[2], h[0], h[1], h[1])
    s12 = minor(h[3], h[0], h[1], h[2])
    s22 = minor(h[4], h[0], h[2], h[2])
    y1 = minor(g[1], h[0], h[1], g[0])
    y2 = minor(g[2], h[0], h[2], g[0])
    last = minor(s22, s11, s12, s12)
    side = minor(y2, s11, s12, y1)
    alpha = g[0][0] / h[0][0]
    l10 = h[1][0] / h[0][0]
    l20 = h[2][0] / h[0][0]
    l21 = ratio(s12[0], s11[0], l10 + (LOW - SHIFT), l10 + (HIGH - SHIFT))
    gamma1 = ratio(y1[0], s11[0], -alpha / LOW, -alpha / HIGH)
    gamma2 = ratio(side[0], last[0], -gamma1 / HIGH, -gamma1 / LOW)
    c1 = gamma1 - gamma2 * l21
    return alpha - c1 * l10 - gamma2 * l20, c1, gamma2


def sigmoid(value):
    return 1.0 / (1.0 + jnp.exp(-SHARP * value))


def finish_kernel(
    visible_hbm, parts, field, first, second, indicator_hbm, crossing_hbm,
    visible, indicator, crossing, level, weight, sem, slot_sems, result_sem,
):
    nx, ny, nz = indicator.shape
    copy = pltpu.make_async_copy(visible_hbm, visible, sem)
    copy.start()
    devices = parts.shape[0]
    tiles = [parts[pl.ds(8 * k, 8)] for k in range(devices // 8)]
    pairs = [(tile, pltpu.roll(tile, nz - SUMS, 1)) for tile in tiles]
    while len(pairs) > 1:
        pairs = [pair_add(a, b) for a, b in zip(pairs[::2], pairs[1::2])]
    total = pairs[0]
    for step in (4, 2, 1):
        total = pair_add(total, (pltpu.roll(total[0], step, 0), pltpu.roll(total[1], step, 0)))

    def spread(value, k):
        return jnp.broadcast_to(value[0:1, k : k + 1], (1, nz))

    item = [(spread(total[0], k), spread(total[1], k)) for k in range(10)]
    c0, c1, c2 = coefficients(item)
    over = c0 * (item[6][0] + item[6][1]) + c1 * (item[7][0] + item[7][1]) + c2 * (item[8][0] + item[8][1])
    iso = over / item[9][0]

    def set_level(x):
        v0 = field[x + WIDE, pl.ds(EDGE, ny + EDGE)]
        v1 = first[x + NEAR, pl.ds(NEAR, ny + NEAR)]
        v2 = second[x + 2, pl.ds(NEAR, ny + NEAR)]
        value = c0 * v0[: ny + NEAR] + c1 * v1 + c2 * v2
        level[x, pl.ds(0, ny + NEAR)] = sigmoid(value - iso)
        return value

    @pl.loop(0, nx, unroll=4)
    def _(x):
        indicator[x] = set_level(x)[:ny]

    set_level(nx)
    result = pltpu.make_async_copy(indicator, indicator_hbm, result_sem)
    result.start()
    outside = sigmoid(-iso)
    lane = lax.broadcasted_iota(jnp.int32, (ny, nz), 1)

    @pl.loop(0, nx, unroll=4)
    def _(x):
        here = level[x, pl.ds(0, ny)]
        above = jnp.where(lane < nz - 1, pltpu.roll(here, nz - 1, 1), outside)
        for edge, there in enumerate((level[x + 1, pl.ds(0, ny)], level[x, pl.ds(1, ny)], above)):
            weight[edge, pl.ds(x * ny, ny)] = here * (1.0 - there) + (1.0 - here) * there

    chunk = lax.broadcasted_iota(jnp.int32, (8, nz), 1) // BLK
    bricks_z = nz // BLK
    per_row = nz // BLK

    copy.wait()

    def out(slot):
        return pltpu.make_async_copy(crossing.at[slot], crossing_hbm.at[slot], slot_sems.at[slot])

    @pl.loop(0, visible.shape[0], unroll=2)
    def _(slot):
        number = visible[slot]
        safe = jnp.maximum(number, 0)
        begin = (safe // bricks_z) * BLK
        column = safe % bricks_z
        used = jnp.where(number >= 0, 1.0, 0.0)
        for edge in range(3):
            for half in range(2):
                for part in range(BLK // per_row):
                    tile = jnp.zeros((8, nz), F32)
                    for row in range(per_row):
                        at = half * 8 * ny + begin + part * per_row + row
                        lines = weight[edge, pl.ds(at, 8, stride=ny)]
                        turn = lax.rem((row - column) * BLK + nz, nz)
                        tile = jnp.where(chunk == row, pltpu.roll(lines, turn, 1), tile)
                    crossing[slot, edge, pl.ds(half * 16 + part, 8, stride=2)] = tile * used
        out(slot).start()

    for slot in range(visible.shape[0]):
        out(slot).wait()
    result.wait()


def whole(*shape):
    return jax.ShapeDtypeStruct(shape, F32)


VMEM = pl.BlockSpec(memory_space=pltpu.VMEM)


HBM = pl.BlockSpec(memory_space=pltpu.HBM)


def kernel(body, inputs, outputs, scratch=(), results=VMEM, alias=None, flops=0):
    return pl.pallas_call(
        body,
        in_specs=list(inputs),
        out_specs=[results] * len(outputs),
        out_shape=list(outputs),
        scratch_shapes=list(scratch),
        input_output_aliases=alias or {},
        cost_estimate=pl.CostEstimate(flops=flops, bytes_accessed=flops // 4, transcendentals=0),
        compiler_params=pltpu.CompilerParams(vmem_limit_bytes=32 * 1024 * 1024),
    )


def in_hbm(value):
    return pltpu.with_memory_space_constraint(value, pltpu.HBM)


def swap(value, axis, first):
    count = lax.axis_size(axis)
    pairs = [(k, k + 1) for k in range(first, count - 1, 2)]
    return lax.ppermute(value, axis, pairs + [(b, a) for a, b in pairs])


def body(right_side, screening, active_blocks, visible_bricks):
    nx, ny, nz = right_side.shape
    active = active_blocks.reshape(-1)
    visible = visible_bricks.reshape(-1)
    devices = lax.axis_size("gx") * lax.axis_size("gy")
    slab = whole(nx, ny, nz)
    planes, near = nx + 2 * WIDE, nx + 2 * NEAR
    wide, rows = ny + 2 * EDGE, ny + 2 * NEAR
    (rim,) = kernel(
        pack_kernel,
        (HBM, HBM, HBM),
        (whole(lax.axis_size("gy"), nx * (WIDE + NEAR), nz),),
        (
            pltpu.SMEM(active.shape, jnp.int32),
            pltpu.VMEM((2, nx, EDGE, nz), F32),
            pltpu.VMEM((2, nx, EDGE, nz), F32),
            pltpu.SemaphoreType.DMA((5,)),
        ),
    )(in_hbm(active), in_hbm(right_side), in_hbm(screening))
    rim = lax.all_to_all(rim, "gy", 0, 0)
    side = whole(WIDE * (ny + 2 * WIDE) + NEAR * rows, nz)
    field, weight, cross, chip = kernel(
        widen_kernel,
        (HBM,) + (VMEM,) * 3,
        (whole(planes, wide, nz), whole(nx, wide, nz), side, side),
        (pltpu.SMEM(active.shape, jnp.int32), pltpu.SemaphoreType.DMA),
    )(in_hbm(active), right_side, screening, rim)
    cross = swap(cross, "gx", 1)
    chip = swap(chip, "gx", 0)
    lines = pltpu.VMEM((planes, wide + EDGE, nz), F32)
    inner = kernel(
        inner_kernel,
        (VMEM,) * 2,
        (whole(near, wide, nz),) * 2
        + (whole(near, rows, nz), whole(nx + NEAR, rows, nz))
        + (whole(planes, rows, nz),) * 2
        + (whole(near, rows, nz),) * 2
        + (whole(nx + NEAR, ny, nz),) * 2,
        (lines, lines),
        flops=20_000_000,
    )(field, weight)
    held = [field, *inner]
    done = kernel(
        outer_kernel,
        (VMEM,) * (2 + len(held)),
        [whole(*item.shape) for item in held] + [whole(1, nz)],
        (lines, lines),
        alias={2 + k: k for k in range(len(held))},
        flops=20_000_000,
    )(cross, chip, *held)
    field, _, _, first, second = done[:5]
    parts = lax.all_to_all(jnp.broadcast_to(done[-1], (devices, 1, nz)), ("gx", "gy"), 0, 0)
    slots = visible.shape[0]
    shape = (slots, 3, BLK**3 // nz, nz)
    indicator, crossing = kernel(
        finish_kernel,
        (HBM,) + (VMEM,) * 4,
        (slab, whole(*shape)),
        (
            pltpu.SMEM(visible.shape, jnp.int32),
            pltpu.VMEM(slab.shape, F32),
            pltpu.VMEM(shape, F32),
            pltpu.VMEM((nx + 1, ny + EDGE, nz), F32),
            pltpu.VMEM((3, nx * ny, nz), F32),
            pltpu.SemaphoreType.DMA,
            pltpu.SemaphoreType.DMA((slots,)),
            pltpu.SemaphoreType.DMA,
        ),
        results=HBM,
    )(in_hbm(visible), parts.reshape(devices, nz), field, first, second)
    return indicator, crossing.reshape(slots, 1, 3, BLK**3)


def solution(mesh):
    return jax.shard_map(
        body,
        mesh=mesh,
        in_specs=(
            P("gx", "gy", None),
            P("gx", "gy", None),
            P("gx", "gy", None),
            P("gx", "gy", None),
        ),
        out_specs=(P("gx", "gy", None), P("gx", "gy", None, None)),
        check_vma=False,
    )
```

```python
import functools

import jax
import jax.numpy as jnp
from jax import lax
from jax.experimental import pallas as pl
from jax.experimental.pallas import tpu as pltpu
from jax.sharding import PartitionSpec as P

BLK = 16
WIDE = 6
NEAR = 4
EDGE = 8
SHARP = 4.0
SCALE = 1.0 / 86400.0
SHIFT = 2.25
LOW, HIGH = 0.5, 7.0
SUMS = 16
F32 = jnp.float32


def mass(mid, one, two):
    return 66.0 * mid + (26.0 * one + two)


def stiff(mid, one, two):
    return 6.0 * mid - (2.0 * one + two)


def block_mask(active, slots, rows, columns):
    y = lax.broadcasted_iota(jnp.int32, (rows, columns), 0)
    z = lax.broadcasted_iota(jnp.int32, (rows, columns), 1)
    number = (y // BLK) * (columns // BLK) + z // BLK
    mask = jnp.zeros((rows, columns), F32)
    for slot in range(slots):
        mask = jnp.where(number == active[slot], 1.0, mask)
    return mask


def on_odd():
    return lax.rem(lax.axis_index("gx"), 2)


def odd_on(axis):
    return lax.rem(lax.axis_index(axis), 2)


def pack_kernel(active_hbm, right_hbm, screen_hbm, far, near, active, right, screen, sems):
    nx, ny, nz = right_hbm.shape
    arrays = ((right_hbm, right, WIDE, 0), (screen_hbm, screen, NEAR, nx * WIDE))
    copies = [pltpu.make_async_copy(active_hbm, active, sems.at[0])]
    for k, (source, target, _, _) in enumerate(arrays):
        for high in range(2):
            rows = pl.ds(high * (ny - EDGE), EDGE)
            copies.append(pltpu.make_async_copy(source.at[:, rows], target.at[high], sems.at[1 + 2 * k + high]))
    for copy in copies:
        copy.start()
    copies[0].wait()
    mask = block_mask(active, active.shape[0], ny, nz)
    for copy in copies[1:]:
        copy.wait()

    def write(high_out, low_out):
        for _, source, wide, base in arrays:
            for x in range(nx):
                rows = pl.ds(base + x * wide, wide)
                low_out[rows] = (source[0, x] * mask[:EDGE])[:wide]
                high_out[rows] = (source[1, x] * mask[ny - EDGE :])[EDGE - wide :]

    odd = odd_on("gy")
    pl.when(odd == 1)(functools.partial(write, far, near))
    pl.when(odd == 0)(functools.partial(write, near, far))


def message_rows(nx, ny):
    row = 0
    for array, wide in enumerate((WIDE, NEAR)):
        for x in range(wide):
            yield array, wide, x, row
            row += ny + 2 * wide


def place_kernel(active_hbm, right, screen, field, weight, cross, chip, active, sem):
    copy = pltpu.make_async_copy(active_hbm, active, sem)
    copy.start()
    nx, ny, nz = right.shape
    copy.wait()
    mask = block_mask(active, active.shape[0], ny, nz)
    for x in range(nx):
        field[WIDE + x, EDGE : EDGE + ny] = right[x] * mask
        weight[x, EDGE : EDGE + ny] = screen[x] * mask
    odd = odd_on("gx")
    for target, high in ((cross, odd), (chip, 1 - odd)):
        for array, wide, x, row in message_rows(nx, ny):
            source, first = ((field, WIDE), (weight, 0))[array]
            value = source[first + high * (nx - wide) + x, EDGE : EDGE + ny]
            target[row + wide : row + wide + ny] = value


def widen_kernel(field_in, weight_in, cross_in, chip_in, far, near, field, weight, cross, chip):
    nx, ny = weight.shape[0], weight.shape[1] - 2 * EDGE
    arrays = ((field, WIDE, 0, WIDE), (weight, NEAR, nx * WIDE, 0))

    def read(low, high):
        for target, wide, base, first in arrays:
            for x in range(nx):
                rows = pl.ds(base + x * wide, wide)
                target[first + x, EDGE - wide : EDGE] = low[rows]
                target[first + x, EDGE + ny : EDGE + ny + wide] = high[rows]

    odd = odd_on("gy")
    pl.when(odd == 1)(functools.partial(read, near, far))
    pl.when(odd == 0)(functools.partial(read, far, near))
    odd = odd_on("gx")
    for target, high in ((cross, odd), (chip, 1 - odd)):
        for array, wide, x, row in message_rows(nx, ny):
            source, first = ((field, WIDE), (weight, 0))[array]
            plane = first + high * (nx - wide) + x
            target[row : row + wide] = source[plane, EDGE - wide : EDGE]
            target[row + wide + ny : row + 2 * wide + ny] = source[plane, EDGE + ny : EDGE + ny + wide]


def along_z(value):
    lane = lax.broadcasted_iota(jnp.int32, value.shape, 1)
    last = value.shape[1]

    def shifted(step):
        before = jnp.where(lane >= step, pltpu.roll(value, step, 1), 0.0)
        after = jnp.where(lane < last - step, pltpu.roll(value, last - step, 1), 0.0)
        return before + after

    one, two = shifted(1), shifted(2)
    return mass(value, one, two), stiff(value, one, two)


def set_weight(keep, shifted, at, rows, weight):
    on = weight > 0.0
    keep[at, rows] = jnp.where(on, SCALE, 0.0)
    shifted[at, rows] = jnp.where(on, weight - SHIFT, 0.0)


def spread(source, za, zb, yp, yq, count, plane, start, rows):
    size = source.shape[1]

    @pl.loop(0, count, unroll=4)
    def _(k):
        x = plane(k)
        a, b = along_z(source[x])
        za[x, pl.ds(EDGE, size)] = a
        zb[x, pl.ds(EDGE, size)] = b

    @pl.loop(0, count, unroll=4)
    def _(k):
        x = plane(k)

        def part(ref, step):
            return ref[x, pl.ds(EDGE + start + step, rows)]

        a0, a1, a2 = part(za, 0), part(za, -1) + part(za, 1), part(za, -2) + part(za, 2)
        b0, b1, b2 = part(zb, 0), part(zb, -1) + part(zb, 1), part(zb, -2) + part(zb, 2)
        yp[x] = mass(a0, a1, a2)
        yq[x] = mass(b0, b1, b2) + stiff(a0, a1, a2)


def across(yp, yq, x):
    q0, q1, q2 = yq[x + 2], yq[x + 1] + yq[x + 3], yq[x] + yq[x + 4]
    p0, p1, p2 = yp[x + 2], yp[x + 1] + yp[x + 3], yp[x] + yp[x + 4]
    return mass(q0, q1, q2) + stiff(p0, p1, p2)


def step_up(target, source, keep, shifted, yp, yq, skip, rows, source_rows, count, plane):
    @pl.loop(0, count, unroll=4)
    def _(k):
        x = plane(k)
        target[x] = keep[x + skip, rows] * across(yp, yq, x) + shifted[x + skip, rows] * source[x + 2, source_rows]


def inner_kernel(field, weight, keep, shifted, first, second, yp1, yq1, yp2, yq2, yp3, yq3, za, zb):
    nx, wide = weight.shape[0], weight.shape[1]
    ny = wide - 2 * EDGE
    rows = ny + 2 * NEAR
    outer, every = pl.ds(EDGE - NEAR, rows), pl.ds(0, rows)
    for x in range(nx):
        set_weight(keep, shifted, NEAR + x, pl.ds(0, wide), weight[x])

    def plane(k):
        return WIDE + k

    spread(field, za, zb, yp1, yq1, nx, plane, EDGE - NEAR, rows)
    step_up(first, field, keep, shifted, yp1, yq1, 0, outer, outer, nx - 4, plane)
    spread(first, za, zb, yp2, yq2, nx - 4, plane, 0, rows)
    step_up(second, first, keep, shifted, yp2, yq2, 2, outer, every, nx - 8, plane)
    spread(second, za, zb, yp3, yq3, nx - 8, plane, NEAR, ny)


def outer_kernel(
    cross, chip, field_in, keep_in, shifted_in, first_in, second_in, p1, q1, p2, q2, p3, q3,
    field, keep, shifted, first, second, yp1, yq1, yp2, yq2, yp3, yq3, sums, za, zb,
):
    planes, wide, nz = field.shape
    nx, ny = planes - 2 * WIDE, wide - 2 * EDGE
    rows = ny + 2 * NEAR
    outer, every = pl.ds(EDGE - NEAR, rows), pl.ds(0, rows)
    odd = odd_on("gx")
    for source, high in ((cross, odd), (chip, 1 - odd)):
        for array, wide, x, row in message_rows(nx, ny):
            value = source[row : row + ny + 2 * wide]
            if array == 0:
                field[high * (nx + wide) + x, EDGE - wide : EDGE + ny + wide] = value
            else:
                set_weight(keep, shifted, high * (nx + wide) + x, outer, value)

    def side(total):
        return lambda k: k + jnp.where(k < WIDE, 0, total - 2 * WIDE)

    count = 2 * WIDE
    plane = side(nx + 2 * WIDE)
    spread(field, za, zb, yp1, yq1, count, plane, EDGE - NEAR, rows)
    plane = side(nx + 2 * NEAR)
    step_up(first, field, keep, shifted, yp1, yq1, 0, outer, outer, count, plane)
    spread(first, za, zb, yp2, yq2, count, plane, 0, rows)
    plane = side(nx + NEAR)
    step_up(second, first, keep, shifted, yp2, yq2, 2, outer, every, count, plane)
    spread(second, za, zb, yp3, yq3, count, plane, NEAR, ny)

    def fold(value):
        return jnp.sum(value.reshape(ny // 8, 8, nz), axis=0)

    mid, own = pl.ds(EDGE, ny), pl.ds(NEAR, ny)

    def add(x, totals):
        v0 = field[x + WIDE, mid]
        v1 = first[x + NEAR, own]
        v2 = second[x + 2, own]
        stay = keep[x + NEAR, mid]
        v3 = stay * across(yp3, yq3, x) + shifted[x + NEAR, mid] * v2
        on = jnp.where(stay > 0.0, 1.0, 0.0)
        new = (v0 * v0, v0 * v1, v1 * v1, v1 * v2, v2 * v2, v2 * v3, v0, v1, v2, on)
        return tuple(total + fold(value) for total, value in zip(totals, new))

    totals = lax.fori_loop(0, nx, add, (jnp.zeros((8, nz), F32),) * 10, unroll=4)
    row = lax.broadcasted_iota(jnp.int32, (SUMS, nz), 0)
    lane = lax.broadcasted_iota(jnp.int32, (SUMS, nz), 1)
    lines = jnp.zeros((SUMS, nz), F32)
    for place, total in enumerate(totals):
        lines = jnp.where(row == place, jnp.sum(total, axis=0, keepdims=True), lines)
    pair = (lines, jnp.zeros_like(lines))
    step = nz // 2
    while step:
        pair = pair_add(pair, (pltpu.roll(pair[0], step, 1), pltpu.roll(pair[1], step, 1)))
        step //= 2
    spot = jnp.where(lane == row, pair[0], jnp.where(lane == row + SUMS, pair[1], 0.0))
    sums[...] = jnp.sum(spot, axis=0, keepdims=True)


def two_sum(a, b):
    total = a + b
    part = total - a
    return total, (a - (total - part)) + (b - part)


def pair_add(a, b):
    total, rest = two_sum(a[0], b[0])
    return total, rest + (a[1] + b[1])


def halves(a):
    wide = 4097.0 * a
    top = wide - (wide - a)
    return top, a - top


def pair_mul(a, b):
    product = a[0] * b[0]
    a_top, a_rest = halves(a[0])
    b_top, b_rest = halves(b[0])
    rest = ((a_top * b_top - product) + a_top * b_rest + a_rest * b_top) + a_rest * b_rest
    rest = rest + (a[0] * b[1] + a[1] * b[0])
    total = product + rest
    return total, rest - (total - product)


def pair_sub(a, b):
    total, rest = two_sum(a[0], -b[0])
    rest = rest + (a[1] - b[1])
    out = total + rest
    return out, rest - (out - total)


def ratio(over, under, low, high):
    good = under > 0.0
    value = jnp.where(good, over / jnp.where(good, under, 1.0), 0.5 * (low + high))
    return jnp.minimum(jnp.maximum(value, low), high)


def coefficients(total):
    scale = 1.0 / total[0][0]
    zero = jnp.zeros_like(scale)
    g = [pair_mul(item, (scale, zero)) for item in total[:6]]
    shift = (jnp.full_like(scale, SHIFT), zero)
    h = [pair_add(g[k + 1], pair_mul(g[k], shift)) for k in range(5)]

    def minor(a, b, c, d):
        return pair_sub(pair_mul(a, b), pair_mul(c, d))

    s11 = minor(h[2], h[0], h[1], h[1])
    s12 = minor(h[3], h[0], h[1], h[2])
    s22 = minor(h[4], h[0], h[2], h[2])
    y1 = minor(g[1], h[0], h[1], g[0])
    y2 = minor(g[2], h[0], h[2], g[0])
    last = minor(s22, s11, s12, s12)
    side = minor(y2, s11, s12, y1)
    alpha = g[0][0] / h[0][0]
    l10 = h[1][0] / h[0][0]
    l20 = h[2][0] / h[0][0]
    l21 = ratio(s12[0], s11[0], l10 + (LOW - SHIFT), l10 + (HIGH - SHIFT))
    gamma1 = ratio(y1[0], s11[0], -alpha / LOW, -alpha / HIGH)
    gamma2 = ratio(side[0], last[0], -gamma1 / HIGH, -gamma1 / LOW)
    c1 = gamma1 - gamma2 * l21
    return alpha - c1 * l10 - gamma2 * l20, c1, gamma2


def sigmoid(value):
    return 1.0 / (1.0 + jnp.exp(-SHARP * value))


def finish_kernel(
    visible_hbm, parts, field, first, second, indicator_hbm, crossing_hbm,
    visible, indicator, crossing, level, weight, sem, slot_sems, result_sem,
):
    nx, ny, nz = indicator.shape
    copy = pltpu.make_async_copy(visible_hbm, visible, sem)
    copy.start()
    devices = parts.shape[0]
    tiles = [parts[pl.ds(8 * k, 8)] for k in range(devices // 8)]
    pairs = [(tile, pltpu.roll(tile, nz - SUMS, 1)) for tile in tiles]
    while len(pairs) > 1:
        pairs = [pair_add(a, b) for a, b in zip(pairs[::2], pairs[1::2])]
    total = pairs[0]
    for step in (4, 2, 1):
        total = pair_add(total, (pltpu.roll(total[0], step, 0), pltpu.roll(total[1], step, 0)))

    def spread(value, k):
        return jnp.broadcast_to(value[0:1, k : k + 1], (1, nz))

    item = [(spread(total[0], k), spread(total[1], k)) for k in range(10)]
    c0, c1, c2 = coefficients(item)
    over = c0 * (item[6][0] + item[6][1]) + c1 * (item[7][0] + item[7][1]) + c2 * (item[8][0] + item[8][1])
    iso = over / item[9][0]

    def set_level(x):
        v0 = field[x + WIDE, pl.ds(EDGE, ny + EDGE)]
        v1 = first[x + NEAR, pl.ds(NEAR, ny + NEAR)]
        v2 = second[x + 2, pl.ds(NEAR, ny + NEAR)]
        value = c0 * v0[: ny + NEAR] + c1 * v1 + c2 * v2
        level[x, pl.ds(0, ny + NEAR)] = sigmoid(value - iso)
        return value

    @pl.loop(0, nx, unroll=4)
    def _(x):
        indicator[x] = set_level(x)[:ny]

    set_level(nx)
    result = pltpu.make_async_copy(indicator, indicator_hbm, result_sem)
    result.start()
    outside = sigmoid(-iso)
    lane = lax.broadcasted_iota(jnp.int32, (ny, nz), 1)

    @pl.loop(0, nx, unroll=4)
    def _(x):
        here = level[x, pl.ds(0, ny)]
        above = jnp.where(lane < nz - 1, pltpu.roll(here, nz - 1, 1), outside)
        for edge, there in enumerate((level[x + 1, pl.ds(0, ny)], level[x, pl.ds(1, ny)], above)):
            weight[edge, pl.ds(x * (ny + 1), ny)] = here * (1.0 - there) + (1.0 - here) * there

    chunk = lax.broadcasted_iota(jnp.int32, (8, nz), 1) // BLK
    bricks_z = nz // BLK
    per_row = nz // BLK

    copy.wait()

    def out(slot):
        return pltpu.make_async_copy(crossing.at[slot], crossing_hbm.at[slot], slot_sems.at[slot])

    @pl.loop(0, visible.shape[0], unroll=2)
    def _(slot):
        number = visible[slot]
        safe = jnp.maximum(number, 0)
        begin = (safe // bricks_z) * BLK
        column = safe % bricks_z
        used = jnp.where(number >= 0, 1.0, 0.0)
        for edge in range(3):
            for half in range(2):
                for part in range(BLK // per_row):
                    tile = jnp.zeros((8, nz), F32)
                    for row in range(per_row):
                        at = half * 8 * (ny + 1) + begin + part * per_row + row
                        lines = weight[edge, pl.ds(at, 8, stride=ny + 1)]
                        turn = lax.rem((row - column) * BLK + nz, nz)
                        tile = jnp.where(chunk == row, pltpu.roll(lines, turn, 1), tile)
                    crossing[slot, edge, pl.ds(half * 16 + part, 8, stride=2)] = tile * used
        out(slot).start()

    for slot in range(visible.shape[0]):
        out(slot).wait()
    result.wait()


def whole(*shape):
    return jax.ShapeDtypeStruct(shape, F32)


VMEM = pl.BlockSpec(memory_space=pltpu.VMEM)


HBM = pl.BlockSpec(memory_space=pltpu.HBM)


def kernel(body, inputs, outputs, scratch=(), results=VMEM, alias=None, flops=0):
    return pl.pallas_call(
        body,
        in_specs=list(inputs),
        out_specs=[results] * len(outputs),
        out_shape=list(outputs),
        scratch_shapes=list(scratch),
        input_output_aliases=alias or {},
        cost_estimate=pl.CostEstimate(flops=flops, bytes_accessed=flops // 4, transcendentals=0),
        compiler_params=pltpu.CompilerParams(vmem_limit_bytes=32 * 1024 * 1024),
    )


def in_hbm(value):
    return pltpu.with_memory_space_constraint(value, pltpu.HBM)


def swap(value, axis, first):
    count = lax.axis_size(axis)
    pairs = [(k, k + 1) for k in range(first, count - 1, 2)]
    return lax.ppermute(value, axis, pairs + [(b, a) for a, b in pairs])


def body(right_side, screening, active_blocks, visible_bricks):
    nx, ny, nz = right_side.shape
    active = active_blocks.reshape(-1)
    visible = visible_bricks.reshape(-1)
    devices = lax.axis_size("gx") * lax.axis_size("gy")
    slab = whole(nx, ny, nz)
    planes, near = nx + 2 * WIDE, nx + 2 * NEAR
    wide, rows = ny + 2 * EDGE, ny + 2 * NEAR
    rim = whole(nx * (WIDE + NEAR), nz)
    lists = pltpu.SMEM(active.shape, jnp.int32)
    far, near_by = kernel(
        pack_kernel,
        (HBM, HBM, HBM),
        (rim, rim),
        (
            lists,
            pltpu.VMEM((2, nx, EDGE, nz), F32),
            pltpu.VMEM((2, nx, EDGE, nz), F32),
            pltpu.SemaphoreType.DMA((5,)),
        ),
    )(in_hbm(active), in_hbm(right_side), in_hbm(screening))
    far = swap(far, "gy", 1)
    near_by = swap(near_by, "gy", 0)
    side = whole(WIDE * (ny + 2 * WIDE) + NEAR * rows, nz)
    placed = (whole(planes, wide, nz), whole(nx, wide, nz), side, side)
    held = kernel(
        place_kernel, (HBM, VMEM, VMEM), placed, (lists, pltpu.SemaphoreType.DMA), flops=4_000_000
    )(in_hbm(active), right_side, screening)
    field, weight, cross, chip = kernel(
        widen_kernel, (VMEM,) * 6, placed, alias={k: k for k in range(4)}
    )(*held, far, near_by)
    cross = swap(cross, "gx", 1)
    chip = swap(chip, "gx", 0)
    lines = pltpu.VMEM((planes, wide + EDGE, nz), F32)
    inner = kernel(
        inner_kernel,
        (VMEM,) * 2,
        (whole(near, wide, nz),) * 2
        + (whole(near, rows, nz), whole(nx + NEAR, rows, nz))
        + (whole(planes, rows, nz),) * 2
        + (whole(near, rows, nz),) * 2
        + (whole(nx + NEAR, ny, nz),) * 2,
        (lines, lines),
        flops=20_000_000,
    )(field, weight)
    held = [field, *inner]
    done = kernel(
        outer_kernel,
        (VMEM,) * (2 + len(held)),
        [whole(*item.shape) for item in held] + [whole(1, nz)],
        (lines, lines),
        alias={2 + k: k for k in range(len(held))},
        flops=20_000_000,
    )(cross, chip, *held)
    field, _, _, first, second = done[:5]
    parts = lax.all_to_all(jnp.broadcast_to(done[-1], (devices, 1, nz)), ("gx", "gy"), 0, 0)
    slots = visible.shape[0]
    shape = (slots, 3, BLK**3 // nz, nz)
    indicator, crossing = kernel(
        finish_kernel,
        (HBM,) + (VMEM,) * 4,
        (slab, whole(*shape)),
        (
            pltpu.SMEM(visible.shape, jnp.int32),
            pltpu.VMEM(slab.shape, F32),
            pltpu.VMEM(shape, F32),
            pltpu.VMEM((nx + 1, ny + EDGE, nz), F32),
            pltpu.VMEM((3, nx * (ny + 1), nz), F32),
            pltpu.SemaphoreType.DMA,
            pltpu.SemaphoreType.DMA((slots,)),
            pltpu.SemaphoreType.DMA,
        ),
        results=HBM,
    )(in_hbm(visible), parts.reshape(devices, nz), field, first, second)
    return indicator, crossing.reshape(slots, 1, 3, BLK**3)


def solution(mesh):
    return jax.shard_map(
        body,
        mesh=mesh,
        in_specs=(
            P("gx", "gy", None),
            P("gx", "gy", None),
            P("gx", "gy", None),
            P("gx", "gy", None),
        ),
        out_specs=(P("gx", "gy", None), P("gx", "gy", None, None)),
        check_vma=False,
    )
```

```python
import functools

import jax
import jax.numpy as jnp
from jax import lax
from jax.experimental import pallas as pl
from jax.experimental.pallas import tpu as pltpu
from jax.sharding import PartitionSpec as P

BLK = 16
WIDE = 6
NEAR = 4
EDGE = 8
SHARP = 4.0
SCALE = 1.0 / 86400.0
SHIFT = 2.25
LOW, HIGH = 0.5, 7.0
SUMS = 16
F32 = jnp.float32


def mass(mid, one, two):
    return 66.0 * mid + (26.0 * one + two)


def stiff(mid, one, two):
    return 6.0 * mid - (2.0 * one + two)


def block_mask(active, slots, rows, columns):
    y = lax.broadcasted_iota(jnp.int32, (rows, columns), 0)
    z = lax.broadcasted_iota(jnp.int32, (rows, columns), 1)
    number = (y // BLK) * (columns // BLK) + z // BLK
    mask = jnp.zeros((rows, columns), F32)
    for slot in range(slots):
        mask = jnp.where(number == active[slot], 1.0, mask)
    return mask


def on_odd():
    return lax.rem(lax.axis_index("gx"), 2)


def odd_on(axis):
    return lax.rem(lax.axis_index(axis), 2)


def pack_kernel(active_hbm, right_hbm, screen_hbm, far, near, active, right, screen, sems):
    nx, ny, nz = right_hbm.shape
    arrays = ((right_hbm, right, WIDE, 0), (screen_hbm, screen, NEAR, nx * WIDE))
    copies = [pltpu.make_async_copy(active_hbm, active, sems.at[0])]
    for k, (source, target, _, _) in enumerate(arrays):
        for high in range(2):
            rows = pl.ds(high * (ny - EDGE), EDGE)
            copies.append(pltpu.make_async_copy(source.at[:, rows], target.at[high], sems.at[1 + 2 * k + high]))
    for copy in copies:
        copy.start()
    copies[0].wait()
    mask = block_mask(active, active.shape[0], ny, nz)
    for copy in copies[1:]:
        copy.wait()

    def write(high_out, low_out):
        for _, source, wide, base in arrays:
            for x in range(nx):
                rows = pl.ds(base + x * wide, wide)
                low_out[rows] = (source[0, x] * mask[:EDGE])[:wide]
                high_out[rows] = (source[1, x] * mask[ny - EDGE :])[EDGE - wide :]

    odd = odd_on("gy")
    pl.when(odd == 1)(functools.partial(write, far, near))
    pl.when(odd == 0)(functools.partial(write, near, far))


def message_rows(nx, ny):
    row = 0
    for array, wide in enumerate((WIDE, NEAR)):
        for x in range(wide):
            yield array, wide, x, row
            row += ny + 2 * wide


def place_kernel(active_hbm, right, screen, field, weight, cross, chip, active, sem):
    copy = pltpu.make_async_copy(active_hbm, active, sem)
    copy.start()
    nx, ny, nz = right.shape
    copy.wait()
    mask = block_mask(active, active.shape[0], ny, nz)
    for x in range(nx):
        field[WIDE + x, EDGE : EDGE + ny] = right[x] * mask
        weight[x, EDGE : EDGE + ny] = screen[x] * mask
    odd = odd_on("gx")
    for target, high in ((cross, odd), (chip, 1 - odd)):
        for array, wide, x, row in message_rows(nx, ny):
            source, first = ((field, WIDE), (weight, 0))[array]
            value = source[first + high * (nx - wide) + x, EDGE : EDGE + ny]
            target[row + wide : row + wide + ny] = value


def widen_kernel(field_in, weight_in, cross_in, chip_in, far, near, field, weight, cross, chip):
    nx, ny = weight.shape[0], weight.shape[1] - 2 * EDGE
    arrays = ((field, WIDE, 0, WIDE), (weight, NEAR, nx * WIDE, 0))

    def read(low, high):
        for target, wide, base, first in arrays:
            for x in range(nx):
                rows = pl.ds(base + x * wide, wide)
                target[first + x, EDGE - wide : EDGE] = low[rows]
                target[first + x, EDGE + ny : EDGE + ny + wide] = high[rows]

    odd = odd_on("gy")
    pl.when(odd == 1)(functools.partial(read, near, far))
    pl.when(odd == 0)(functools.partial(read, far, near))
    odd = odd_on("gx")
    for target, high in ((cross, odd), (chip, 1 - odd)):
        for array, wide, x, row in message_rows(nx, ny):
            source, first = ((field, WIDE), (weight, 0))[array]
            plane = first + high * (nx - wide) + x
            target[row : row + wide] = source[plane, EDGE - wide : EDGE]
            target[row + wide + ny : row + 2 * wide + ny] = source[plane, EDGE + ny : EDGE + ny + wide]


def along_z(value):
    lane = lax.broadcasted_iota(jnp.int32, value.shape, 1)
    last = value.shape[1]

    def shifted(step):
        before = jnp.where(lane >= step, pltpu.roll(value, step, 1), 0.0)
        after = jnp.where(lane < last - step, pltpu.roll(value, last - step, 1), 0.0)
        return before + after

    one, two = shifted(1), shifted(2)
    return mass(value, one, two), stiff(value, one, two)


def set_weight(keep, shifted, at, rows, weight):
    on = weight > 0.0
    keep[at, rows] = jnp.where(on, SCALE, 0.0)
    shifted[at, rows] = jnp.where(on, weight - SHIFT, 0.0)


def spread(source, za, zb, yp, yq, count, plane, start, rows):
    size = source.shape[1]

    @pl.loop(0, count, unroll=4)
    def _(k):
        x = plane(k)
        a, b = along_z(source[x])
        za[x, pl.ds(EDGE, size)] = a
        zb[x, pl.ds(EDGE, size)] = b

    @pl.loop(0, count, unroll=4)
    def _(k):
        x = plane(k)

        def part(ref, step):
            return ref[x, pl.ds(EDGE + start + step, rows)]

        a0, a1, a2 = part(za, 0), part(za, -1) + part(za, 1), part(za, -2) + part(za, 2)
        b0, b1, b2 = part(zb, 0), part(zb, -1) + part(zb, 1), part(zb, -2) + part(zb, 2)
        yp[x] = mass(a0, a1, a2)
        yq[x] = mass(b0, b1, b2) + stiff(a0, a1, a2)


def across(yp, yq, x):
    q0, q1, q2 = yq[x + 2], yq[x + 1] + yq[x + 3], yq[x] + yq[x + 4]
    p0, p1, p2 = yp[x + 2], yp[x + 1] + yp[x + 3], yp[x] + yp[x + 4]
    return mass(q0, q1, q2) + stiff(p0, p1, p2)


def step_up(target, source, keep, shifted, yp, yq, skip, rows, source_rows, count, plane):
    @pl.loop(0, count, unroll=4)
    def _(k):
        x = plane(k)
        target[x] = keep[x + skip, rows] * across(yp, yq, x) + shifted[x + skip, rows] * source[x + 2, source_rows]


def inner_kernel(field, weight, keep, shifted, first, second, yp1, yq1, yp2, yq2, yp3, yq3, za, zb):
    nx, wide = weight.shape[0], weight.shape[1]
    ny = wide - 2 * EDGE
    rows = ny + 2 * NEAR
    outer, every = pl.ds(EDGE - NEAR, rows), pl.ds(0, rows)
    for x in range(nx):
        set_weight(keep, shifted, NEAR + x, pl.ds(0, wide), weight[x])

    def plane(k):
        return WIDE + k

    spread(field, za, zb, yp1, yq1, nx, plane, EDGE - NEAR, rows)
    step_up(first, field, keep, shifted, yp1, yq1, 0, outer, outer, nx - 4, plane)
    spread(first, za, zb, yp2, yq2, nx - 4, plane, 0, rows)
    step_up(second, first, keep, shifted, yp2, yq2, 2, outer, every, nx - 8, plane)
    spread(second, za, zb, yp3, yq3, nx - 8, plane, NEAR, ny)


def outer_kernel(
    cross, chip, field_in, keep_in, shifted_in, first_in, second_in, p1, q1, p2, q2, p3, q3,
    field, keep, shifted, first, second, yp1, yq1, yp2, yq2, yp3, yq3, sums, za, zb,
):
    planes, wide, nz = field.shape
    nx, ny = planes - 2 * WIDE, wide - 2 * EDGE
    rows = ny + 2 * NEAR
    outer, every = pl.ds(EDGE - NEAR, rows), pl.ds(0, rows)
    odd = odd_on("gx")
    for source, high in ((cross, odd), (chip, 1 - odd)):
        for array, wide, x, row in message_rows(nx, ny):
            value = source[row : row + ny + 2 * wide]
            if array == 0:
                field[high * (nx + wide) + x, EDGE - wide : EDGE + ny + wide] = value
            else:
                set_weight(keep, shifted, high * (nx + wide) + x, outer, value)

    def side(total):
        return lambda k: k + jnp.where(k < WIDE, 0, total - 2 * WIDE)

    count = 2 * WIDE
    plane = side(nx + 2 * WIDE)
    spread(field, za, zb, yp1, yq1, count, plane, EDGE - NEAR, rows)
    plane = side(nx + 2 * NEAR)
    step_up(first, field, keep, shifted, yp1, yq1, 0, outer, outer, count, plane)
    spread(first, za, zb, yp2, yq2, count, plane, 0, rows)
    plane = side(nx + NEAR)
    step_up(second, first, keep, shifted, yp2, yq2, 2, outer, every, count, plane)
    spread(second, za, zb, yp3, yq3, count, plane, NEAR, ny)

    def fold(value):
        return jnp.sum(value.reshape(ny // 8, 8, nz), axis=0)

    mid, own = pl.ds(EDGE, ny), pl.ds(NEAR, ny)

    def add(x, totals):
        v0 = field[x + WIDE, mid]
        v1 = first[x + NEAR, own]
        v2 = second[x + 2, own]
        stay = keep[x + NEAR, mid]
        v3 = stay * across(yp3, yq3, x) + shifted[x + NEAR, mid] * v2
        on = jnp.where(stay > 0.0, 1.0, 0.0)
        new = (v0 * v0, v0 * v1, v1 * v1, v1 * v2, v2 * v2, v2 * v3, v0, v1, v2, on)
        return tuple(total + fold(value) for total, value in zip(totals, new))

    totals = lax.fori_loop(0, nx, add, (jnp.zeros((8, nz), F32),) * 10, unroll=4)
    row = lax.broadcasted_iota(jnp.int32, (SUMS, nz), 0)
    lane = lax.broadcasted_iota(jnp.int32, (SUMS, nz), 1)
    lines = jnp.zeros((SUMS, nz), F32)
    for place, total in enumerate(totals):
        lines = jnp.where(row == place, jnp.sum(total, axis=0, keepdims=True), lines)
    pair = (lines, jnp.zeros_like(lines))
    step = nz // 2
    while step:
        pair = pair_add(pair, (pltpu.roll(pair[0], step, 1), pltpu.roll(pair[1], step, 1)))
        step //= 2
    spot = jnp.where(lane == row, pair[0], jnp.where(lane == row + SUMS, pair[1], 0.0))
    sums[...] = jnp.sum(spot, axis=0, keepdims=True)


def two_sum(a, b):
    total = a + b
    part = total - a
    return total, (a - (total - part)) + (b - part)


def pair_add(a, b):
    total, rest = two_sum(a[0], b[0])
    return total, rest + (a[1] + b[1])


def halves(a):
    wide = 4097.0 * a
    top = wide - (wide - a)
    return top, a - top


def pair_mul(a, b):
    product = a[0] * b[0]
    a_top, a_rest = halves(a[0])
    b_top, b_rest = halves(b[0])
    rest = ((a_top * b_top - product) + a_top * b_rest + a_rest * b_top) + a_rest * b_rest
    rest = rest + (a[0] * b[1] + a[1] * b[0])
    total = product + rest
    return total, rest - (total - product)


def pair_sub(a, b):
    total, rest = two_sum(a[0], -b[0])
    rest = rest + (a[1] - b[1])
    out = total + rest
    return out, rest - (out - total)


def ratio(over, under, low, high):
    good = under > 0.0
    value = jnp.where(good, over / jnp.where(good, under, 1.0), 0.5 * (low + high))
    return jnp.minimum(jnp.maximum(value, low), high)


def coefficients(total):
    scale = 1.0 / total[0][0]
    zero = jnp.zeros_like(scale)
    g = [pair_mul(item, (scale, zero)) for item in total[:6]]
    shift = (jnp.full_like(scale, SHIFT), zero)
    h = [pair_add(g[k + 1], pair_mul(g[k], shift)) for k in range(5)]

    def minor(a, b, c, d):
        return pair_sub(pair_mul(a, b), pair_mul(c, d))

    s11 = minor(h[2], h[0], h[1], h[1])
    s12 = minor(h[3], h[0], h[1], h[2])
    s22 = minor(h[4], h[0], h[2], h[2])
    y1 = minor(g[1], h[0], h[1], g[0])
    y2 = minor(g[2], h[0], h[2], g[0])
    last = minor(s22, s11, s12, s12)
    side = minor(y2, s11, s12, y1)
    alpha = g[0][0] / h[0][0]
    l10 = h[1][0] / h[0][0]
    l20 = h[2][0] / h[0][0]
    l21 = ratio(s12[0], s11[0], l10 + (LOW - SHIFT), l10 + (HIGH - SHIFT))
    gamma1 = ratio(y1[0], s11[0], -alpha / LOW, -alpha / HIGH)
    gamma2 = ratio(side[0], last[0], -gamma1 / HIGH, -gamma1 / LOW)
    c1 = gamma1 - gamma2 * l21
    return alpha - c1 * l10 - gamma2 * l20, c1, gamma2


def sigmoid(value):
    return 1.0 / (1.0 + jnp.exp(-SHARP * value))


def finish_kernel(
    visible_hbm, parts, field, first, second, indicator_hbm, crossing_hbm,
    visible, indicator, crossing, level, weight, sem, slot_sems, result_sem,
):
    nx, ny, nz = indicator.shape
    copy = pltpu.make_async_copy(visible_hbm, visible, sem)
    copy.start()
    devices = parts.shape[0]
    tiles = [parts[pl.ds(8 * k, 8)] for k in range(devices // 8)]
    pairs = [(tile, pltpu.roll(tile, nz - SUMS, 1)) for tile in tiles]
    while len(pairs) > 1:
        pairs = [pair_add(a, b) for a, b in zip(pairs[::2], pairs[1::2])]
    total = pairs[0]
    for step in (4, 2, 1):
        total = pair_add(total, (pltpu.roll(total[0], step, 0), pltpu.roll(total[1], step, 0)))

    def spread(value, k):
        return jnp.broadcast_to(value[0:1, k : k + 1], (1, nz))

    item = [(spread(total[0], k), spread(total[1], k)) for k in range(10)]
    c0, c1, c2 = coefficients(item)
    over = c0 * (item[6][0] + item[6][1]) + c1 * (item[7][0] + item[7][1]) + c2 * (item[8][0] + item[8][1])
    iso = over / item[9][0]

    def set_level(x):
        v0 = field[x + WIDE, pl.ds(EDGE, ny + EDGE)]
        v1 = first[x + NEAR, pl.ds(NEAR, ny + NEAR)]
        v2 = second[x + 2, pl.ds(NEAR, ny + NEAR)]
        value = c0 * v0[: ny + NEAR] + c1 * v1 + c2 * v2
        level[x, pl.ds(0, ny + NEAR)] = sigmoid(value - iso)
        return value

    @pl.loop(0, nx, unroll=4)
    def _(x):
        indicator[x] = set_level(x)[:ny]

    set_level(nx)
    result = pltpu.make_async_copy(indicator, indicator_hbm, result_sem)
    result.start()
    outside = sigmoid(-iso)
    lane = lax.broadcasted_iota(jnp.int32, (ny, nz), 1)

    @pl.loop(0, nx, unroll=4)
    def _(x):
        here = level[x, pl.ds(0, ny)]
        above = jnp.where(lane < nz - 1, pltpu.roll(here, nz - 1, 1), outside)
        for edge, there in enumerate((level[x + 1, pl.ds(0, ny)], level[x, pl.ds(1, ny)], above)):
            weight[edge, pl.ds(x * (ny + 1), ny)] = here * (1.0 - there) + (1.0 - here) * there

    chunk = lax.broadcasted_iota(jnp.int32, (8, nz), 1) // BLK
    bricks_z = nz // BLK
    per_row = nz // BLK

    copy.wait()

    def out(slot):
        return pltpu.make_async_copy(crossing.at[slot], crossing_hbm.at[slot], slot_sems.at[slot])

    @pl.loop(0, visible.shape[0], unroll=2)
    def _(slot):
        number = visible[slot]
        safe = jnp.maximum(number, 0)
        begin = (safe // bricks_z) * BLK
        column = safe % bricks_z
        used = jnp.where(number >= 0, 1.0, 0.0)
        for edge in range(3):
            for half in range(2):
                for part in range(BLK // per_row):
                    tile = jnp.zeros((8, nz), F32)
                    for row in range(per_row):
                        at = half * 8 * (ny + 1) + begin + part * per_row + row
                        lines = weight[edge, pl.ds(at, 8, stride=ny + 1)]
                        turn = lax.rem((row - column) * BLK + nz, nz)
                        tile = jnp.where(chunk == row, pltpu.roll(lines, turn, 1), tile)
                    crossing[slot, edge, pl.ds(half * 16 + part, 8, stride=2)] = tile * used
        out(slot).start()

    for slot in range(visible.shape[0]):
        out(slot).wait()
    result.wait()


def whole(*shape):
    return jax.ShapeDtypeStruct(shape, F32)


VMEM = pl.BlockSpec(memory_space=pltpu.VMEM)


HBM = pl.BlockSpec(memory_space=pltpu.HBM)


def kernel(body, inputs, outputs, scratch=(), results=VMEM, alias=None, flops=0):
    return pl.pallas_call(
        body,
        in_specs=list(inputs),
        out_specs=[results] * len(outputs),
        out_shape=list(outputs),
        scratch_shapes=list(scratch),
        input_output_aliases=alias or {},
        cost_estimate=pl.CostEstimate(flops=flops, bytes_accessed=flops // 4, transcendentals=0),
        compiler_params=pltpu.CompilerParams(vmem_limit_bytes=32 * 1024 * 1024),
    )


def in_hbm(value):
    return pltpu.with_memory_space_constraint(value, pltpu.HBM)


def swap(value, axis, first):
    count = lax.axis_size(axis)
    pairs = [(k, k + 1) for k in range(first, count - 1, 2)]
    return lax.ppermute(value, axis, pairs + [(b, a) for a, b in pairs])


def body(right_side, screening, active_blocks, visible_bricks):
    nx, ny, nz = right_side.shape
    active = active_blocks.reshape(-1)
    visible = visible_bricks.reshape(-1)
    slab = whole(nx, ny, nz)
    planes, near = nx + 2 * WIDE, nx + 2 * NEAR
    wide, rows = ny + 2 * EDGE, ny + 2 * NEAR
    rim = whole(nx * (WIDE + NEAR), nz)
    lists = pltpu.SMEM(active.shape, jnp.int32)
    far, near_by = kernel(
        pack_kernel,
        (HBM, HBM, HBM),
        (rim, rim),
        (
            lists,
            pltpu.VMEM((2, nx, EDGE, nz), F32),
            pltpu.VMEM((2, nx, EDGE, nz), F32),
            pltpu.SemaphoreType.DMA((5,)),
        ),
    )(in_hbm(active), in_hbm(right_side), in_hbm(screening))
    far = swap(far, "gy", 1)
    near_by = swap(near_by, "gy", 0)
    side = whole(WIDE * (ny + 2 * WIDE) + NEAR * rows, nz)
    placed = (whole(planes, wide, nz), whole(nx, wide, nz), side, side)
    held = kernel(
        place_kernel, (HBM, VMEM, VMEM), placed, (lists, pltpu.SemaphoreType.DMA), flops=4_000_000
    )(in_hbm(active), right_side, screening)
    field, weight, cross, chip = kernel(
        widen_kernel, (VMEM,) * 6, placed, alias={k: k for k in range(4)}
    )(*held, far, near_by)
    cross = swap(cross, "gx", 1)
    chip = swap(chip, "gx", 0)
    lines = pltpu.VMEM((planes, wide + EDGE, nz), F32)
    inner = kernel(
        inner_kernel,
        (VMEM,) * 2,
        (whole(near, wide, nz),) * 2
        + (whole(near, rows, nz), whole(nx + NEAR, rows, nz))
        + (whole(planes, rows, nz),) * 2
        + (whole(near, rows, nz),) * 2
        + (whole(nx + NEAR, ny, nz),) * 2,
        (lines, lines),
        flops=20_000_000,
    )(field, weight)
    held = [field, *inner]
    done = kernel(
        outer_kernel,
        (VMEM,) * (2 + len(held)),
        [whole(*item.shape) for item in held] + [whole(1, nz)],
        (lines, lines),
        alias={2 + k: k for k in range(len(held))},
        flops=20_000_000,
    )(cross, chip, *held)
    field, _, _, first, second = done[:5]
    parts = done[-1]
    for axis in ("gx", "gy"):
        count = lax.axis_size(axis)
        parts = lax.all_to_all(jnp.broadcast_to(parts, (count,) + parts.shape), axis, 0, 0)
        parts = parts.reshape(-1, nz)
    slots = visible.shape[0]
    shape = (slots, 3, BLK**3 // nz, nz)
    indicator, crossing = kernel(
        finish_kernel,
        (HBM,) + (VMEM,) * 4,
        (slab, whole(*shape)),
        (
            pltpu.SMEM(visible.shape, jnp.int32),
            pltpu.VMEM(slab.shape, F32),
            pltpu.VMEM(shape, F32),
            pltpu.VMEM((nx + 1, ny + EDGE, nz), F32),
            pltpu.VMEM((3, nx * (ny + 1), nz), F32),
            pltpu.SemaphoreType.DMA,
            pltpu.SemaphoreType.DMA((slots,)),
            pltpu.SemaphoreType.DMA,
        ),
        results=HBM,
    )(in_hbm(visible), parts, field, first, second)
    return indicator, crossing.reshape(slots, 1, 3, BLK**3)


def solution(mesh):
    return jax.shard_map(
        body,
        mesh=mesh,
        in_specs=(
            P("gx", "gy", None),
            P("gx", "gy", None),
            P("gx", "gy", None),
            P("gx", "gy", None),
        ),
        out_specs=(P("gx", "gy", None), P("gx", "gy", None, None)),
        check_vma=False,
    )
```

```python
import functools

import jax
import jax.numpy as jnp
from jax import lax
from jax.experimental import pallas as pl
from jax.experimental.pallas import tpu as pltpu
from jax.sharding import PartitionSpec as P

BLK = 16
WIDE = 5
NEAR = 3
HEM = 4
EDGE = 8
SHARP = 4.0
SCALE = 1.0 / 86400.0
SHIFT = 2.25
LOW, HIGH = 0.5, 7.0
SUMS = 16
HELD = 11
F32 = jnp.float32


def mass(mid, one, two):
    return 66.0 * mid + (26.0 * one + two)


def stiff(mid, one, two):
    return 6.0 * mid - (2.0 * one + two)


def block_mask(active, slots, rows, columns):
    y = lax.broadcasted_iota(jnp.int32, (rows, columns), 0)
    z = lax.broadcasted_iota(jnp.int32, (rows, columns), 1)
    number = (y // BLK) * (columns // BLK) + z // BLK
    mask = jnp.zeros((rows, columns), F32)
    for slot in range(slots):
        mask = jnp.where(number == active[slot], 1.0, mask)
    return mask


def on_odd():
    return lax.rem(lax.axis_index("gx"), 2)


def odd_on(axis):
    return lax.rem(lax.axis_index(axis), 2)


def pack_kernel(active_hbm, right_hbm, screen_hbm, far, near, active, right, screen, sems):
    nx, ny, nz = right_hbm.shape
    arrays = ((right_hbm, right, WIDE, 0), (screen_hbm, screen, NEAR, nx * WIDE))
    copies = [pltpu.make_async_copy(active_hbm, active, sems.at[0])]
    for k, (source, target, _, _) in enumerate(arrays):
        for high in range(2):
            rows = pl.ds(high * (ny - EDGE), EDGE)
            copies.append(pltpu.make_async_copy(source.at[:, rows], target.at[high], sems.at[1 + 2 * k + high]))
    for copy in copies:
        copy.start()
    copies[0].wait()
    mask = block_mask(active, active.shape[0], ny, nz)
    for copy in copies[1:]:
        copy.wait()

    def write(high_out, low_out):
        for _, source, wide, base in arrays:
            for x in range(nx):
                rows = pl.ds(base + x * wide, wide)
                low_out[rows] = (source[0, x] * mask[:EDGE])[:wide]
                high_out[rows] = (source[1, x] * mask[ny - EDGE :])[EDGE - wide :]

    odd = odd_on("gy")
    pl.when(odd == 1)(functools.partial(write, far, near))
    pl.when(odd == 0)(functools.partial(write, near, far))


def message_rows(nx, ny):
    row = 0
    for array, wide in enumerate((WIDE, NEAR)):
        for x in range(wide):
            yield array, wide, x, row
            row += ny + 2 * wide


def place_kernel(active_hbm, right, screen, field, weight, cross, chip, active, sem):
    copy = pltpu.make_async_copy(active_hbm, active, sem)
    copy.start()
    nx, ny, nz = right.shape
    copy.wait()
    mask = block_mask(active, active.shape[0], ny, nz)
    for x in range(nx):
        field[WIDE + x, EDGE : EDGE + ny] = right[x] * mask
        weight[x, EDGE : EDGE + ny] = screen[x] * mask
    odd = odd_on("gx")
    for target, high in ((cross, odd), (chip, 1 - odd)):
        for array, wide, x, row in message_rows(nx, ny):
            source, first = ((field, WIDE), (weight, 0))[array]
            value = source[first + high * (nx - wide) + x, EDGE : EDGE + ny]
            target[row + wide : row + wide + ny] = value


def widen_kernel(field_in, weight_in, cross_in, chip_in, far, near, field, weight, cross, chip):
    nx, ny = weight.shape[0], weight.shape[1] - 2 * EDGE
    arrays = ((field, WIDE, 0, WIDE), (weight, NEAR, nx * WIDE, 0))

    def read(low, high):
        for target, wide, base, first in arrays:
            for x in range(nx):
                rows = pl.ds(base + x * wide, wide)
                target[first + x, EDGE - wide : EDGE] = low[rows]
                target[first + x, EDGE + ny : EDGE + ny + wide] = high[rows]

    odd = odd_on("gy")
    pl.when(odd == 1)(functools.partial(read, near, far))
    pl.when(odd == 0)(functools.partial(read, far, near))
    odd = odd_on("gx")
    for target, high in ((cross, odd), (chip, 1 - odd)):
        for array, wide, x, row in message_rows(nx, ny):
            source, first = ((field, WIDE), (weight, 0))[array]
            plane = first + high * (nx - wide) + x
            target[row : row + wide] = source[plane, EDGE - wide : EDGE]
            target[row + wide + ny : row + 2 * wide + ny] = source[plane, EDGE + ny : EDGE + ny + wide]


def along_z(value):
    lane = lax.broadcasted_iota(jnp.int32, value.shape, 1)
    last = value.shape[1]

    def shifted(step):
        before = jnp.where(lane >= step, pltpu.roll(value, step, 1), 0.0)
        after = jnp.where(lane < last - step, pltpu.roll(value, last - step, 1), 0.0)
        return before + after

    one, two = shifted(1), shifted(2)
    return mass(value, one, two), stiff(value, one, two)


def set_weight(keep, shifted, at, rows, weight):
    on = weight > 0.0
    keep[at, rows] = jnp.where(on, SCALE, 0.0)
    shifted[at, rows] = jnp.where(on, weight - SHIFT, 0.0)


def spread(source, za, zb, yp, yq, count, first, start, rows, skip=0, folded=False):
    size = source.shape[1]
    unroll = count if count < 8 else 4

    @pl.loop(0, count, unroll=unroll)
    def _(k):
        a, b = along_z(source[first + k])
        za[k, pl.ds(EDGE, size)] = a
        zb[k, pl.ds(EDGE, size)] = b

    row = lax.broadcasted_iota(jnp.int32, (8, source.shape[2]), 0)

    def far(below, above):
        if not folded:
            return below + above
        top = jnp.where(row == 0, 0.0, jnp.where(row == 1, 2.0 * below[:8], below[:8]))
        end = jnp.where(row == 7, 0.0, jnp.where(row == 6, 2.0 * above[-8:], above[-8:]))
        return jnp.concatenate([top, below[8:]], axis=0) + jnp.concatenate([above[:-8], end], axis=0)

    @pl.loop(0, count, unroll=unroll)
    def _(k):
        def part(ref, step):
            return ref[k, pl.ds(EDGE + start + step, rows)]

        a0, a1, a2 = part(za, 0), part(za, -1) + part(za, 1), far(part(za, -2), part(za, 2))
        b0, b1, b2 = part(zb, 0), part(zb, -1) + part(zb, 1), far(part(zb, -2), part(zb, 2))
        yp[first + skip + k] = mass(a0, a1, a2)
        yq[first + skip + k] = mass(b0, b1, b2) + stiff(a0, a1, a2)


def across(yp, yq, x):
    q0, q1, q2 = yq[x + 2], yq[x + 1] + yq[x + 3], yq[x] + yq[x + 4]
    p0, p1, p2 = yp[x + 2], yp[x + 1] + yp[x + 3], yp[x] + yp[x + 4]
    return mass(q0, q1, q2) + stiff(p0, p1, p2)


def step_up(target, source, keep, shifted, yp, yq, skip, rows, source_rows, count, first):
    @pl.loop(0, count, unroll=count if count < 8 else 4)
    def _(k):
        x = first + k
        target[x] = keep[x + skip, rows] * across(yp, yq, x) + shifted[x + skip, rows] * source[x + 2, source_rows]


def fold(value):
    return jnp.sum(value.reshape(-1, 8, value.shape[1]), axis=0)


def add_sums(totals, arrays, count, first_x):
    field, _, shifted, first, second, yp, yq = arrays
    ny = yp.shape[1]
    mid, own = pl.ds(EDGE, ny), pl.ds(HEM, ny)

    def add(k, totals):
        x = first_x + k
        v0 = field[x + WIDE, mid]
        v1 = first[x + NEAR, own]
        v2 = second[x + 1, own]
        weight = shifted[x + NEAR, mid]
        form = v2 * (SCALE * across(yp, yq, x) + weight * v2)
        on = jnp.where(arrays[1][x + NEAR, mid] > 0.0, 1.0, 0.0)
        new = (v0 * v0, v0 * v1, v1 * v1, v1 * v2, v2 * v2, form, v0, v1, v2, on)
        return tuple(total + fold(value) for total, value in zip(totals, new))

    return lax.fori_loop(0, count, add, totals, unroll=2)


def inner_kernel(field, weight, keep, shifted, first, second, yp1, yq1, yp2, yq2, yp3, yq3, sums, za, zb):
    nx, wide, nz = weight.shape
    ny = wide - 2 * EDGE
    rows = ny + 2 * HEM
    outer, every = pl.ds(EDGE - HEM, rows), pl.ds(0, rows)
    for x in range(nx):
        set_weight(keep, shifted, NEAR + x, pl.ds(0, wide), weight[x])
    spread(field, za, zb, yp1, yq1, nx, WIDE, EDGE - HEM, rows)
    step_up(first, field, keep, shifted, yp1, yq1, 0, outer, outer, nx - 4, WIDE)
    spread(first, za, zb, yp2, yq2, nx - 4, WIDE, 0, rows)
    step_up(second, first, keep, shifted, yp2, yq2, 2, outer, every, nx - 8, WIDE)
    spread(second, za, zb, yp3, yq3, nx - 8, WIDE, HEM, ny, 1, True)
    arrays = (field, keep, shifted, first, second, yp3, yq3)
    totals = add_sums((jnp.zeros((8, nz), F32),) * 10, arrays, nx - 12, WIDE + 1)
    for place, total in enumerate(totals):
        sums[place] = total


def side_kernel(last, message, *refs):
    sums_in = refs[HELD]
    field, keep, shifted, first, second, yp1, yq1, yp2, yq2, yp3, yq3, sums, za, zb = refs[HELD + 1 :]
    planes, wide, nz = field.shape
    nx, ny = planes - 2 * WIDE, wide - 2 * EDGE
    rows = ny + 2 * HEM
    outer, every = pl.ds(EDGE - HEM, rows), pl.ds(0, rows)
    odd = odd_on("gx")
    high = odd if last else 1 - odd
    for array, depth, x, row in message_rows(nx, ny):
        value = message[row : row + ny + 2 * depth]
        plane, span = high * (nx + depth) + x, pl.ds(EDGE - depth, ny + 2 * depth)
        if array == 0:
            field[plane, span] = value
        else:
            set_weight(keep, shifted, plane, span, value)
    spread(field, za, zb, yp1, yq1, WIDE, high * (planes - WIDE), EDGE - HEM, rows)
    base = high * (nx + 2 * NEAR - WIDE)
    step_up(first, field, keep, shifted, yp1, yq1, 0, outer, outer, WIDE, base)
    spread(first, za, zb, yp2, yq2, WIDE, base, 0, rows)
    base = high * (nx + 2 - WIDE)
    step_up(second, first, keep, shifted, yp2, yq2, 2, outer, every, WIDE, base)
    spread(second, za, zb, yp3, yq3, WIDE, base, HEM, ny, 1, True)
    none = jnp.zeros((ny, nz), F32)
    yp3[high * (nx + 3)] = none
    yq3[high * (nx + 3)] = none
    totals = tuple(sums_in[place] for place in range(10))
    arrays = (field, keep, shifted, first, second, yp3, yq3)
    totals = list(add_sums(totals, arrays, WIDE + 1, high * (nx - WIDE - 1)))
    own = pl.ds(HEM, ny)
    beside, edge, next_edge = 1 + high * (nx + 1), 2 + high * (nx - 1), 3 + high * (nx - 3)
    give = 13.0 * yq3[edge] - yp3[edge] + (yq3[next_edge] - yp3[next_edge])
    take = 13.0 * yq3[beside] - yp3[beside]
    totals[5] += SCALE * fold(second[beside - 1, own] * give - second[edge - 1, own] * take)
    if not last:
        for place, total in enumerate(totals):
            sums[place] = total
        return
    row = lax.broadcasted_iota(jnp.int32, (SUMS, nz), 0)
    lane = lax.broadcasted_iota(jnp.int32, (SUMS, nz), 1)
    lines = jnp.zeros((SUMS, nz), F32)
    for place, total in enumerate(totals):
        lines = jnp.where(row == place, jnp.sum(total, axis=0, keepdims=True), lines)
    pair = (lines, jnp.zeros_like(lines))
    step = nz // 2
    while step:
        pair = pair_add(pair, (pltpu.roll(pair[0], step, 1), pltpu.roll(pair[1], step, 1)))
        step //= 2
    spot = jnp.where(lane == row, pair[0], jnp.where(lane == row + SUMS, pair[1], 0.0))
    sums[...] = jnp.sum(spot, axis=0, keepdims=True)


def two_sum(a, b):
    total = a + b
    part = total - a
    return total, (a - (total - part)) + (b - part)


def pair_add(a, b):
    total, rest = two_sum(a[0], b[0])
    return total, rest + (a[1] + b[1])


def halves(a):
    wide = 4097.0 * a
    top = wide - (wide - a)
    return top, a - top


def pair_mul(a, b):
    product = a[0] * b[0]
    a_top, a_rest = halves(a[0])
    b_top, b_rest = halves(b[0])
    rest = ((a_top * b_top - product) + a_top * b_rest + a_rest * b_top) + a_rest * b_rest
    rest = rest + (a[0] * b[1] + a[1] * b[0])
    total = product + rest
    return total, rest - (total - product)


def pair_sub(a, b):
    total, rest = two_sum(a[0], -b[0])
    rest = rest + (a[1] - b[1])
    out = total + rest
    return out, rest - (out - total)


def ratio(over, under, low, high):
    good = under > 0.0
    value = jnp.where(good, over / jnp.where(good, under, 1.0), 0.5 * (low + high))
    return jnp.minimum(jnp.maximum(value, low), high)


def coefficients(total):
    scale = 1.0 / total[0][0]
    zero = jnp.zeros_like(scale)
    g = [pair_mul(item, (scale, zero)) for item in total[:6]]
    shift = (jnp.full_like(scale, SHIFT), zero)
    h = [pair_add(g[k + 1], pair_mul(g[k], shift)) for k in range(5)]

    def minor(a, b, c, d):
        return pair_sub(pair_mul(a, b), pair_mul(c, d))

    s11 = minor(h[2], h[0], h[1], h[1])
    s12 = minor(h[3], h[0], h[1], h[2])
    s22 = minor(h[4], h[0], h[2], h[2])
    y1 = minor(g[1], h[0], h[1], g[0])
    y2 = minor(g[2], h[0], h[2], g[0])
    last = minor(s22, s11, s12, s12)
    side = minor(y2, s11, s12, y1)
    alpha = g[0][0] / h[0][0]
    l10 = h[1][0] / h[0][0]
    l20 = h[2][0] / h[0][0]
    l21 = ratio(s12[0], s11[0], l10 + (LOW - SHIFT), l10 + (HIGH - SHIFT))
    gamma1 = ratio(y1[0], s11[0], -alpha / LOW, -alpha / HIGH)
    gamma2 = ratio(side[0], last[0], -gamma1 / HIGH, -gamma1 / LOW)
    c1 = gamma1 - gamma2 * l21
    return alpha - c1 * l10 - gamma2 * l20, c1, gamma2


def sigmoid(value):
    return 1.0 / (1.0 + jnp.exp(-SHARP * value))


def finish_kernel(
    visible_hbm, parts, field, first, second, indicator_hbm, crossing_hbm,
    visible, indicator, crossing, level, weight, sem, slot_sems, result_sem,
):
    nx, ny, nz = indicator.shape
    copy = pltpu.make_async_copy(visible_hbm, visible, sem)
    copy.start()
    devices = parts.shape[0]
    tiles = [parts[pl.ds(8 * k, 8)] for k in range(devices // 8)]
    pairs = [(tile, pltpu.roll(tile, nz - SUMS, 1)) for tile in tiles]
    while len(pairs) > 1:
        pairs = [pair_add(a, b) for a, b in zip(pairs[::2], pairs[1::2])]
    total = pairs[0]
    for step in (4, 2, 1):
        total = pair_add(total, (pltpu.roll(total[0], step, 0), pltpu.roll(total[1], step, 0)))

    def spread(value, k):
        return jnp.broadcast_to(value[0:1, k : k + 1], (1, nz))

    item = [(spread(total[0], k), spread(total[1], k)) for k in range(10)]
    c0, c1, c2 = coefficients(item)
    over = c0 * (item[6][0] + item[6][1]) + c1 * (item[7][0] + item[7][1]) + c2 * (item[8][0] + item[8][1])
    iso = over / item[9][0]

    def set_level(x):
        v0 = field[x + WIDE, pl.ds(EDGE, ny + EDGE)]
        v1 = first[x + NEAR, pl.ds(HEM, ny + HEM)]
        v2 = second[x + 1, pl.ds(HEM, ny + HEM)]
        value = c0 * v0[: ny + HEM] + c1 * v1 + c2 * v2
        level[x, pl.ds(0, ny + HEM)] = sigmoid(value - iso)
        return value

    @pl.loop(0, nx, unroll=4)
    def _(x):
        indicator[x] = set_level(x)[:ny]

    set_level(nx)
    result = pltpu.make_async_copy(indicator, indicator_hbm, result_sem)
    result.start()
    outside = sigmoid(-iso)
    lane = lax.broadcasted_iota(jnp.int32, (ny, nz), 1)

    @pl.loop(0, nx, unroll=4)
    def _(x):
        here = level[x, pl.ds(0, ny)]
        above = jnp.where(lane < nz - 1, pltpu.roll(here, nz - 1, 1), outside)
        for edge, there in enumerate((level[x + 1, pl.ds(0, ny)], level[x, pl.ds(1, ny)], above)):
            weight[edge, pl.ds(x * (ny + 1), ny)] = here * (1.0 - there) + (1.0 - here) * there

    chunk = lax.broadcasted_iota(jnp.int32, (8, nz), 1) // BLK
    bricks_z = nz // BLK
    per_row = nz // BLK

    copy.wait()

    def out(slot):
        return pltpu.make_async_copy(crossing.at[slot], crossing_hbm.at[slot], slot_sems.at[slot])

    @pl.loop(0, visible.shape[0], unroll=2)
    def _(slot):
        number = visible[slot]
        safe = jnp.maximum(number, 0)
        begin = (safe // bricks_z) * BLK
        column = safe % bricks_z
        used = jnp.where(number >= 0, 1.0, 0.0)
        for edge in range(3):
            for half in range(2):
                for part in range(BLK // per_row):
                    tile = jnp.zeros((8, nz), F32)
                    for row in range(per_row):
                        at = half * 8 * (ny + 1) + begin + part * per_row + row
                        lines = weight[edge, pl.ds(at, 8, stride=ny + 1)]
                        turn = lax.rem((row - column) * BLK + nz, nz)
                        tile = jnp.where(chunk == row, pltpu.roll(lines, turn, 1), tile)
                    crossing[slot, edge, pl.ds(half * 16 + part, 8, stride=2)] = tile * used
        out(slot).start()

    for slot in range(visible.shape[0]):
        out(slot).wait()
    result.wait()


def whole(*shape):
    return jax.ShapeDtypeStruct(shape, F32)


VMEM = pl.BlockSpec(memory_space=pltpu.VMEM)


HBM = pl.BlockSpec(memory_space=pltpu.HBM)


def kernel(body, inputs, outputs, scratch=(), results=VMEM, alias=None, flops=0):
    return pl.pallas_call(
        body,
        in_specs=list(inputs),
        out_specs=[results] * len(outputs),
        out_shape=list(outputs),
        scratch_shapes=list(scratch),
        input_output_aliases=alias or {},
        cost_estimate=pl.CostEstimate(flops=flops, bytes_accessed=flops // 4, transcendentals=0),
        compiler_params=pltpu.CompilerParams(vmem_limit_bytes=32 * 1024 * 1024),
    )


def in_hbm(value):
    return pltpu.with_memory_space_constraint(value, pltpu.HBM)


def swap(value, axis, first):
    count = lax.axis_size(axis)
    pairs = [(k, k + 1) for k in range(first, count - 1, 2)]
    return lax.ppermute(value, axis, pairs + [(b, a) for a, b in pairs])


def body(right_side, screening, active_blocks, visible_bricks):
    nx, ny, nz = right_side.shape
    active = active_blocks.reshape(-1)
    visible = visible_bricks.reshape(-1)
    devices = lax.axis_size("gx") * lax.axis_size("gy")
    slab = whole(nx, ny, nz)
    planes, near, third = nx + 2 * WIDE, nx + 2 * NEAR, nx + 2
    wide, rows = ny + 2 * EDGE, ny + 2 * HEM
    rim = whole(nx * (WIDE + NEAR), nz)
    lists = pltpu.SMEM(active.shape, jnp.int32)
    far, near_by = kernel(
        pack_kernel,
        (HBM, HBM, HBM),
        (rim, rim),
        (
            lists,
            pltpu.VMEM((2, nx, EDGE, nz), F32),
            pltpu.VMEM((2, nx, EDGE, nz), F32),
            pltpu.SemaphoreType.DMA((5,)),
        ),
    )(in_hbm(active), in_hbm(right_side), in_hbm(screening))
    far = swap(far, "gy", 1)
    near_by = swap(near_by, "gy", 0)
    lines = WIDE * (ny + 2 * WIDE) + NEAR * (ny + 2 * NEAR)
    side = whole(-(-lines // 8) * 8, nz)
    placed = (whole(planes, wide, nz), whole(nx, wide, nz), side, side)
    held = kernel(
        place_kernel, (HBM, VMEM, VMEM), placed, (lists, pltpu.SemaphoreType.DMA), flops=4_000_000
    )(in_hbm(active), right_side, screening)
    field, weight, cross, chip = kernel(
        widen_kernel, (VMEM,) * 6, placed, alias={k: k for k in range(4)}
    )(*held, far, near_by)
    cross = swap(cross, "gx", 1)
    chip = swap(chip, "gx", 0)
    work = (pltpu.VMEM((planes, wide + EDGE, nz), F32),) * 2
    kept = [whole(planes, wide, nz)] + [whole(near, wide, nz)] * 2
    kept += [whole(near, rows, nz), whole(third, rows, nz)]
    kept += [whole(planes, rows, nz)] * 2 + [whole(near, rows, nz)] * 2 + [whole(third + 2, ny, nz)] * 2
    tallies = whole(10, 8, nz)
    held = kernel(inner_kernel, (VMEM,) * 2, kept[1:] + [tallies], work, flops=20_000_000)(field, weight)
    held = [field, *held]
    for last, message in ((False, chip), (True, cross)):
        held = kernel(
            functools.partial(side_kernel, last),
            (VMEM,) * (HELD + 2),
            kept + [whole(1, nz) if last else tallies],
            work,
            alias={1 + k: k for k in range(HELD)},
            flops=10_000_000,
        )(message, *held)
    field, _, _, first, second = held[:5]
    devices = lax.axis_size("gx") * lax.axis_size("gy")
    parts = lax.all_to_all(jnp.broadcast_to(held[-1], (devices, 1, nz)), ("gx", "gy"), 0, 0)
    slots = visible.shape[0]
    shape = (slots, 3, BLK**3 // nz, nz)
    indicator, crossing = kernel(
        finish_kernel,
        (HBM,) + (VMEM,) * 4,
        (slab, whole(*shape)),
        (
            pltpu.SMEM(visible.shape, jnp.int32),
            pltpu.VMEM(slab.shape, F32),
            pltpu.VMEM(shape, F32),
            pltpu.VMEM((nx + 1, ny + EDGE, nz), F32),
            pltpu.VMEM((3, nx * (ny + 1), nz), F32),
            pltpu.SemaphoreType.DMA,
            pltpu.SemaphoreType.DMA((slots,)),
            pltpu.SemaphoreType.DMA,
        ),
        results=HBM,
    )(in_hbm(visible), parts.reshape(devices, nz), field, first, second)
    return indicator, crossing.reshape(slots, 1, 3, BLK**3)


def solution(mesh):
    return jax.shard_map(
        body,
        mesh=mesh,
        in_specs=(
            P("gx", "gy", None),
            P("gx", "gy", None),
            P("gx", "gy", None),
            P("gx", "gy", None),
        ),
        out_specs=(P("gx", "gy", None), P("gx", "gy", None, None)),
        check_vma=False,
    )
```

```python
import functools

import jax
import jax.numpy as jnp
from jax import lax
from jax.experimental import pallas as pl
from jax.experimental.pallas import tpu as pltpu
from jax.sharding import PartitionSpec as P

BLK = 16
WIDE = 5
NEAR = 3
HEM = 4
EDGE = 8
SHARP = 4.0
SCALE = 1.0 / 86400.0
SHIFT = 2.25
LOW, HIGH = 0.5, 7.0
SUMS = 16
HELD = 11
F32 = jnp.float32


def mass(mid, one, two):
    return 66.0 * mid + (26.0 * one + two)


def stiff(mid, one, two):
    return 6.0 * mid - (2.0 * one + two)


def block_mask(active, slots, rows, columns):
    y = lax.broadcasted_iota(jnp.int32, (rows, columns), 0)
    z = lax.broadcasted_iota(jnp.int32, (rows, columns), 1)
    number = (y // BLK) * (columns // BLK) + z // BLK
    mask = jnp.zeros((rows, columns), F32)
    for slot in range(slots):
        mask = jnp.where(number == active[slot], 1.0, mask)
    return mask


def on_odd():
    return lax.rem(lax.axis_index("gx"), 2)


def odd_on(axis):
    return lax.rem(lax.axis_index(axis), 2)


def pack_kernel(active_hbm, right_hbm, screen_hbm, far, near, active, right, screen, sems):
    nx, ny, nz = right_hbm.shape
    arrays = ((right_hbm, right, WIDE, 0), (screen_hbm, screen, NEAR, nx * WIDE))
    copies = [pltpu.make_async_copy(active_hbm, active, sems.at[0])]
    for k, (source, target, _, _) in enumerate(arrays):
        for high in range(2):
            rows = pl.ds(high * (ny - EDGE), EDGE)
            copies.append(pltpu.make_async_copy(source.at[:, rows], target.at[high], sems.at[1 + 2 * k + high]))
    for copy in copies:
        copy.start()
    copies[0].wait()
    mask = block_mask(active, active.shape[0], ny, nz)
    for copy in copies[1:]:
        copy.wait()

    def write(high_out, low_out):
        for _, source, wide, base in arrays:
            for x in range(nx):
                rows = pl.ds(base + x * wide, wide)
                low_out[rows] = (source[0, x] * mask[:EDGE])[:wide]
                high_out[rows] = (source[1, x] * mask[ny - EDGE :])[EDGE - wide :]

    odd = odd_on("gy")
    pl.when(odd == 1)(functools.partial(write, far, near))
    pl.when(odd == 0)(functools.partial(write, near, far))


def message_rows(nx, ny):
    row = 0
    for array, wide in enumerate((WIDE, NEAR)):
        for x in range(wide):
            yield array, wide, x, row
            row += ny + 2 * wide


def place_kernel(active_hbm, right, screen, field, weight, cross, chip, active, sem):
    copy = pltpu.make_async_copy(active_hbm, active, sem)
    copy.start()
    nx, ny, nz = right.shape
    copy.wait()
    mask = block_mask(active, active.shape[0], ny, nz)
    for x in range(nx):
        field[WIDE + x, EDGE : EDGE + ny] = right[x] * mask
        weight[x, EDGE : EDGE + ny] = screen[x] * mask
    odd = odd_on("gx")
    for target, high in ((cross, odd), (chip, 1 - odd)):
        for array, wide, x, row in message_rows(nx, ny):
            source, first = ((field, WIDE), (weight, 0))[array]
            value = source[first + high * (nx - wide) + x, EDGE : EDGE + ny]
            target[row + wide : row + wide + ny] = value


def widen_kernel(field_in, weight_in, cross_in, chip_in, far, near, field, weight, cross, chip):
    nx, ny = weight.shape[0], weight.shape[1] - 2 * EDGE
    arrays = ((field, WIDE, 0, WIDE), (weight, NEAR, nx * WIDE, 0))

    def read(low, high):
        for target, wide, base, first in arrays:
            for x in range(nx):
                rows = pl.ds(base + x * wide, wide)
                target[first + x, EDGE - wide : EDGE] = low[rows]
                target[first + x, EDGE + ny : EDGE + ny + wide] = high[rows]

    odd = odd_on("gy")
    pl.when(odd == 1)(functools.partial(read, near, far))
    pl.when(odd == 0)(functools.partial(read, far, near))
    odd = odd_on("gx")
    for target, high in ((cross, odd), (chip, 1 - odd)):
        for array, wide, x, row in message_rows(nx, ny):
            source, first = ((field, WIDE), (weight, 0))[array]
            plane = first + high * (nx - wide) + x
            target[row : row + wide] = source[plane, EDGE - wide : EDGE]
            target[row + wide + ny : row + 2 * wide + ny] = source[plane, EDGE + ny : EDGE + ny + wide]


def along_z(value):
    lane = lax.broadcasted_iota(jnp.int32, value.shape, 1)
    last = value.shape[1]

    def shifted(step):
        before = jnp.where(lane >= step, pltpu.roll(value, step, 1), 0.0)
        after = jnp.where(lane < last - step, pltpu.roll(value, last - step, 1), 0.0)
        return before + after

    one, two = shifted(1), shifted(2)
    return mass(value, one, two), stiff(value, one, two)


def set_weight(keep, shifted, at, rows, weight):
    on = weight > 0.0
    keep[at, rows] = jnp.where(on, SCALE, 0.0)
    shifted[at, rows] = jnp.where(on, weight - SHIFT, 0.0)


def spread(source, za, zb, yp, yq, count, first, start, rows, skip=0, folded=False):
    size = source.shape[1]
    unroll = count if count < 8 else 4

    @pl.loop(0, count, unroll=unroll)
    def _(k):
        a, b = along_z(source[first + k])
        za[k, pl.ds(EDGE, size)] = a
        zb[k, pl.ds(EDGE, size)] = b

    row = lax.broadcasted_iota(jnp.int32, (8, source.shape[2]), 0)

    def far(below, above):
        if not folded:
            return below + above
        top = jnp.where(row == 0, 0.0, jnp.where(row == 1, 2.0 * below[:8], below[:8]))
        end = jnp.where(row == 7, 0.0, jnp.where(row == 6, 2.0 * above[-8:], above[-8:]))
        return jnp.concatenate([top, below[8:]], axis=0) + jnp.concatenate([above[:-8], end], axis=0)

    @pl.loop(0, count, unroll=unroll)
    def _(k):
        def part(ref, step):
            return ref[k, pl.ds(EDGE + start + step, rows)]

        a0, a1, a2 = part(za, 0), part(za, -1) + part(za, 1), far(part(za, -2), part(za, 2))
        b0, b1, b2 = part(zb, 0), part(zb, -1) + part(zb, 1), far(part(zb, -2), part(zb, 2))
        yp[first + skip + k] = mass(a0, a1, a2)
        yq[first + skip + k] = mass(b0, b1, b2) + stiff(a0, a1, a2)


def across(yp, yq, x):
    q0, q1, q2 = yq[x + 2], yq[x + 1] + yq[x + 3], yq[x] + yq[x + 4]
    p0, p1, p2 = yp[x + 2], yp[x + 1] + yp[x + 3], yp[x] + yp[x + 4]
    return mass(q0, q1, q2) + stiff(p0, p1, p2)


def step_up(target, source, keep, shifted, yp, yq, skip, rows, source_rows, count, first):
    @pl.loop(0, count, unroll=count if count < 8 else 4)
    def _(k):
        x = first + k
        target[x] = keep[x + skip, rows] * across(yp, yq, x) + shifted[x + skip, rows] * source[x + 2, source_rows]


def fold(value):
    return jnp.sum(value.reshape(-1, 8, value.shape[1]), axis=0)


def add_sums(totals, arrays, count, first_x):
    field, _, shifted, first, second, yp, yq = arrays
    ny = yp.shape[1]
    mid, own = pl.ds(EDGE, ny), pl.ds(HEM, ny)

    def add(k, totals):
        x = first_x + k
        v0 = field[x + WIDE, mid]
        v1 = first[x + NEAR, own]
        v2 = second[x + 1, own]
        weight = shifted[x + NEAR, mid]
        form = v2 * (SCALE * across(yp, yq, x) + weight * v2)
        on = jnp.where(arrays[1][x + NEAR, mid] > 0.0, 1.0, 0.0)
        new = (v0 * v0, v0 * v1, v1 * v1, v1 * v2, v2 * v2, form, v0, v1, v2, on)
        return tuple(total + fold(value) for total, value in zip(totals, new))

    return lax.fori_loop(0, count, add, totals, unroll=2)


def inner_kernel(field, weight, keep, shifted, first, second, yp1, yq1, yp2, yq2, yp3, yq3, sums, za, zb):
    nx, wide, nz = weight.shape
    ny = wide - 2 * EDGE
    rows = ny + 2 * HEM
    outer, every = pl.ds(EDGE - HEM, rows), pl.ds(0, rows)
    for x in range(nx):
        set_weight(keep, shifted, NEAR + x, pl.ds(0, wide), weight[x])
    spread(field, za, zb, yp1, yq1, nx, WIDE, EDGE - HEM, rows)
    step_up(first, field, keep, shifted, yp1, yq1, 0, outer, outer, nx - 4, WIDE)
    spread(first, za, zb, yp2, yq2, nx - 4, WIDE, 0, rows)
    step_up(second, first, keep, shifted, yp2, yq2, 2, outer, every, nx - 8, WIDE)
    spread(second, za, zb, yp3, yq3, nx - 8, WIDE, HEM, ny, 1, True)
    arrays = (field, keep, shifted, first, second, yp3, yq3)
    totals = add_sums((jnp.zeros((8, nz), F32),) * 10, arrays, nx - 12, WIDE + 1)
    for place, total in enumerate(totals):
        sums[place] = total


def side_kernel(last, message, *refs):
    sums_in = refs[HELD]
    field, keep, shifted, first, second, yp1, yq1, yp2, yq2, yp3, yq3, sums, za, zb = refs[HELD + 1 :]
    planes, wide, nz = field.shape
    nx, ny = planes - 2 * WIDE, wide - 2 * EDGE
    rows = ny + 2 * HEM
    outer, every = pl.ds(EDGE - HEM, rows), pl.ds(0, rows)
    odd = odd_on("gx")
    high = odd if last else 1 - odd
    for array, depth, x, row in message_rows(nx, ny):
        value = message[row : row + ny + 2 * depth]
        plane, span = high * (nx + depth) + x, pl.ds(EDGE - depth, ny + 2 * depth)
        if array == 0:
            field[plane, span] = value
        else:
            set_weight(keep, shifted, plane, span, value)
    spread(field, za, zb, yp1, yq1, WIDE, high * (planes - WIDE), EDGE - HEM, rows)
    base = high * (nx + 2 * NEAR - WIDE)
    step_up(first, field, keep, shifted, yp1, yq1, 0, outer, outer, WIDE, base)
    spread(first, za, zb, yp2, yq2, WIDE, base, 0, rows)
    base = high * (nx + 2 - WIDE)
    step_up(second, first, keep, shifted, yp2, yq2, 2, outer, every, WIDE, base)
    spread(second, za, zb, yp3, yq3, WIDE, base, HEM, ny, 1, True)
    none = jnp.zeros((ny, nz), F32)
    yp3[high * (nx + 3)] = none
    yq3[high * (nx + 3)] = none
    totals = tuple(sums_in[place] for place in range(10))
    arrays = (field, keep, shifted, first, second, yp3, yq3)
    totals = list(add_sums(totals, arrays, WIDE + 1, high * (nx - WIDE - 1)))
    own = pl.ds(HEM, ny)
    beside, edge, next_edge = 1 + high * (nx + 1), 2 + high * (nx - 1), 3 + high * (nx - 3)
    give = 13.0 * yq3[edge] - yp3[edge] + (yq3[next_edge] - yp3[next_edge])
    take = 13.0 * yq3[beside] - yp3[beside]
    totals[5] += SCALE * fold(second[beside - 1, own] * give - second[edge - 1, own] * take)
    if not last:
        for place, total in enumerate(totals):
            sums[place] = total
        return
    row = lax.broadcasted_iota(jnp.int32, (SUMS, nz), 0)
    lane = lax.broadcasted_iota(jnp.int32, (SUMS, nz), 1)
    lines = jnp.zeros((SUMS, nz), F32)
    for place, total in enumerate(totals):
        lines = jnp.where(row == place, jnp.sum(total, axis=0, keepdims=True), lines)
    pair = (lines, jnp.zeros_like(lines))
    step = nz // 2
    while step:
        pair = pair_add(pair, (pltpu.roll(pair[0], step, 1), pltpu.roll(pair[1], step, 1)))
        step //= 2
    spot = jnp.where(lane == row, pair[0], jnp.where(lane == row + SUMS, pair[1], 0.0))
    sums[...] = jnp.sum(spot, axis=0, keepdims=True)


def two_sum(a, b):
    total = a + b
    part = total - a
    return total, (a - (total - part)) + (b - part)


def pair_add(a, b):
    total, rest = two_sum(a[0], b[0])
    return total, rest + (a[1] + b[1])


def halves(a):
    wide = 4097.0 * a
    top = wide - (wide - a)
    return top, a - top


def pair_mul(a, b):
    product = a[0] * b[0]
    a_top, a_rest = halves(a[0])
    b_top, b_rest = halves(b[0])
    rest = ((a_top * b_top - product) + a_top * b_rest + a_rest * b_top) + a_rest * b_rest
    rest = rest + (a[0] * b[1] + a[1] * b[0])
    total = product + rest
    return total, rest - (total - product)


def pair_sub(a, b):
    total, rest = two_sum(a[0], -b[0])
    rest = rest + (a[1] - b[1])
    out = total + rest
    return out, rest - (out - total)


def ratio(over, under, low, high):
    good = under > 0.0
    value = jnp.where(good, over / jnp.where(good, under, 1.0), 0.5 * (low + high))
    return jnp.minimum(jnp.maximum(value, low), high)


def coefficients(total):
    scale = 1.0 / total[0][0]
    zero = jnp.zeros_like(scale)
    g = [pair_mul(item, (scale, zero)) for item in total[:6]]
    shift = (jnp.full_like(scale, SHIFT), zero)
    h = [pair_add(g[k + 1], pair_mul(g[k], shift)) for k in range(5)]

    def minor(a, b, c, d):
        return pair_sub(pair_mul(a, b), pair_mul(c, d))

    s11 = minor(h[2], h[0], h[1], h[1])
    s12 = minor(h[3], h[0], h[1], h[2])
    s22 = minor(h[4], h[0], h[2], h[2])
    y1 = minor(g[1], h[0], h[1], g[0])
    y2 = minor(g[2], h[0], h[2], g[0])
    last = minor(s22, s11, s12, s12)
    side = minor(y2, s11, s12, y1)
    alpha = g[0][0] / h[0][0]
    l10 = h[1][0] / h[0][0]
    l20 = h[2][0] / h[0][0]
    l21 = ratio(s12[0], s11[0], l10 + (LOW - SHIFT), l10 + (HIGH - SHIFT))
    gamma1 = ratio(y1[0], s11[0], -alpha / LOW, -alpha / HIGH)
    gamma2 = ratio(side[0], last[0], -gamma1 / HIGH, -gamma1 / LOW)
    c1 = gamma1 - gamma2 * l21
    return alpha - c1 * l10 - gamma2 * l20, c1, gamma2


def sigmoid(value):
    return 1.0 / (1.0 + jnp.exp(-SHARP * value))


def finish_kernel(
    visible_hbm, parts, field, first, second, indicator_hbm, crossing_hbm,
    visible, indicator, crossing, level, weight, sem, slot_sems, result_sem,
):
    nx, ny, nz = indicator.shape
    copy = pltpu.make_async_copy(visible_hbm, visible, sem)
    copy.start()
    devices = parts.shape[0]
    tiles = [parts[pl.ds(8 * k, 8)] for k in range(devices // 8)]
    pairs = [(tile, pltpu.roll(tile, nz - SUMS, 1)) for tile in tiles]
    while len(pairs) > 1:
        pairs = [pair_add(a, b) for a, b in zip(pairs[::2], pairs[1::2])]
    total = pairs[0]
    for step in (4, 2, 1):
        total = pair_add(total, (pltpu.roll(total[0], step, 0), pltpu.roll(total[1], step, 0)))

    def spread(value, k):
        return jnp.broadcast_to(value[0:1, k : k + 1], (1, nz))

    item = [(spread(total[0], k), spread(total[1], k)) for k in range(10)]
    c0, c1, c2 = coefficients(item)
    over = c0 * (item[6][0] + item[6][1]) + c1 * (item[7][0] + item[7][1]) + c2 * (item[8][0] + item[8][1])
    iso = over / item[9][0]

    def set_level(x):
        v0 = field[x + WIDE, pl.ds(EDGE, ny + EDGE)]
        v1 = first[x + NEAR, pl.ds(HEM, ny + HEM)]
        v2 = second[x + 1, pl.ds(HEM, ny + HEM)]
        value = c0 * v0[: ny + HEM] + c1 * v1 + c2 * v2
        level[x, pl.ds(0, ny + HEM)] = sigmoid(value - iso)
        return value

    @pl.loop(0, nx, unroll=4)
    def _(x):
        indicator[x] = set_level(x)[:ny]

    set_level(nx)
    result = pltpu.make_async_copy(indicator, indicator_hbm, result_sem)
    result.start()
    outside = sigmoid(-iso)
    lane = lax.broadcasted_iota(jnp.int32, (ny, nz), 1)

    @pl.loop(0, nx, unroll=4)
    def _(x):
        here = level[x, pl.ds(0, ny)]
        above = jnp.where(lane < nz - 1, pltpu.roll(here, nz - 1, 1), outside)
        for edge, there in enumerate((level[x + 1, pl.ds(0, ny)], level[x, pl.ds(1, ny)], above)):
            weight[edge, pl.ds(x * (ny + 1), ny)] = here * (1.0 - there) + (1.0 - here) * there

    chunk = lax.broadcasted_iota(jnp.int32, (8, nz), 1) // BLK
    bricks_z = nz // BLK
    per_row = nz // BLK

    copy.wait()

    def out(slot):
        return pltpu.make_async_copy(crossing.at[slot], crossing_hbm.at[slot], slot_sems.at[slot])

    @pl.loop(0, visible.shape[0], unroll=2)
    def _(slot):
        number = visible[slot]
        safe = jnp.maximum(number, 0)
        begin = (safe // bricks_z) * BLK
        column = safe % bricks_z
        used = jnp.where(number >= 0, 1.0, 0.0)
        for edge in range(3):
            for half in range(2):
                for part in range(BLK // per_row):
                    tile = jnp.zeros((8, nz), F32)
                    for row in range(per_row):
                        at = half * 8 * (ny + 1) + begin + part * per_row + row
                        lines = weight[edge, pl.ds(at, 8, stride=ny + 1)]
                        turn = lax.rem((row - column) * BLK + nz, nz)
                        tile = jnp.where(chunk == row, pltpu.roll(lines, turn, 1), tile)
                    crossing[slot, edge, pl.ds(half * 16 + part, 8, stride=2)] = tile * used
        out(slot).start()

    for slot in range(visible.shape[0]):
        out(slot).wait()
    result.wait()


def whole(*shape):
    return jax.ShapeDtypeStruct(shape, F32)


VMEM = pl.BlockSpec(memory_space=pltpu.VMEM)


HBM = pl.BlockSpec(memory_space=pltpu.HBM)


def kernel(body, inputs, outputs, scratch=(), results=VMEM, alias=None, flops=0):
    return pl.pallas_call(
        body,
        in_specs=list(inputs),
        out_specs=[results] * len(outputs),
        out_shape=list(outputs),
        scratch_shapes=list(scratch),
        input_output_aliases=alias or {},
        cost_estimate=pl.CostEstimate(flops=flops, bytes_accessed=flops // 4, transcendentals=0),
        compiler_params=pltpu.CompilerParams(vmem_limit_bytes=32 * 1024 * 1024),
    )


def in_hbm(value):
    return pltpu.with_memory_space_constraint(value, pltpu.HBM)


def swap(value, axis, first):
    count = lax.axis_size(axis)
    pairs = [(k, k + 1) for k in range(first, count - 1, 2)]
    return lax.ppermute(value, axis, pairs + [(b, a) for a, b in pairs])


def body(right_side, screening, active_blocks, visible_bricks):
    nx, ny, nz = right_side.shape
    active = active_blocks.reshape(-1)
    visible = visible_bricks.reshape(-1)
    devices = lax.axis_size("gx") * lax.axis_size("gy")
    slab = whole(nx, ny, nz)
    planes, near, third = nx + 2 * WIDE, nx + 2 * NEAR, nx + 2
    wide, rows = ny + 2 * EDGE, ny + 2 * HEM
    rim = whole(nx * (WIDE + NEAR), nz)
    lists = pltpu.SMEM(active.shape, jnp.int32)
    far, near_by = kernel(
        pack_kernel,
        (HBM, HBM, HBM),
        (rim, rim),
        (
            lists,
            pltpu.VMEM((2, nx, EDGE, nz), F32),
            pltpu.VMEM((2, nx, EDGE, nz), F32),
            pltpu.SemaphoreType.DMA((5,)),
        ),
    )(in_hbm(active), in_hbm(right_side), in_hbm(screening))
    far = swap(far, "gy", 1)
    near_by = swap(near_by, "gy", 0)
    lines = WIDE * (ny + 2 * WIDE) + NEAR * (ny + 2 * NEAR)
    side = whole(-(-lines // 8) * 8, nz)
    placed = (whole(planes, wide, nz), whole(nx, wide, nz), side, side)
    held = kernel(
        place_kernel, (HBM, VMEM, VMEM), placed, (lists, pltpu.SemaphoreType.DMA), flops=4_000_000
    )(in_hbm(active), right_side, screening)
    field, weight, cross, chip = kernel(
        widen_kernel, (VMEM,) * 6, placed, alias={k: k for k in range(4)}
    )(*held, far, near_by)
    cross = swap(cross, "gx", 1)
    chip = swap(chip, "gx", 0)
    work = (pltpu.VMEM((planes, wide + EDGE, nz), F32),) * 2
    kept = [whole(planes, wide, nz)] + [whole(near, wide, nz)] * 2
    kept += [whole(near, rows, nz), whole(third, rows, nz)]
    kept += [whole(planes, rows, nz)] * 2 + [whole(near, rows, nz)] * 2 + [whole(third + 2, ny, nz)] * 2
    tallies = whole(10, 8, nz)
    held = kernel(inner_kernel, (VMEM,) * 2, kept[1:] + [tallies], work, flops=20_000_000)(field, weight)
    held = [field, *held]
    for last, message in ((False, chip), (True, cross)):
        held = kernel(
            functools.partial(side_kernel, last),
            (VMEM,) * (HELD + 2),
            kept + [whole(1, nz) if last else tallies],
            work,
            alias={1 + k: k for k in range(HELD)},
            flops=10_000_000,
        )(message, *held)
    field, _, _, first, second = held[:5]
    devices = lax.axis_size("gx") * lax.axis_size("gy")
    order = [list(range(devices - 1, -1, -1))]
    parts = jnp.broadcast_to(held[-1], (devices, 1, nz))
    parts = lax.all_to_all(parts, ("gx", "gy"), 0, 0, axis_index_groups=order)
    slots = visible.shape[0]
    shape = (slots, 3, BLK**3 // nz, nz)
    indicator, crossing = kernel(
        finish_kernel,
        (HBM,) + (VMEM,) * 4,
        (slab, whole(*shape)),
        (
            pltpu.SMEM(visible.shape, jnp.int32),
            pltpu.VMEM(slab.shape, F32),
            pltpu.VMEM(shape, F32),
            pltpu.VMEM((nx + 1, ny + EDGE, nz), F32),
            pltpu.VMEM((3, nx * (ny + 1), nz), F32),
            pltpu.SemaphoreType.DMA,
            pltpu.SemaphoreType.DMA((slots,)),
            pltpu.SemaphoreType.DMA,
        ),
        results=HBM,
    )(in_hbm(visible), parts.reshape(devices, nz), field, first, second)
    return indicator, crossing.reshape(slots, 1, 3, BLK**3)


def solution(mesh):
    return jax.shard_map(
        body,
        mesh=mesh,
        in_specs=(
            P("gx", "gy", None),
            P("gx", "gy", None),
            P("gx", "gy", None),
            P("gx", "gy", None),
        ),
        out_specs=(P("gx", "gy", None), P("gx", "gy", None, None)),
        check_vma=False,
    )
```

```python
import functools

import jax
import jax.numpy as jnp
from jax import lax
from jax.experimental import pallas as pl
from jax.experimental.pallas import tpu as pltpu
from jax.sharding import PartitionSpec as P

BLK = 16
WIDE = 5
NEAR = 3
HEM = 4
EDGE = 8
SHARP = 4.0
SCALE = 1.0 / 86400.0
SHIFT = 2.25
LOW, HIGH = 0.5, 7.0
SUMS = 16
HELD = 11
F32 = jnp.float32


def mass(mid, one, two):
    return 66.0 * mid + (26.0 * one + two)


def stiff(mid, one, two):
    return 6.0 * mid - (2.0 * one + two)


def block_mask(active, slots, rows, columns):
    y = lax.broadcasted_iota(jnp.int32, (rows, columns), 0)
    z = lax.broadcasted_iota(jnp.int32, (rows, columns), 1)
    number = (y // BLK) * (columns // BLK) + z // BLK
    mask = jnp.zeros((rows, columns), F32)
    for slot in range(slots):
        mask = jnp.where(number == active[slot], 1.0, mask)
    return mask


def on_odd():
    return lax.rem(lax.axis_index("gx"), 2)


def odd_on(axis):
    return lax.rem(lax.axis_index(axis), 2)


def pack_kernel(active_hbm, right_hbm, screen_hbm, far, near, active, right, screen, sems):
    nx, ny, nz = right_hbm.shape
    arrays = ((right_hbm, right, WIDE, 0), (screen_hbm, screen, NEAR, nx * WIDE))
    copies = [pltpu.make_async_copy(active_hbm, active, sems.at[0])]
    for k, (source, target, _, _) in enumerate(arrays):
        for high in range(2):
            rows = pl.ds(high * (ny - EDGE), EDGE)
            copies.append(pltpu.make_async_copy(source.at[:, rows], target.at[high], sems.at[1 + 2 * k + high]))
    for copy in copies:
        copy.start()
    copies[0].wait()
    mask = block_mask(active, active.shape[0], ny, nz)
    for copy in copies[1:]:
        copy.wait()

    def write(high_out, low_out):
        for _, source, wide, base in arrays:
            for x in range(nx):
                rows = pl.ds(base + x * wide, wide)
                low_out[rows] = (source[0, x] * mask[:EDGE])[:wide]
                high_out[rows] = (source[1, x] * mask[ny - EDGE :])[EDGE - wide :]

    odd = odd_on("gy")
    pl.when(odd == 1)(functools.partial(write, far, near))
    pl.when(odd == 0)(functools.partial(write, near, far))


def message_rows(nx, ny):
    row = 0
    for array, wide in enumerate((WIDE, NEAR)):
        for x in range(wide):
            yield array, wide, x, row
            row += ny + 2 * wide


def place_kernel(active_hbm, right, screen, field, weight, cross, chip, active, sem):
    copy = pltpu.make_async_copy(active_hbm, active, sem)
    copy.start()
    nx, ny, nz = right.shape
    copy.wait()
    mask = block_mask(active, active.shape[0], ny, nz)
    for x in range(nx):
        field[WIDE + x, EDGE : EDGE + ny] = right[x] * mask
        weight[x, EDGE : EDGE + ny] = screen[x] * mask
    odd = odd_on("gx")
    for target, high in ((cross, odd), (chip, 1 - odd)):
        for array, wide, x, row in message_rows(nx, ny):
            source, first = ((field, WIDE), (weight, 0))[array]
            value = source[first + high * (nx - wide) + x, EDGE : EDGE + ny]
            target[row + wide : row + wide + ny] = value


def widen_kernel(field_in, weight_in, cross_in, chip_in, far, near, field, weight, cross, chip):
    nx, ny = weight.shape[0], weight.shape[1] - 2 * EDGE
    arrays = ((field, WIDE, 0, WIDE), (weight, NEAR, nx * WIDE, 0))

    def read(low, high):
        for target, wide, base, first in arrays:
            for x in range(nx):
                rows = pl.ds(base + x * wide, wide)
                target[first + x, EDGE - wide : EDGE] = low[rows]
                target[first + x, EDGE + ny : EDGE + ny + wide] = high[rows]

    odd = odd_on("gy")
    pl.when(odd == 1)(functools.partial(read, near, far))
    pl.when(odd == 0)(functools.partial(read, far, near))
    odd = odd_on("gx")
    for target, high in ((cross, odd), (chip, 1 - odd)):
        for array, wide, x, row in message_rows(nx, ny):
            source, first = ((field, WIDE), (weight, 0))[array]
            plane = first + high * (nx - wide) + x
            target[row : row + wide] = source[plane, EDGE - wide : EDGE]
            target[row + wide + ny : row + 2 * wide + ny] = source[plane, EDGE + ny : EDGE + ny + wide]


def along_z(value):
    lane = lax.broadcasted_iota(jnp.int32, value.shape, 1)
    last = value.shape[1]

    def shifted(step):
        before = jnp.where(lane >= step, pltpu.roll(value, step, 1), 0.0)
        after = jnp.where(lane < last - step, pltpu.roll(value, last - step, 1), 0.0)
        return before + after

    one, two = shifted(1), shifted(2)
    return mass(value, one, two), stiff(value, one, two)


def set_weight(keep, shifted, at, rows, weight):
    on = weight > 0.0
    keep[at, rows] = jnp.where(on, SCALE, 0.0)
    shifted[at, rows] = jnp.where(on, weight - SHIFT, 0.0)


def spread(source, za, zb, yp, yq, count, first, start, rows, skip=0, folded=False):
    size = source.shape[1]
    unroll = count if count < 8 else 4

    @pl.loop(0, count, unroll=unroll)
    def _(k):
        a, b = along_z(source[first + k])
        za[k, pl.ds(EDGE, size)] = a
        zb[k, pl.ds(EDGE, size)] = b

    row = lax.broadcasted_iota(jnp.int32, (8, source.shape[2]), 0)

    def far(below, above):
        if not folded:
            return below + above
        top = jnp.where(row == 0, 0.0, jnp.where(row == 1, 2.0 * below[:8], below[:8]))
        end = jnp.where(row == 7, 0.0, jnp.where(row == 6, 2.0 * above[-8:], above[-8:]))
        return jnp.concatenate([top, below[8:]], axis=0) + jnp.concatenate([above[:-8], end], axis=0)

    @pl.loop(0, count, unroll=unroll)
    def _(k):
        def part(ref, step):
            return ref[k, pl.ds(EDGE + start + step, rows)]

        a0, a1, a2 = part(za, 0), part(za, -1) + part(za, 1), far(part(za, -2), part(za, 2))
        b0, b1, b2 = part(zb, 0), part(zb, -1) + part(zb, 1), far(part(zb, -2), part(zb, 2))
        yp[first + skip + k] = mass(a0, a1, a2)
        yq[first + skip + k] = mass(b0, b1, b2) + stiff(a0, a1, a2)


def across(yp, yq, x):
    q0, q1, q2 = yq[x + 2], yq[x + 1] + yq[x + 3], yq[x] + yq[x + 4]
    p0, p1, p2 = yp[x + 2], yp[x + 1] + yp[x + 3], yp[x] + yp[x + 4]
    return mass(q0, q1, q2) + stiff(p0, p1, p2)


def step_up(target, source, keep, shifted, yp, yq, skip, rows, source_rows, count, first):
    @pl.loop(0, count, unroll=count if count < 8 else 4)
    def _(k):
        x = first + k
        target[x] = keep[x + skip, rows] * across(yp, yq, x) + shifted[x + skip, rows] * source[x + 2, source_rows]


def fold(value):
    return jnp.sum(value.reshape(-1, 8, value.shape[1]), axis=0)


def add_sums(totals, arrays, count, first_x):
    field, _, shifted, first, second, yp, yq = arrays
    ny = yp.shape[1]
    mid, own = pl.ds(EDGE, ny), pl.ds(HEM, ny)

    def add(k, totals):
        x = first_x + k
        v0 = field[x + WIDE, mid]
        v1 = first[x + NEAR, own]
        v2 = second[x + 1, own]
        weight = shifted[x + NEAR, mid]
        form = v2 * (SCALE * across(yp, yq, x) + weight * v2)
        on = jnp.where(arrays[1][x + NEAR, mid] > 0.0, 1.0, 0.0)
        new = (v0 * v0, v0 * v1, v1 * v1, v1 * v2, v2 * v2, form, v0, v1, v2, on)
        return tuple(total + fold(value) for total, value in zip(totals, new))

    return lax.fori_loop(0, count, add, totals, unroll=2)


def inner_kernel(field, weight, keep, shifted, first, second, yp1, yq1, yp2, yq2, yp3, yq3, sums, za, zb):
    nx, wide, nz = weight.shape
    ny = wide - 2 * EDGE
    rows = ny + 2 * HEM
    outer, every = pl.ds(EDGE - HEM, rows), pl.ds(0, rows)
    for x in range(nx):
        set_weight(keep, shifted, NEAR + x, pl.ds(0, wide), weight[x])
    spread(field, za, zb, yp1, yq1, nx, WIDE, EDGE - HEM, rows)
    step_up(first, field, keep, shifted, yp1, yq1, 0, outer, outer, nx - 4, WIDE)
    spread(first, za, zb, yp2, yq2, nx - 4, WIDE, 0, rows)
    step_up(second, first, keep, shifted, yp2, yq2, 2, outer, every, nx - 8, WIDE)
    spread(second, za, zb, yp3, yq3, nx - 8, WIDE, HEM, ny, 1, True)
    arrays = (field, keep, shifted, first, second, yp3, yq3)
    totals = add_sums((jnp.zeros((8, nz), F32),) * 10, arrays, nx - 12, WIDE + 1)
    for place, total in enumerate(totals):
        sums[place] = total


def side_kernel(last, message, *refs):
    sums_in = refs[HELD]
    field, keep, shifted, first, second, yp1, yq1, yp2, yq2, yp3, yq3, sums, za, zb = refs[HELD + 1 :]
    planes, wide, nz = field.shape
    nx, ny = planes - 2 * WIDE, wide - 2 * EDGE
    rows = ny + 2 * HEM
    outer, every = pl.ds(EDGE - HEM, rows), pl.ds(0, rows)
    odd = odd_on("gx")
    high = odd if last else 1 - odd
    for array, depth, x, row in message_rows(nx, ny):
        value = message[row : row + ny + 2 * depth]
        plane, span = high * (nx + depth) + x, pl.ds(EDGE - depth, ny + 2 * depth)
        if array == 0:
            field[plane, span] = value
        else:
            set_weight(keep, shifted, plane, span, value)
    spread(field, za, zb, yp1, yq1, WIDE, high * (planes - WIDE), EDGE - HEM, rows)
    base = high * (nx + 2 * NEAR - WIDE)
    step_up(first, field, keep, shifted, yp1, yq1, 0, outer, outer, WIDE, base)
    spread(first, za, zb, yp2, yq2, WIDE, base, 0, rows)
    base = high * (nx + 2 - WIDE)
    step_up(second, first, keep, shifted, yp2, yq2, 2, outer, every, WIDE, base)
    spread(second, za, zb, yp3, yq3, WIDE, base, HEM, ny, 1, True)
    none = jnp.zeros((ny, nz), F32)
    yp3[high * (nx + 3)] = none
    yq3[high * (nx + 3)] = none
    totals = tuple(sums_in[place] for place in range(10))
    arrays = (field, keep, shifted, first, second, yp3, yq3)
    totals = list(add_sums(totals, arrays, WIDE + 1, high * (nx - WIDE - 1)))
    own = pl.ds(HEM, ny)
    beside, edge, next_edge = 1 + high * (nx + 1), 2 + high * (nx - 1), 3 + high * (nx - 3)
    give = 13.0 * yq3[edge] - yp3[edge] + (yq3[next_edge] - yp3[next_edge])
    take = 13.0 * yq3[beside] - yp3[beside]
    totals[5] += SCALE * fold(second[beside - 1, own] * give - second[edge - 1, own] * take)
    if not last:
        for place, total in enumerate(totals):
            sums[place] = total
        return
    row = lax.broadcasted_iota(jnp.int32, (SUMS, nz), 0)
    lane = lax.broadcasted_iota(jnp.int32, (SUMS, nz), 1)
    lines = jnp.zeros((SUMS, nz), F32)
    for place, total in enumerate(totals):
        lines = jnp.where(row == place, jnp.sum(total, axis=0, keepdims=True), lines)
    pair = (lines, jnp.zeros_like(lines))
    step = nz // 2
    while step:
        pair = pair_add(pair, (pltpu.roll(pair[0], step, 1), pltpu.roll(pair[1], step, 1)))
        step //= 2
    spot = jnp.where(lane == row, pair[0], jnp.where(lane == row + SUMS, pair[1], 0.0))
    sums[...] = jnp.sum(spot, axis=0, keepdims=True)


def two_sum(a, b):
    total = a + b
    part = total - a
    return total, (a - (total - part)) + (b - part)


def pair_add(a, b):
    total, rest = two_sum(a[0], b[0])
    return total, rest + (a[1] + b[1])


def halves(a):
    wide = 4097.0 * a
    top = wide - (wide - a)
    return top, a - top


def pair_mul(a, b):
    product = a[0] * b[0]
    a_top, a_rest = halves(a[0])
    b_top, b_rest = halves(b[0])
    rest = ((a_top * b_top - product) + a_top * b_rest + a_rest * b_top) + a_rest * b_rest
    rest = rest + (a[0] * b[1] + a[1] * b[0])
    total = product + rest
    return total, rest - (total - product)


def pair_sub(a, b):
    total, rest = two_sum(a[0], -b[0])
    rest = rest + (a[1] - b[1])
    out = total + rest
    return out, rest - (out - total)


def ratio(over, under, low, high):
    good = under > 0.0
    value = jnp.where(good, over / jnp.where(good, under, 1.0), 0.5 * (low + high))
    return jnp.minimum(jnp.maximum(value, low), high)


def coefficients(total):
    scale = 1.0 / total[0][0]
    zero = jnp.zeros_like(scale)
    g = [pair_mul(item, (scale, zero)) for item in total[:6]]
    shift = (jnp.full_like(scale, SHIFT), zero)
    h = [pair_add(g[k + 1], pair_mul(g[k], shift)) for k in range(5)]

    def minor(a, b, c, d):
        return pair_sub(pair_mul(a, b), pair_mul(c, d))

    s11 = minor(h[2], h[0], h[1], h[1])
    s12 = minor(h[3], h[0], h[1], h[2])
    s22 = minor(h[4], h[0], h[2], h[2])
    y1 = minor(g[1], h[0], h[1], g[0])
    y2 = minor(g[2], h[0], h[2], g[0])
    last = minor(s22, s11, s12, s12)
    side = minor(y2, s11, s12, y1)
    alpha = g[0][0] / h[0][0]
    l10 = h[1][0] / h[0][0]
    l20 = h[2][0] / h[0][0]
    l21 = ratio(s12[0], s11[0], l10 + (LOW - SHIFT), l10 + (HIGH - SHIFT))
    gamma1 = ratio(y1[0], s11[0], -alpha / LOW, -alpha / HIGH)
    gamma2 = ratio(side[0], last[0], -gamma1 / HIGH, -gamma1 / LOW)
    c1 = gamma1 - gamma2 * l21
    return alpha - c1 * l10 - gamma2 * l20, c1, gamma2


def sigmoid(value):
    return 1.0 / (1.0 + jnp.exp(-SHARP * value))


def finish_kernel(
    visible_hbm, parts, field, first, second, indicator_hbm, crossing_hbm,
    visible, indicator, crossing, level, weight, sem, slot_sems, result_sem,
):
    nx, ny, nz = indicator.shape
    copy = pltpu.make_async_copy(visible_hbm, visible, sem)
    copy.start()
    devices = parts.shape[0]
    tiles = [parts[pl.ds(8 * k, 8)] for k in range(devices // 8)]
    pairs = [(tile, pltpu.roll(tile, nz - SUMS, 1)) for tile in tiles]
    while len(pairs) > 1:
        pairs = [pair_add(a, b) for a, b in zip(pairs[::2], pairs[1::2])]
    total = pairs[0]
    for step in (4, 2, 1):
        total = pair_add(total, (pltpu.roll(total[0], step, 0), pltpu.roll(total[1], step, 0)))

    def spread(value, k):
        return jnp.broadcast_to(value[0:1, k : k + 1], (1, nz))

    item = [(spread(total[0], k), spread(total[1], k)) for k in range(10)]
    c0, c1, c2 = coefficients(item)
    over = c0 * (item[6][0] + item[6][1]) + c1 * (item[7][0] + item[7][1]) + c2 * (item[8][0] + item[8][1])
    iso = over / item[9][0]

    def set_level(x):
        v0 = field[x + WIDE, pl.ds(EDGE, ny + EDGE)]
        v1 = first[x + NEAR, pl.ds(HEM, ny + HEM)]
        v2 = second[x + 1, pl.ds(HEM, ny + HEM)]
        value = c0 * v0[: ny + HEM] + c1 * v1 + c2 * v2
        level[x, pl.ds(0, ny + HEM)] = sigmoid(value - iso)
        return value

    @pl.loop(0, nx, unroll=4)
    def _(x):
        indicator[x] = set_level(x)[:ny]

    set_level(nx)
    result = pltpu.make_async_copy(indicator, indicator_hbm, result_sem)
    result.start()
    outside = sigmoid(-iso)
    lane = lax.broadcasted_iota(jnp.int32, (ny, nz), 1)

    @pl.loop(0, nx, unroll=4)
    def _(x):
        here = level[x, pl.ds(0, ny)]
        above = jnp.where(lane < nz - 1, pltpu.roll(here, nz - 1, 1), outside)
        for edge, there in enumerate((level[x + 1, pl.ds(0, ny)], level[x, pl.ds(1, ny)], above)):
            weight[edge, pl.ds(x * (ny + 1), ny)] = here * (1.0 - there) + (1.0 - here) * there

    chunk = lax.broadcasted_iota(jnp.int32, (8, nz), 1) // BLK
    bricks_z = nz // BLK
    per_row = nz // BLK

    copy.wait()

    def out(slot):
        return pltpu.make_async_copy(crossing.at[slot], crossing_hbm.at[slot], slot_sems.at[slot])

    @pl.loop(0, visible.shape[0], unroll=2)
    def _(slot):
        number = visible[slot]
        safe = jnp.maximum(number, 0)
        begin = (safe // bricks_z) * BLK
        column = safe % bricks_z
        used = jnp.where(number >= 0, 1.0, 0.0)
        for edge in range(3):
            for half in range(2):
                for part in range(BLK // per_row):
                    tile = jnp.zeros((8, nz), F32)
                    for row in range(per_row):
                        at = half * 8 * (ny + 1) + begin + part * per_row + row
                        lines = weight[edge, pl.ds(at, 8, stride=ny + 1)]
                        turn = lax.rem((row - column) * BLK + nz, nz)
                        tile = jnp.where(chunk == row, pltpu.roll(lines, turn, 1), tile)
                    crossing[slot, edge, pl.ds(half * 16 + part, 8, stride=2)] = tile * used
        out(slot).start()

    for slot in range(visible.shape[0]):
        out(slot).wait()
    result.wait()


def whole(*shape):
    return jax.ShapeDtypeStruct(shape, F32)


VMEM = pl.BlockSpec(memory_space=pltpu.VMEM)


HBM = pl.BlockSpec(memory_space=pltpu.HBM)


def kernel(body, inputs, outputs, scratch=(), results=VMEM, alias=None, flops=0):
    return pl.pallas_call(
        body,
        in_specs=list(inputs),
        out_specs=[results] * len(outputs),
        out_shape=list(outputs),
        scratch_shapes=list(scratch),
        input_output_aliases=alias or {},
        cost_estimate=pl.CostEstimate(flops=flops, bytes_accessed=flops // 4, transcendentals=0),
        compiler_params=pltpu.CompilerParams(vmem_limit_bytes=32 * 1024 * 1024),
    )


def in_hbm(value):
    return pltpu.with_memory_space_constraint(value, pltpu.HBM)


def swap(value, axis, first):
    count = lax.axis_size(axis)
    pairs = [(k, k + 1) for k in range(first, count - 1, 2)]
    return lax.ppermute(value, axis, pairs + [(b, a) for a, b in pairs])


def body(right_side, screening, active_blocks, visible_bricks):
    nx, ny, nz = right_side.shape
    active = active_blocks.reshape(-1)
    visible = visible_bricks.reshape(-1)
    devices = lax.axis_size("gx") * lax.axis_size("gy")
    slab = whole(nx, ny, nz)
    planes, near, third = nx + 2 * WIDE, nx + 2 * NEAR, nx + 2
    wide, rows = ny + 2 * EDGE, ny + 2 * HEM
    rim = whole(nx * (WIDE + NEAR), nz)
    lists = pltpu.SMEM(active.shape, jnp.int32)
    far, near_by = kernel(
        pack_kernel,
        (HBM, HBM, HBM),
        (rim, rim),
        (
            lists,
            pltpu.VMEM((2, nx, EDGE, nz), F32),
            pltpu.VMEM((2, nx, EDGE, nz), F32),
            pltpu.SemaphoreType.DMA((5,)),
        ),
    )(in_hbm(active), in_hbm(right_side), in_hbm(screening))
    far = swap(far, "gy", 1)
    near_by = swap(near_by, "gy", 0)
    lines = WIDE * (ny + 2 * WIDE) + NEAR * (ny + 2 * NEAR)
    side = whole(-(-lines // 8) * 8, nz)
    longer = whole(side.shape[0] + 8, nz)
    placed = (whole(planes, wide, nz), whole(nx, wide, nz), longer, side)
    held = kernel(
        place_kernel, (HBM, VMEM, VMEM), placed, (lists, pltpu.SemaphoreType.DMA), flops=4_000_000
    )(in_hbm(active), right_side, screening)
    field, weight, cross, chip = kernel(
        widen_kernel, (VMEM,) * 6, placed, alias={k: k for k in range(4)}
    )(*held, far, near_by)
    cross = swap(cross, "gx", 1)
    chip = swap(chip, "gx", 0)
    work = (pltpu.VMEM((planes, wide + EDGE, nz), F32),) * 2
    kept = [whole(planes, wide, nz)] + [whole(near, wide, nz)] * 2
    kept += [whole(near, rows, nz), whole(third, rows, nz)]
    kept += [whole(planes, rows, nz)] * 2 + [whole(near, rows, nz)] * 2 + [whole(third + 2, ny, nz)] * 2
    tallies = whole(10, 8, nz)
    held = kernel(inner_kernel, (VMEM,) * 2, kept[1:] + [tallies], work, flops=20_000_000)(field, weight)
    held = [field, *held]
    for last, message in ((False, chip), (True, cross)):
        held = kernel(
            functools.partial(side_kernel, last),
            (VMEM,) * (HELD + 2),
            kept + [whole(1, nz) if last else tallies],
            work,
            alias={1 + k: k for k in range(HELD)},
            flops=10_000_000,
        )(message, *held)
    field, _, _, first, second = held[:5]
    devices = lax.axis_size("gx") * lax.axis_size("gy")
    parts = lax.all_to_all(jnp.broadcast_to(held[-1], (devices, 1, nz)), ("gx", "gy"), 0, 0)
    slots = visible.shape[0]
    shape = (slots, 3, BLK**3 // nz, nz)
    indicator, crossing = kernel(
        finish_kernel,
        (HBM,) + (VMEM,) * 4,
        (slab, whole(*shape)),
        (
            pltpu.SMEM(visible.shape, jnp.int32),
            pltpu.VMEM(slab.shape, F32),
            pltpu.VMEM(shape, F32),
            pltpu.VMEM((nx + 1, ny + EDGE, nz), F32),
            pltpu.VMEM((3, nx * (ny + 1), nz), F32),
            pltpu.SemaphoreType.DMA,
            pltpu.SemaphoreType.DMA((slots,)),
            pltpu.SemaphoreType.DMA,
        ),
        results=HBM,
    )(in_hbm(visible), parts.reshape(devices, nz), field, first, second)
    return indicator, crossing.reshape(slots, 1, 3, BLK**3)


def solution(mesh):
    return jax.shard_map(
        body,
        mesh=mesh,
        in_specs=(
            P("gx", "gy", None),
            P("gx", "gy", None),
            P("gx", "gy", None),
            P("gx", "gy", None),
        ),
        out_specs=(P("gx", "gy", None), P("gx", "gy", None, None)),
        check_vma=False,
    )
```

```python
import functools

import jax
import jax.numpy as jnp
from jax import lax
from jax.experimental import pallas as pl
from jax.experimental.pallas import tpu as pltpu
from jax.sharding import PartitionSpec as P

BLK = 16
WIDE = 5
NEAR = 3
HEM = 4
EDGE = 8
SHARP = 4.0
SCALE = 1.0 / 86400.0
SHIFT = 2.25
LOW, HIGH = 0.5, 7.0
SUMS = 16
HELD = 11
F32 = jnp.float32


def mass(mid, one, two):
    return 66.0 * mid + (26.0 * one + two)


def stiff(mid, one, two):
    return 6.0 * mid - (2.0 * one + two)


def block_mask(active, slots, rows, columns):
    y = lax.broadcasted_iota(jnp.int32, (rows, columns), 0)
    z = lax.broadcasted_iota(jnp.int32, (rows, columns), 1)
    number = (y // BLK) * (columns // BLK) + z // BLK
    mask = jnp.zeros((rows, columns), F32)
    for slot in range(slots):
        mask = jnp.where(number == active[slot], 1.0, mask)
    return mask


def on_odd():
    return lax.rem(lax.axis_index("gx"), 2)


def odd_on(axis):
    return lax.rem(lax.axis_index(axis), 2)


def pack_kernel(active_hbm, right_hbm, screen_hbm, far, near, active, right, screen, sems):
    nx, ny, nz = right_hbm.shape
    arrays = ((right_hbm, right, WIDE, 0), (screen_hbm, screen, NEAR, nx * WIDE))
    copies = [pltpu.make_async_copy(active_hbm, active, sems.at[0])]
    for k, (source, target, _, _) in enumerate(arrays):
        for high in range(2):
            rows = pl.ds(high * (ny - EDGE), EDGE)
            copies.append(pltpu.make_async_copy(source.at[:, rows], target.at[high], sems.at[1 + 2 * k + high]))
    for copy in copies:
        copy.start()
    copies[0].wait()
    mask = block_mask(active, active.shape[0], ny, nz)
    for copy in copies[1:]:
        copy.wait()

    def write(high_out, low_out):
        for _, source, wide, base in arrays:
            for x in range(nx):
                rows = pl.ds(base + x * wide, wide)
                low_out[rows] = (source[0, x] * mask[:EDGE])[:wide]
                high_out[rows] = (source[1, x] * mask[ny - EDGE :])[EDGE - wide :]

    odd = odd_on("gy")
    pl.when(odd == 1)(functools.partial(write, far, near))
    pl.when(odd == 0)(functools.partial(write, near, far))


def message_rows(nx, ny):
    row = 0
    for array, wide in enumerate((WIDE, NEAR)):
        for x in range(wide):
            yield array, wide, x, row
            row += ny + 2 * wide


def place_kernel(active_hbm, right, screen, field, weight, cross, chip, active, sem):
    copy = pltpu.make_async_copy(active_hbm, active, sem)
    copy.start()
    nx, ny, nz = right.shape
    copy.wait()
    mask = block_mask(active, active.shape[0], ny, nz)
    for x in range(nx):
        field[WIDE + x, EDGE : EDGE + ny] = right[x] * mask
        weight[x, EDGE : EDGE + ny] = screen[x] * mask
    odd = odd_on("gx")
    for target, high in ((cross, odd), (chip, 1 - odd)):
        for array, wide, x, row in message_rows(nx, ny):
            source, first = ((field, WIDE), (weight, 0))[array]
            value = source[first + high * (nx - wide) + x, EDGE : EDGE + ny]
            target[row + wide : row + wide + ny] = value


def widen_kernel(field_in, weight_in, cross_in, chip_in, far, near, field, weight, cross, chip):
    nx, ny = weight.shape[0], weight.shape[1] - 2 * EDGE
    arrays = ((field, WIDE, 0, WIDE), (weight, NEAR, nx * WIDE, 0))

    def read(low, high):
        for target, wide, base, first in arrays:
            for x in range(nx):
                rows = pl.ds(base + x * wide, wide)
                target[first + x, EDGE - wide : EDGE] = low[rows]
                target[first + x, EDGE + ny : EDGE + ny + wide] = high[rows]

    odd = odd_on("gy")
    pl.when(odd == 1)(functools.partial(read, near, far))
    pl.when(odd == 0)(functools.partial(read, far, near))
    odd = odd_on("gx")
    for target, high in ((cross, odd), (chip, 1 - odd)):
        for array, wide, x, row in message_rows(nx, ny):
            source, first = ((field, WIDE), (weight, 0))[array]
            plane = first + high * (nx - wide) + x
            target[row : row + wide] = source[plane, EDGE - wide : EDGE]
            target[row + wide + ny : row + 2 * wide + ny] = source[plane, EDGE + ny : EDGE + ny + wide]


def near_z(value):
    lane = lax.broadcasted_iota(jnp.int32, value.shape, 1)
    last = value.shape[1]

    def shifted(step):
        before = jnp.where(lane >= step, pltpu.roll(value, step, 1), 0.0)
        after = jnp.where(lane < last - step, pltpu.roll(value, last - step, 1), 0.0)
        return before + after

    return shifted(1), shifted(2)


def set_weight(keep, shifted, at, rows, weight):
    on = weight > 0.0
    keep[at, rows] = jnp.where(on, SCALE, 0.0)
    shifted[at, rows] = jnp.where(on, weight - SHIFT, 0.0)


def along_yz(source, x, row, top=False, end=False):
    def part(step):
        return source[x, pl.ds(row + step, 8)]

    here, below, above = part(0), part(-2), part(2)
    place = lax.broadcasted_iota(jnp.int32, here.shape, 0)
    if top:
        below = jnp.where(place == 0, 0.0, jnp.where(place == 1, 2.0 * below, below))
    if end:
        above = jnp.where(place == 7, 0.0, jnp.where(place == 6, 2.0 * above, above))
    one, two = part(-1) + part(1), below + above
    heavy, stretched = mass(here, one, two), stiff(here, one, two)
    heavy_near, stretched_near = near_z(heavy), near_z(stretched)
    return mass(heavy, *heavy_near), stiff(heavy, *heavy_near) + mass(stretched, *stretched_near)


def across(window):
    p, q = zip(*window)
    return mass(q[2], q[1] + q[3], q[0] + q[4]) + stiff(p[2], p[1] + p[3], p[0] + p[4])


def power(target, source, row, keep, shifted, skip, x, group, window):
    rows, at = pl.ds(EDGE + 8 * group, 8), pl.ds(EDGE - HEM + 8 * group, 8)
    center = source[x + 2, pl.ds(row + 8 * group, 8)]
    target[x, rows] = keep[x + skip, at] * across(window) + shifted[x + skip, at] * center


def advance(target, source, row, keep, shifted, skip, yp, yq, count, first):
    groups = target.shape[1] // 8 - 2

    def some(chosen):
        def planes(x, windows, output):
            windows = [list(window) for window in windows]
            for k in range(4):
                for window, group in zip(windows, chosen):
                    p, q = along_yz(source, x + k, row + 8 * group)
                    rows = pl.ds(8 * group, 8)
                    yp[x + k, rows] = p
                    yq[x + k, rows] = q
                    window.append((p, q))
                    if output:
                        power(target, source, row, keep, shifted, skip, x + k - 4, group, window[-5:])
            return tuple(tuple(window[-4:]) for window in windows)

        windows = planes(first, ((),) * len(chosen), False)
        lax.fori_loop(1, count // 4, lambda k, carry: planes(first + 4 * k, carry, True), windows)

    for begin in range(0, groups, 3):
        some(range(begin, min(begin + 3, groups)))


def advance_side(target, source, row, keep, shifted, skip, yp, yq, high):
    groups = target.shape[1] // 8 - 2
    base = high * (target.shape[0] - WIDE)
    start = high * (source.shape[0] - WIDE)
    for group in range(groups):
        rows = pl.ds(8 * group, 8)
        for k in range(WIDE):
            p, q = along_yz(source, start + k, row + 8 * group)
            yp[start + k, rows] = p
            yq[start + k, rows] = q
    for group in range(groups):
        rows = pl.ds(8 * group, 8)
        window = [(yp[base + k, rows], yq[base + k, rows]) for k in range(WIDE + 4)]
        for k in range(WIDE):
            power(target, source, row, keep, shifted, skip, base + k, group, window[k : k + 5])


def last_rows(source, yp, yq, count, first):
    groups = yp.shape[1] // 8
    for group in range(groups):
        rows = pl.ds(8 * group, 8)
        for k in range(count):
            p, q = along_yz(source, first + k, EDGE + HEM + 8 * group, group == 0, group == groups - 1)
            yp[first + 1 + k, rows] = p
            yq[first + 1 + k, rows] = q


def fold(value):
    return jnp.sum(value.reshape(-1, 8, value.shape[1]), axis=0)


def add_sums(totals, arrays, count, first_x):
    field, keep, shifted, first, second, yp, yq = arrays
    totals = list(totals)
    for group in range(yp.shape[1] // 8):
        rows = pl.ds(8 * group, 8)
        mid, own = pl.ds(EDGE + 8 * group, 8), pl.ds(EDGE + HEM + 8 * group, 8)
        window = [(yp[first_x + k, rows], yq[first_x + k, rows]) for k in range(count + 4)]
        for k in range(count):
            x = first_x + k
            v0 = field[x + WIDE, mid]
            v1 = first[x + NEAR, own]
            v2 = second[x + 1, own]
            form = v2 * (SCALE * across(window[k : k + 5]) + shifted[x + NEAR, mid] * v2)
            on = jnp.where(keep[x + NEAR, mid] > 0.0, 1.0, 0.0)
            new = (v0 * v0, v0 * v1, v1 * v1, v1 * v2, v2 * v2, form, v0, v1, v2, on)
            totals = [total + value for total, value in zip(totals, new)]
    return totals


def inner_kernel(field, weight, keep, shifted, first, second, yp1, yq1, yp2, yq2, yp3, yq3, sums):
    nx, wide, nz = weight.shape
    for x in range(nx):
        set_weight(keep, shifted, NEAR + x, pl.ds(0, wide), weight[x])
    advance(first, field, EDGE - HEM, keep, shifted, 0, yp1, yq1, nx, WIDE)
    advance(second, first, EDGE, keep, shifted, 2, yp2, yq2, nx - 4, WIDE)
    last_rows(second, yp3, yq3, nx - 8, WIDE)
    arrays = (field, keep, shifted, first, second, yp3, yq3)
    totals = add_sums((jnp.zeros((8, nz), F32),) * 10, arrays, nx - 12, WIDE + 1)
    for place, total in enumerate(totals):
        sums[place] = total


def side_kernel(last, message, *refs):
    sums_in = refs[HELD]
    field, keep, shifted, first, second, yp1, yq1, yp2, yq2, yp3, yq3, sums = refs[HELD + 1 :]
    planes, wide, nz = field.shape
    nx, ny = planes - 2 * WIDE, wide - 2 * EDGE
    odd = odd_on("gx")
    high = odd if last else 1 - odd
    for array, depth, x, row in message_rows(nx, ny):
        value = message[row : row + ny + 2 * depth]
        plane, span = high * (nx + depth) + x, pl.ds(EDGE - depth, ny + 2 * depth)
        if array == 0:
            field[plane, span] = value
        else:
            set_weight(keep, shifted, plane, span, value)
    advance_side(first, field, EDGE - HEM, keep, shifted, 0, yp1, yq1, high)
    advance_side(second, first, EDGE, keep, shifted, 2, yp2, yq2, high)
    last_rows(second, yp3, yq3, WIDE, high * (nx + 2 - WIDE))
    none = jnp.zeros((ny, nz), F32)
    yp3[high * (nx + 3)] = none
    yq3[high * (nx + 3)] = none
    totals = tuple(sums_in[place] for place in range(10))
    arrays = (field, keep, shifted, first, second, yp3, yq3)
    totals = list(add_sums(totals, arrays, WIDE + 1, high * (nx - WIDE - 1)))
    own = pl.ds(EDGE + HEM, ny)
    beside, edge, next_edge = 1 + high * (nx + 1), 2 + high * (nx - 1), 3 + high * (nx - 3)
    give = 13.0 * yq3[edge] - yp3[edge] + (yq3[next_edge] - yp3[next_edge])
    take = 13.0 * yq3[beside] - yp3[beside]
    totals[5] += SCALE * fold(second[beside - 1, own] * give - second[edge - 1, own] * take)
    if not last:
        for place, total in enumerate(totals):
            sums[place] = total
        return
    row = lax.broadcasted_iota(jnp.int32, (SUMS, nz), 0)
    lane = lax.broadcasted_iota(jnp.int32, (SUMS, nz), 1)
    lines = jnp.zeros((SUMS, nz), F32)
    for place, total in enumerate(totals):
        lines = jnp.where(row == place, jnp.sum(total, axis=0, keepdims=True), lines)
    pair = (lines, jnp.zeros_like(lines))
    step = nz // 2
    while step:
        pair = pair_add(pair, (pltpu.roll(pair[0], step, 1), pltpu.roll(pair[1], step, 1)))
        step //= 2
    spot = jnp.where(lane == row, pair[0], jnp.where(lane == row + SUMS, pair[1], 0.0))
    sums[...] = jnp.sum(spot, axis=0, keepdims=True)


def two_sum(a, b):
    total = a + b
    part = total - a
    return total, (a - (total - part)) + (b - part)


def pair_add(a, b):
    total, rest = two_sum(a[0], b[0])
    return total, rest + (a[1] + b[1])


def halves(a):
    wide = 4097.0 * a
    top = wide - (wide - a)
    return top, a - top


def pair_mul(a, b):
    product = a[0] * b[0]
    a_top, a_rest = halves(a[0])
    b_top, b_rest = halves(b[0])
    rest = ((a_top * b_top - product) + a_top * b_rest + a_rest * b_top) + a_rest * b_rest
    rest = rest + (a[0] * b[1] + a[1] * b[0])
    total = product + rest
    return total, rest - (total - product)


def pair_sub(a, b):
    total, rest = two_sum(a[0], -b[0])
    rest = rest + (a[1] - b[1])
    out = total + rest
    return out, rest - (out - total)


def ratio(over, under, low, high):
    good = under > 0.0
    value = jnp.where(good, over / jnp.where(good, under, 1.0), 0.5 * (low + high))
    return jnp.minimum(jnp.maximum(value, low), high)


def coefficients(total):
    scale = 1.0 / total[0][0]
    zero = jnp.zeros_like(scale)
    g = [pair_mul(item, (scale, zero)) for item in total[:6]]
    shift = (jnp.full_like(scale, SHIFT), zero)
    h = [pair_add(g[k + 1], pair_mul(g[k], shift)) for k in range(5)]

    def minor(a, b, c, d):
        return pair_sub(pair_mul(a, b), pair_mul(c, d))

    s11 = minor(h[2], h[0], h[1], h[1])
    s12 = minor(h[3], h[0], h[1], h[2])
    s22 = minor(h[4], h[0], h[2], h[2])
    y1 = minor(g[1], h[0], h[1], g[0])
    y2 = minor(g[2], h[0], h[2], g[0])
    last = minor(s22, s11, s12, s12)
    side = minor(y2, s11, s12, y1)
    alpha = g[0][0] / h[0][0]
    l10 = h[1][0] / h[0][0]
    l20 = h[2][0] / h[0][0]
    l21 = ratio(s12[0], s11[0], l10 + (LOW - SHIFT), l10 + (HIGH - SHIFT))
    gamma1 = ratio(y1[0], s11[0], -alpha / LOW, -alpha / HIGH)
    gamma2 = ratio(side[0], last[0], -gamma1 / HIGH, -gamma1 / LOW)
    c1 = gamma1 - gamma2 * l21
    return alpha - c1 * l10 - gamma2 * l20, c1, gamma2


def sigmoid(value):
    return 1.0 / (1.0 + jnp.exp(-SHARP * value))


def finish_kernel(
    visible_hbm, parts, field, first, second, indicator_hbm, crossing_hbm,
    visible, indicator, crossing, level, weight, sem, slot_sems, result_sem,
):
    nx, ny, nz = indicator.shape
    copy = pltpu.make_async_copy(visible_hbm, visible, sem)
    copy.start()
    devices = parts.shape[0]
    tiles = [parts[pl.ds(8 * k, 8)] for k in range(devices // 8)]
    pairs = [(tile, pltpu.roll(tile, nz - SUMS, 1)) for tile in tiles]
    while len(pairs) > 1:
        pairs = [pair_add(a, b) for a, b in zip(pairs[::2], pairs[1::2])]
    total = pairs[0]
    for step in (4, 2, 1):
        total = pair_add(total, (pltpu.roll(total[0], step, 0), pltpu.roll(total[1], step, 0)))

    def spread(value, k):
        return jnp.broadcast_to(value[0:1, k : k + 1], (1, nz))

    item = [(spread(total[0], k), spread(total[1], k)) for k in range(10)]
    c0, c1, c2 = coefficients(item)
    over = c0 * (item[6][0] + item[6][1]) + c1 * (item[7][0] + item[7][1]) + c2 * (item[8][0] + item[8][1])
    iso = over / item[9][0]

    def set_level(x):
        v0 = field[x + WIDE, pl.ds(EDGE, ny + EDGE)]
        v1 = first[x + NEAR, pl.ds(EDGE + HEM, ny + HEM)]
        v2 = second[x + 1, pl.ds(EDGE + HEM, ny + HEM)]
        value = c0 * v0[: ny + HEM] + c1 * v1 + c2 * v2
        level[x, pl.ds(0, ny + HEM)] = sigmoid(value - iso)
        return value

    @pl.loop(0, nx, unroll=4)
    def _(x):
        indicator[x] = set_level(x)[:ny]

    set_level(nx)
    result = pltpu.make_async_copy(indicator, indicator_hbm, result_sem)
    result.start()
    outside = sigmoid(-iso)
    lane = lax.broadcasted_iota(jnp.int32, (ny, nz), 1)

    @pl.loop(0, nx, unroll=4)
    def _(x):
        here = level[x, pl.ds(0, ny)]
        above = jnp.where(lane < nz - 1, pltpu.roll(here, nz - 1, 1), outside)
        for edge, there in enumerate((level[x + 1, pl.ds(0, ny)], level[x, pl.ds(1, ny)], above)):
            weight[edge, pl.ds(x * (ny + 1), ny)] = here * (1.0 - there) + (1.0 - here) * there

    chunk = lax.broadcasted_iota(jnp.int32, (8, nz), 1) // BLK
    bricks_z = nz // BLK
    per_row = nz // BLK

    copy.wait()

    def out(slot):
        return pltpu.make_async_copy(crossing.at[slot], crossing_hbm.at[slot], slot_sems.at[slot])

    @pl.loop(0, visible.shape[0], unroll=2)
    def _(slot):
        number = visible[slot]
        safe = jnp.maximum(number, 0)
        begin = (safe // bricks_z) * BLK
        column = safe % bricks_z
        used = jnp.where(number >= 0, 1.0, 0.0)
        for edge in range(3):
            for half in range(2):
                for part in range(BLK // per_row):
                    tile = jnp.zeros((8, nz), F32)
                    for row in range(per_row):
                        at = half * 8 * (ny + 1) + begin + part * per_row + row
                        lines = weight[edge, pl.ds(at, 8, stride=ny + 1)]
                        turn = lax.rem((row - column) * BLK + nz, nz)
                        tile = jnp.where(chunk == row, pltpu.roll(lines, turn, 1), tile)
                    crossing[slot, edge, pl.ds(half * 16 + part, 8, stride=2)] = tile * used
        out(slot).start()

    for slot in range(visible.shape[0]):
        out(slot).wait()
    result.wait()


def whole(*shape):
    return jax.ShapeDtypeStruct(shape, F32)


VMEM = pl.BlockSpec(memory_space=pltpu.VMEM)


HBM = pl.BlockSpec(memory_space=pltpu.HBM)


def kernel(body, inputs, outputs, scratch=(), results=VMEM, alias=None, flops=0):
    return pl.pallas_call(
        body,
        in_specs=list(inputs),
        out_specs=[results] * len(outputs),
        out_shape=list(outputs),
        scratch_shapes=list(scratch),
        input_output_aliases=alias or {},
        cost_estimate=pl.CostEstimate(flops=flops, bytes_accessed=flops // 4, transcendentals=0),
        compiler_params=pltpu.CompilerParams(vmem_limit_bytes=32 * 1024 * 1024),
    )


def in_hbm(value):
    return pltpu.with_memory_space_constraint(value, pltpu.HBM)


def swap(value, axis, first):
    count = lax.axis_size(axis)
    pairs = [(k, k + 1) for k in range(first, count - 1, 2)]
    return lax.ppermute(value, axis, pairs + [(b, a) for a, b in pairs])


def body(right_side, screening, active_blocks, visible_bricks):
    nx, ny, nz = right_side.shape
    active = active_blocks.reshape(-1)
    visible = visible_bricks.reshape(-1)
    devices = lax.axis_size("gx") * lax.axis_size("gy")
    slab = whole(nx, ny, nz)
    planes, near, third = nx + 2 * WIDE, nx + 2 * NEAR, nx + 2
    wide, rows = ny + 2 * EDGE, ny + 2 * HEM
    rim = whole(nx * (WIDE + NEAR), nz)
    lists = pltpu.SMEM(active.shape, jnp.int32)
    far, near_by = kernel(
        pack_kernel,
        (HBM, HBM, HBM),
        (rim, rim),
        (
            lists,
            pltpu.VMEM((2, nx, EDGE, nz), F32),
            pltpu.VMEM((2, nx, EDGE, nz), F32),
            pltpu.SemaphoreType.DMA((5,)),
        ),
    )(in_hbm(active), in_hbm(right_side), in_hbm(screening))
    far = swap(far, "gy", 1)
    near_by = swap(near_by, "gy", 0)
    lines = WIDE * (ny + 2 * WIDE) + NEAR * (ny + 2 * NEAR)
    side = whole(-(-lines // 8) * 8, nz)
    longer = whole(side.shape[0] + 8, nz)
    placed = (whole(planes, wide, nz), whole(nx, wide, nz), longer, side)
    held = kernel(
        place_kernel, (HBM, VMEM, VMEM), placed, (lists, pltpu.SemaphoreType.DMA), flops=4_000_000
    )(in_hbm(active), right_side, screening)
    field, weight, cross, chip = kernel(
        widen_kernel, (VMEM,) * 6, placed, alias={k: k for k in range(4)}
    )(*held, far, near_by)
    cross = swap(cross, "gx", 1)
    chip = swap(chip, "gx", 0)
    kept = [whole(planes, wide, nz)] + [whole(near, wide, nz)] * 2
    kept += [whole(near, rows + 2 * EDGE, nz), whole(third, rows + 2 * EDGE, nz)]
    kept += [whole(planes, rows, nz)] * 2 + [whole(near, rows, nz)] * 2 + [whole(third + 2, ny, nz)] * 2
    tallies = whole(10, 8, nz)
    held = kernel(inner_kernel, (VMEM,) * 2, kept[1:] + [tallies], flops=20_000_000)(field, weight)
    held = [field, *held]
    for last, message in ((False, chip), (True, cross)):
        held = kernel(
            functools.partial(side_kernel, last),
            (VMEM,) * (HELD + 2),
            kept + [whole(1, nz) if last else tallies],
            alias={1 + k: k for k in range(HELD)},
            flops=10_000_000,
        )(message, *held)
    field, _, _, first, second = held[:5]
    devices = lax.axis_size("gx") * lax.axis_size("gy")
    parts = lax.all_to_all(jnp.broadcast_to(held[-1], (devices, 1, nz)), ("gx", "gy"), 0, 0)
    slots = visible.shape[0]
    shape = (slots, 3, BLK**3 // nz, nz)
    indicator, crossing = kernel(
        finish_kernel,
        (HBM,) + (VMEM,) * 4,
        (slab, whole(*shape)),
        (
            pltpu.SMEM(visible.shape, jnp.int32),
            pltpu.VMEM(slab.shape, F32),
            pltpu.VMEM(shape, F32),
            pltpu.VMEM((nx + 1, ny + EDGE, nz), F32),
            pltpu.VMEM((3, nx * (ny + 1), nz), F32),
            pltpu.SemaphoreType.DMA,
            pltpu.SemaphoreType.DMA((slots,)),
            pltpu.SemaphoreType.DMA,
        ),
        results=HBM,
    )(in_hbm(visible), parts.reshape(devices, nz), field, first, second)
    return indicator, crossing.reshape(slots, 1, 3, BLK**3)


def solution(mesh):
    return jax.shard_map(
        body,
        mesh=mesh,
        in_specs=(
            P("gx", "gy", None),
            P("gx", "gy", None),
            P("gx", "gy", None),
            P("gx", "gy", None),
        ),
        out_specs=(P("gx", "gy", None), P("gx", "gy", None, None)),
        check_vma=False,
    )
```

```python
import functools

import jax
import jax.numpy as jnp
from jax import lax
from jax.experimental import pallas as pl
from jax.experimental.pallas import tpu as pltpu
from jax.sharding import PartitionSpec as P

BLK = 16
WIDE = 5
NEAR = 3
HEM = 4
EDGE = 8
SHARP = 4.0
SCALE = 1.0 / 86400.0
SHIFT = 2.25
LOW, HIGH = 0.5, 7.0
SUMS = 16
HELD = 11
F32 = jnp.float32


def mass(mid, one, two):
    return 66.0 * mid + (26.0 * one + two)


def stiff(mid, one, two):
    return 6.0 * mid - (2.0 * one + two)


def block_mask(active, slots, rows, columns):
    y = lax.broadcasted_iota(jnp.int32, (rows, columns), 0)
    z = lax.broadcasted_iota(jnp.int32, (rows, columns), 1)
    number = (y // BLK) * (columns // BLK) + z // BLK
    mask = jnp.zeros((rows, columns), F32)
    for slot in range(slots):
        mask = jnp.where(number == active[slot], 1.0, mask)
    return mask


def on_odd():
    return lax.rem(lax.axis_index("gx"), 2)


def odd_on(axis):
    return lax.rem(lax.axis_index(axis), 2)


def pack_kernel(active_hbm, right_hbm, screen_hbm, far, near, active, right, screen, sems):
    nx, ny, nz = right_hbm.shape
    arrays = ((right_hbm, right, WIDE, 0), (screen_hbm, screen, NEAR, nx * WIDE))
    copies = [pltpu.make_async_copy(active_hbm, active, sems.at[0])]
    for k, (source, target, _, _) in enumerate(arrays):
        for high in range(2):
            rows = pl.ds(high * (ny - EDGE), EDGE)
            copies.append(pltpu.make_async_copy(source.at[:, rows], target.at[high], sems.at[1 + 2 * k + high]))
    for copy in copies:
        copy.start()
    copies[0].wait()
    mask = block_mask(active, active.shape[0], ny, nz)
    for copy in copies[1:]:
        copy.wait()

    def write(high_out, low_out):
        for _, source, wide, base in arrays:
            for x in range(nx):
                rows = pl.ds(base + x * wide, wide)
                low_out[rows] = (source[0, x] * mask[:EDGE])[:wide]
                high_out[rows] = (source[1, x] * mask[ny - EDGE :])[EDGE - wide :]

    odd = odd_on("gy")
    pl.when(odd == 1)(functools.partial(write, far, near))
    pl.when(odd == 0)(functools.partial(write, near, far))


def message_rows(nx, ny):
    row = 0
    for array, wide in enumerate((WIDE, NEAR)):
        for x in range(wide):
            yield array, wide, x, row
            row += ny + 2 * wide


def place_kernel(active_hbm, right, screen, field, weight, cross, chip, active, sem):
    copy = pltpu.make_async_copy(active_hbm, active, sem)
    copy.start()
    nx, ny, nz = right.shape
    copy.wait()
    mask = block_mask(active, active.shape[0], ny, nz)
    for x in range(nx):
        field[WIDE + x, EDGE : EDGE + ny] = right[x] * mask
        weight[x, EDGE : EDGE + ny] = screen[x] * mask
    odd = odd_on("gx")
    for target, high in ((cross, odd), (chip, 1 - odd)):
        for array, wide, x, row in message_rows(nx, ny):
            source, first = ((field, WIDE), (weight, 0))[array]
            value = source[first + high * (nx - wide) + x, EDGE : EDGE + ny]
            target[row + wide : row + wide + ny] = value


def widen_kernel(field_in, weight_in, cross_in, chip_in, far, near, field, weight, cross, chip):
    nx, ny = weight.shape[0], weight.shape[1] - 2 * EDGE
    arrays = ((field, WIDE, 0, WIDE), (weight, NEAR, nx * WIDE, 0))

    def read(low, high):
        for target, wide, base, first in arrays:
            for x in range(nx):
                rows = pl.ds(base + x * wide, wide)
                target[first + x, EDGE - wide : EDGE] = low[rows]
                target[first + x, EDGE + ny : EDGE + ny + wide] = high[rows]

    odd = odd_on("gy")
    pl.when(odd == 1)(functools.partial(read, near, far))
    pl.when(odd == 0)(functools.partial(read, far, near))
    odd = odd_on("gx")
    for target, high in ((cross, odd), (chip, 1 - odd)):
        for array, wide, x, row in message_rows(nx, ny):
            source, first = ((field, WIDE), (weight, 0))[array]
            plane = first + high * (nx - wide) + x
            target[row : row + wide] = source[plane, EDGE - wide : EDGE]
            target[row + wide + ny : row + 2 * wide + ny] = source[plane, EDGE + ny : EDGE + ny + wide]


def near_z(value):
    lane = lax.broadcasted_iota(jnp.int32, value.shape, 1)
    last = value.shape[1]

    def shifted(step):
        before = jnp.where(lane >= step, pltpu.roll(value, step, 1), 0.0)
        after = jnp.where(lane < last - step, pltpu.roll(value, last - step, 1), 0.0)
        return before + after

    return shifted(1), shifted(2)


def set_weight(keep, shifted, at, rows, weight):
    on = weight > 0.0
    keep[at, rows] = jnp.where(on, SCALE, 0.0)
    shifted[at, rows] = jnp.where(on, weight - SHIFT, 0.0)


def along_z(source, za, zb, count, first, rows):
    @pl.loop(0, count, unroll=count if count < 8 else 4)
    def _(k):
        value = source[first + k, rows]
        near = near_z(value)
        za[first + k, rows] = mass(value, *near)
        zb[first + k, rows] = stiff(value, *near)


def along_y(za, zb, x, row, top=False, end=False):
    def parts(source):
        def part(step):
            return source[x, pl.ds(row + step, 8)]

        below, above = part(-2), part(2)
        place = lax.broadcasted_iota(jnp.int32, below.shape, 0)
        if top:
            below = jnp.where(place == 0, 0.0, jnp.where(place == 1, 2.0 * below, below))
        if end:
            above = jnp.where(place == 7, 0.0, jnp.where(place == 6, 2.0 * above, above))
        return part(0), part(-1) + part(1), below + above

    a, b = parts(za), parts(zb)
    return mass(*a), mass(*b) + stiff(*a)


def across(window):
    p, q = zip(*window)
    return mass(q[2], q[1] + q[3], q[0] + q[4]) + stiff(p[2], p[1] + p[3], p[0] + p[4])


def power(target, source, row, keep, shifted, skip, x, group, window):
    rows, at = pl.ds(EDGE + 8 * group, 8), pl.ds(EDGE - HEM + 8 * group, 8)
    center = source[x + 2, pl.ds(row + 8 * group, 8)]
    target[x, rows] = keep[x + skip, at] * across(window) + shifted[x + skip, at] * center


def z_rows(source, row):
    return pl.ds(0, source.shape[1]) if row < EDGE else pl.ds(EDGE, source.shape[1] - 2 * EDGE)


def advance(target, source, row, keep, shifted, skip, yp, yq, za, zb, count, first):
    groups = target.shape[1] // 8 - 2
    along_z(source, za, zb, count, first, z_rows(source, row))

    def some(chosen):
        def planes(x, windows, output):
            windows = [list(window) for window in windows]
            for k in range(4):
                for window, group in zip(windows, chosen):
                    p, q = along_y(za, zb, x + k, row + 8 * group)
                    rows = pl.ds(8 * group, 8)
                    yp[x + k, rows] = p
                    yq[x + k, rows] = q
                    window.append((p, q))
                    if output:
                        power(target, source, row, keep, shifted, skip, x + k - 4, group, window[-5:])
            return tuple(tuple(window[-4:]) for window in windows)

        windows = planes(first, ((),) * len(chosen), False)
        lax.fori_loop(1, count // 4, lambda k, carry: planes(first + 4 * k, carry, True), windows)

    for begin in range(0, groups, 3):
        some(range(begin, min(begin + 3, groups)))


def advance_side(target, source, row, keep, shifted, skip, yp, yq, za, zb, high):
    groups = target.shape[1] // 8 - 2
    base = high * (target.shape[0] - WIDE)
    start = high * (source.shape[0] - WIDE)
    along_z(source, za, zb, WIDE, start, z_rows(source, row))
    for group in range(groups):
        rows = pl.ds(8 * group, 8)
        for k in range(WIDE):
            p, q = along_y(za, zb, start + k, row + 8 * group)
            yp[start + k, rows] = p
            yq[start + k, rows] = q
    for group in range(groups):
        rows = pl.ds(8 * group, 8)
        window = [(yp[base + k, rows], yq[base + k, rows]) for k in range(WIDE + 4)]
        for k in range(WIDE):
            power(target, source, row, keep, shifted, skip, base + k, group, window[k : k + 5])


def last_rows(source, yp, yq, za, zb, count, first):
    groups = yp.shape[1] // 8
    along_z(source, za, zb, count, first, z_rows(source, EDGE))
    for group in range(groups):
        rows = pl.ds(8 * group, 8)
        for k in range(count):
            p, q = along_y(za, zb, first + k, EDGE + HEM + 8 * group, group == 0, group == groups - 1)
            yp[first + 1 + k, rows] = p
            yq[first + 1 + k, rows] = q


def fold(value):
    return jnp.sum(value.reshape(-1, 8, value.shape[1]), axis=0)


def add_sums(totals, arrays, count, first_x):
    field, keep, shifted, first, second, yp, yq = arrays
    totals = list(totals)
    for group in range(yp.shape[1] // 8):
        rows = pl.ds(8 * group, 8)
        mid, own = pl.ds(EDGE + 8 * group, 8), pl.ds(EDGE + HEM + 8 * group, 8)
        window = [(yp[first_x + k, rows], yq[first_x + k, rows]) for k in range(count + 4)]
        for k in range(count):
            x = first_x + k
            v0 = field[x + WIDE, mid]
            v1 = first[x + NEAR, own]
            v2 = second[x + 1, own]
            form = v2 * (SCALE * across(window[k : k + 5]) + shifted[x + NEAR, mid] * v2)
            on = jnp.where(keep[x + NEAR, mid] > 0.0, 1.0, 0.0)
            new = (v0 * v0, v0 * v1, v1 * v1, v1 * v2, v2 * v2, form, v0, v1, v2, on)
            totals = [total + value for total, value in zip(totals, new)]
    return totals


def inner_kernel(field, weight, keep, shifted, first, second, yp1, yq1, yp2, yq2, yp3, yq3, sums, za, zb):
    nx, wide, nz = weight.shape
    for x in range(nx):
        set_weight(keep, shifted, NEAR + x, pl.ds(0, wide), weight[x])
    advance(first, field, EDGE - HEM, keep, shifted, 0, yp1, yq1, za, zb, nx, WIDE)
    advance(second, first, EDGE, keep, shifted, 2, yp2, yq2, za, zb, nx - 4, WIDE)
    last_rows(second, yp3, yq3, za, zb, nx - 8, WIDE)
    arrays = (field, keep, shifted, first, second, yp3, yq3)
    totals = add_sums((jnp.zeros((8, nz), F32),) * 10, arrays, nx - 12, WIDE + 1)
    for place, total in enumerate(totals):
        sums[place] = total


def side_kernel(last, message, *refs):
    sums_in = refs[HELD]
    field, keep, shifted, first, second, yp1, yq1, yp2, yq2, yp3, yq3, sums, za, zb = refs[HELD + 1 :]
    planes, wide, nz = field.shape
    nx, ny = planes - 2 * WIDE, wide - 2 * EDGE
    odd = odd_on("gx")
    high = odd if last else 1 - odd
    for array, depth, x, row in message_rows(nx, ny):
        value = message[row : row + ny + 2 * depth]
        plane, span = high * (nx + depth) + x, pl.ds(EDGE - depth, ny + 2 * depth)
        if array == 0:
            field[plane, span] = value
        else:
            set_weight(keep, shifted, plane, span, value)
    advance_side(first, field, EDGE - HEM, keep, shifted, 0, yp1, yq1, za, zb, high)
    advance_side(second, first, EDGE, keep, shifted, 2, yp2, yq2, za, zb, high)
    last_rows(second, yp3, yq3, za, zb, WIDE, high * (nx + 2 - WIDE))
    none = jnp.zeros((ny, nz), F32)
    yp3[high * (nx + 3)] = none
    yq3[high * (nx + 3)] = none
    totals = tuple(sums_in[place] for place in range(10))
    arrays = (field, keep, shifted, first, second, yp3, yq3)
    totals = list(add_sums(totals, arrays, WIDE + 1, high * (nx - WIDE - 1)))
    own = pl.ds(EDGE + HEM, ny)
    beside, edge, next_edge = 1 + high * (nx + 1), 2 + high * (nx - 1), 3 + high * (nx - 3)
    give = 13.0 * yq3[edge] - yp3[edge] + (yq3[next_edge] - yp3[next_edge])
    take = 13.0 * yq3[beside] - yp3[beside]
    totals[5] += SCALE * fold(second[beside - 1, own] * give - second[edge - 1, own] * take)
    if not last:
        for place, total in enumerate(totals):
            sums[place] = total
        return
    row = lax.broadcasted_iota(jnp.int32, (SUMS, nz), 0)
    lane = lax.broadcasted_iota(jnp.int32, (SUMS, nz), 1)
    lines = jnp.zeros((SUMS, nz), F32)
    for place, total in enumerate(totals):
        lines = jnp.where(row == place, jnp.sum(total, axis=0, keepdims=True), lines)
    pieces, rest = [], lines
    for _ in range(3):
        pieces.append(rest.astype(jnp.bfloat16))
        rest = rest - pieces[-1].astype(F32)
    ones = jnp.ones((nz, nz), jnp.bfloat16)
    whole_sums = jnp.dot(jnp.concatenate(pieces, axis=0), ones, preferred_element_type=F32)
    top, rest = two_sum(whole_sums[:SUMS], whole_sums[SUMS : 2 * SUMS])
    pair = two_sum(top, rest + whole_sums[2 * SUMS :])
    spot = jnp.where(lane == row, pair[0], jnp.where(lane == row + SUMS, pair[1], 0.0))
    sums[...] = jnp.sum(spot, axis=0, keepdims=True)


def two_sum(a, b):
    total = a + b
    part = total - a
    return total, (a - (total - part)) + (b - part)


def pair_add(a, b):
    total, rest = two_sum(a[0], b[0])
    return total, rest + (a[1] + b[1])


def halves(a):
    wide = 4097.0 * a
    top = wide - (wide - a)
    return top, a - top


def pair_mul(a, b):
    product = a[0] * b[0]
    a_top, a_rest = halves(a[0])
    b_top, b_rest = halves(b[0])
    rest = ((a_top * b_top - product) + a_top * b_rest + a_rest * b_top) + a_rest * b_rest
    rest = rest + (a[0] * b[1] + a[1] * b[0])
    total = product + rest
    return total, rest - (total - product)


def pair_sub(a, b):
    total, rest = two_sum(a[0], -b[0])
    rest = rest + (a[1] - b[1])
    out = total + rest
    return out, rest - (out - total)


def ratio(over, under, low, high):
    good = under > 0.0
    value = jnp.where(good, over / jnp.where(good, under, 1.0), 0.5 * (low + high))
    return jnp.minimum(jnp.maximum(value, low), high)


def coefficients(total):
    scale = 1.0 / total[0][0]
    zero = jnp.zeros_like(scale)
    g = [pair_mul(item, (scale, zero)) for item in total[:6]]
    shift = (jnp.full_like(scale, SHIFT), zero)
    h = [pair_add(g[k + 1], pair_mul(g[k], shift)) for k in range(5)]

    def minor(a, b, c, d):
        return pair_sub(pair_mul(a, b), pair_mul(c, d))

    s11 = minor(h[2], h[0], h[1], h[1])
    s12 = minor(h[3], h[0], h[1], h[2])
    s22 = minor(h[4], h[0], h[2], h[2])
    y1 = minor(g[1], h[0], h[1], g[0])
    y2 = minor(g[2], h[0], h[2], g[0])
    last = minor(s22, s11, s12, s12)
    side = minor(y2, s11, s12, y1)
    alpha = g[0][0] / h[0][0]
    l10 = h[1][0] / h[0][0]
    l20 = h[2][0] / h[0][0]
    l21 = ratio(s12[0], s11[0], l10 + (LOW - SHIFT), l10 + (HIGH - SHIFT))
    gamma1 = ratio(y1[0], s11[0], -alpha / LOW, -alpha / HIGH)
    gamma2 = ratio(side[0], last[0], -gamma1 / HIGH, -gamma1 / LOW)
    c1 = gamma1 - gamma2 * l21
    return alpha - c1 * l10 - gamma2 * l20, c1, gamma2


def sigmoid(value):
    return 1.0 / (1.0 + jnp.exp(-SHARP * value))


def finish_kernel(
    visible_hbm, parts, field, first, second, indicator_hbm, crossing_hbm,
    visible, indicator, crossing, level, weight, sem, slot_sems, result_sem,
):
    nx, ny, nz = indicator.shape
    copy = pltpu.make_async_copy(visible_hbm, visible, sem)
    copy.start()
    devices = parts.shape[0]
    tiles = [parts[pl.ds(8 * k, 8)] for k in range(devices // 8)]
    pairs = [(tile, pltpu.roll(tile, nz - SUMS, 1)) for tile in tiles]
    while len(pairs) > 1:
        pairs = [pair_add(a, b) for a, b in zip(pairs[::2], pairs[1::2])]
    total = pairs[0]
    for step in (4, 2, 1):
        total = pair_add(total, (pltpu.roll(total[0], step, 0), pltpu.roll(total[1], step, 0)))

    def spread(value, k):
        return jnp.broadcast_to(value[0:1, k : k + 1], (1, nz))

    item = [(spread(total[0], k), spread(total[1], k)) for k in range(10)]
    c0, c1, c2 = coefficients(item)
    over = c0 * (item[6][0] + item[6][1]) + c1 * (item[7][0] + item[7][1]) + c2 * (item[8][0] + item[8][1])
    iso = over / item[9][0]

    def set_level(x):
        v0 = field[x + WIDE, pl.ds(EDGE, ny + EDGE)]
        v1 = first[x + NEAR, pl.ds(EDGE + HEM, ny + HEM)]
        v2 = second[x + 1, pl.ds(EDGE + HEM, ny + HEM)]
        value = c0 * v0[: ny + HEM] + c1 * v1 + c2 * v2
        level[x, pl.ds(0, ny + HEM)] = sigmoid(value - iso)
        return value

    @pl.loop(0, nx, unroll=4)
    def _(x):
        indicator[x] = set_level(x)[:ny]

    set_level(nx)
    result = pltpu.make_async_copy(indicator, indicator_hbm, result_sem)
    result.start()
    outside = sigmoid(-iso)
    lane = lax.broadcasted_iota(jnp.int32, (ny, nz), 1)

    @pl.loop(0, nx, unroll=4)
    def _(x):
        here = level[x, pl.ds(0, ny)]
        above = jnp.where(lane < nz - 1, pltpu.roll(here, nz - 1, 1), outside)
        for edge, there in enumerate((level[x + 1, pl.ds(0, ny)], level[x, pl.ds(1, ny)], above)):
            value = here * (1.0 - there) + (1.0 - here) * there
            for row in range(0, ny, 8):
                turned = pltpu.roll(value[row : row + 8], 0, 1, stride=BLK, stride_axis=0)
                weight[edge, pl.ds(x * (ny + 1) + row, 8)] = turned

    chunk = lax.broadcasted_iota(jnp.int32, (8, nz), 1) // BLK
    bricks_z = nz // BLK
    per_row = nz // BLK

    copy.wait()

    def out(slot):
        return pltpu.make_async_copy(crossing.at[slot], crossing_hbm.at[slot], slot_sems.at[slot])

    @pl.loop(0, visible.shape[0], unroll=2)
    def _(slot):
        number = visible[slot]
        safe = jnp.maximum(number, 0)
        begin = (safe // bricks_z) * BLK
        column = safe % bricks_z
        used = jnp.where(number >= 0, 1.0, 0.0)
        spots = [chunk == lax.rem(column + row, per_row) for row in range(per_row)]
        turn = lax.rem(nz - column * BLK, nz)
        for edge in range(3):
            for half in range(2):
                for part in range(BLK // per_row):
                    at = half * 8 * (ny + 1) + begin + part * per_row
                    tile = weight[edge, pl.ds(at, 8, stride=ny + 1)]
                    for row in range(1, per_row):
                        lines = weight[edge, pl.ds(at + row, 8, stride=ny + 1)]
                        tile = jnp.where(spots[row], lines, tile)
                    tile = pltpu.roll(tile, turn, 1) * used
                    crossing[slot, edge, pl.ds(half * 16 + part, 8, stride=2)] = tile
        out(slot).start()

    for slot in range(visible.shape[0]):
        out(slot).wait()
    result.wait()


def whole(*shape):
    return jax.ShapeDtypeStruct(shape, F32)


VMEM = pl.BlockSpec(memory_space=pltpu.VMEM)


HBM = pl.BlockSpec(memory_space=pltpu.HBM)


def kernel(body, inputs, outputs, scratch=(), results=VMEM, alias=None, flops=0):
    return pl.pallas_call(
        body,
        in_specs=list(inputs),
        out_specs=[results] * len(outputs),
        out_shape=list(outputs),
        scratch_shapes=list(scratch),
        input_output_aliases=alias or {},
        cost_estimate=pl.CostEstimate(flops=flops, bytes_accessed=flops // 4, transcendentals=0),
        compiler_params=pltpu.CompilerParams(vmem_limit_bytes=32 * 1024 * 1024),
    )


def in_hbm(value):
    return pltpu.with_memory_space_constraint(value, pltpu.HBM)


def swap(value, axis, first):
    count = lax.axis_size(axis)
    pairs = [(k, k + 1) for k in range(first, count - 1, 2)]
    return lax.ppermute(value, axis, pairs + [(b, a) for a, b in pairs])


def body(right_side, screening, active_blocks, visible_bricks):
    nx, ny, nz = right_side.shape
    active = active_blocks.reshape(-1)
    visible = visible_bricks.reshape(-1)
    devices = lax.axis_size("gx") * lax.axis_size("gy")
    slab = whole(nx, ny, nz)
    planes, near, third = nx + 2 * WIDE, nx + 2 * NEAR, nx + 2
    wide, rows = ny + 2 * EDGE, ny + 2 * HEM
    rim = whole(nx * (WIDE + NEAR), nz)
    lists = pltpu.SMEM(active.shape, jnp.int32)
    far, near_by = kernel(
        pack_kernel,
        (HBM, HBM, HBM),
        (rim, rim),
        (
            lists,
            pltpu.VMEM((2, nx, EDGE, nz), F32),
            pltpu.VMEM((2, nx, EDGE, nz), F32),
            pltpu.SemaphoreType.DMA((5,)),
        ),
    )(in_hbm(active), in_hbm(right_side), in_hbm(screening))
    far = swap(far, "gy", 1)
    near_by = swap(near_by, "gy", 0)
    lines = WIDE * (ny + 2 * WIDE) + NEAR * (ny + 2 * NEAR)
    side = whole(-(-lines // 8) * 8, nz)
    longer = whole(side.shape[0] + 8, nz)
    placed = (whole(planes, wide, nz), whole(nx, wide, nz), longer, side)
    held = kernel(
        place_kernel, (HBM, VMEM, VMEM), placed, (lists, pltpu.SemaphoreType.DMA), flops=4_000_000
    )(in_hbm(active), right_side, screening)
    field, weight, cross, chip = kernel(
        widen_kernel, (VMEM,) * 6, placed, alias={k: k for k in range(4)}
    )(*held, far, near_by)
    cross = swap(cross, "gx", 1)
    chip = swap(chip, "gx", 0)
    kept = [whole(planes, wide, nz)] + [whole(near, wide, nz)] * 2
    kept += [whole(near, rows + 2 * EDGE, nz), whole(third, rows + 2 * EDGE, nz)]
    kept += [whole(planes, rows, nz)] * 2 + [whole(near, rows, nz)] * 2 + [whole(third + 2, ny, nz)] * 2
    tallies = whole(10, 8, nz)
    work = (pltpu.VMEM((planes, wide + 2 * EDGE, nz), F32),) * 2
    held = kernel(inner_kernel, (VMEM,) * 2, kept[1:] + [tallies], work, flops=20_000_000)(field, weight)
    held = [field, *held]
    for last, message in ((False, chip), (True, cross)):
        held = kernel(
            functools.partial(side_kernel, last),
            (VMEM,) * (HELD + 2),
            kept + [whole(1, nz) if last else tallies],
            work,
            alias={1 + k: k for k in range(HELD)},
            flops=10_000_000,
        )(message, *held)
    field, _, _, first, second = held[:5]
    devices = lax.axis_size("gx") * lax.axis_size("gy")
    parts = lax.all_to_all(jnp.broadcast_to(held[-1], (devices, 1, nz)), ("gx", "gy"), 0, 0)
    slots = visible.shape[0]
    shape = (slots, 3, BLK**3 // nz, nz)
    indicator, crossing = kernel(
        finish_kernel,
        (HBM,) + (VMEM,) * 4,
        (slab, whole(*shape)),
        (
            pltpu.SMEM(visible.shape, jnp.int32),
            pltpu.VMEM(slab.shape, F32),
            pltpu.VMEM(shape, F32),
            pltpu.VMEM((nx + 1, ny + EDGE, nz), F32),
            pltpu.VMEM((3, nx * (ny + 1), nz), F32),
            pltpu.SemaphoreType.DMA,
            pltpu.SemaphoreType.DMA((slots,)),
            pltpu.SemaphoreType.DMA,
        ),
        results=HBM,
    )(in_hbm(visible), parts.reshape(devices, nz), field, first, second)
    return indicator, crossing.reshape(slots, 1, 3, BLK**3)


def solution(mesh):
    return jax.shard_map(
        body,
        mesh=mesh,
        in_specs=(
            P("gx", "gy", None),
            P("gx", "gy", None),
            P("gx", "gy", None),
            P("gx", "gy", None),
        ),
        out_specs=(P("gx", "gy", None), P("gx", "gy", None, None)),
        check_vma=False,
    )
```

```python
import functools

import jax
import jax.numpy as jnp
from jax import lax
from jax.experimental import pallas as pl
from jax.experimental.pallas import tpu as pltpu
from jax.sharding import PartitionSpec as P

BLK = 16
WIDE = 5
NEAR = 3
HEM = 4
EDGE = 8
SHARP = 4.0
SCALE = 1.0 / 86400.0
SHIFT = 2.25
LOW, HIGH = 0.5, 7.0
SUMS = 16
EXTRA, INNER, SIDE = 96, 0, 0
HELD = 11
F32 = jnp.float32


def mass(mid, one, two):
    return 66.0 * mid + (26.0 * one + two)


def stiff(mid, one, two):
    return 6.0 * mid - (2.0 * one + two)


def block_mask(active, slots, rows, columns):
    y = lax.broadcasted_iota(jnp.int32, (rows, columns), 0)
    z = lax.broadcasted_iota(jnp.int32, (rows, columns), 1)
    number = (y // BLK) * (columns // BLK) + z // BLK
    mask = jnp.zeros((rows, columns), F32)
    for slot in range(slots):
        mask = jnp.where(number == active[slot], 1.0, mask)
    return mask


def on_odd():
    return lax.rem(lax.axis_index("gx"), 2)


def odd_on(axis):
    return lax.rem(lax.axis_index(axis), 2)


def pack_kernel(active_hbm, right_hbm, screen_hbm, far, near, mask_out, active, right, screen, sems):
    nx, ny, nz = right_hbm.shape
    copies = [pltpu.make_async_copy(active_hbm, active, sems.at[0])]
    for k, (source, target) in enumerate(((right_hbm, right), (screen_hbm, screen))):
        for high in range(2):
            rows = pl.ds(high * (ny - EDGE), EDGE)
            copies.append(pltpu.make_async_copy(source.at[:, rows], target.at[high], sems.at[1 + 2 * k + high]))
    for copy in copies:
        copy.start()
    copies[0].wait()
    mask = block_mask(active, active.shape[0], ny, nz)
    mask_out[...] = mask
    row = lax.broadcasted_iota(jnp.int32, (EDGE, nz), 0)
    for copy in copies[1:]:
        copy.wait()

    def write(high_out, low_out):
        for x in range(nx):
            rows = pl.ds(x * EDGE, EDGE)
            low_out[rows] = jnp.where(row < WIDE, right[0, x], pltpu.roll(screen[0, x], WIDE, 0)) * mask[:EDGE]
            beside = pltpu.roll(screen[1, x] * mask[ny - EDGE :], NEAR, 0)
            high_out[rows] = jnp.where(row >= NEAR, right[1, x] * mask[ny - EDGE :], beside)

    odd = odd_on("gy")
    pl.when(odd == 1)(functools.partial(write, far, near))
    pl.when(odd == 0)(functools.partial(write, near, far))


def place_kernel(mask_in, right, screen, field, weight, cross, chip):
    nx, ny, nz = right.shape
    mask = mask_in[...]
    own = pl.ds(EDGE, ny)
    for x in range(nx):
        field[WIDE + x, own] = right[x] * mask
        weight[x, own] = screen[x] * mask
    odd = odd_on("gx")
    for target, high in ((cross, odd), (chip, 1 - odd)):
        for x in range(WIDE):
            target[x * ny : (x + 1) * ny] = field[WIDE + high * (nx - WIDE) + x, own]
        for x in range(NEAR):
            row = (WIDE + x) * ny
            target[row : row + ny] = weight[high * (nx - NEAR) + x, own]


def widen_kernel(far, near, chip_in, chip, corner):
    nx = far.shape[0] // EDGE
    base = chip.shape[0] - corner.shape[0]
    odd = odd_on("gx")

    def fill(low, high):
        for target, start, side in ((corner, 0, odd), (chip, base, 1 - odd)):
            for x in range(WIDE):
                tile = pl.ds((side * (nx - WIDE) + x) * EDGE, EDGE)
                row = start + 2 * x * EDGE
                target[row : row + EDGE] = low[tile]
                target[row + EDGE : row + 2 * EDGE] = high[tile]

    by_y(fill, far, near)


def by_y(action, far, near):
    odd = odd_on("gy")
    pl.when(odd == 1)(functools.partial(action, near, far))
    pl.when(odd == 0)(functools.partial(action, far, near))


def near_z(value):
    lane = lax.broadcasted_iota(jnp.int32, value.shape, 1)
    last = value.shape[1]

    def shifted(step):
        before = jnp.where(lane >= step, pltpu.roll(value, step, 1), 0.0)
        after = jnp.where(lane < last - step, pltpu.roll(value, last - step, 1), 0.0)
        return before + after

    return shifted(1), shifted(2)


def set_beside(field, x, keep, shifted, weight_x, tile, high):
    start = field.shape[1] - EDGE if high else 0
    field[x, start : start + EDGE] = tile
    if weight_x is not None:
        set_weight(keep, shifted, weight_x, pl.ds(start, EDGE), pltpu.roll(tile, NEAR if high else WIDE, 0))


def set_weight(keep, shifted, at, rows, weight):
    on = weight > 0.0
    keep[at, rows] = jnp.where(on, SCALE, 0.0)
    shifted[at, rows] = jnp.where(on, weight - SHIFT, 0.0)


def along_z(source, za, zb, count, first, rows):
    @pl.loop(0, count, unroll=count if count < 8 else 4)
    def _(k):
        value = source[first + k, rows]
        near = near_z(value)
        za[first + k, rows] = mass(value, *near)
        zb[first + k, rows] = stiff(value, *near)


def near_y(source, x, row, top, end):
    def part(step):
        return source[x, pl.ds(row + step, 8)]

    below, above = part(-2), part(2)
    place = lax.broadcasted_iota(jnp.int32, below.shape, 0)
    if top:
        below = jnp.where(place == 0, 0.0, jnp.where(place == 1, 2.0 * below, below))
    if end:
        above = jnp.where(place == 7, 0.0, jnp.where(place == 6, 2.0 * above, above))
    return part(0), part(-1) + part(1), below + above


def along_y(za, zb, x, row, top=False, end=False):
    a, b = near_y(za, x, row, top, end), near_y(zb, x, row, top, end)
    return mass(*a), mass(*b) + stiff(*a)


def along_yz(source, x, row, top=False, end=False):
    here, one, two = near_y(source, x, row, top, end)
    heavy, stretched = mass(here, one, two), stiff(here, one, two)
    heavy_near, stretched_near = near_z(heavy), near_z(stretched)
    return mass(heavy, *heavy_near), stiff(heavy, *heavy_near) + mass(stretched, *stretched_near)


def across(window):
    p, q = zip(*window)
    return mass(q[2], q[1] + q[3], q[0] + q[4]) + stiff(p[2], p[1] + p[3], p[0] + p[4])


def power(target, source, row, keep, shifted, skip, x, group, window):
    rows, at = pl.ds(EDGE + 8 * group, 8), pl.ds(EDGE - HEM + 8 * group, 8)
    center = source[x + 2, pl.ds(row + 8 * group, 8)]
    target[x, rows] = keep[x + skip, at] * across(window) + shifted[x + skip, at] * center


def z_rows(source, row):
    return pl.ds(0, source.shape[1]) if row < EDGE else pl.ds(EDGE, source.shape[1] - 2 * EDGE)


def advance(target, source, row, keep, shifted, skip, yp, yq, za, zb, count, first):
    groups = target.shape[1] // 8 - 2
    along_z(source, za, zb, count, first, z_rows(source, row))

    def some(chosen):
        def planes(x, windows, output):
            windows = [list(window) for window in windows]
            for k in range(4):
                for window, group in zip(windows, chosen):
                    p, q = along_y(za, zb, x + k, row + 8 * group)
                    rows = pl.ds(8 * group, 8)
                    yp[x + k, rows] = p
                    yq[x + k, rows] = q
                    window.append((p, q))
                    if output:
                        power(target, source, row, keep, shifted, skip, x + k - 4, group, window[-5:])
            return tuple(tuple(window[-4:]) for window in windows)

        windows = planes(first, ((),) * len(chosen), False)
        lax.fori_loop(1, count // 4, lambda k, carry: planes(first + 4 * k, carry, True), windows)

    for begin in range(0, groups, 3):
        some(range(begin, min(begin + 3, groups)))


def advance_side(target, source, row, keep, shifted, skip, yp, yq, high):
    groups = target.shape[1] // 8 - 2
    base = high * (target.shape[0] - WIDE)
    start = high * (source.shape[0] - WIDE)
    for group in range(groups):
        rows = pl.ds(8 * group, 8)
        for k in range(WIDE):
            p, q = along_yz(source, start + k, row + 8 * group)
            yp[start + k, rows] = p
            yq[start + k, rows] = q
    for group in range(groups):
        rows = pl.ds(8 * group, 8)
        window = [(yp[base + k, rows], yq[base + k, rows]) for k in range(WIDE + 4)]
        for k in range(WIDE):
            power(target, source, row, keep, shifted, skip, base + k, group, window[k : k + 5])


def last_rows(stencils, yp, yq, count, first):
    groups = yp.shape[1] // 8
    for group in range(groups):
        rows = pl.ds(8 * group, 8)
        for k in range(count):
            p, q = stencils(first + k, EDGE + HEM + 8 * group, group == 0, group == groups - 1)
            yp[first + 1 + k, rows] = p
            yq[first + 1 + k, rows] = q


def fold(value):
    return jnp.sum(value.reshape(-1, 8, value.shape[1]), axis=0)


def add_sums(totals, arrays, count, first_x):
    field, keep, shifted, first, second, yp, yq = arrays
    totals = list(totals)
    for group in range(yp.shape[1] // 8):
        rows = pl.ds(8 * group, 8)
        mid, own = pl.ds(EDGE + 8 * group, 8), pl.ds(EDGE + HEM + 8 * group, 8)
        window = [(yp[first_x + k, rows], yq[first_x + k, rows]) for k in range(count + 4)]
        for k in range(count):
            x = first_x + k
            v0 = field[x + WIDE, mid]
            v1 = first[x + NEAR, own]
            v2 = second[x + 1, own]
            form = v2 * (SCALE * across(window[k : k + 5]) + shifted[x + NEAR, mid] * v2)
            on = jnp.where(keep[x + NEAR, mid] > 0.0, 1.0, 0.0)
            new = (v0 * v0, v0 * v1, v1 * v1, v1 * v2, v2 * v2, form, v0, v1, v2, on)
            totals = [total + value for total, value in zip(totals, new)]
    return totals


def inner_kernel(
    far, near, field_in, weight, field, keep, shifted, first, second, yp1, yq1, yp2, yq2, yp3, yq3, sums, za, zb
):
    nx, wide, nz = weight.shape
    ny = wide - 2 * EDGE

    def fill(low, high):
        for x in range(nx):
            set_beside(field, WIDE + x, keep, shifted, NEAR + x, low[EDGE * x : EDGE * (x + 1)], False)
            set_beside(field, WIDE + x, keep, shifted, NEAR + x, high[EDGE * x : EDGE * (x + 1)], True)

    by_y(fill, far, near)
    own = pl.ds(EDGE, ny)
    for x in range(nx):
        set_weight(keep, shifted, NEAR + x, own, weight[x, own])
    advance(first, field, EDGE - HEM, keep, shifted, 0, yp1, yq1, za, zb, nx, WIDE)
    advance(second, first, EDGE, keep, shifted, 2, yp2, yq2, za, zb, nx - 4, WIDE)
    along_z(second, za, zb, nx - 8, WIDE, z_rows(second, EDGE))
    last_rows(functools.partial(along_y, za, zb), yp3, yq3, nx - 8, WIDE)
    arrays = (field, keep, shifted, first, second, yp3, yq3)
    totals = add_sums((jnp.zeros((8, nz), F32),) * 10, arrays, nx - 12, WIDE + 1)
    for place, total in enumerate(totals):
        sums[place] = total


def side_kernel(last, message, corner, *refs):
    sums_in = refs[HELD]
    field, keep, shifted, first, second, yp1, yq1, yp2, yq2, yp3, yq3, sums = refs[HELD + 1 :]
    planes, wide, nz = field.shape
    nx, ny = planes - 2 * WIDE, wide - 2 * EDGE
    odd = odd_on("gx")
    high = odd if last else 1 - odd
    own = pl.ds(EDGE, ny)
    base = corner.shape[0] - 2 * WIDE * EDGE
    for x in range(WIDE):
        plane = high * (nx + WIDE) + x
        field[plane, own] = message[x * ny : (x + 1) * ny]
        for up in range(2):
            row = base + (2 * x + up) * EDGE
            set_beside(field, plane, keep, shifted, None, corner[row : row + EDGE], up == 1)
    for x in range(NEAR):
        plane = high * (nx + NEAR) + x
        row = (WIDE + x) * ny
        set_weight(keep, shifted, plane, own, message[row : row + ny])
        place = base + (x + (1 - high) * (WIDE - NEAR)) * 2 * EDGE
        for up in range(2):
            tile = corner[pl.ds(place + up * EDGE, EDGE)]
            rows = pl.ds(up * (wide - EDGE), EDGE)
            set_weight(keep, shifted, plane, rows, pltpu.roll(tile, NEAR if up else WIDE, 0))
    advance_side(first, field, EDGE - HEM, keep, shifted, 0, yp1, yq1, high)
    advance_side(second, first, EDGE, keep, shifted, 2, yp2, yq2, high)
    last_rows(functools.partial(along_yz, second), yp3, yq3, WIDE, high * (nx + 2 - WIDE))
    none = jnp.zeros((ny, nz), F32)
    yp3[high * (nx + 3)] = none
    yq3[high * (nx + 3)] = none
    totals = tuple(sums_in[place] for place in range(10))
    arrays = (field, keep, shifted, first, second, yp3, yq3)
    totals = list(add_sums(totals, arrays, WIDE + 1, high * (nx - WIDE - 1)))
    own = pl.ds(EDGE + HEM, ny)
    beside, edge, next_edge = 1 + high * (nx + 1), 2 + high * (nx - 1), 3 + high * (nx - 3)
    give = 13.0 * yq3[edge] - yp3[edge] + (yq3[next_edge] - yp3[next_edge])
    take = 13.0 * yq3[beside] - yp3[beside]
    totals[5] += SCALE * fold(second[beside - 1, own] * give - second[edge - 1, own] * take)
    if not last:
        for place, total in enumerate(totals):
            sums[place] = total
        return
    row = lax.broadcasted_iota(jnp.int32, (SUMS, nz), 0)
    lane = lax.broadcasted_iota(jnp.int32, (SUMS, nz), 1)
    lines = jnp.zeros((SUMS, nz), F32)
    for place, total in enumerate(totals):
        lines = jnp.where(row == place, jnp.sum(total, axis=0, keepdims=True), lines)
    pieces, rest = [], lines
    for _ in range(3):
        pieces.append(rest.astype(jnp.bfloat16))
        rest = rest - pieces[-1].astype(F32)
    ones = jnp.ones((nz, nz), jnp.bfloat16)
    whole_sums = jnp.dot(jnp.concatenate(pieces, axis=0), ones, preferred_element_type=F32)
    top, rest = two_sum(whole_sums[:SUMS], whole_sums[SUMS : 2 * SUMS])
    pair = two_sum(top, rest + whole_sums[2 * SUMS :])
    spot = jnp.where(lane == row, pair[0], jnp.where(lane == row + SUMS, pair[1], 0.0))
    sums[...] = jnp.sum(spot, axis=0, keepdims=True)


def two_sum(a, b):
    total = a + b
    part = total - a
    return total, (a - (total - part)) + (b - part)


def pair_add(a, b):
    total, rest = two_sum(a[0], b[0])
    return total, rest + (a[1] + b[1])


def halves(a):
    wide = 4097.0 * a
    top = wide - (wide - a)
    return top, a - top


def pair_mul(a, b):
    product = a[0] * b[0]
    a_top, a_rest = halves(a[0])
    b_top, b_rest = halves(b[0])
    rest = ((a_top * b_top - product) + a_top * b_rest + a_rest * b_top) + a_rest * b_rest
    rest = rest + (a[0] * b[1] + a[1] * b[0])
    total = product + rest
    return total, rest - (total - product)


def pair_sub(a, b):
    total, rest = two_sum(a[0], -b[0])
    rest = rest + (a[1] - b[1])
    out = total + rest
    return out, rest - (out - total)


def ratio(over, under, low, high):
    good = under > 0.0
    value = jnp.where(good, over / jnp.where(good, under, 1.0), 0.5 * (low + high))
    return jnp.minimum(jnp.maximum(value, low), high)


def coefficients(total):
    scale = 1.0 / total[0][0]
    zero = jnp.zeros_like(scale)
    g = [pair_mul(item, (scale, zero)) for item in total[:6]]
    shift = (jnp.full_like(scale, SHIFT), zero)
    h = [pair_add(g[k + 1], pair_mul(g[k], shift)) for k in range(5)]

    def minor(a, b, c, d):
        return pair_sub(pair_mul(a, b), pair_mul(c, d))

    s11 = minor(h[2], h[0], h[1], h[1])
    s12 = minor(h[3], h[0], h[1], h[2])
    s22 = minor(h[4], h[0], h[2], h[2])
    y1 = minor(g[1], h[0], h[1], g[0])
    y2 = minor(g[2], h[0], h[2], g[0])
    last = minor(s22, s11, s12, s12)
    side = minor(y2, s11, s12, y1)
    alpha = g[0][0] / h[0][0]
    l10 = h[1][0] / h[0][0]
    l20 = h[2][0] / h[0][0]
    l21 = ratio(s12[0], s11[0], l10 + (LOW - SHIFT), l10 + (HIGH - SHIFT))
    gamma1 = ratio(y1[0], s11[0], -alpha / LOW, -alpha / HIGH)
    gamma2 = ratio(side[0], last[0], -gamma1 / HIGH, -gamma1 / LOW)
    c1 = gamma1 - gamma2 * l21
    return alpha - c1 * l10 - gamma2 * l20, c1, gamma2


def sigmoid(value):
    return 1.0 / (1.0 + jnp.exp(-SHARP * value))


def finish_kernel(
    visible_hbm, parts, field, first, second, indicator_hbm, crossing_hbm,
    visible, indicator, crossing, level, weight, sem, slot_sems, result_sem,
):
    nx, ny, nz = indicator.shape
    copy = pltpu.make_async_copy(visible_hbm, visible, sem)
    copy.start()
    devices = parts.shape[0]
    tiles = [parts[pl.ds(8 * k, 8)] for k in range(devices // 8)]
    pairs = [(tile, pltpu.roll(tile, nz - SUMS, 1)) for tile in tiles]
    while len(pairs) > 1:
        pairs = [pair_add(a, b) for a, b in zip(pairs[::2], pairs[1::2])]
    total = pairs[0]
    for step in (4, 2, 1):
        total = pair_add(total, (pltpu.roll(total[0], step, 0), pltpu.roll(total[1], step, 0)))

    def spread(value, k):
        return jnp.broadcast_to(value[0:1, k : k + 1], (1, nz))

    item = [(spread(total[0], k), spread(total[1], k)) for k in range(10)]
    c0, c1, c2 = coefficients(item)
    over = c0 * (item[6][0] + item[6][1]) + c1 * (item[7][0] + item[7][1]) + c2 * (item[8][0] + item[8][1])
    iso = over / item[9][0]

    def set_level(x):
        v0 = field[x + WIDE, pl.ds(EDGE, ny + EDGE)]
        v1 = first[x + NEAR, pl.ds(EDGE + HEM, ny + HEM)]
        v2 = second[x + 1, pl.ds(EDGE + HEM, ny + HEM)]
        value = c0 * v0[: ny + HEM] + c1 * v1 + c2 * v2
        level[x, pl.ds(0, ny + HEM)] = sigmoid(value - iso)
        return value

    @pl.loop(0, nx, unroll=4)
    def _(x):
        indicator[x] = set_level(x)[:ny]

    set_level(nx)
    result = pltpu.make_async_copy(indicator, indicator_hbm, result_sem)
    result.start()
    outside = sigmoid(-iso)
    lane = lax.broadcasted_iota(jnp.int32, (ny, nz), 1)

    @pl.loop(0, nx, unroll=4)
    def _(x):
        here = level[x, pl.ds(0, ny)]
        above = jnp.where(lane < nz - 1, pltpu.roll(here, nz - 1, 1), outside)
        for edge, there in enumerate((level[x + 1, pl.ds(0, ny)], level[x, pl.ds(1, ny)], above)):
            value = here * (1.0 - there) + (1.0 - here) * there
            for row in range(0, ny, 8):
                turned = pltpu.roll(value[row : row + 8], 0, 1, stride=BLK, stride_axis=0)
                weight[edge, pl.ds(x * (ny + 1) + row, 8)] = turned

    chunk = lax.broadcasted_iota(jnp.int32, (8, nz), 1) // BLK
    bricks_z = nz // BLK
    per_row = nz // BLK

    copy.wait()

    def out(slot):
        return pltpu.make_async_copy(crossing.at[slot], crossing_hbm.at[slot], slot_sems.at[slot])

    @pl.loop(0, visible.shape[0], unroll=2)
    def _(slot):
        number = visible[slot]
        safe = jnp.maximum(number, 0)
        begin = (safe // bricks_z) * BLK
        column = safe % bricks_z
        used = jnp.where(number >= 0, 1.0, 0.0)
        spots = [chunk == lax.rem(column + row, per_row) for row in range(per_row)]
        turn = lax.rem(nz - column * BLK, nz)
        for edge in range(3):
            for half in range(2):
                for part in range(BLK // per_row):
                    at = half * 8 * (ny + 1) + begin + part * per_row
                    tile = weight[edge, pl.ds(at, 8, stride=ny + 1)]
                    for row in range(1, per_row):
                        lines = weight[edge, pl.ds(at + row, 8, stride=ny + 1)]
                        tile = jnp.where(spots[row], lines, tile)
                    tile = pltpu.roll(tile, turn, 1) * used
                    crossing[slot, edge, pl.ds(half * 16 + part, 8, stride=2)] = tile
        out(slot).start()

    for slot in range(visible.shape[0]):
        out(slot).wait()
    result.wait()


def whole(*shape):
    return jax.ShapeDtypeStruct(shape, F32)


VMEM = pl.BlockSpec(memory_space=pltpu.VMEM)


HBM = pl.BlockSpec(memory_space=pltpu.HBM)


def kernel(body, inputs, outputs, scratch=(), results=VMEM, alias=None, flops=0):
    return pl.pallas_call(
        body,
        in_specs=list(inputs),
        out_specs=[results] * len(outputs),
        out_shape=list(outputs),
        scratch_shapes=list(scratch),
        input_output_aliases=alias or {},
        cost_estimate=pl.CostEstimate(flops=flops, bytes_accessed=flops // 4, transcendentals=0),
        compiler_params=pltpu.CompilerParams(vmem_limit_bytes=32 * 1024 * 1024),
    )


def in_hbm(value):
    return pltpu.with_memory_space_constraint(value, pltpu.HBM)


def swap(value, axis, first):
    count = lax.axis_size(axis)
    pairs = [(k, k + 1) for k in range(first, count - 1, 2)]
    return lax.ppermute(value, axis, pairs + [(b, a) for a, b in pairs])


def body(right_side, screening, active_blocks, visible_bricks):
    nx, ny, nz = right_side.shape
    active = active_blocks.reshape(-1)
    visible = visible_bricks.reshape(-1)
    devices = lax.axis_size("gx") * lax.axis_size("gy")
    slab = whole(nx, ny, nz)
    planes, near, third = nx + 2 * WIDE, nx + 2 * NEAR, nx + 2
    wide, rows = ny + 2 * EDGE, ny + 2 * HEM
    rim = whole(nx * EDGE, nz)
    edges = pltpu.VMEM((2, nx, EDGE, nz), F32)
    far, near_by, mask = kernel(
        pack_kernel,
        (HBM, HBM, HBM),
        (rim, rim, whole(ny, nz)),
        (pltpu.SMEM(active.shape, jnp.int32), edges, edges, pltpu.SemaphoreType.DMA((5,))),
    )(in_hbm(active), in_hbm(right_side), in_hbm(screening))
    far = swap(far, "gy", 1)
    near_by = swap(near_by, "gy", 0)
    straight, corners = (WIDE + NEAR) * ny, 2 * WIDE * EDGE
    side = whole(straight + corners, nz)
    field, weight, cross, chip = kernel(
        place_kernel,
        (VMEM,) * 3,
        (whole(planes, wide, nz), whole(nx, wide, nz), whole(straight + EXTRA, nz), side),
    )(mask, right_side, screening)
    cross = swap(cross, "gx", 1)
    chip, corner = kernel(widen_kernel, (VMEM,) * 3, (side, whole(corners, nz)), alias={2: 0})(far, near_by, chip)
    chip = swap(chip, "gx", 0)
    corner = swap(corner, "gx", 1)
    kept = [whole(planes, wide, nz)] + [whole(near, wide, nz)] * 2
    kept += [whole(near, rows + 2 * EDGE, nz), whole(third, rows + 2 * EDGE, nz)]
    kept += [whole(planes, rows, nz)] * 2 + [whole(near, rows, nz)] * 2 + [whole(third + 2, ny, nz)] * 2
    tallies = whole(10, 8, nz)
    work = (pltpu.VMEM((planes, wide + 2 * EDGE, nz), F32),) * 2
    held = kernel(inner_kernel, (VMEM,) * 4, kept + [tallies], work, alias={2: 0}, flops=INNER)(
        far, near_by, field, weight
    )
    for last, messages in ((False, (chip, chip)), (True, (cross, corner))):
        held = kernel(
            functools.partial(side_kernel, last),
            (VMEM,) * (HELD + 3),
            kept + [whole(1, nz) if last else tallies],
            alias={2 + k: k for k in range(HELD)},
            flops=SIDE,
        )(*messages, *held)
    field, _, _, first, second = held[:5]
    devices = lax.axis_size("gx") * lax.axis_size("gy")
    parts = lax.all_to_all(jnp.broadcast_to(held[-1], (devices, 1, nz)), ("gx", "gy"), 0, 0)
    slots = visible.shape[0]
    shape = (slots, 3, BLK**3 // nz, nz)
    indicator, crossing = kernel(
        finish_kernel,
        (HBM,) + (VMEM,) * 4,
        (slab, whole(*shape)),
        (
            pltpu.SMEM(visible.shape, jnp.int32),
            pltpu.VMEM(slab.shape, F32),
            pltpu.VMEM(shape, F32),
            pltpu.VMEM((nx + 1, ny + EDGE, nz), F32),
            pltpu.VMEM((3, nx * (ny + 1), nz), F32),
            pltpu.SemaphoreType.DMA,
            pltpu.SemaphoreType.DMA((slots,)),
            pltpu.SemaphoreType.DMA,
        ),
        results=HBM,
    )(in_hbm(visible), parts.reshape(devices, nz), field, first, second)
    return indicator, crossing.reshape(slots, 1, 3, BLK**3)


def solution(mesh):
    return jax.shard_map(
        body,
        mesh=mesh,
        in_specs=(
            P("gx", "gy", None),
            P("gx", "gy", None),
            P("gx", "gy", None),
            P("gx", "gy", None),
        ),
        out_specs=(P("gx", "gy", None), P("gx", "gy", None, None)),
        check_vma=False,
    )
```

```python
import functools

import jax
import jax.numpy as jnp
from jax import lax
from jax.experimental import pallas as pl
from jax.experimental.pallas import tpu as pltpu
from jax.sharding import PartitionSpec as P

BLK = 16
WIDE = 5
NEAR = 3
HEM = 4
EDGE = 8
SHARP = 4.0
SCALE = 1.0 / 86400.0
SHIFT = 2.25
LOW, HIGH = 0.5, 7.0
SUMS = 16
EXTRA, INNER, SIDE = 96, 0, 0
EARLY = 13
HELD = 11
F32 = jnp.float32


def mass(mid, one, two):
    return 66.0 * mid + (26.0 * one + two)


def stiff(mid, one, two):
    return 6.0 * mid - (2.0 * one + two)


def block_mask(active, slots, rows, columns):
    y = lax.broadcasted_iota(jnp.int32, (rows, columns), 0)
    z = lax.broadcasted_iota(jnp.int32, (rows, columns), 1)
    number = (y // BLK) * (columns // BLK) + z // BLK
    mask = jnp.zeros((rows, columns), F32)
    for slot in range(slots):
        mask = jnp.where(number == active[slot], 1.0, mask)
    return mask


def on_odd():
    return lax.rem(lax.axis_index("gx"), 2)


def odd_on(axis):
    return lax.rem(lax.axis_index(axis), 2)


def pack_kernel(active_hbm, right_hbm, screen_hbm, far, near, mask_out, active, right, screen, sems):
    nx, ny, nz = right_hbm.shape
    copies = [pltpu.make_async_copy(active_hbm, active, sems.at[0])]
    for k, (source, target) in enumerate(((right_hbm, right), (screen_hbm, screen))):
        for high in range(2):
            rows = pl.ds(high * (ny - EDGE), EDGE)
            copies.append(pltpu.make_async_copy(source.at[:, rows], target.at[high], sems.at[1 + 2 * k + high]))
    for copy in copies:
        copy.start()
    copies[0].wait()
    mask = block_mask(active, active.shape[0], ny, nz)
    mask_out[...] = mask
    row = lax.broadcasted_iota(jnp.int32, (EDGE, nz), 0)
    for copy in copies[1:]:
        copy.wait()

    def write(high_out, low_out):
        for x in range(nx):
            rows = pl.ds(x * EDGE, EDGE)
            low_out[rows] = jnp.where(row < WIDE, right[0, x], pltpu.roll(screen[0, x], WIDE, 0)) * mask[:EDGE]
            beside = pltpu.roll(screen[1, x] * mask[ny - EDGE :], NEAR, 0)
            high_out[rows] = jnp.where(row >= NEAR, right[1, x] * mask[ny - EDGE :], beside)

    odd = odd_on("gy")
    pl.when(odd == 1)(functools.partial(write, far, near))
    pl.when(odd == 0)(functools.partial(write, near, far))


def place_kernel(mask_in, right, screen, cross, chip, *arrays):
    field, keep, shifted = arrays[:3]
    nx, ny, nz = right.shape
    mask = mask_in[...]
    own = pl.ds(EDGE, ny)
    for x in range(nx):
        field[WIDE + x, own] = right[x] * mask
        set_weight(keep, shifted, NEAR + x, own, screen[x] * mask)
    odd = odd_on("gx")
    for target, high in ((cross, odd), (chip, 1 - odd)):
        for x in range(WIDE):
            target[x * ny : (x + 1) * ny] = right[high * (nx - WIDE) + x] * mask
        for x in range(NEAR):
            row = (WIDE + x) * ny
            target[row : row + ny] = screen[high * (nx - NEAR) + x] * mask
    pl.when(odd == 1)(functools.partial(early_powers, *arrays))


def early_kernel(*refs):
    pl.when(odd_on("gx") == 0)(functools.partial(early_powers, *refs[EARLY + 2 :]))


def early_powers(field, keep, shifted, first, second, yp1, yq1, yp2, yq2, za1, zb1, za2, zb2):
    nx, ny = field.shape[0] - 2 * WIDE, field.shape[1] - 2 * EDGE
    groups = (ny + 2 * HEM) // 8
    along_z(field, za1, zb1, nx, WIDE, pl.ds(EDGE, ny))
    middle = range(1, groups - 1)
    advance(first, field, EDGE - HEM, keep, shifted, 0, yp1, yq1, za1, zb1, nx, WIDE, middle)
    along_z(first, za2, zb2, nx - 4, WIDE, pl.ds(EDGE + 8, 8 * (groups - 2)))
    middle = range(2, groups - 2)
    advance(second, first, EDGE, keep, shifted, 2, yp2, yq2, za2, zb2, nx - 4, WIDE, middle)


def widen_kernel(far, near, chip_in, chip, corner):
    nx = far.shape[0] // EDGE
    base = chip.shape[0] - corner.shape[0]
    odd = odd_on("gx")

    def fill(low, high):
        for target, start, side in ((corner, 0, odd), (chip, base, 1 - odd)):
            for x in range(WIDE):
                tile = pl.ds((side * (nx - WIDE) + x) * EDGE, EDGE)
                row = start + 2 * x * EDGE
                target[row : row + EDGE] = low[tile]
                target[row + EDGE : row + 2 * EDGE] = high[tile]

    by_y(fill, far, near)


def by_y(action, far, near):
    odd = odd_on("gy")
    pl.when(odd == 1)(functools.partial(action, near, far))
    pl.when(odd == 0)(functools.partial(action, far, near))


def near_z(value):
    lane = lax.broadcasted_iota(jnp.int32, value.shape, 1)
    last = value.shape[1]

    def shifted(step):
        before = jnp.where(lane >= step, pltpu.roll(value, step, 1), 0.0)
        after = jnp.where(lane < last - step, pltpu.roll(value, last - step, 1), 0.0)
        return before + after

    return shifted(1), shifted(2)


def set_beside(field, x, keep, shifted, weight_x, tile, high):
    start = field.shape[1] - EDGE if high else 0
    field[x, start : start + EDGE] = tile
    if weight_x is not None:
        set_weight(keep, shifted, weight_x, pl.ds(start, EDGE), pltpu.roll(tile, NEAR if high else WIDE, 0))


def set_weight(keep, shifted, at, rows, weight):
    on = weight > 0.0
    keep[at, rows] = jnp.where(on, SCALE, 0.0)
    shifted[at, rows] = jnp.where(on, weight - SHIFT, 0.0)


def along_z(source, za, zb, count, first, rows):
    @pl.loop(0, count, unroll=count if count < 8 else 4)
    def _(k):
        value = source[first + k, rows]
        near = near_z(value)
        za[first + k, rows] = mass(value, *near)
        zb[first + k, rows] = stiff(value, *near)


def near_y(source, x, row, top, end):
    def part(step):
        return source[x, pl.ds(row + step, 8)]

    below, above = part(-2), part(2)
    place = lax.broadcasted_iota(jnp.int32, below.shape, 0)
    if top:
        below = jnp.where(place == 0, 0.0, jnp.where(place == 1, 2.0 * below, below))
    if end:
        above = jnp.where(place == 7, 0.0, jnp.where(place == 6, 2.0 * above, above))
    return part(0), part(-1) + part(1), below + above


def along_y(za, zb, x, row, top=False, end=False):
    a, b = near_y(za, x, row, top, end), near_y(zb, x, row, top, end)
    return mass(*a), mass(*b) + stiff(*a)


def along_yz(source, x, row, top=False, end=False):
    here, one, two = near_y(source, x, row, top, end)
    heavy, stretched = mass(here, one, two), stiff(here, one, two)
    heavy_near, stretched_near = near_z(heavy), near_z(stretched)
    return mass(heavy, *heavy_near), stiff(heavy, *heavy_near) + mass(stretched, *stretched_near)


def across(window):
    p, q = zip(*window)
    return mass(q[2], q[1] + q[3], q[0] + q[4]) + stiff(p[2], p[1] + p[3], p[0] + p[4])


def power(target, source, row, keep, shifted, skip, x, group, window):
    rows, at = pl.ds(EDGE + 8 * group, 8), pl.ds(EDGE - HEM + 8 * group, 8)
    center = source[x + 2, pl.ds(row + 8 * group, 8)]
    target[x, rows] = keep[x + skip, at] * across(window) + shifted[x + skip, at] * center


def advance(target, source, row, keep, shifted, skip, yp, yq, za, zb, count, first, groups):
    def some(chosen):
        def planes(x, windows, output):
            windows = [list(window) for window in windows]
            for k in range(4):
                for window, group in zip(windows, chosen):
                    p, q = along_y(za, zb, x + k, row + 8 * group)
                    rows = pl.ds(8 * group, 8)
                    yp[x + k, rows] = p
                    yq[x + k, rows] = q
                    window.append((p, q))
                    if output:
                        power(target, source, row, keep, shifted, skip, x + k - 4, group, window[-5:])
            return tuple(tuple(window[-4:]) for window in windows)

        windows = planes(first, ((),) * len(chosen), False)
        lax.fori_loop(1, count // 4, lambda k, carry: planes(first + 4 * k, carry, True), windows)

    for begin in range(0, len(groups), 3):
        some(groups[begin : begin + 3])


def advance_side(target, source, row, keep, shifted, skip, yp, yq, high):
    groups = target.shape[1] // 8 - 2
    base = high * (target.shape[0] - WIDE)
    start = high * (source.shape[0] - WIDE)
    for group in range(groups):
        rows = pl.ds(8 * group, 8)
        for k in range(WIDE):
            p, q = along_yz(source, start + k, row + 8 * group)
            yp[start + k, rows] = p
            yq[start + k, rows] = q
    for group in range(groups):
        rows = pl.ds(8 * group, 8)
        window = [(yp[base + k, rows], yq[base + k, rows]) for k in range(WIDE + 4)]
        for k in range(WIDE):
            power(target, source, row, keep, shifted, skip, base + k, group, window[k : k + 5])


def last_rows(stencils, yp, yq, count, first):
    groups = yp.shape[1] // 8
    for group in range(groups):
        rows = pl.ds(8 * group, 8)
        for k in range(count):
            p, q = stencils(first + k, EDGE + HEM + 8 * group, group == 0, group == groups - 1)
            yp[first + 1 + k, rows] = p
            yq[first + 1 + k, rows] = q


def fold(value):
    return jnp.sum(value.reshape(-1, 8, value.shape[1]), axis=0)


def add_sums(totals, arrays, count, first_x):
    field, keep, shifted, first, second, yp, yq = arrays
    totals = list(totals)
    for group in range(yp.shape[1] // 8):
        rows = pl.ds(8 * group, 8)
        mid, own = pl.ds(EDGE + 8 * group, 8), pl.ds(EDGE + HEM + 8 * group, 8)
        window = [(yp[first_x + k, rows], yq[first_x + k, rows]) for k in range(count + 4)]
        for k in range(count):
            x = first_x + k
            v0 = field[x + WIDE, mid]
            v1 = first[x + NEAR, own]
            v2 = second[x + 1, own]
            form = v2 * (SCALE * across(window[k : k + 5]) + shifted[x + NEAR, mid] * v2)
            on = jnp.where(keep[x + NEAR, mid] > 0.0, 1.0, 0.0)
            new = (v0 * v0, v0 * v1, v1 * v1, v1 * v2, v2 * v2, form, v0, v1, v2, on)
            totals = [total + value for total, value in zip(totals, new)]
    return totals


def inner_kernel(far, near, *refs):
    field, keep, shifted, first, second, yp1, yq1, yp2, yq2, za1, zb1, za2, zb2 = refs[EARLY : 2 * EARLY]
    yp3, yq3, sums, za, zb = refs[2 * EARLY :]
    planes, wide, nz = field.shape
    nx, ny = planes - 2 * WIDE, wide - 2 * EDGE
    groups = (ny + 2 * HEM) // 8

    def fill(low, high):
        for x in range(nx):
            set_beside(field, WIDE + x, keep, shifted, NEAR + x, low[EDGE * x : EDGE * (x + 1)], False)
            set_beside(field, WIDE + x, keep, shifted, NEAR + x, high[EDGE * x : EDGE * (x + 1)], True)

    by_y(fill, far, near)
    for start in (0, wide - EDGE):
        along_z(field, za1, zb1, nx, WIDE, pl.ds(start, EDGE))
    outer = (0, groups - 1)
    advance(first, field, EDGE - HEM, keep, shifted, 0, yp1, yq1, za1, zb1, nx, WIDE, outer)
    for group in outer:
        along_z(first, za2, zb2, nx - 4, WIDE, pl.ds(EDGE + 8 * group, 8))
    outer = (0, 1, groups - 2, groups - 1)
    advance(second, first, EDGE, keep, shifted, 2, yp2, yq2, za2, zb2, nx - 4, WIDE, outer)
    along_z(second, za, zb, nx - 8, WIDE, pl.ds(EDGE, ny + 2 * HEM))
    last_rows(functools.partial(along_y, za, zb), yp3, yq3, nx - 8, WIDE)
    arrays = (field, keep, shifted, first, second, yp3, yq3)
    totals = add_sums((jnp.zeros((8, nz), F32),) * 10, arrays, nx - 12, WIDE + 1)
    for place, total in enumerate(totals):
        sums[place] = total


def side_kernel(last, message, corner, *refs):
    sums_in = refs[HELD]
    field, keep, shifted, first, second, yp1, yq1, yp2, yq2, yp3, yq3, sums = refs[HELD + 1 :]
    planes, wide, nz = field.shape
    nx, ny = planes - 2 * WIDE, wide - 2 * EDGE
    odd = odd_on("gx")
    high = odd if last else 1 - odd
    own = pl.ds(EDGE, ny)
    base = corner.shape[0] - 2 * WIDE * EDGE
    for x in range(WIDE):
        plane = high * (nx + WIDE) + x
        field[plane, own] = message[x * ny : (x + 1) * ny]
        for up in range(2):
            row = base + (2 * x + up) * EDGE
            set_beside(field, plane, keep, shifted, None, corner[row : row + EDGE], up == 1)
    for x in range(NEAR):
        plane = high * (nx + NEAR) + x
        row = (WIDE + x) * ny
        set_weight(keep, shifted, plane, own, message[row : row + ny])
        place = base + (x + (1 - high) * (WIDE - NEAR)) * 2 * EDGE
        for up in range(2):
            tile = corner[pl.ds(place + up * EDGE, EDGE)]
            rows = pl.ds(up * (wide - EDGE), EDGE)
            set_weight(keep, shifted, plane, rows, pltpu.roll(tile, NEAR if up else WIDE, 0))
    advance_side(first, field, EDGE - HEM, keep, shifted, 0, yp1, yq1, high)
    advance_side(second, first, EDGE, keep, shifted, 2, yp2, yq2, high)
    last_rows(functools.partial(along_yz, second), yp3, yq3, WIDE, high * (nx + 2 - WIDE))
    none = jnp.zeros((ny, nz), F32)
    yp3[high * (nx + 3)] = none
    yq3[high * (nx + 3)] = none
    totals = tuple(sums_in[place] for place in range(10))
    arrays = (field, keep, shifted, first, second, yp3, yq3)
    totals = list(add_sums(totals, arrays, WIDE + 1, high * (nx - WIDE - 1)))
    own = pl.ds(EDGE + HEM, ny)
    beside, edge, next_edge = 1 + high * (nx + 1), 2 + high * (nx - 1), 3 + high * (nx - 3)
    give = 13.0 * yq3[edge] - yp3[edge] + (yq3[next_edge] - yp3[next_edge])
    take = 13.0 * yq3[beside] - yp3[beside]
    totals[5] += SCALE * fold(second[beside - 1, own] * give - second[edge - 1, own] * take)
    if not last:
        for place, total in enumerate(totals):
            sums[place] = total
        return
    row = lax.broadcasted_iota(jnp.int32, (SUMS, nz), 0)
    lane = lax.broadcasted_iota(jnp.int32, (SUMS, nz), 1)
    lines = jnp.zeros((SUMS, nz), F32)
    for place, total in enumerate(totals):
        lines = jnp.where(row == place, jnp.sum(total, axis=0, keepdims=True), lines)
    pieces, rest = [], lines
    for _ in range(3):
        pieces.append(rest.astype(jnp.bfloat16))
        rest = rest - pieces[-1].astype(F32)
    ones = jnp.ones((nz, nz), jnp.bfloat16)
    whole_sums = jnp.dot(jnp.concatenate(pieces, axis=0), ones, preferred_element_type=F32)
    top, rest = two_sum(whole_sums[:SUMS], whole_sums[SUMS : 2 * SUMS])
    pair = two_sum(top, rest + whole_sums[2 * SUMS :])
    spot = jnp.where(lane == row, pair[0], jnp.where(lane == row + SUMS, pair[1], 0.0))
    sums[...] = jnp.sum(spot, axis=0, keepdims=True)


def two_sum(a, b):
    total = a + b
    part = total - a
    return total, (a - (total - part)) + (b - part)


def pair_add(a, b):
    total, rest = two_sum(a[0], b[0])
    return total, rest + (a[1] + b[1])


def halves(a):
    wide = 4097.0 * a
    top = wide - (wide - a)
    return top, a - top


def pair_mul(a, b):
    product = a[0] * b[0]
    a_top, a_rest = halves(a[0])
    b_top, b_rest = halves(b[0])
    rest = ((a_top * b_top - product) + a_top * b_rest + a_rest * b_top) + a_rest * b_rest
    rest = rest + (a[0] * b[1] + a[1] * b[0])
    total = product + rest
    return total, rest - (total - product)


def pair_sub(a, b):
    total, rest = two_sum(a[0], -b[0])
    rest = rest + (a[1] - b[1])
    out = total + rest
    return out, rest - (out - total)


def ratio(over, under, low, high):
    good = under > 0.0
    value = jnp.where(good, over / jnp.where(good, under, 1.0), 0.5 * (low + high))
    return jnp.minimum(jnp.maximum(value, low), high)


def coefficients(total):
    scale = 1.0 / total[0][0]
    zero = jnp.zeros_like(scale)
    g = [pair_mul(item, (scale, zero)) for item in total[:6]]
    shift = (jnp.full_like(scale, SHIFT), zero)
    h = [pair_add(g[k + 1], pair_mul(g[k], shift)) for k in range(5)]

    def minor(a, b, c, d):
        return pair_sub(pair_mul(a, b), pair_mul(c, d))

    s11 = minor(h[2], h[0], h[1], h[1])
    s12 = minor(h[3], h[0], h[1], h[2])
    s22 = minor(h[4], h[0], h[2], h[2])
    y1 = minor(g[1], h[0], h[1], g[0])
    y2 = minor(g[2], h[0], h[2], g[0])
    last = minor(s22, s11, s12, s12)
    side = minor(y2, s11, s12, y1)
    alpha = g[0][0] / h[0][0]
    l10 = h[1][0] / h[0][0]
    l20 = h[2][0] / h[0][0]
    l21 = ratio(s12[0], s11[0], l10 + (LOW - SHIFT), l10 + (HIGH - SHIFT))
    gamma1 = ratio(y1[0], s11[0], -alpha / LOW, -alpha / HIGH)
    gamma2 = ratio(side[0], last[0], -gamma1 / HIGH, -gamma1 / LOW)
    c1 = gamma1 - gamma2 * l21
    return alpha - c1 * l10 - gamma2 * l20, c1, gamma2


def sigmoid(value):
    return 1.0 / (1.0 + jnp.exp(-SHARP * value))


def finish_kernel(
    visible_hbm, parts, field, first, second, indicator_hbm, crossing_hbm,
    visible, indicator, crossing, level, weight, sem, slot_sems, result_sem,
):
    nx, ny, nz = indicator.shape
    copy = pltpu.make_async_copy(visible_hbm, visible, sem)
    copy.start()
    devices = parts.shape[0]
    tiles = [parts[pl.ds(8 * k, 8)] for k in range(devices // 8)]
    pairs = [(tile, pltpu.roll(tile, nz - SUMS, 1)) for tile in tiles]
    while len(pairs) > 1:
        pairs = [pair_add(a, b) for a, b in zip(pairs[::2], pairs[1::2])]
    total = pairs[0]
    for step in (4, 2, 1):
        total = pair_add(total, (pltpu.roll(total[0], step, 0), pltpu.roll(total[1], step, 0)))

    def spread(value, k):
        return jnp.broadcast_to(value[0:1, k : k + 1], (1, nz))

    item = [(spread(total[0], k), spread(total[1], k)) for k in range(10)]
    c0, c1, c2 = coefficients(item)
    over = c0 * (item[6][0] + item[6][1]) + c1 * (item[7][0] + item[7][1]) + c2 * (item[8][0] + item[8][1])
    iso = over / item[9][0]

    def set_level(x):
        v0 = field[x + WIDE, pl.ds(EDGE, ny + EDGE)]
        v1 = first[x + NEAR, pl.ds(EDGE + HEM, ny + HEM)]
        v2 = second[x + 1, pl.ds(EDGE + HEM, ny + HEM)]
        value = c0 * v0[: ny + HEM] + c1 * v1 + c2 * v2
        level[x, pl.ds(0, ny + HEM)] = sigmoid(value - iso)
        return value

    @pl.loop(0, nx, unroll=4)
    def _(x):
        indicator[x] = set_level(x)[:ny]

    set_level(nx)
    result = pltpu.make_async_copy(indicator, indicator_hbm, result_sem)
    result.start()
    outside = sigmoid(-iso)
    lane = lax.broadcasted_iota(jnp.int32, (ny, nz), 1)

    @pl.loop(0, nx, unroll=4)
    def _(x):
        here = level[x, pl.ds(0, ny)]
        above = jnp.where(lane < nz - 1, pltpu.roll(here, nz - 1, 1), outside)
        for edge, there in enumerate((level[x + 1, pl.ds(0, ny)], level[x, pl.ds(1, ny)], above)):
            value = here * (1.0 - there) + (1.0 - here) * there
            for row in range(0, ny, 8):
                turned = pltpu.roll(value[row : row + 8], 0, 1, stride=BLK, stride_axis=0)
                weight[edge, pl.ds(x * (ny + 1) + row, 8)] = turned

    chunk = lax.broadcasted_iota(jnp.int32, (8, nz), 1) // BLK
    bricks_z = nz // BLK
    per_row = nz // BLK

    copy.wait()

    def out(slot):
        return pltpu.make_async_copy(crossing.at[slot], crossing_hbm.at[slot], slot_sems.at[slot])

    @pl.loop(0, visible.shape[0], unroll=2)
    def _(slot):
        number = visible[slot]
        safe = jnp.maximum(number, 0)
        begin = (safe // bricks_z) * BLK
        column = safe % bricks_z
        used = jnp.where(number >= 0, 1.0, 0.0)
        spots = [chunk == lax.rem(column + row, per_row) for row in range(per_row)]
        turn = lax.rem(nz - column * BLK, nz)
        for edge in range(3):
            for half in range(2):
                for part in range(BLK // per_row):
                    at = half * 8 * (ny + 1) + begin + part * per_row
                    tile = weight[edge, pl.ds(at, 8, stride=ny + 1)]
                    for row in range(1, per_row):
                        lines = weight[edge, pl.ds(at + row, 8, stride=ny + 1)]
                        tile = jnp.where(spots[row], lines, tile)
                    tile = pltpu.roll(tile, turn, 1) * used
                    crossing[slot, edge, pl.ds(half * 16 + part, 8, stride=2)] = tile
        out(slot).start()

    for slot in range(visible.shape[0]):
        out(slot).wait()
    result.wait()


def whole(*shape):
    return jax.ShapeDtypeStruct(shape, F32)


VMEM = pl.BlockSpec(memory_space=pltpu.VMEM)


HBM = pl.BlockSpec(memory_space=pltpu.HBM)


def kernel(body, inputs, outputs, scratch=(), results=VMEM, alias=None, flops=0):
    return pl.pallas_call(
        body,
        in_specs=list(inputs),
        out_specs=[results] * len(outputs),
        out_shape=list(outputs),
        scratch_shapes=list(scratch),
        input_output_aliases=alias or {},
        cost_estimate=pl.CostEstimate(flops=flops, bytes_accessed=flops // 4, transcendentals=0),
        compiler_params=pltpu.CompilerParams(vmem_limit_bytes=32 * 1024 * 1024),
    )


def in_hbm(value):
    return pltpu.with_memory_space_constraint(value, pltpu.HBM)


def swap(value, axis, first):
    count = lax.axis_size(axis)
    pairs = [(k, k + 1) for k in range(first, count - 1, 2)]
    return lax.ppermute(value, axis, pairs + [(b, a) for a, b in pairs])


def body(right_side, screening, active_blocks, visible_bricks):
    nx, ny, nz = right_side.shape
    active = active_blocks.reshape(-1)
    visible = visible_bricks.reshape(-1)
    devices = lax.axis_size("gx") * lax.axis_size("gy")
    slab = whole(nx, ny, nz)
    planes, near, third = nx + 2 * WIDE, nx + 2 * NEAR, nx + 2
    wide, rows = ny + 2 * EDGE, ny + 2 * HEM
    rim = whole(nx * EDGE, nz)
    edges = pltpu.VMEM((2, nx, EDGE, nz), F32)
    far, near_by, mask = kernel(
        pack_kernel,
        (HBM, HBM, HBM),
        (rim, rim, whole(ny, nz)),
        (pltpu.SMEM(active.shape, jnp.int32), edges, edges, pltpu.SemaphoreType.DMA((5,))),
    )(in_hbm(active), in_hbm(right_side), in_hbm(screening))
    far = swap(far, "gy", 1)
    near_by = swap(near_by, "gy", 0)
    straight, corners = (WIDE + NEAR) * ny, 2 * WIDE * EDGE
    side = whole(straight + corners, nz)
    kept = [whole(planes, wide, nz)] + [whole(near, wide, nz)] * 2
    kept += [whole(near, rows + 2 * EDGE, nz), whole(third, rows + 2 * EDGE, nz)]
    kept += [whole(planes, rows, nz)] * 2 + [whole(near, rows, nz)] * 2 + [whole(third + 2, ny, nz)] * 2
    work = (planes, wide + 2 * EDGE, nz)
    arrays = kept[:-2] + [whole(*work)] * 4
    cross, chip, *held = kernel(
        place_kernel, (VMEM,) * 3, [whole(straight + EXTRA, nz), side] + arrays
    )(mask, right_side, screening)
    cross = swap(cross, "gx", 1)
    chip, *held = kernel(
        early_kernel, (VMEM,) * (EARLY + 1), [side] + arrays, alias={k: k for k in range(EARLY + 1)}
    )(chip, *held)
    chip, corner = kernel(widen_kernel, (VMEM,) * 3, (side, whole(corners, nz)), alias={2: 0})(far, near_by, chip)
    chip = swap(chip, "gx", 0)
    corner = swap(corner, "gx", 1)
    tallies = whole(10, 8, nz)
    *held, last_p, last_q, sums = kernel(
        inner_kernel,
        (VMEM,) * (EARLY + 2),
        arrays + kept[-2:] + [tallies],
        (pltpu.VMEM(work, F32),) * 2,
        alias={2 + k: k for k in range(EARLY)},
        flops=INNER,
    )(far, near_by, *held)
    held = [*held[:-4], last_p, last_q, sums]
    for last, messages in ((False, (chip, chip)), (True, (cross, corner))):
        held = kernel(
            functools.partial(side_kernel, last),
            (VMEM,) * (HELD + 3),
            kept + [whole(1, nz) if last else tallies],
            alias={2 + k: k for k in range(HELD)},
            flops=SIDE,
        )(*messages, *held)
    field, _, _, first, second = held[:5]
    devices = lax.axis_size("gx") * lax.axis_size("gy")
    parts = lax.all_to_all(jnp.broadcast_to(held[-1], (devices, 1, nz)), ("gx", "gy"), 0, 0)
    slots = visible.shape[0]
    shape = (slots, 3, BLK**3 // nz, nz)
    indicator, crossing = kernel(
        finish_kernel,
        (HBM,) + (VMEM,) * 4,
        (slab, whole(*shape)),
        (
            pltpu.SMEM(visible.shape, jnp.int32),
            pltpu.VMEM(slab.shape, F32),
            pltpu.VMEM(shape, F32),
            pltpu.VMEM((nx + 1, ny + EDGE, nz), F32),
            pltpu.VMEM((3, nx * (ny + 1), nz), F32),
            pltpu.SemaphoreType.DMA,
            pltpu.SemaphoreType.DMA((slots,)),
            pltpu.SemaphoreType.DMA,
        ),
        results=HBM,
    )(in_hbm(visible), parts.reshape(devices, nz), field, first, second)
    return indicator, crossing.reshape(slots, 1, 3, BLK**3)


def solution(mesh):
    return jax.shard_map(
        body,
        mesh=mesh,
        in_specs=(
            P("gx", "gy", None),
            P("gx", "gy", None),
            P("gx", "gy", None),
            P("gx", "gy", None),
        ),
        out_specs=(P("gx", "gy", None), P("gx", "gy", None, None)),
        check_vma=False,
    )
```

```python
import functools

import jax
import jax.numpy as jnp
from jax import lax
from jax.experimental import pallas as pl
from jax.experimental.pallas import tpu as pltpu
from jax.sharding import PartitionSpec as P

BLK = 16
WIDE = 5
NEAR = 3
HEM = 4
EDGE = 8
SHARP = 4.0
SCALE = 1.0 / 86400.0
SHIFT = 2.25
LOW, HIGH = 0.5, 7.0
SUMS = 16
EXTRA, INNER, SIDE = 96, 0, 0
HELD = 11
F32 = jnp.float32


def mass(mid, one, two):
    return 66.0 * mid + (26.0 * one + two)


def stiff(mid, one, two):
    return 6.0 * mid - (2.0 * one + two)


def block_mask(active, slots, rows, columns):
    y = lax.broadcasted_iota(jnp.int32, (rows, columns), 0)
    z = lax.broadcasted_iota(jnp.int32, (rows, columns), 1)
    number = (y // BLK) * (columns // BLK) + z // BLK
    mask = jnp.zeros((rows, columns), F32)
    for slot in range(slots):
        mask = jnp.where(number == active[slot], 1.0, mask)
    return mask


def on_odd():
    return lax.rem(lax.axis_index("gx"), 2)


def odd_on(axis):
    return lax.rem(lax.axis_index(axis), 2)


def pack_kernel(active_hbm, right_hbm, screen_hbm, far, near, mask_out, active, right, screen, sems):
    nx, ny, nz = right_hbm.shape
    copies = [pltpu.make_async_copy(active_hbm, active, sems.at[0])]
    for k, (source, target) in enumerate(((right_hbm, right), (screen_hbm, screen))):
        for high in range(2):
            rows = pl.ds(high * (ny - EDGE), EDGE)
            copies.append(pltpu.make_async_copy(source.at[:, rows], target.at[high], sems.at[1 + 2 * k + high]))
    for copy in copies:
        copy.start()
    copies[0].wait()
    mask = block_mask(active, active.shape[0], ny, nz)
    mask_out[...] = mask
    row = lax.broadcasted_iota(jnp.int32, (EDGE, nz), 0)
    for copy in copies[1:]:
        copy.wait()

    def write(high_out, low_out):
        for x in range(nx):
            rows = pl.ds(x * EDGE, EDGE)
            low_out[rows] = jnp.where(row < WIDE, right[0, x], pltpu.roll(screen[0, x], WIDE, 0)) * mask[:EDGE]
            beside = pltpu.roll(screen[1, x] * mask[ny - EDGE :], NEAR, 0)
            high_out[rows] = jnp.where(row >= NEAR, right[1, x] * mask[ny - EDGE :], beside)

    odd = odd_on("gy")
    pl.when(odd == 1)(functools.partial(write, far, near))
    pl.when(odd == 0)(functools.partial(write, near, far))


def place_kernel(mask_in, right, screen, field, weight, cross, chip):
    nx, ny, nz = right.shape
    mask = mask_in[...]
    own = pl.ds(EDGE, ny)
    for x in range(nx):
        field[WIDE + x, own] = right[x] * mask
        weight[x, own] = screen[x] * mask
    odd = odd_on("gx")
    for target, high in ((cross, odd), (chip, 1 - odd)):
        for x in range(WIDE):
            target[x * ny : (x + 1) * ny] = field[WIDE + high * (nx - WIDE) + x, own]
        for x in range(NEAR):
            row = (WIDE + x) * ny
            target[row : row + ny] = weight[high * (nx - NEAR) + x, own]


def widen_kernel(far, near, chip_in, chip, corner):
    nx = far.shape[0] // EDGE
    base = chip.shape[0] - corner.shape[0]
    odd = odd_on("gx")

    def fill(low, high):
        for target, start, side in ((corner, 0, odd), (chip, base, 1 - odd)):
            for x in range(WIDE):
                tile = pl.ds((side * (nx - WIDE) + x) * EDGE, EDGE)
                row = start + 2 * x * EDGE
                target[row : row + EDGE] = low[tile]
                target[row + EDGE : row + 2 * EDGE] = high[tile]

    by_y(fill, far, near)


def by_y(action, far, near):
    odd = odd_on("gy")
    pl.when(odd == 1)(functools.partial(action, near, far))
    pl.when(odd == 0)(functools.partial(action, far, near))


def near_z(value):
    lane = lax.broadcasted_iota(jnp.int32, value.shape, 1)
    last = value.shape[1]

    def shifted(step):
        before = jnp.where(lane >= step, pltpu.roll(value, step, 1), 0.0)
        after = jnp.where(lane < last - step, pltpu.roll(value, last - step, 1), 0.0)
        return before + after

    return shifted(1), shifted(2)


def set_beside(field, x, keep, shifted, weight_x, tile, high):
    start = field.shape[1] - EDGE if high else 0
    field[x, start : start + EDGE] = tile
    if weight_x is not None:
        set_weight(keep, shifted, weight_x, pl.ds(start, EDGE), pltpu.roll(tile, NEAR if high else WIDE, 0))


def set_weight(keep, shifted, at, rows, weight):
    on = weight > 0.0
    keep[at, rows] = jnp.where(on, SCALE, 0.0)
    shifted[at, rows] = jnp.where(on, weight - SHIFT, 0.0)


def near_y(source, x, row, top, end):
    def part(step):
        return source[x, pl.ds(row + step, 8)]

    below, above = part(-2), part(2)
    place = lax.broadcasted_iota(jnp.int32, below.shape, 0)
    if top:
        below = jnp.where(place == 0, 0.0, jnp.where(place == 1, 2.0 * below, below))
    if end:
        above = jnp.where(place == 7, 0.0, jnp.where(place == 6, 2.0 * above, above))
    return part(0), part(-1) + part(1), below + above


def along_yz(source, x, row, top=False, end=False):
    here, one, two = near_y(source, x, row, top, end)
    heavy, stretched = mass(here, one, two), stiff(here, one, two)
    heavy_near, stretched_near = near_z(heavy), near_z(stretched)
    return mass(heavy, *heavy_near), stiff(heavy, *heavy_near) + mass(stretched, *stretched_near)


def across(window):
    p, q = zip(*window)
    return mass(q[2], q[1] + q[3], q[0] + q[4]) + stiff(p[2], p[1] + p[3], p[0] + p[4])


def power(target, source, row, keep, shifted, skip, x, group, window):
    rows, at = pl.ds(EDGE + 8 * group, 8), pl.ds(EDGE - HEM + 8 * group, 8)
    center = source[x + 2, pl.ds(row + 8 * group, 8)]
    target[x, rows] = keep[x + skip, at] * across(window) + shifted[x + skip, at] * center


def advance(target, source, row, keep, shifted, skip, yp, yq, count, first):
    for group in range(target.shape[1] // 8 - 2):
        rows = pl.ds(8 * group, 8)
        window = []
        for x in range(first, first + count):
            p, q = along_yz(source, x, row + 8 * group)
            yp[x, rows] = p
            yq[x, rows] = q
            window = window[-4:] + [(p, q)]
            if len(window) == 5:
                power(target, source, row, keep, shifted, skip, x - 4, group, window)


def advance_side(target, source, row, keep, shifted, skip, yp, yq, high):
    groups = target.shape[1] // 8 - 2
    base = high * (target.shape[0] - WIDE)
    start = high * (source.shape[0] - WIDE)
    for group in range(groups):
        rows = pl.ds(8 * group, 8)
        for k in range(WIDE):
            p, q = along_yz(source, start + k, row + 8 * group)
            yp[start + k, rows] = p
            yq[start + k, rows] = q
    for group in range(groups):
        rows = pl.ds(8 * group, 8)
        window = [(yp[base + k, rows], yq[base + k, rows]) for k in range(WIDE + 4)]
        for k in range(WIDE):
            power(target, source, row, keep, shifted, skip, base + k, group, window[k : k + 5])


def last_rows(source, yp, yq, count, first):
    groups = yp.shape[1] // 8
    for group in range(groups):
        rows = pl.ds(8 * group, 8)
        for k in range(count):
            p, q = along_yz(source, first + k, EDGE + HEM + 8 * group, group == 0, group == groups - 1)
            yp[first + 1 + k, rows] = p
            yq[first + 1 + k, rows] = q


def fold(value):
    return jnp.sum(value.reshape(-1, 8, value.shape[1]), axis=0)


def add_sums(totals, arrays, count, first_x):
    field, keep, shifted, first, second, yp, yq = arrays
    totals = list(totals)
    for group in range(yp.shape[1] // 8):
        rows = pl.ds(8 * group, 8)
        mid, own = pl.ds(EDGE + 8 * group, 8), pl.ds(EDGE + HEM + 8 * group, 8)
        window = [(yp[first_x + k, rows], yq[first_x + k, rows]) for k in range(count + 4)]
        for k in range(count):
            x = first_x + k
            v0 = field[x + WIDE, mid]
            v1 = first[x + NEAR, own]
            v2 = second[x + 1, own]
            form = v2 * (SCALE * across(window[k : k + 5]) + shifted[x + NEAR, mid] * v2)
            on = jnp.where(keep[x + NEAR, mid] > 0.0, 1.0, 0.0)
            new = (v0 * v0, v0 * v1, v1 * v1, v1 * v2, v2 * v2, form, v0, v1, v2, on)
            totals = [total + value for total, value in zip(totals, new)]
    return totals


def inner_kernel(
    far, near, field_in, weight, field, keep, shifted, first, second, yp1, yq1, yp2, yq2, yp3, yq3, sums
):
    nx, wide, nz = weight.shape
    ny = wide - 2 * EDGE

    def fill(low, high):
        for x in range(nx):
            set_beside(field, WIDE + x, keep, shifted, NEAR + x, low[EDGE * x : EDGE * (x + 1)], False)
            set_beside(field, WIDE + x, keep, shifted, NEAR + x, high[EDGE * x : EDGE * (x + 1)], True)

    by_y(fill, far, near)
    own = pl.ds(EDGE, ny)
    for x in range(nx):
        set_weight(keep, shifted, NEAR + x, own, weight[x, own])
    advance(first, field, EDGE - HEM, keep, shifted, 0, yp1, yq1, nx, WIDE)
    advance(second, first, EDGE, keep, shifted, 2, yp2, yq2, nx - 4, WIDE)
    last_rows(second, yp3, yq3, nx - 8, WIDE)
    arrays = (field, keep, shifted, first, second, yp3, yq3)
    totals = add_sums((jnp.zeros((8, nz), F32),) * 10, arrays, nx - 12, WIDE + 1)
    for place, total in enumerate(totals):
        sums[place] = total


def side_kernel(last, message, corner, *refs):
    sums_in = refs[HELD]
    field, keep, shifted, first, second, yp1, yq1, yp2, yq2, yp3, yq3, sums = refs[HELD + 1 :]
    planes, wide, nz = field.shape
    nx, ny = planes - 2 * WIDE, wide - 2 * EDGE
    odd = odd_on("gx")
    high = odd if last else 1 - odd
    own = pl.ds(EDGE, ny)
    base = corner.shape[0] - 2 * WIDE * EDGE
    for x in range(WIDE):
        plane = high * (nx + WIDE) + x
        field[plane, own] = message[x * ny : (x + 1) * ny]
        for up in range(2):
            row = base + (2 * x + up) * EDGE
            set_beside(field, plane, keep, shifted, None, corner[row : row + EDGE], up == 1)
    for x in range(NEAR):
        plane = high * (nx + NEAR) + x
        row = (WIDE + x) * ny
        set_weight(keep, shifted, plane, own, message[row : row + ny])
        place = base + (x + (1 - high) * (WIDE - NEAR)) * 2 * EDGE
        for up in range(2):
            tile = corner[pl.ds(place + up * EDGE, EDGE)]
            rows = pl.ds(up * (wide - EDGE), EDGE)
            set_weight(keep, shifted, plane, rows, pltpu.roll(tile, NEAR if up else WIDE, 0))
    advance_side(first, field, EDGE - HEM, keep, shifted, 0, yp1, yq1, high)
    advance_side(second, first, EDGE, keep, shifted, 2, yp2, yq2, high)
    last_rows(second, yp3, yq3, WIDE, high * (nx + 2 - WIDE))
    none = jnp.zeros((ny, nz), F32)
    yp3[high * (nx + 3)] = none
    yq3[high * (nx + 3)] = none
    totals = tuple(sums_in[place] for place in range(10))
    arrays = (field, keep, shifted, first, second, yp3, yq3)
    totals = list(add_sums(totals, arrays, WIDE + 1, high * (nx - WIDE - 1)))
    own = pl.ds(EDGE + HEM, ny)
    beside, edge, next_edge = 1 + high * (nx + 1), 2 + high * (nx - 1), 3 + high * (nx - 3)
    give = 13.0 * yq3[edge] - yp3[edge] + (yq3[next_edge] - yp3[next_edge])
    take = 13.0 * yq3[beside] - yp3[beside]
    totals[5] += SCALE * fold(second[beside - 1, own] * give - second[edge - 1, own] * take)
    if not last:
        for place, total in enumerate(totals):
            sums[place] = total
        return
    row = lax.broadcasted_iota(jnp.int32, (SUMS, nz), 0)
    lane = lax.broadcasted_iota(jnp.int32, (SUMS, nz), 1)
    lines = jnp.zeros((SUMS, nz), F32)
    for place, total in enumerate(totals):
        lines = jnp.where(row == place, jnp.sum(total, axis=0, keepdims=True), lines)
    pieces, rest = [], lines
    for _ in range(3):
        pieces.append(rest.astype(jnp.bfloat16))
        rest = rest - pieces[-1].astype(F32)
    ones = jnp.ones((nz, nz), jnp.bfloat16)
    whole_sums = jnp.dot(jnp.concatenate(pieces, axis=0), ones, preferred_element_type=F32)
    top, rest = two_sum(whole_sums[:SUMS], whole_sums[SUMS : 2 * SUMS])
    pair = two_sum(top, rest + whole_sums[2 * SUMS :])
    spot = jnp.where(lane == row, pair[0], jnp.where(lane == row + SUMS, pair[1], 0.0))
    sums[...] = jnp.sum(spot, axis=0, keepdims=True)


def two_sum(a, b):
    total = a + b
    part = total - a
    return total, (a - (total - part)) + (b - part)


def pair_add(a, b):
    total, rest = two_sum(a[0], b[0])
    return total, rest + (a[1] + b[1])


def halves(a):
    wide = 4097.0 * a
    top = wide - (wide - a)
    return top, a - top


def pair_mul(a, b):
    product = a[0] * b[0]
    a_top, a_rest = halves(a[0])
    b_top, b_rest = halves(b[0])
    rest = ((a_top * b_top - product) + a_top * b_rest + a_rest * b_top) + a_rest * b_rest
    rest = rest + (a[0] * b[1] + a[1] * b[0])
    total = product + rest
    return total, rest - (total - product)


def pair_sub(a, b):
    total, rest = two_sum(a[0], -b[0])
    rest = rest + (a[1] - b[1])
    out = total + rest
    return out, rest - (out - total)


def ratio(over, under, low, high):
    good = under > 0.0
    value = jnp.where(good, over / jnp.where(good, under, 1.0), 0.5 * (low + high))
    return jnp.minimum(jnp.maximum(value, low), high)


def coefficients(total):
    scale = 1.0 / total[0][0]
    zero = jnp.zeros_like(scale)
    g = [pair_mul(item, (scale, zero)) for item in total[:6]]
    shift = (jnp.full_like(scale, SHIFT), zero)
    h = [pair_add(g[k + 1], pair_mul(g[k], shift)) for k in range(5)]

    def minor(a, b, c, d):
        return pair_sub(pair_mul(a, b), pair_mul(c, d))

    s11 = minor(h[2], h[0], h[1], h[1])
    s12 = minor(h[3], h[0], h[1], h[2])
    s22 = minor(h[4], h[0], h[2], h[2])
    y1 = minor(g[1], h[0], h[1], g[0])
    y2 = minor(g[2], h[0], h[2], g[0])
    last = minor(s22, s11, s12, s12)
    side = minor(y2, s11, s12, y1)
    alpha = g[0][0] / h[0][0]
    l10 = h[1][0] / h[0][0]
    l20 = h[2][0] / h[0][0]
    l21 = ratio(s12[0], s11[0], l10 + (LOW - SHIFT), l10 + (HIGH - SHIFT))
    gamma1 = ratio(y1[0], s11[0], -alpha / LOW, -alpha / HIGH)
    gamma2 = ratio(side[0], last[0], -gamma1 / HIGH, -gamma1 / LOW)
    c1 = gamma1 - gamma2 * l21
    return alpha - c1 * l10 - gamma2 * l20, c1, gamma2


def sigmoid(value):
    return 1.0 / (1.0 + jnp.exp(-SHARP * value))


def finish_kernel(
    visible_hbm, parts, field, first, second, indicator_hbm, crossing_hbm,
    visible, indicator, crossing, level, weight, sem, slot_sems, result_sem,
):
    nx, ny, nz = indicator.shape
    copy = pltpu.make_async_copy(visible_hbm, visible, sem)
    copy.start()
    devices = parts.shape[0]
    tiles = [parts[pl.ds(8 * k, 8)] for k in range(devices // 8)]
    pairs = [(tile, pltpu.roll(tile, nz - SUMS, 1)) for tile in tiles]
    while len(pairs) > 1:
        pairs = [pair_add(a, b) for a, b in zip(pairs[::2], pairs[1::2])]
    total = pairs[0]
    for step in (4, 2, 1):
        total = pair_add(total, (pltpu.roll(total[0], step, 0), pltpu.roll(total[1], step, 0)))

    def spread(value, k):
        return jnp.broadcast_to(value[0:1, k : k + 1], (1, nz))

    item = [(spread(total[0], k), spread(total[1], k)) for k in range(10)]
    c0, c1, c2 = coefficients(item)
    over = c0 * (item[6][0] + item[6][1]) + c1 * (item[7][0] + item[7][1]) + c2 * (item[8][0] + item[8][1])
    iso = over / item[9][0]

    def set_level(x):
        v0 = field[x + WIDE, pl.ds(EDGE, ny + EDGE)]
        v1 = first[x + NEAR, pl.ds(EDGE + HEM, ny + HEM)]
        v2 = second[x + 1, pl.ds(EDGE + HEM, ny + HEM)]
        value = c0 * v0[: ny + HEM] + c1 * v1 + c2 * v2
        level[x, pl.ds(0, ny + HEM)] = sigmoid(value - iso)
        return value

    @pl.loop(0, nx, unroll=4)
    def _(x):
        indicator[x] = set_level(x)[:ny]

    set_level(nx)
    result = pltpu.make_async_copy(indicator, indicator_hbm, result_sem)
    result.start()
    outside = sigmoid(-iso)
    lane = lax.broadcasted_iota(jnp.int32, (ny, nz), 1)

    @pl.loop(0, nx, unroll=4)
    def _(x):
        here = level[x, pl.ds(0, ny)]
        above = jnp.where(lane < nz - 1, pltpu.roll(here, nz - 1, 1), outside)
        for edge, there in enumerate((level[x + 1, pl.ds(0, ny)], level[x, pl.ds(1, ny)], above)):
            value = here * (1.0 - there) + (1.0 - here) * there
            for row in range(0, ny, 8):
                turned = pltpu.roll(value[row : row + 8], 0, 1, stride=BLK, stride_axis=0)
                weight[edge, pl.ds(x * (ny + 1) + row, 8)] = turned

    chunk = lax.broadcasted_iota(jnp.int32, (8, nz), 1) // BLK
    bricks_z = nz // BLK
    per_row = nz // BLK

    copy.wait()

    def out(slot):
        return pltpu.make_async_copy(crossing.at[slot], crossing_hbm.at[slot], slot_sems.at[slot])

    @pl.loop(0, visible.shape[0], unroll=2)
    def _(slot):
        number = visible[slot]
        safe = jnp.maximum(number, 0)
        begin = (safe // bricks_z) * BLK
        column = safe % bricks_z
        used = jnp.where(number >= 0, 1.0, 0.0)
        spots = [chunk == lax.rem(column + row, per_row) for row in range(per_row)]
        turn = lax.rem(nz - column * BLK, nz)
        for edge in range(3):
            for half in range(2):
                for part in range(BLK // per_row):
                    at = half * 8 * (ny + 1) + begin + part * per_row
                    tile = weight[edge, pl.ds(at, 8, stride=ny + 1)]
                    for row in range(1, per_row):
                        lines = weight[edge, pl.ds(at + row, 8, stride=ny + 1)]
                        tile = jnp.where(spots[row], lines, tile)
                    tile = pltpu.roll(tile, turn, 1) * used
                    crossing[slot, edge, pl.ds(half * 16 + part, 8, stride=2)] = tile
        out(slot).start()

    for slot in range(visible.shape[0]):
        out(slot).wait()
    result.wait()


def whole(*shape):
    return jax.ShapeDtypeStruct(shape, F32)


VMEM = pl.BlockSpec(memory_space=pltpu.VMEM)


HBM = pl.BlockSpec(memory_space=pltpu.HBM)


def kernel(body, inputs, outputs, scratch=(), results=VMEM, alias=None, flops=0):
    return pl.pallas_call(
        body,
        in_specs=list(inputs),
        out_specs=[results] * len(outputs),
        out_shape=list(outputs),
        scratch_shapes=list(scratch),
        input_output_aliases=alias or {},
        cost_estimate=pl.CostEstimate(flops=flops, bytes_accessed=flops // 4, transcendentals=0),
        compiler_params=pltpu.CompilerParams(vmem_limit_bytes=32 * 1024 * 1024),
    )


def in_hbm(value):
    return pltpu.with_memory_space_constraint(value, pltpu.HBM)


def swap(value, axis, first):
    count = lax.axis_size(axis)
    pairs = [(k, k + 1) for k in range(first, count - 1, 2)]
    return lax.ppermute(value, axis, pairs + [(b, a) for a, b in pairs])


def body(right_side, screening, active_blocks, visible_bricks):
    nx, ny, nz = right_side.shape
    active = active_blocks.reshape(-1)
    visible = visible_bricks.reshape(-1)
    devices = lax.axis_size("gx") * lax.axis_size("gy")
    slab = whole(nx, ny, nz)
    planes, near, third = nx + 2 * WIDE, nx + 2 * NEAR, nx + 2
    wide, rows = ny + 2 * EDGE, ny + 2 * HEM
    rim = whole(nx * EDGE, nz)
    edges = pltpu.VMEM((2, nx, EDGE, nz), F32)
    far, near_by, mask = kernel(
        pack_kernel,
        (HBM, HBM, HBM),
        (rim, rim, whole(ny, nz)),
        (pltpu.SMEM(active.shape, jnp.int32), edges, edges, pltpu.SemaphoreType.DMA((5,))),
    )(in_hbm(active), in_hbm(right_side), in_hbm(screening))
    far = swap(far, "gy", 1)
    near_by = swap(near_by, "gy", 0)
    straight, corners = (WIDE + NEAR) * ny, 2 * WIDE * EDGE
    side = whole(straight + corners, nz)
    field, weight, cross, chip = kernel(
        place_kernel,
        (VMEM,) * 3,
        (whole(planes, wide, nz), whole(nx, wide, nz), whole(straight + EXTRA, nz), side),
    )(mask, right_side, screening)
    cross = swap(cross, "gx", 1)
    chip, corner = kernel(widen_kernel, (VMEM,) * 3, (side, whole(corners, nz)), alias={2: 0})(far, near_by, chip)
    chip = swap(chip, "gx", 0)
    corner = swap(corner, "gx", 1)
    kept = [whole(planes, wide, nz)] + [whole(near, wide, nz)] * 2
    kept += [whole(near, rows + 2 * EDGE, nz), whole(third, rows + 2 * EDGE, nz)]
    kept += [whole(planes, rows, nz)] * 2 + [whole(near, rows, nz)] * 2 + [whole(third + 2, ny, nz)] * 2
    tallies = whole(10, 8, nz)
    held = kernel(inner_kernel, (VMEM,) * 4, kept + [tallies], alias={2: 0}, flops=INNER)(
        far, near_by, field, weight
    )
    for last, messages in ((False, (chip, chip)), (True, (cross, corner))):
        held = kernel(
            functools.partial(side_kernel, last),
            (VMEM,) * (HELD + 3),
            kept + [whole(1, nz) if last else tallies],
            alias={2 + k: k for k in range(HELD)},
            flops=SIDE,
        )(*messages, *held)
    field, _, _, first, second = held[:5]
    devices = lax.axis_size("gx") * lax.axis_size("gy")
    parts = lax.all_to_all(jnp.broadcast_to(held[-1], (devices, 1, nz)), ("gx", "gy"), 0, 0)
    slots = visible.shape[0]
    shape = (slots, 3, BLK**3 // nz, nz)
    indicator, crossing = kernel(
        finish_kernel,
        (HBM,) + (VMEM,) * 4,
        (slab, whole(*shape)),
        (
            pltpu.SMEM(visible.shape, jnp.int32),
            pltpu.VMEM(slab.shape, F32),
            pltpu.VMEM(shape, F32),
            pltpu.VMEM((nx + 1, ny + EDGE, nz), F32),
            pltpu.VMEM((3, nx * (ny + 1), nz), F32),
            pltpu.SemaphoreType.DMA,
            pltpu.SemaphoreType.DMA((slots,)),
            pltpu.SemaphoreType.DMA,
        ),
        results=HBM,
    )(in_hbm(visible), parts.reshape(devices, nz), field, first, second)
    return indicator, crossing.reshape(slots, 1, 3, BLK**3)


def solution(mesh):
    return jax.shard_map(
        body,
        mesh=mesh,
        in_specs=(
            P("gx", "gy", None),
            P("gx", "gy", None),
            P("gx", "gy", None),
            P("gx", "gy", None),
        ),
        out_specs=(P("gx", "gy", None), P("gx", "gy", None, None)),
        check_vma=False,
    )
```

```python
import functools

import jax
import jax.numpy as jnp
from jax import lax
from jax.experimental import pallas as pl
from jax.experimental.pallas import tpu as pltpu
from jax.sharding import PartitionSpec as P

BLK = 16
WIDE = 5
NEAR = 3
HEM = 4
EDGE = 8
SHARP = 4.0
SCALE = 1.0 / 86400.0
SHIFT = 2.25
LOW, HIGH = 0.5, 7.0
SUMS = 16
EXTRA, INNER, SIDE = 96, 0, 0
HELD = 11
F32 = jnp.float32


def mass(mid, one, two):
    return 66.0 * mid + (26.0 * one + two)


def stiff(mid, one, two):
    return 6.0 * mid - (2.0 * one + two)


def block_mask(active, slots, rows, columns):
    y = lax.broadcasted_iota(jnp.int32, (rows, columns), 0)
    z = lax.broadcasted_iota(jnp.int32, (rows, columns), 1)
    number = (y // BLK) * (columns // BLK) + z // BLK
    mask = jnp.zeros((rows, columns), F32)
    for slot in range(slots):
        mask = jnp.where(number == active[slot], 1.0, mask)
    return mask


def on_odd():
    return lax.rem(lax.axis_index("gx"), 2)


def odd_on(axis):
    return lax.rem(lax.axis_index(axis), 2)


def pack_kernel(active_hbm, right_hbm, screen_hbm, far, near, mask_out, active, right, screen, sems):
    nx, ny, nz = right_hbm.shape
    copies = [pltpu.make_async_copy(active_hbm, active, sems.at[0])]
    for k, (source, target) in enumerate(((right_hbm, right), (screen_hbm, screen))):
        for high in range(2):
            rows = pl.ds(high * (ny - EDGE), EDGE)
            copies.append(pltpu.make_async_copy(source.at[:, rows], target.at[high], sems.at[1 + 2 * k + high]))
    for copy in copies:
        copy.start()
    copies[0].wait()
    mask = block_mask(active, active.shape[0], ny, nz)
    mask_out[...] = mask
    row = lax.broadcasted_iota(jnp.int32, (EDGE, nz), 0)
    for copy in copies[1:]:
        copy.wait()

    def write(high_out, low_out):
        for x in range(nx):
            rows = pl.ds(x * EDGE, EDGE)
            low_out[rows] = jnp.where(row < WIDE, right[0, x], pltpu.roll(screen[0, x], WIDE, 0)) * mask[:EDGE]
            beside = pltpu.roll(screen[1, x] * mask[ny - EDGE :], NEAR, 0)
            high_out[rows] = jnp.where(row >= NEAR, right[1, x] * mask[ny - EDGE :], beside)

    odd = odd_on("gy")
    pl.when(odd == 1)(functools.partial(write, far, near))
    pl.when(odd == 0)(functools.partial(write, near, far))


def place_kernel(mask_in, right, screen, field, weight, cross, chip):
    nx, ny, nz = right.shape
    mask = mask_in[...]
    own = pl.ds(EDGE, ny)
    for x in range(nx):
        field[WIDE + x, own] = right[x] * mask
        weight[x, own] = screen[x] * mask
    odd = odd_on("gx")
    for target, high in ((cross, odd), (chip, 1 - odd)):
        for x in range(WIDE):
            target[x * ny : (x + 1) * ny] = field[WIDE + high * (nx - WIDE) + x, own]
        for x in range(NEAR):
            row = (WIDE + x) * ny
            target[row : row + ny] = weight[high * (nx - NEAR) + x, own]


def widen_kernel(far, near, chip_in, chip, corner):
    nx = far.shape[0] // EDGE
    base = chip.shape[0] - corner.shape[0]
    odd = odd_on("gx")

    def fill(low, high):
        for target, start, side in ((corner, 0, odd), (chip, base, 1 - odd)):
            for x in range(WIDE):
                tile = pl.ds((side * (nx - WIDE) + x) * EDGE, EDGE)
                row = start + 2 * x * EDGE
                target[row : row + EDGE] = low[tile]
                target[row + EDGE : row + 2 * EDGE] = high[tile]

    by_y(fill, far, near)


def by_y(action, far, near):
    odd = odd_on("gy")
    pl.when(odd == 1)(functools.partial(action, near, far))
    pl.when(odd == 0)(functools.partial(action, far, near))


def near_z(value):
    lane = lax.broadcasted_iota(jnp.int32, value.shape, 1)
    last = value.shape[1]

    def shifted(step):
        before = jnp.where(lane >= step, pltpu.roll(value, step, 1), 0.0)
        after = jnp.where(lane < last - step, pltpu.roll(value, last - step, 1), 0.0)
        return before + after

    return shifted(1), shifted(2)


def set_beside(field, x, keep, shifted, weight_x, tile, high):
    start = field.shape[1] - EDGE if high else 0
    field[x, start : start + EDGE] = tile
    if weight_x is not None:
        set_weight(keep, shifted, weight_x, pl.ds(start, EDGE), pltpu.roll(tile, NEAR if high else WIDE, 0))


def set_weight(keep, shifted, at, rows, weight):
    on = weight > 0.0
    keep[at, rows] = jnp.where(on, SCALE, 0.0)
    shifted[at, rows] = jnp.where(on, weight - SHIFT, 0.0)


def near_y(source, x, row, top, end):
    def part(step):
        return source[x, pl.ds(row + step, 8)]

    below, above = part(-2), part(2)
    place = lax.broadcasted_iota(jnp.int32, below.shape, 0)
    if top:
        below = jnp.where(place == 0, 0.0, jnp.where(place == 1, 2.0 * below, below))
    if end:
        above = jnp.where(place == 7, 0.0, jnp.where(place == 6, 2.0 * above, above))
    return part(0), part(-1) + part(1), below + above


def along_yz(source, x, row, top=False, end=False):
    here, one, two = near_y(source, x, row, top, end)
    heavy, stretched = mass(here, one, two), stiff(here, one, two)
    heavy_near, stretched_near = near_z(heavy), near_z(stretched)
    return mass(heavy, *heavy_near), stiff(heavy, *heavy_near) + mass(stretched, *stretched_near)


def across(window):
    p, q = zip(*window)
    return mass(q[2], q[1] + q[3], q[0] + q[4]) + stiff(p[2], p[1] + p[3], p[0] + p[4])


def power(target, source, row, keep, shifted, skip, x, group, window):
    rows, at = pl.ds(EDGE + 8 * group, 8), pl.ds(EDGE - HEM + 8 * group, 8)
    center = source[x + 2, pl.ds(row + 8 * group, 8)]
    target[x, rows] = keep[x + skip, at] * across(window) + shifted[x + skip, at] * center


def advance(target, source, row, keep, shifted, skip, yp, yq, count, first):
    for group in range(target.shape[1] // 8 - 2):
        rows = pl.ds(8 * group, 8)
        window = []
        for x in range(first, first + count):
            p, q = along_yz(source, x, row + 8 * group)
            yp[x, rows] = p
            yq[x, rows] = q
            window = window[-4:] + [(p, q)]
            if len(window) == 5:
                power(target, source, row, keep, shifted, skip, x - 4, group, window)


def advance_side(target, source, row, keep, shifted, skip, yp, yq, high):
    groups = target.shape[1] // 8 - 2
    base = high * (target.shape[0] - WIDE)
    start = high * (source.shape[0] - WIDE)
    for group in range(groups):
        rows = pl.ds(8 * group, 8)
        for k in range(WIDE):
            p, q = along_yz(source, start + k, row + 8 * group)
            yp[start + k, rows] = p
            yq[start + k, rows] = q
    for group in range(groups):
        rows = pl.ds(8 * group, 8)
        window = [(yp[base + k, rows], yq[base + k, rows]) for k in range(WIDE + 4)]
        for k in range(WIDE):
            power(target, source, row, keep, shifted, skip, base + k, group, window[k : k + 5])


def last_rows(source, yp, yq, count, first):
    groups = yp.shape[1] // 8
    for group in range(groups):
        rows = pl.ds(8 * group, 8)
        for k in range(count):
            p, q = along_yz(source, first + k, EDGE + HEM + 8 * group, group == 0, group == groups - 1)
            yp[first + 1 + k, rows] = p
            yq[first + 1 + k, rows] = q


def fold(value):
    return jnp.sum(value.reshape(-1, 8, value.shape[1]), axis=0)


def add_sums(totals, arrays, count, first_x):
    field, keep, shifted, first, second, yp, yq = arrays
    totals = list(totals)
    for group in range(yp.shape[1] // 8):
        rows = pl.ds(8 * group, 8)
        mid, own = pl.ds(EDGE + 8 * group, 8), pl.ds(EDGE + HEM + 8 * group, 8)
        window = [(yp[first_x + k, rows], yq[first_x + k, rows]) for k in range(count + 4)]
        for k in range(count):
            x = first_x + k
            v0 = field[x + WIDE, mid]
            v1 = first[x + NEAR, own]
            v2 = second[x + 1, own]
            form = v2 * (SCALE * across(window[k : k + 5]) + shifted[x + NEAR, mid] * v2)
            on = jnp.where(keep[x + NEAR, mid] > 0.0, 1.0, 0.0)
            new = (v0 * v0, v0 * v1, v1 * v1, v1 * v2, v2 * v2, form, v0, v1, v2, on)
            totals = [total + value for total, value in zip(totals, new)]
    return totals


def inner_kernel(
    far, near, field_in, weight, field, keep, shifted, first, second, yp1, yq1, yp2, yq2, yp3, yq3, sums
):
    nx, wide, nz = weight.shape
    ny = wide - 2 * EDGE

    def fill(low, high):
        for x in range(nx):
            set_beside(field, WIDE + x, keep, shifted, NEAR + x, low[EDGE * x : EDGE * (x + 1)], False)
            set_beside(field, WIDE + x, keep, shifted, NEAR + x, high[EDGE * x : EDGE * (x + 1)], True)

    by_y(fill, far, near)
    own = pl.ds(EDGE, ny)
    for x in range(nx):
        set_weight(keep, shifted, NEAR + x, own, weight[x, own])
    advance(first, field, EDGE - HEM, keep, shifted, 0, yp1, yq1, nx, WIDE)
    advance(second, first, EDGE, keep, shifted, 2, yp2, yq2, nx - 4, WIDE)
    last_rows(second, yp3, yq3, nx - 8, WIDE)
    arrays = (field, keep, shifted, first, second, yp3, yq3)
    totals = add_sums((jnp.zeros((8, nz), F32),) * 10, arrays, nx - 12, WIDE + 1)
    for place, total in enumerate(totals):
        sums[place] = total


def side_kernel(last, message, corner, *refs):
    sums_in = refs[HELD]
    field, keep, shifted, first, second, yp1, yq1, yp2, yq2, yp3, yq3, sums = refs[HELD + 1 :]
    planes, wide, nz = field.shape
    nx, ny = planes - 2 * WIDE, wide - 2 * EDGE
    odd = odd_on("gx")
    high = odd if last else 1 - odd
    own = pl.ds(EDGE, ny)
    base = corner.shape[0] - 2 * WIDE * EDGE
    for x in range(WIDE):
        plane = high * (nx + WIDE) + x
        field[plane, own] = message[x * ny : (x + 1) * ny]
        for up in range(2):
            row = base + (2 * x + up) * EDGE
            set_beside(field, plane, keep, shifted, None, corner[row : row + EDGE], up == 1)
    for x in range(NEAR):
        plane = high * (nx + NEAR) + x
        row = (WIDE + x) * ny
        set_weight(keep, shifted, plane, own, message[row : row + ny])
        place = base + (x + (1 - high) * (WIDE - NEAR)) * 2 * EDGE
        for up in range(2):
            tile = corner[pl.ds(place + up * EDGE, EDGE)]
            rows = pl.ds(up * (wide - EDGE), EDGE)
            set_weight(keep, shifted, plane, rows, pltpu.roll(tile, NEAR if up else WIDE, 0))
    advance_side(first, field, EDGE - HEM, keep, shifted, 0, yp1, yq1, high)
    advance_side(second, first, EDGE, keep, shifted, 2, yp2, yq2, high)
    last_rows(second, yp3, yq3, WIDE, high * (nx + 2 - WIDE))
    none = jnp.zeros((ny, nz), F32)
    yp3[high * (nx + 3)] = none
    yq3[high * (nx + 3)] = none
    totals = tuple(sums_in[place] for place in range(10))
    arrays = (field, keep, shifted, first, second, yp3, yq3)
    totals = list(add_sums(totals, arrays, WIDE + 1, high * (nx - WIDE - 1)))
    own = pl.ds(EDGE + HEM, ny)
    beside, edge, next_edge = 1 + high * (nx + 1), 2 + high * (nx - 1), 3 + high * (nx - 3)
    give = 13.0 * yq3[edge] - yp3[edge] + (yq3[next_edge] - yp3[next_edge])
    take = 13.0 * yq3[beside] - yp3[beside]
    totals[5] += SCALE * fold(second[beside - 1, own] * give - second[edge - 1, own] * take)
    if not last:
        for place, total in enumerate(totals):
            sums[place] = total
        return
    row = lax.broadcasted_iota(jnp.int32, (SUMS, nz), 0)
    lane = lax.broadcasted_iota(jnp.int32, (SUMS, nz), 1)
    lines = jnp.zeros((SUMS, nz), F32)
    for place, total in enumerate(totals):
        lines = jnp.where(row == place, jnp.sum(total, axis=0, keepdims=True), lines)
    pieces, rest = [], lines
    for _ in range(3):
        pieces.append(rest.astype(jnp.bfloat16))
        rest = rest - pieces[-1].astype(F32)
    ones = jnp.ones((nz, nz), jnp.bfloat16)
    whole_sums = jnp.dot(jnp.concatenate(pieces, axis=0), ones, preferred_element_type=F32)
    top, rest = two_sum(whole_sums[:SUMS], whole_sums[SUMS : 2 * SUMS])
    pair = two_sum(top, rest + whole_sums[2 * SUMS :])
    spot = jnp.where(lane == row, pair[0], jnp.where(lane == row + SUMS, pair[1], 0.0))
    sums[...] = jnp.sum(spot, axis=0, keepdims=True)


def two_sum(a, b):
    total = a + b
    part = total - a
    return total, (a - (total - part)) + (b - part)


def pair_add(a, b):
    total, rest = two_sum(a[0], b[0])
    return total, rest + (a[1] + b[1])


def halves(a):
    wide = 4097.0 * a
    top = wide - (wide - a)
    return top, a - top


def pair_mul(a, b):
    product = a[0] * b[0]
    a_top, a_rest = halves(a[0])
    b_top, b_rest = halves(b[0])
    rest = ((a_top * b_top - product) + a_top * b_rest + a_rest * b_top) + a_rest * b_rest
    rest = rest + (a[0] * b[1] + a[1] * b[0])
    total = product + rest
    return total, rest - (total - product)


def pair_sub(a, b):
    total, rest = two_sum(a[0], -b[0])
    rest = rest + (a[1] - b[1])
    out = total + rest
    return out, rest - (out - total)


def ratio(over, under, low, high):
    good = under > 0.0
    value = jnp.where(good, over / jnp.where(good, under, 1.0), 0.5 * (low + high))
    return jnp.minimum(jnp.maximum(value, low), high)


def coefficients(total):
    scale = 1.0 / total[0][0]
    zero = jnp.zeros_like(scale)
    g = [pair_mul(item, (scale, zero)) for item in total[:6]]
    shift = (jnp.full_like(scale, SHIFT), zero)
    h = [pair_add(g[k + 1], pair_mul(g[k], shift)) for k in range(5)]

    def minor(a, b, c, d):
        return pair_sub(pair_mul(a, b), pair_mul(c, d))

    s11 = minor(h[2], h[0], h[1], h[1])
    s12 = minor(h[3], h[0], h[1], h[2])
    s22 = minor(h[4], h[0], h[2], h[2])
    y1 = minor(g[1], h[0], h[1], g[0])
    y2 = minor(g[2], h[0], h[2], g[0])
    last = minor(s22, s11, s12, s12)
    side = minor(y2, s11, s12, y1)
    alpha = g[0][0] / h[0][0]
    l10 = h[1][0] / h[0][0]
    l20 = h[2][0] / h[0][0]
    l21 = ratio(s12[0], s11[0], l10 + (LOW - SHIFT), l10 + (HIGH - SHIFT))
    gamma1 = ratio(y1[0], s11[0], -alpha / LOW, -alpha / HIGH)
    gamma2 = ratio(side[0], last[0], -gamma1 / HIGH, -gamma1 / LOW)
    c1 = gamma1 - gamma2 * l21
    return alpha - c1 * l10 - gamma2 * l20, c1, gamma2


def sigmoid(value):
    return 1.0 / (1.0 + jnp.exp(-SHARP * value))


def finish_kernel(
    visible_hbm, parts, field, first, second, indicator_hbm, crossing_hbm,
    visible, indicator, crossing, level, weight, sem, slot_sems, result_sem,
):
    nx, ny, nz = indicator.shape
    copy = pltpu.make_async_copy(visible_hbm, visible, sem)
    copy.start()
    devices = parts.shape[0]
    tiles = [parts[pl.ds(8 * k, 8)] for k in range(devices // 8)]
    pairs = [(tile, pltpu.roll(tile, nz - SUMS, 1)) for tile in tiles]
    while len(pairs) > 1:
        pairs = [pair_add(a, b) for a, b in zip(pairs[::2], pairs[1::2])]
    total = pairs[0]
    for step in (4, 2, 1):
        total = pair_add(total, (pltpu.roll(total[0], step, 0), pltpu.roll(total[1], step, 0)))

    def spread(value, k):
        return jnp.broadcast_to(value[0:1, k : k + 1], (1, nz))

    item = [(spread(total[0], k), spread(total[1], k)) for k in range(10)]
    c0, c1, c2 = coefficients(item)
    over = c0 * (item[6][0] + item[6][1]) + c1 * (item[7][0] + item[7][1]) + c2 * (item[8][0] + item[8][1])
    iso = over / item[9][0]

    def set_level(x):
        v0 = field[x + WIDE, pl.ds(EDGE, ny + EDGE)]
        v1 = first[x + NEAR, pl.ds(EDGE + HEM, ny + HEM)]
        v2 = second[x + 1, pl.ds(EDGE + HEM, ny + HEM)]
        value = c0 * v0[: ny + HEM] + c1 * v1 + c2 * v2
        level[x, pl.ds(0, ny + HEM)] = sigmoid(value - iso)
        return value

    for x in range(nx):
        indicator[x] = set_level(x)[:ny]

    set_level(nx)
    result = pltpu.make_async_copy(indicator, indicator_hbm, result_sem)
    result.start()
    outside = sigmoid(-iso)
    lane = lax.broadcasted_iota(jnp.int32, (ny, nz), 1)

    for x in range(nx):
        here = level[x, pl.ds(0, ny)]
        above = jnp.where(lane < nz - 1, pltpu.roll(here, nz - 1, 1), outside)
        for edge, there in enumerate((level[x + 1, pl.ds(0, ny)], level[x, pl.ds(1, ny)], above)):
            value = here * (1.0 - there) + (1.0 - here) * there
            for row in range(0, ny, 8):
                turned = pltpu.roll(value[row : row + 8], 0, 1, stride=BLK, stride_axis=0)
                weight[edge, pl.ds(x * (ny + 1) + row, 8)] = turned

    chunk = lax.broadcasted_iota(jnp.int32, (8, nz), 1) // BLK
    bricks_z = nz // BLK
    per_row = nz // BLK

    copy.wait()

    def out(slot):
        return pltpu.make_async_copy(crossing.at[slot], crossing_hbm.at[slot], slot_sems.at[slot])

    for slot in range(visible.shape[0]):
        number = visible[slot]
        safe = jnp.maximum(number, 0)
        begin = (safe // bricks_z) * BLK
        column = safe % bricks_z
        spots = [chunk == lax.rem(column + row, per_row) for row in range(per_row)]
        turn = lax.rem(nz - column * BLK, nz)
        for edge in range(3):
            for half in range(2):
                for part in range(BLK // per_row):
                    at = half * 8 * (ny + 1) + begin + part * per_row
                    tile = weight[edge, pl.ds(at, 8, stride=ny + 1)]
                    for row in range(1, per_row):
                        lines = weight[edge, pl.ds(at + row, 8, stride=ny + 1)]
                        tile = jnp.where(spots[row], lines, tile)
                    tile = jnp.where(number >= 0, pltpu.roll(tile, turn, 1), 0.0)
                    crossing[slot, edge, pl.ds(half * 16 + part, 8, stride=2)] = tile
        out(slot).start()

    for slot in range(visible.shape[0]):
        out(slot).wait()
    result.wait()


def whole(*shape):
    return jax.ShapeDtypeStruct(shape, F32)


VMEM = pl.BlockSpec(memory_space=pltpu.VMEM)


HBM = pl.BlockSpec(memory_space=pltpu.HBM)


def kernel(body, inputs, outputs, scratch=(), results=VMEM, alias=None, flops=0):
    return pl.pallas_call(
        body,
        in_specs=list(inputs),
        out_specs=[results] * len(outputs),
        out_shape=list(outputs),
        scratch_shapes=list(scratch),
        input_output_aliases=alias or {},
        cost_estimate=pl.CostEstimate(flops=flops, bytes_accessed=flops // 4, transcendentals=0),
        compiler_params=pltpu.CompilerParams(vmem_limit_bytes=32 * 1024 * 1024),
    )


def in_hbm(value):
    return pltpu.with_memory_space_constraint(value, pltpu.HBM)


def swap(value, axis, first):
    count = lax.axis_size(axis)
    pairs = [(k, k + 1) for k in range(first, count - 1, 2)]
    return lax.ppermute(value, axis, pairs + [(b, a) for a, b in pairs])


def body(right_side, screening, active_blocks, visible_bricks):
    nx, ny, nz = right_side.shape
    active = active_blocks.reshape(-1)
    visible = visible_bricks.reshape(-1)
    devices = lax.axis_size("gx") * lax.axis_size("gy")
    slab = whole(nx, ny, nz)
    planes, near, third = nx + 2 * WIDE, nx + 2 * NEAR, nx + 2
    wide, rows = ny + 2 * EDGE, ny + 2 * HEM
    rim = whole(nx * EDGE, nz)
    edges = pltpu.VMEM((2, nx, EDGE, nz), F32)
    far, near_by, mask = kernel(
        pack_kernel,
        (HBM, HBM, HBM),
        (rim, rim, whole(ny, nz)),
        (pltpu.SMEM(active.shape, jnp.int32), edges, edges, pltpu.SemaphoreType.DMA((5,))),
    )(in_hbm(active), in_hbm(right_side), in_hbm(screening))
    far = swap(far, "gy", 1)
    near_by = swap(near_by, "gy", 0)
    straight, corners = (WIDE + NEAR) * ny, 2 * WIDE * EDGE
    side = whole(straight + corners, nz)
    field, weight, cross, chip = kernel(
        place_kernel,
        (VMEM,) * 3,
        (whole(planes, wide, nz), whole(nx, wide, nz), whole(straight + EXTRA, nz), side),
    )(mask, right_side, screening)
    cross = swap(cross, "gx", 1)
    chip, corner = kernel(widen_kernel, (VMEM,) * 3, (side, whole(corners, nz)), alias={2: 0})(far, near_by, chip)
    chip = swap(chip, "gx", 0)
    corner = swap(corner, "gx", 1)
    kept = [whole(planes, wide, nz)] + [whole(near, wide, nz)] * 2
    kept += [whole(near, rows + 2 * EDGE, nz), whole(third, rows + 2 * EDGE, nz)]
    kept += [whole(planes, rows, nz)] * 2 + [whole(near, rows, nz)] * 2 + [whole(third + 2, ny, nz)] * 2
    tallies = whole(10, 8, nz)
    held = kernel(inner_kernel, (VMEM,) * 4, kept + [tallies], alias={2: 0}, flops=INNER)(
        far, near_by, field, weight
    )
    for last, messages in ((False, (chip, chip)), (True, (cross, corner))):
        held = kernel(
            functools.partial(side_kernel, last),
            (VMEM,) * (HELD + 3),
            kept + [whole(1, nz) if last else tallies],
            alias={2 + k: k for k in range(HELD)},
            flops=SIDE,
        )(*messages, *held)
    field, _, _, first, second = held[:5]
    devices = lax.axis_size("gx") * lax.axis_size("gy")
    parts = lax.all_to_all(jnp.broadcast_to(held[-1], (devices, 1, nz)), ("gx", "gy"), 0, 0)
    slots = visible.shape[0]
    shape = (slots, 3, BLK**3 // nz, nz)
    indicator, crossing = kernel(
        finish_kernel,
        (HBM,) + (VMEM,) * 4,
        (slab, whole(*shape)),
        (
            pltpu.SMEM(visible.shape, jnp.int32),
            pltpu.VMEM(slab.shape, F32),
            pltpu.VMEM(shape, F32),
            pltpu.VMEM((nx + 1, ny + EDGE, nz), F32),
            pltpu.VMEM((3, nx * (ny + 1), nz), F32),
            pltpu.SemaphoreType.DMA,
            pltpu.SemaphoreType.DMA((slots,)),
            pltpu.SemaphoreType.DMA,
        ),
        results=HBM,
    )(in_hbm(visible), parts.reshape(devices, nz), field, first, second)
    return indicator, crossing.reshape(slots, 1, 3, BLK**3)


def solution(mesh):
    return jax.shard_map(
        body,
        mesh=mesh,
        in_specs=(
            P("gx", "gy", None),
            P("gx", "gy", None),
            P("gx", "gy", None),
            P("gx", "gy", None),
        ),
        out_specs=(P("gx", "gy", None), P("gx", "gy", None, None)),
        check_vma=False,
    )
```

```python
import functools

import jax
import jax.numpy as jnp
from jax import lax
from jax.experimental import pallas as pl
from jax.experimental.pallas import tpu as pltpu
from jax.sharding import PartitionSpec as P

BLK = 16
WIDE = 5
NEAR = 3
HEM = 4
EDGE = 8
SHARP = 4.0
SCALE = 1.0 / 86400.0
SHIFT = 2.0
LOW, HIGH = 0.5, 7.0
SUMS = 16
EXTRA, INNER, SIDE = 96, 0, 0
HELD = 11
F32 = jnp.float32


def mass(mid, one, two):
    return 66.0 * mid + (26.0 * one + two)


def stiff(mid, one, two):
    return 6.0 * mid - (2.0 * one + two)


def block_mask(active, slots, rows, columns):
    y = lax.broadcasted_iota(jnp.int32, (rows, columns), 0)
    z = lax.broadcasted_iota(jnp.int32, (rows, columns), 1)
    number = (y // BLK) * (columns // BLK) + z // BLK
    mask = jnp.zeros((rows, columns), F32)
    for slot in range(slots):
        mask = jnp.where(number == active[slot], 1.0, mask)
    return mask


def on_odd():
    return lax.rem(lax.axis_index("gx"), 2)


def odd_on(axis):
    return lax.rem(lax.axis_index(axis), 2)


def pack_kernel(active_hbm, right_hbm, screen_hbm, far, near, mask_out, active, right, screen, sems):
    nx, ny, nz = right_hbm.shape
    copies = [pltpu.make_async_copy(active_hbm, active, sems.at[0])]
    for k, (source, target) in enumerate(((right_hbm, right), (screen_hbm, screen))):
        for high in range(2):
            rows = pl.ds(high * (ny - EDGE), EDGE)
            copies.append(pltpu.make_async_copy(source.at[:, rows], target.at[high], sems.at[1 + 2 * k + high]))
    for copy in copies:
        copy.start()
    copies[0].wait()
    mask = block_mask(active, active.shape[0], ny, nz)
    mask_out[...] = mask
    row = lax.broadcasted_iota(jnp.int32, (EDGE, nz), 0)
    for copy in copies[1:]:
        copy.wait()

    def write(high_out, low_out):
        for x in range(nx):
            rows = pl.ds(x * EDGE, EDGE)
            low_out[rows] = jnp.where(row < WIDE, right[0, x], pltpu.roll(screen[0, x], WIDE, 0)) * mask[:EDGE]
            beside = pltpu.roll(screen[1, x] * mask[ny - EDGE :], NEAR, 0)
            high_out[rows] = jnp.where(row >= NEAR, right[1, x] * mask[ny - EDGE :], beside)

    odd = odd_on("gy")
    pl.when(odd == 1)(functools.partial(write, far, near))
    pl.when(odd == 0)(functools.partial(write, near, far))


def place_kernel(mask_in, right, screen, field, weight, cross, chip):
    nx, ny, nz = right.shape
    mask = mask_in[...]
    own = pl.ds(EDGE, ny)
    for x in range(nx):
        field[WIDE + x, own] = right[x] * mask
        weight[x, own] = screen[x] * mask
    odd = odd_on("gx")
    for target, high in ((cross, odd), (chip, 1 - odd)):
        for x in range(WIDE):
            target[x * ny : (x + 1) * ny] = field[WIDE + high * (nx - WIDE) + x, own]
        for x in range(NEAR):
            row = (WIDE + x) * ny
            target[row : row + ny] = weight[high * (nx - NEAR) + x, own]


def widen_kernel(far, near, chip_in, chip, corner):
    nx = far.shape[0] // EDGE
    base = chip.shape[0] - corner.shape[0]
    odd = odd_on("gx")

    def fill(low, high):
        for target, start, side in ((corner, 0, odd), (chip, base, 1 - odd)):
            for x in range(WIDE):
                tile = pl.ds((side * (nx - WIDE) + x) * EDGE, EDGE)
                row = start + 2 * x * EDGE
                target[row : row + EDGE] = low[tile]
                target[row + EDGE : row + 2 * EDGE] = high[tile]

    by_y(fill, far, near)


def by_y(action, far, near):
    odd = odd_on("gy")
    pl.when(odd == 1)(functools.partial(action, near, far))
    pl.when(odd == 0)(functools.partial(action, far, near))


def near_z(value):
    lane = lax.broadcasted_iota(jnp.int32, value.shape, 1)
    last = value.shape[1]

    def shifted(step):
        before = jnp.where(lane >= step, pltpu.roll(value, step, 1), 0.0)
        after = jnp.where(lane < last - step, pltpu.roll(value, last - step, 1), 0.0)
        return before + after

    return shifted(1), shifted(2)


def set_beside(field, x, keep, shifted, weight_x, tile, high):
    start = field.shape[1] - EDGE if high else 0
    field[x, start : start + EDGE] = tile
    if weight_x is not None:
        set_weight(keep, shifted, weight_x, pl.ds(start, EDGE), pltpu.roll(tile, NEAR if high else WIDE, 0))


def set_weight(keep, shifted, at, rows, weight):
    on = weight > 0.0
    keep[at, rows] = jnp.where(on, SCALE, 0.0)
    shifted[at, rows] = jnp.where(on, weight - SHIFT, 0.0)


def near_y(source, x, row, top, end):
    def part(step):
        return source[x, pl.ds(row + step, 8)]

    below, above = part(-2), part(2)
    place = lax.broadcasted_iota(jnp.int32, below.shape, 0)
    if top:
        below = jnp.where(place == 0, 0.0, jnp.where(place == 1, 2.0 * below, below))
    if end:
        above = jnp.where(place == 7, 0.0, jnp.where(place == 6, 2.0 * above, above))
    return part(0), part(-1) + part(1), below + above


def along_yz(source, x, row, top=False, end=False):
    here, one, two = near_y(source, x, row, top, end)
    heavy, stretched = mass(here, one, two), stiff(here, one, two)
    heavy_near, stretched_near = near_z(heavy), near_z(stretched)
    return mass(heavy, *heavy_near), stiff(heavy, *heavy_near) + mass(stretched, *stretched_near)


def across(window):
    p, q = zip(*window)
    return mass(q[2], q[1] + q[3], q[0] + q[4]) + stiff(p[2], p[1] + p[3], p[0] + p[4])


def power(target, source, row, keep, shifted, skip, x, group, window):
    rows, at = pl.ds(EDGE + 8 * group, 8), pl.ds(EDGE - HEM + 8 * group, 8)
    center = source[x + 2, pl.ds(row + 8 * group, 8)]
    target[x, rows] = keep[x + skip, at] * across(window) + shifted[x + skip, at] * center


def advance(target, source, row, keep, shifted, skip, yp, yq, count, first):
    for group in range(target.shape[1] // 8 - 2):
        rows = pl.ds(8 * group, 8)
        window = []
        for x in range(first, first + count):
            p, q = along_yz(source, x, row + 8 * group)
            yp[x, rows] = p
            yq[x, rows] = q
            window = window[-4:] + [(p, q)]
            if len(window) == 5:
                power(target, source, row, keep, shifted, skip, x - 4, group, window)


def advance_side(target, source, row, keep, shifted, skip, yp, yq, high):
    groups = target.shape[1] // 8 - 2
    base = high * (target.shape[0] - WIDE)
    start = high * (source.shape[0] - WIDE)
    for group in range(groups):
        rows = pl.ds(8 * group, 8)
        for k in range(WIDE):
            p, q = along_yz(source, start + k, row + 8 * group)
            yp[start + k, rows] = p
            yq[start + k, rows] = q
    for group in range(groups):
        rows = pl.ds(8 * group, 8)
        window = [(yp[base + k, rows], yq[base + k, rows]) for k in range(WIDE + 4)]
        for k in range(WIDE):
            power(target, source, row, keep, shifted, skip, base + k, group, window[k : k + 5])


def last_rows(source, yp, yq, count, first):
    groups = yp.shape[1] // 8
    for group in range(groups):
        rows = pl.ds(8 * group, 8)
        for k in range(count):
            p, q = along_yz(source, first + k, EDGE + HEM + 8 * group, group == 0, group == groups - 1)
            yp[first + 1 + k, rows] = p
            yq[first + 1 + k, rows] = q


def fold(value):
    return jnp.sum(value.reshape(-1, 8, value.shape[1]), axis=0)


def add_each(left, right):
    return [a + b for a, b in zip(left, right)]


def add_sums(totals, arrays, count, first_x):
    field, keep, shifted, first, second, yp, yq = arrays
    parts = []
    for group in range(yp.shape[1] // 8):
        rows = pl.ds(8 * group, 8)
        mid, own = pl.ds(EDGE + 8 * group, 8), pl.ds(EDGE + HEM + 8 * group, 8)
        window = [(yp[first_x + k, rows], yq[first_x + k, rows]) for k in range(count + 4)]
        part = None
        for k in range(count):
            x = first_x + k
            v0 = field[x + WIDE, mid]
            v1 = first[x + NEAR, own]
            v2 = second[x + 1, own]
            form = v2 * (SCALE * across(window[k : k + 5]) + shifted[x + NEAR, mid] * v2)
            on = jnp.where(keep[x + NEAR, mid] > 0.0, 1.0, 0.0)
            new = (v0 * v0, v0 * v1, v1 * v1, v1 * v2, v2 * v2, form, v0, v1, v2, on)
            part = new if part is None else add_each(part, new)
        parts.append(part)
    while len(parts) > 1:
        parts = [add_each(*parts[k : k + 2]) for k in range(0, len(parts), 2)]
    return list(parts[0]) if totals is None else add_each(totals, parts[0])


def inner_kernel(
    far, near, field_in, weight, field, keep, shifted, first, second, yp1, yq1, yp2, yq2, yp3, yq3, sums
):
    nx, wide, nz = weight.shape
    ny = wide - 2 * EDGE

    def fill(low, high):
        for x in range(nx):
            set_beside(field, WIDE + x, keep, shifted, NEAR + x, low[EDGE * x : EDGE * (x + 1)], False)
            set_beside(field, WIDE + x, keep, shifted, NEAR + x, high[EDGE * x : EDGE * (x + 1)], True)

    by_y(fill, far, near)
    own = pl.ds(EDGE, ny)
    for x in range(nx):
        set_weight(keep, shifted, NEAR + x, own, weight[x, own])
    advance(first, field, EDGE - HEM, keep, shifted, 0, yp1, yq1, nx, WIDE)
    advance(second, first, EDGE, keep, shifted, 2, yp2, yq2, nx - 4, WIDE)
    last_rows(second, yp3, yq3, nx - 8, WIDE)
    arrays = (field, keep, shifted, first, second, yp3, yq3)
    totals = add_sums(None, arrays, nx - 12, WIDE + 1)
    for place, total in enumerate(totals):
        sums[place] = total


def side_kernel(last, message, corner, *refs):
    sums_in = refs[HELD]
    field, keep, shifted, first, second, yp1, yq1, yp2, yq2, yp3, yq3, sums = refs[HELD + 1 :]
    planes, wide, nz = field.shape
    nx, ny = planes - 2 * WIDE, wide - 2 * EDGE
    odd = odd_on("gx")
    high = odd if last else 1 - odd
    own = pl.ds(EDGE, ny)
    base = corner.shape[0] - 2 * WIDE * EDGE
    for x in range(WIDE):
        plane = high * (nx + WIDE) + x
        field[plane, own] = message[x * ny : (x + 1) * ny]
        for up in range(2):
            row = base + (2 * x + up) * EDGE
            set_beside(field, plane, keep, shifted, None, corner[row : row + EDGE], up == 1)
    for x in range(NEAR):
        plane = high * (nx + NEAR) + x
        row = (WIDE + x) * ny
        set_weight(keep, shifted, plane, own, message[row : row + ny])
        place = base + (x + (1 - high) * (WIDE - NEAR)) * 2 * EDGE
        for up in range(2):
            tile = corner[pl.ds(place + up * EDGE, EDGE)]
            rows = pl.ds(up * (wide - EDGE), EDGE)
            set_weight(keep, shifted, plane, rows, pltpu.roll(tile, NEAR if up else WIDE, 0))
    advance_side(first, field, EDGE - HEM, keep, shifted, 0, yp1, yq1, high)
    advance_side(second, first, EDGE, keep, shifted, 2, yp2, yq2, high)
    last_rows(second, yp3, yq3, WIDE, high * (nx + 2 - WIDE))
    none = jnp.zeros((ny, nz), F32)
    yp3[high * (nx + 3)] = none
    yq3[high * (nx + 3)] = none
    totals = tuple(sums_in[place] for place in range(10))
    arrays = (field, keep, shifted, first, second, yp3, yq3)
    totals = list(add_sums(totals, arrays, WIDE + 1, high * (nx - WIDE - 1)))
    own = pl.ds(EDGE + HEM, ny)
    beside, edge, next_edge = 1 + high * (nx + 1), 2 + high * (nx - 1), 3 + high * (nx - 3)
    give = 13.0 * yq3[edge] - yp3[edge] + (yq3[next_edge] - yp3[next_edge])
    take = 13.0 * yq3[beside] - yp3[beside]
    totals[5] += SCALE * fold(second[beside - 1, own] * give - second[edge - 1, own] * take)
    if not last:
        for place, total in enumerate(totals):
            sums[place] = total
        return
    row = lax.broadcasted_iota(jnp.int32, (SUMS, nz), 0)
    lane = lax.broadcasted_iota(jnp.int32, (SUMS, nz), 1)
    lines = jnp.zeros((SUMS, nz), F32)
    for place, total in enumerate(totals):
        lines = jnp.where(row == place, jnp.sum(total, axis=0, keepdims=True), lines)
    pieces, rest = [], lines
    for _ in range(3):
        pieces.append(rest.astype(jnp.bfloat16))
        rest = rest - pieces[-1].astype(F32)
    ones = jnp.ones((nz, nz), jnp.bfloat16)
    whole_sums = jnp.dot(jnp.concatenate(pieces, axis=0), ones, preferred_element_type=F32)
    top, rest = two_sum(whole_sums[:SUMS], whole_sums[SUMS : 2 * SUMS])
    pair = two_sum(top, rest + whole_sums[2 * SUMS :])
    spot = jnp.where(lane == row, pair[0], jnp.where(lane == row + SUMS, pair[1], 0.0))
    sums[...] = jnp.sum(spot, axis=0, keepdims=True)


def two_sum(a, b):
    total = a + b
    part = total - a
    return total, (a - (total - part)) + (b - part)


def pair_add(a, b):
    total, rest = two_sum(a[0], b[0])
    return total, rest + (a[1] + b[1])


def halves(a):
    wide = 4097.0 * a
    top = wide - (wide - a)
    return top, a - top


def pair_mul(a, b):
    product = a[0] * b[0]
    a_top, a_rest = halves(a[0])
    b_top, b_rest = halves(b[0])
    rest = ((a_top * b_top - product) + a_top * b_rest + a_rest * b_top) + a_rest * b_rest
    rest = rest + (a[0] * b[1] + a[1] * b[0])
    total = product + rest
    return total, rest - (total - product)


def pair_sub(a, b):
    total, rest = two_sum(a[0], -b[0])
    rest = rest + (a[1] - b[1])
    out = total + rest
    return out, rest - (out - total)


def ratio(over, under, low, high):
    good = under > 0.0
    value = jnp.where(good, over / jnp.where(good, under, 1.0), 0.5 * (low + high))
    return jnp.minimum(jnp.maximum(value, low), high)


def coefficients(total):
    scale = 1.0 / total[0][0]
    zero = jnp.zeros_like(scale)
    g = [pair_mul(item, (scale, zero)) for item in total[:6]]
    shift = (jnp.full_like(scale, SHIFT), zero)
    h = [pair_add(g[k + 1], pair_mul(g[k], shift)) for k in range(5)]

    def minor(a, b, c, d):
        return pair_sub(pair_mul(a, b), pair_mul(c, d))

    s11 = minor(h[2], h[0], h[1], h[1])
    s12 = minor(h[3], h[0], h[1], h[2])
    s22 = minor(h[4], h[0], h[2], h[2])
    y1 = minor(g[1], h[0], h[1], g[0])
    y2 = minor(g[2], h[0], h[2], g[0])
    last = minor(s22, s11, s12, s12)
    side = minor(y2, s11, s12, y1)
    alpha = g[0][0] / h[0][0]
    l10 = h[1][0] / h[0][0]
    l20 = h[2][0] / h[0][0]
    l21 = ratio(s12[0], s11[0], l10 + (LOW - SHIFT), l10 + (HIGH - SHIFT))
    gamma1 = ratio(y1[0], s11[0], -alpha / LOW, -alpha / HIGH)
    gamma2 = ratio(side[0], last[0], -gamma1 / HIGH, -gamma1 / LOW)
    c1 = gamma1 - gamma2 * l21
    return alpha - c1 * l10 - gamma2 * l20, c1, gamma2


def sigmoid(value):
    return 1.0 / (1.0 + jnp.exp(-SHARP * value))


def finish_kernel(
    visible_hbm, parts, field, first, second, indicator_hbm, crossing_hbm,
    visible, indicator, crossing, level, weight, sem, slot_sems, result_sem,
):
    nx, ny, nz = indicator.shape
    copy = pltpu.make_async_copy(visible_hbm, visible, sem)
    copy.start()
    devices = parts.shape[0]
    tiles = [parts[pl.ds(8 * k, 8)] for k in range(devices // 8)]
    pairs = [(tile, pltpu.roll(tile, nz - SUMS, 1)) for tile in tiles]
    while len(pairs) > 1:
        pairs = [pair_add(a, b) for a, b in zip(pairs[::2], pairs[1::2])]
    total = pairs[0]
    for step in (4, 2, 1):
        total = pair_add(total, (pltpu.roll(total[0], step, 0), pltpu.roll(total[1], step, 0)))

    def spread(value, k):
        return jnp.broadcast_to(value[0:1, k : k + 1], (1, nz))

    item = [(spread(total[0], k), spread(total[1], k)) for k in range(10)]
    c0, c1, c2 = coefficients(item)
    over = c0 * (item[6][0] + item[6][1]) + c1 * (item[7][0] + item[7][1]) + c2 * (item[8][0] + item[8][1])
    iso = over / item[9][0]

    def set_level(x):
        v0 = field[x + WIDE, pl.ds(EDGE, ny + EDGE)]
        v1 = first[x + NEAR, pl.ds(EDGE + HEM, ny + HEM)]
        v2 = second[x + 1, pl.ds(EDGE + HEM, ny + HEM)]
        value = c0 * v0[: ny + HEM] + c1 * v1 + c2 * v2
        level[x, pl.ds(0, ny + HEM)] = sigmoid(value - iso)
        return value

    for x in range(nx):
        indicator[x] = set_level(x)[:ny]

    set_level(nx)
    result = pltpu.make_async_copy(indicator, indicator_hbm, result_sem)
    result.start()
    outside = sigmoid(-iso)
    lane = lax.broadcasted_iota(jnp.int32, (ny, nz), 1)

    for x in range(nx):
        here = level[x, pl.ds(0, ny)]
        above = jnp.where(lane < nz - 1, pltpu.roll(here, nz - 1, 1), outside)
        for edge, there in enumerate((level[x + 1, pl.ds(0, ny)], level[x, pl.ds(1, ny)], above)):
            value = here * (1.0 - there) + (1.0 - here) * there
            for row in range(0, ny, 8):
                turned = pltpu.roll(value[row : row + 8], 0, 1, stride=BLK, stride_axis=0)
                weight[edge, pl.ds(x * (ny + 1) + row, 8)] = turned

    chunk = lax.broadcasted_iota(jnp.int32, (8, nz), 1) // BLK
    bricks_z = nz // BLK
    per_row = nz // BLK

    copy.wait()

    def out(slot):
        return pltpu.make_async_copy(crossing.at[slot], crossing_hbm.at[slot], slot_sems.at[slot])

    for slot in range(visible.shape[0]):
        number = visible[slot]
        safe = jnp.maximum(number, 0)
        begin = (safe // bricks_z) * BLK
        column = safe % bricks_z
        spots = [chunk == lax.rem(column + row, per_row) for row in range(per_row)]
        turn = lax.rem(nz - column * BLK, nz)
        for edge in range(3):
            for half in range(2):
                for part in range(BLK // per_row):
                    at = half * 8 * (ny + 1) + begin + part * per_row
                    tile = weight[edge, pl.ds(at, 8, stride=ny + 1)]
                    for row in range(1, per_row):
                        lines = weight[edge, pl.ds(at + row, 8, stride=ny + 1)]
                        tile = jnp.where(spots[row], lines, tile)
                    tile = jnp.where(number >= 0, pltpu.roll(tile, turn, 1), 0.0)
                    crossing[slot, edge, pl.ds(half * 16 + part, 8, stride=2)] = tile
        out(slot).start()

    for slot in range(visible.shape[0]):
        out(slot).wait()
    result.wait()


def whole(*shape):
    return jax.ShapeDtypeStruct(shape, F32)


VMEM = pl.BlockSpec(memory_space=pltpu.VMEM)


HBM = pl.BlockSpec(memory_space=pltpu.HBM)


def kernel(body, inputs, outputs, scratch=(), results=VMEM, alias=None, flops=0):
    return pl.pallas_call(
        body,
        in_specs=list(inputs),
        out_specs=[results] * len(outputs),
        out_shape=list(outputs),
        scratch_shapes=list(scratch),
        input_output_aliases=alias or {},
        cost_estimate=pl.CostEstimate(flops=flops, bytes_accessed=flops // 4, transcendentals=0),
        compiler_params=pltpu.CompilerParams(vmem_limit_bytes=32 * 1024 * 1024),
    )


def in_hbm(value):
    return pltpu.with_memory_space_constraint(value, pltpu.HBM)


def swap(value, axis, first):
    count = lax.axis_size(axis)
    pairs = [(k, k + 1) for k in range(first, count - 1, 2)]
    return lax.ppermute(value, axis, pairs + [(b, a) for a, b in pairs])


def body(right_side, screening, active_blocks, visible_bricks):
    nx, ny, nz = right_side.shape
    active = active_blocks.reshape(-1)
    visible = visible_bricks.reshape(-1)
    devices = lax.axis_size("gx") * lax.axis_size("gy")
    slab = whole(nx, ny, nz)
    planes, near, third = nx + 2 * WIDE, nx + 2 * NEAR, nx + 2
    wide, rows = ny + 2 * EDGE, ny + 2 * HEM
    rim = whole(nx * EDGE, nz)
    edges = pltpu.VMEM((2, nx, EDGE, nz), F32)
    far, near_by, mask = kernel(
        pack_kernel,
        (HBM, HBM, HBM),
        (rim, rim, whole(ny, nz)),
        (pltpu.SMEM(active.shape, jnp.int32), edges, edges, pltpu.SemaphoreType.DMA((5,))),
    )(in_hbm(active), in_hbm(right_side), in_hbm(screening))
    far = swap(far, "gy", 1)
    near_by = swap(near_by, "gy", 0)
    straight, corners = (WIDE + NEAR) * ny, 2 * WIDE * EDGE
    side = whole(straight + corners, nz)
    field, weight, cross, chip = kernel(
        place_kernel,
        (VMEM,) * 3,
        (whole(planes, wide, nz), whole(nx, wide, nz), whole(straight + EXTRA, nz), side),
    )(mask, right_side, screening)
    cross = swap(cross, "gx", 1)
    chip, corner = kernel(widen_kernel, (VMEM,) * 3, (side, whole(corners, nz)), alias={2: 0})(far, near_by, chip)
    chip = swap(chip, "gx", 0)
    corner = swap(corner, "gx", 1)
    kept = [whole(planes, wide, nz)] + [whole(near, wide, nz)] * 2
    kept += [whole(near, rows + 2 * EDGE, nz), whole(third, rows + 2 * EDGE, nz)]
    kept += [whole(planes, rows, nz)] * 2 + [whole(near, rows, nz)] * 2 + [whole(third + 2, ny, nz)] * 2
    tallies = whole(10, 8, nz)
    held = kernel(inner_kernel, (VMEM,) * 4, kept + [tallies], alias={2: 0}, flops=INNER)(
        far, near_by, field, weight
    )
    for last, messages in ((False, (chip, chip)), (True, (cross, corner))):
        held = kernel(
            functools.partial(side_kernel, last),
            (VMEM,) * (HELD + 3),
            kept + [whole(1, nz) if last else tallies],
            alias={2 + k: k for k in range(HELD)},
            flops=SIDE,
        )(*messages, *held)
    field, _, _, first, second = held[:5]
    devices = lax.axis_size("gx") * lax.axis_size("gy")
    parts = lax.all_to_all(jnp.broadcast_to(held[-1], (devices, 1, nz)), ("gx", "gy"), 0, 0)
    slots = visible.shape[0]
    shape = (slots, 3, BLK**3 // nz, nz)
    indicator, crossing = kernel(
        finish_kernel,
        (HBM,) + (VMEM,) * 4,
        (slab, whole(*shape)),
        (
            pltpu.SMEM(visible.shape, jnp.int32),
            pltpu.VMEM(slab.shape, F32),
            pltpu.VMEM(shape, F32),
            pltpu.VMEM((nx + 1, ny + EDGE, nz), F32),
            pltpu.VMEM((3, nx * (ny + 1), nz), F32),
            pltpu.SemaphoreType.DMA,
            pltpu.SemaphoreType.DMA((slots,)),
            pltpu.SemaphoreType.DMA,
        ),
        results=HBM,
    )(in_hbm(visible), parts.reshape(devices, nz), field, first, second)
    return indicator, crossing.reshape(slots, 1, 3, BLK**3)


def solution(mesh):
    return jax.shard_map(
        body,
        mesh=mesh,
        in_specs=(
            P("gx", "gy", None),
            P("gx", "gy", None),
            P("gx", "gy", None),
            P("gx", "gy", None),
        ),
        out_specs=(P("gx", "gy", None), P("gx", "gy", None, None)),
        check_vma=False,
    )
```

```python
import functools

import jax
import jax.numpy as jnp
from jax import lax
from jax.experimental import pallas as pl
from jax.experimental.pallas import tpu as pltpu
from jax.sharding import PartitionSpec as P

BLK = 16
WIDE = 5
NEAR = 3
HEM = 4
EDGE = 8
SHARP = 4.0
SCALE = 1.0 / 86400.0
SHIFT = 2.0
LOW, HIGH = 0.5, 7.0
SUMS = 16
EXTRA, INNER, SIDE = 96, 0, 0
HELD = 11
F32 = jnp.float32


def mass(mid, one, two):
    return 66.0 * mid + (26.0 * one + two)


def stiff(mid, one, two):
    return 6.0 * mid - (2.0 * one + two)


def block_mask(active, slots, rows, columns):
    y = lax.broadcasted_iota(jnp.int32, (rows, columns), 0)
    z = lax.broadcasted_iota(jnp.int32, (rows, columns), 1)
    number = (y // BLK) * (columns // BLK) + z // BLK
    mask = jnp.zeros((rows, columns), F32)
    for slot in range(slots):
        mask = jnp.where(number == active[slot], 1.0, mask)
    return mask


def on_odd():
    return lax.rem(lax.axis_index("gx"), 2)


def odd_on(axis):
    return lax.rem(lax.axis_index(axis), 2)


def pack_kernel(active_hbm, right_hbm, screen_hbm, far, near, mask_out, active, right, screen, sems):
    nx, ny, nz = right_hbm.shape
    copies = [pltpu.make_async_copy(active_hbm, active, sems.at[0])]
    for k, (source, target) in enumerate(((right_hbm, right), (screen_hbm, screen))):
        for high in range(2):
            rows = pl.ds(high * (ny - EDGE), EDGE)
            copies.append(pltpu.make_async_copy(source.at[:, rows], target.at[high], sems.at[1 + 2 * k + high]))
    for copy in copies:
        copy.start()
    copies[0].wait()
    mask = block_mask(active, active.shape[0], ny, nz)
    mask_out[...] = mask
    row = lax.broadcasted_iota(jnp.int32, (EDGE, nz), 0)
    for copy in copies[1:]:
        copy.wait()

    def write(high_out, low_out):
        for x in range(nx):
            rows = pl.ds(x * EDGE, EDGE)
            low_out[rows] = jnp.where(row < WIDE, right[0, x], pltpu.roll(screen[0, x], WIDE, 0)) * mask[:EDGE]
            beside = pltpu.roll(screen[1, x] * mask[ny - EDGE :], NEAR, 0)
            high_out[rows] = jnp.where(row >= NEAR, right[1, x] * mask[ny - EDGE :], beside)

    odd = odd_on("gy")
    pl.when(odd == 1)(functools.partial(write, far, near))
    pl.when(odd == 0)(functools.partial(write, near, far))


def place_kernel(mask_in, right, screen, field, weight, cross, chip):
    nx, ny, nz = right.shape
    mask = mask_in[...]
    own = pl.ds(EDGE, ny)
    for x in range(nx):
        field[WIDE + x, own] = right[x] * mask
        weight[x, own] = screen[x] * mask
    odd = odd_on("gx")
    for target, high in ((cross, odd), (chip, 1 - odd)):
        for x in range(WIDE):
            target[x * ny : (x + 1) * ny] = field[WIDE + high * (nx - WIDE) + x, own]
        for x in range(NEAR):
            row = (WIDE + x) * ny
            target[row : row + ny] = weight[high * (nx - NEAR) + x, own]


def widen_kernel(far, near, chip_in, chip, corner):
    nx = far.shape[0] // EDGE
    base = chip.shape[0] - corner.shape[0]
    odd = odd_on("gx")

    def fill(low, high):
        for target, start, side in ((corner, 0, odd), (chip, base, 1 - odd)):
            for x in range(WIDE):
                tile = pl.ds((side * (nx - WIDE) + x) * EDGE, EDGE)
                row = start + 2 * x * EDGE
                target[row : row + EDGE] = low[tile]
                target[row + EDGE : row + 2 * EDGE] = high[tile]

    by_y(fill, far, near)


def by_y(action, far, near):
    odd = odd_on("gy")
    pl.when(odd == 1)(functools.partial(action, near, far))
    pl.when(odd == 0)(functools.partial(action, far, near))


def near_z(value):
    lane = lax.broadcasted_iota(jnp.int32, value.shape, 1)
    last = value.shape[1]

    def shifted(step):
        before = jnp.where(lane >= step, pltpu.roll(value, step, 1), 0.0)
        after = jnp.where(lane < last - step, pltpu.roll(value, last - step, 1), 0.0)
        return before + after

    return shifted(1), shifted(2)


def set_beside(field, x, keep, shifted, weight_x, tile, high):
    start = field.shape[1] - EDGE if high else 0
    field[x, start : start + EDGE] = tile
    if weight_x is not None:
        set_weight(keep, shifted, weight_x, pl.ds(start, EDGE), pltpu.roll(tile, NEAR if high else WIDE, 0))


def set_weight(keep, shifted, at, rows, weight):
    on = weight > 0.0
    keep[at, rows] = jnp.where(on, SCALE, 0.0)
    shifted[at, rows] = jnp.where(on, weight - SHIFT, 0.0)


def near_y(source, x, row, top, end):
    def part(step):
        return source[x, pl.ds(row + step, 8)]

    below, above = part(-2), part(2)
    place = lax.broadcasted_iota(jnp.int32, below.shape, 0)
    if top:
        below = jnp.where(place == 0, 0.0, jnp.where(place == 1, 2.0 * below, below))
    if end:
        above = jnp.where(place == 7, 0.0, jnp.where(place == 6, 2.0 * above, above))
    return part(0), part(-1) + part(1), below + above


def along_yz(source, x, row, top=False, end=False):
    here, one, two = near_y(source, x, row, top, end)
    heavy, stretched = mass(here, one, two), stiff(here, one, two)
    heavy_near, stretched_near = near_z(heavy), near_z(stretched)
    return mass(heavy, *heavy_near), stiff(heavy, *heavy_near) + mass(stretched, *stretched_near)


def across(window):
    p, q = zip(*window)
    return mass(q[2], q[1] + q[3], q[0] + q[4]) + stiff(p[2], p[1] + p[3], p[0] + p[4])


def power(target, source, row, keep, shifted, skip, x, group, window):
    rows, at = pl.ds(EDGE + 8 * group, 8), pl.ds(EDGE - HEM + 8 * group, 8)
    center = source[x + 2, pl.ds(row + 8 * group, 8)]
    target[x, rows] = keep[x + skip, at] * across(window) + shifted[x + skip, at] * center


def advance(target, source, row, keep, shifted, skip, yp, yq, count, first):
    for group in range(target.shape[1] // 8 - 2):
        rows = pl.ds(8 * group, 8)
        window = []
        for x in range(first, first + count):
            p, q = along_yz(source, x, row + 8 * group)
            yp[x, rows] = p
            yq[x, rows] = q
            window = window[-4:] + [(p, q)]
            if len(window) == 5:
                power(target, source, row, keep, shifted, skip, x - 4, group, window)


def advance_side(target, source, row, keep, shifted, skip, yp, yq, high, groups):
    base = high * (target.shape[0] - WIDE)
    start = high * (source.shape[0] - WIDE)
    for group in groups:
        rows = pl.ds(8 * group, 8)
        for k in range(WIDE):
            p, q = along_yz(source, start + k, row + 8 * group)
            yp[start + k, rows] = p
            yq[start + k, rows] = q
    for group in groups:
        rows = pl.ds(8 * group, 8)
        window = [(yp[base + k, rows], yq[base + k, rows]) for k in range(WIDE + 4)]
        for k in range(WIDE):
            power(target, source, row, keep, shifted, skip, base + k, group, window[k : k + 5])


def last_rows(source, yp, yq, count, first):
    groups = yp.shape[1] // 8
    for group in range(groups):
        rows = pl.ds(8 * group, 8)
        for k in range(count):
            p, q = along_yz(source, first + k, EDGE + HEM + 8 * group, group == 0, group == groups - 1)
            yp[first + 1 + k, rows] = p
            yq[first + 1 + k, rows] = q


def fold(value):
    return jnp.sum(value.reshape(-1, 8, value.shape[1]), axis=0)


def add_each(left, right):
    return [a + b for a, b in zip(left, right)]


def add_sums(totals, arrays, count, first_x):
    field, keep, shifted, first, second, yp, yq = arrays
    parts = []
    for group in range(yp.shape[1] // 8):
        rows = pl.ds(8 * group, 8)
        mid, own = pl.ds(EDGE + 8 * group, 8), pl.ds(EDGE + HEM + 8 * group, 8)
        window = [(yp[first_x + k, rows], yq[first_x + k, rows]) for k in range(count + 4)]
        part = None
        for k in range(count):
            x = first_x + k
            v0 = field[x + WIDE, mid]
            v1 = first[x + NEAR, own]
            v2 = second[x + 1, own]
            form = v2 * (SCALE * across(window[k : k + 5]) + shifted[x + NEAR, mid] * v2)
            on = jnp.where(keep[x + NEAR, mid] > 0.0, 1.0, 0.0)
            new = (v0 * v0, v0 * v1, v1 * v1, v1 * v2, v2 * v2, form, v0, v1, v2, on)
            part = new if part is None else add_each(part, new)
        parts.append(part)
    while len(parts) > 1:
        parts = [add_each(*parts[k : k + 2]) for k in range(0, len(parts), 2)]
    return list(parts[0]) if totals is None else add_each(totals, parts[0])


def inner_kernel(
    far, near, field_in, weight, field, keep, shifted, first, second, yp1, yq1, yp2, yq2, yp3, yq3, sums
):
    nx, wide, nz = weight.shape
    ny = wide - 2 * EDGE

    def fill(low, high):
        for x in range(nx):
            set_beside(field, WIDE + x, keep, shifted, NEAR + x, low[EDGE * x : EDGE * (x + 1)], False)
            set_beside(field, WIDE + x, keep, shifted, NEAR + x, high[EDGE * x : EDGE * (x + 1)], True)

    by_y(fill, far, near)
    own = pl.ds(EDGE, ny)
    for x in range(nx):
        set_weight(keep, shifted, NEAR + x, own, weight[x, own])
    advance(first, field, EDGE - HEM, keep, shifted, 0, yp1, yq1, nx, WIDE)
    advance(second, first, EDGE, keep, shifted, 2, yp2, yq2, nx - 4, WIDE)
    last_rows(second, yp3, yq3, nx - 8, WIDE)
    arrays = (field, keep, shifted, first, second, yp3, yq3)
    totals = add_sums(None, arrays, nx - 12, WIDE + 1)
    for place, total in enumerate(totals):
        sums[place] = total


def side_straight(message, high, held, groups):
    field, keep, shifted, first, second, yp1, yq1, yp2, yq2 = held[:9]
    nx, ny = field.shape[0] - 2 * WIDE, field.shape[1] - 2 * EDGE
    own = pl.ds(EDGE, ny)
    for x in range(WIDE):
        field[high * (nx + WIDE) + x, own] = message[x * ny : (x + 1) * ny]
    for x in range(NEAR):
        row = (WIDE + x) * ny
        set_weight(keep, shifted, high * (nx + NEAR) + x, own, message[row : row + ny])
    advance_side(first, field, EDGE - HEM, keep, shifted, 0, yp1, yq1, high, groups[1:-1])
    advance_side(second, first, EDGE, keep, shifted, 2, yp2, yq2, high, groups[2:-2])


def straight_kernel(message, *refs):
    field = refs[0]
    groups = range((field.shape[1] - 2 * EDGE + 2 * HEM) // 8)
    side_straight(message, odd_on("gx"), refs[HELD:], groups)


def side_kernel(last, message, corner, *refs):
    sums_in = refs[HELD]
    field, keep, shifted, first, second, yp1, yq1, yp2, yq2, yp3, yq3, sums = refs[HELD + 1 :]
    planes, wide, nz = field.shape
    nx, ny = planes - 2 * WIDE, wide - 2 * EDGE
    odd = odd_on("gx")
    high = odd if last else 1 - odd
    groups = range((ny + 2 * HEM) // 8)
    if not last:
        side_straight(message, high, refs[HELD + 1 :], groups)
    base = corner.shape[0] - 2 * WIDE * EDGE
    for x in range(WIDE):
        for up in range(2):
            row = base + (2 * x + up) * EDGE
            set_beside(field, high * (nx + WIDE) + x, keep, shifted, None, corner[row : row + EDGE], up == 1)
    for x in range(NEAR):
        place = base + (x + (1 - high) * (WIDE - NEAR)) * 2 * EDGE
        for up in range(2):
            tile = corner[pl.ds(place + up * EDGE, EDGE)]
            rows = pl.ds(up * (wide - EDGE), EDGE)
            set_weight(keep, shifted, high * (nx + NEAR) + x, rows, pltpu.roll(tile, NEAR if up else WIDE, 0))
    outer = (groups[0], groups[-1])
    advance_side(first, field, EDGE - HEM, keep, shifted, 0, yp1, yq1, high, outer)
    outer = (*groups[:2], *groups[-2:])
    advance_side(second, first, EDGE, keep, shifted, 2, yp2, yq2, high, outer)
    last_rows(second, yp3, yq3, WIDE, high * (nx + 2 - WIDE))
    none = jnp.zeros((ny, nz), F32)
    yp3[high * (nx + 3)] = none
    yq3[high * (nx + 3)] = none
    totals = tuple(sums_in[place] for place in range(10))
    arrays = (field, keep, shifted, first, second, yp3, yq3)
    totals = list(add_sums(totals, arrays, WIDE + 1, high * (nx - WIDE - 1)))
    own = pl.ds(EDGE + HEM, ny)
    beside, edge, next_edge = 1 + high * (nx + 1), 2 + high * (nx - 1), 3 + high * (nx - 3)
    give = 13.0 * yq3[edge] - yp3[edge] + (yq3[next_edge] - yp3[next_edge])
    take = 13.0 * yq3[beside] - yp3[beside]
    totals[5] += SCALE * fold(second[beside - 1, own] * give - second[edge - 1, own] * take)
    if not last:
        for place, total in enumerate(totals):
            sums[place] = total
        return
    row = lax.broadcasted_iota(jnp.int32, (SUMS, nz), 0)
    lane = lax.broadcasted_iota(jnp.int32, (SUMS, nz), 1)
    lines = jnp.zeros((SUMS, nz), F32)
    for place, total in enumerate(totals):
        lines = jnp.where(row == place, jnp.sum(total, axis=0, keepdims=True), lines)
    pieces, rest = [], lines
    for _ in range(3):
        pieces.append(rest.astype(jnp.bfloat16))
        rest = rest - pieces[-1].astype(F32)
    ones = jnp.ones((nz, nz), jnp.bfloat16)
    whole_sums = jnp.dot(jnp.concatenate(pieces, axis=0), ones, preferred_element_type=F32)
    top, rest = two_sum(whole_sums[:SUMS], whole_sums[SUMS : 2 * SUMS])
    pair = two_sum(top, rest + whole_sums[2 * SUMS :])
    spot = jnp.where(lane == row, pair[0], jnp.where(lane == row + SUMS, pair[1], 0.0))
    sums[...] = jnp.sum(spot, axis=0, keepdims=True)


def two_sum(a, b):
    total = a + b
    part = total - a
    return total, (a - (total - part)) + (b - part)


def pair_add(a, b):
    total, rest = two_sum(a[0], b[0])
    return total, rest + (a[1] + b[1])


def halves(a):
    wide = 4097.0 * a
    top = wide - (wide - a)
    return top, a - top


def pair_mul(a, b):
    product = a[0] * b[0]
    a_top, a_rest = halves(a[0])
    b_top, b_rest = halves(b[0])
    rest = ((a_top * b_top - product) + a_top * b_rest + a_rest * b_top) + a_rest * b_rest
    rest = rest + (a[0] * b[1] + a[1] * b[0])
    total = product + rest
    return total, rest - (total - product)


def pair_sub(a, b):
    total, rest = two_sum(a[0], -b[0])
    rest = rest + (a[1] - b[1])
    out = total + rest
    return out, rest - (out - total)


def ratio(over, under, low, high):
    good = under > 0.0
    value = jnp.where(good, over / jnp.where(good, under, 1.0), 0.5 * (low + high))
    return jnp.minimum(jnp.maximum(value, low), high)


def coefficients(total):
    scale = 1.0 / total[0][0]
    zero = jnp.zeros_like(scale)
    g = [pair_mul(item, (scale, zero)) for item in total[:6]]
    shift = (jnp.full_like(scale, SHIFT), zero)
    h = [pair_add(g[k + 1], pair_mul(g[k], shift)) for k in range(5)]

    def minor(a, b, c, d):
        return pair_sub(pair_mul(a, b), pair_mul(c, d))

    s11 = minor(h[2], h[0], h[1], h[1])
    s12 = minor(h[3], h[0], h[1], h[2])
    s22 = minor(h[4], h[0], h[2], h[2])
    y1 = minor(g[1], h[0], h[1], g[0])
    y2 = minor(g[2], h[0], h[2], g[0])
    last = minor(s22, s11, s12, s12)
    side = minor(y2, s11, s12, y1)
    alpha = g[0][0] / h[0][0]
    l10 = h[1][0] / h[0][0]
    l20 = h[2][0] / h[0][0]
    l21 = ratio(s12[0], s11[0], l10 + (LOW - SHIFT), l10 + (HIGH - SHIFT))
    gamma1 = ratio(y1[0], s11[0], -alpha / LOW, -alpha / HIGH)
    gamma2 = ratio(side[0], last[0], -gamma1 / HIGH, -gamma1 / LOW)
    c1 = gamma1 - gamma2 * l21
    return alpha - c1 * l10 - gamma2 * l20, c1, gamma2


def sigmoid(value):
    return 1.0 / (1.0 + jnp.exp(-SHARP * value))


def finish_kernel(
    visible_hbm, parts, field, first, second, indicator_hbm, crossing_hbm,
    visible, indicator, crossing, level, weight, sem, slot_sems, result_sem,
):
    nx, ny, nz = indicator.shape
    copy = pltpu.make_async_copy(visible_hbm, visible, sem)
    copy.start()
    devices = parts.shape[0]
    tiles = [parts[pl.ds(8 * k, 8)] for k in range(devices // 8)]
    pairs = [(tile, pltpu.roll(tile, nz - SUMS, 1)) for tile in tiles]
    while len(pairs) > 1:
        pairs = [pair_add(a, b) for a, b in zip(pairs[::2], pairs[1::2])]
    total = pairs[0]
    for step in (4, 2, 1):
        total = pair_add(total, (pltpu.roll(total[0], step, 0), pltpu.roll(total[1], step, 0)))

    def spread(value, k):
        return jnp.broadcast_to(value[0:1, k : k + 1], (1, nz))

    item = [(spread(total[0], k), spread(total[1], k)) for k in range(10)]
    c0, c1, c2 = coefficients(item)
    over = c0 * (item[6][0] + item[6][1]) + c1 * (item[7][0] + item[7][1]) + c2 * (item[8][0] + item[8][1])
    iso = over / item[9][0]

    def set_level(x):
        v0 = field[x + WIDE, pl.ds(EDGE, ny + EDGE)]
        v1 = first[x + NEAR, pl.ds(EDGE + HEM, ny + HEM)]
        v2 = second[x + 1, pl.ds(EDGE + HEM, ny + HEM)]
        value = c0 * v0[: ny + HEM] + c1 * v1 + c2 * v2
        level[x, pl.ds(0, ny + HEM)] = sigmoid(value - iso)
        return value

    for x in range(nx):
        indicator[x] = set_level(x)[:ny]

    set_level(nx)
    result = pltpu.make_async_copy(indicator, indicator_hbm, result_sem)
    result.start()
    outside = sigmoid(-iso)
    lane = lax.broadcasted_iota(jnp.int32, (ny, nz), 1)

    for x in range(nx):
        here = level[x, pl.ds(0, ny)]
        above = jnp.where(lane < nz - 1, pltpu.roll(here, nz - 1, 1), outside)
        for edge, there in enumerate((level[x + 1, pl.ds(0, ny)], level[x, pl.ds(1, ny)], above)):
            value = here * (1.0 - there) + (1.0 - here) * there
            for row in range(0, ny, 8):
                turned = pltpu.roll(value[row : row + 8], 0, 1, stride=BLK, stride_axis=0)
                weight[edge, pl.ds(x * (ny + 1) + row, 8)] = turned

    chunk = lax.broadcasted_iota(jnp.int32, (8, nz), 1) // BLK
    bricks_z = nz // BLK
    per_row = nz // BLK

    copy.wait()

    def out(slot):
        return pltpu.make_async_copy(crossing.at[slot], crossing_hbm.at[slot], slot_sems.at[slot])

    for slot in range(visible.shape[0]):
        number = visible[slot]
        safe = jnp.maximum(number, 0)
        begin = (safe // bricks_z) * BLK
        column = safe % bricks_z
        spots = [chunk == lax.rem(column + row, per_row) for row in range(per_row)]
        turn = lax.rem(nz - column * BLK, nz)
        for edge in range(3):
            for half in range(2):
                for part in range(BLK // per_row):
                    at = half * 8 * (ny + 1) + begin + part * per_row
                    tile = weight[edge, pl.ds(at, 8, stride=ny + 1)]
                    for row in range(1, per_row):
                        lines = weight[edge, pl.ds(at + row, 8, stride=ny + 1)]
                        tile = jnp.where(spots[row], lines, tile)
                    tile = jnp.where(number >= 0, pltpu.roll(tile, turn, 1), 0.0)
                    crossing[slot, edge, pl.ds(half * 16 + part, 8, stride=2)] = tile
        out(slot).start()

    for slot in range(visible.shape[0]):
        out(slot).wait()
    result.wait()


def whole(*shape):
    return jax.ShapeDtypeStruct(shape, F32)


VMEM = pl.BlockSpec(memory_space=pltpu.VMEM)


HBM = pl.BlockSpec(memory_space=pltpu.HBM)


def kernel(body, inputs, outputs, scratch=(), results=VMEM, alias=None, flops=0):
    return pl.pallas_call(
        body,
        in_specs=list(inputs),
        out_specs=[results] * len(outputs),
        out_shape=list(outputs),
        scratch_shapes=list(scratch),
        input_output_aliases=alias or {},
        cost_estimate=pl.CostEstimate(flops=flops, bytes_accessed=flops // 4, transcendentals=0),
        compiler_params=pltpu.CompilerParams(vmem_limit_bytes=32 * 1024 * 1024),
    )


def in_hbm(value):
    return pltpu.with_memory_space_constraint(value, pltpu.HBM)


def swap(value, axis, first):
    count = lax.axis_size(axis)
    pairs = [(k, k + 1) for k in range(first, count - 1, 2)]
    return lax.ppermute(value, axis, pairs + [(b, a) for a, b in pairs])


def body(right_side, screening, active_blocks, visible_bricks):
    nx, ny, nz = right_side.shape
    active = active_blocks.reshape(-1)
    visible = visible_bricks.reshape(-1)
    devices = lax.axis_size("gx") * lax.axis_size("gy")
    slab = whole(nx, ny, nz)
    planes, near, third = nx + 2 * WIDE, nx + 2 * NEAR, nx + 2
    wide, rows = ny + 2 * EDGE, ny + 2 * HEM
    rim = whole(nx * EDGE, nz)
    edges = pltpu.VMEM((2, nx, EDGE, nz), F32)
    far, near_by, mask = kernel(
        pack_kernel,
        (HBM, HBM, HBM),
        (rim, rim, whole(ny, nz)),
        (pltpu.SMEM(active.shape, jnp.int32), edges, edges, pltpu.SemaphoreType.DMA((5,))),
    )(in_hbm(active), in_hbm(right_side), in_hbm(screening))
    far = swap(far, "gy", 1)
    near_by = swap(near_by, "gy", 0)
    straight, corners = (WIDE + NEAR) * ny, 2 * WIDE * EDGE
    side = whole(straight + corners, nz)
    field, weight, cross, chip = kernel(
        place_kernel,
        (VMEM,) * 3,
        (whole(planes, wide, nz), whole(nx, wide, nz), whole(straight + EXTRA, nz), side),
    )(mask, right_side, screening)
    cross = swap(cross, "gx", 1)
    chip, corner = kernel(widen_kernel, (VMEM,) * 3, (side, whole(corners, nz)), alias={2: 0})(far, near_by, chip)
    chip = swap(chip, "gx", 0)
    corner = swap(corner, "gx", 1)
    kept = [whole(planes, wide, nz)] + [whole(near, wide, nz)] * 2
    kept += [whole(near, rows + 2 * EDGE, nz), whole(third, rows + 2 * EDGE, nz)]
    kept += [whole(planes, rows, nz)] * 2 + [whole(near, rows, nz)] * 2 + [whole(third + 2, ny, nz)] * 2
    tallies = whole(10, 8, nz)
    held = kernel(inner_kernel, (VMEM,) * 4, kept + [tallies], alias={2: 0}, flops=INNER)(
        far, near_by, field, weight
    )
    for last, messages in ((False, (chip, chip)), (True, (cross, corner))):
        if last:
            *head, tally = held
            head = kernel(
                straight_kernel,
                (VMEM,) * (HELD + 1),
                kept,
                alias={1 + k: k for k in range(HELD)},
                flops=SIDE,
            )(cross, *head)
            held = [*head, tally]
        held = kernel(
            functools.partial(side_kernel, last),
            (VMEM,) * (HELD + 3),
            kept + [whole(1, nz) if last else tallies],
            alias={2 + k: k for k in range(HELD)},
            flops=SIDE,
        )(*messages, *held)
    field, _, _, first, second = held[:5]
    devices = lax.axis_size("gx") * lax.axis_size("gy")
    parts = lax.all_to_all(jnp.broadcast_to(held[-1], (devices, 1, nz)), ("gx", "gy"), 0, 0)
    slots = visible.shape[0]
    shape = (slots, 3, BLK**3 // nz, nz)
    indicator, crossing = kernel(
        finish_kernel,
        (HBM,) + (VMEM,) * 4,
        (slab, whole(*shape)),
        (
            pltpu.SMEM(visible.shape, jnp.int32),
            pltpu.VMEM(slab.shape, F32),
            pltpu.VMEM(shape, F32),
            pltpu.VMEM((nx + 1, ny + EDGE, nz), F32),
            pltpu.VMEM((3, nx * (ny + 1), nz), F32),
            pltpu.SemaphoreType.DMA,
            pltpu.SemaphoreType.DMA((slots,)),
            pltpu.SemaphoreType.DMA,
        ),
        results=HBM,
    )(in_hbm(visible), parts.reshape(devices, nz), field, first, second)
    return indicator, crossing.reshape(slots, 1, 3, BLK**3)


def solution(mesh):
    return jax.shard_map(
        body,
        mesh=mesh,
        in_specs=(
            P("gx", "gy", None),
            P("gx", "gy", None),
            P("gx", "gy", None),
            P("gx", "gy", None),
        ),
        out_specs=(P("gx", "gy", None), P("gx", "gy", None, None)),
        check_vma=False,
    )
```

```python
import functools

import jax
import jax.numpy as jnp
from jax import lax
from jax.experimental import pallas as pl
from jax.experimental.pallas import tpu as pltpu
from jax.sharding import PartitionSpec as P

BLK = 16
WIDE = 5
NEAR = 3
HEM = 4
EDGE = 8
SHARP = 4.0
SCALE = 1.0 / 86400.0
SHIFT = 2.0
LOW, HIGH = 0.5, 7.0
SUMS = 16
EXTRA, INNER, SIDE = 96, 0, 0
EARLY = 9
HELD = 11
F32 = jnp.float32


def mass(mid, one, two):
    return 66.0 * mid + (26.0 * one + two)


def stiff(mid, one, two):
    return 6.0 * mid - (2.0 * one + two)


def block_mask(active, slots, rows, columns):
    y = lax.broadcasted_iota(jnp.int32, (rows, columns), 0)
    z = lax.broadcasted_iota(jnp.int32, (rows, columns), 1)
    number = (y // BLK) * (columns // BLK) + z // BLK
    mask = jnp.zeros((rows, columns), F32)
    for slot in range(slots):
        mask = jnp.where(number == active[slot], 1.0, mask)
    return mask


def on_odd():
    return lax.rem(lax.axis_index("gx"), 2)


def odd_on(axis):
    return lax.rem(lax.axis_index(axis), 2)


def pack_kernel(active_hbm, right_hbm, screen_hbm, far, near, mask_out, active, right, screen, sems):
    nx, ny, nz = right_hbm.shape
    copies = [pltpu.make_async_copy(active_hbm, active, sems.at[0])]
    for k, (source, target) in enumerate(((right_hbm, right), (screen_hbm, screen))):
        for high in range(2):
            rows = pl.ds(high * (ny - EDGE), EDGE)
            copies.append(pltpu.make_async_copy(source.at[:, rows], target.at[high], sems.at[1 + 2 * k + high]))
    for copy in copies:
        copy.start()
    copies[0].wait()
    mask = block_mask(active, active.shape[0], ny, nz)
    mask_out[...] = mask
    row = lax.broadcasted_iota(jnp.int32, (EDGE, nz), 0)
    for copy in copies[1:]:
        copy.wait()

    def write(high_out, low_out):
        for x in range(nx):
            rows = pl.ds(x * EDGE, EDGE)
            low_out[rows] = jnp.where(row < WIDE, right[0, x], pltpu.roll(screen[0, x], WIDE, 0)) * mask[:EDGE]
            beside = pltpu.roll(screen[1, x] * mask[ny - EDGE :], NEAR, 0)
            high_out[rows] = jnp.where(row >= NEAR, right[1, x] * mask[ny - EDGE :], beside)

    odd = odd_on("gy")
    pl.when(odd == 1)(functools.partial(write, far, near))
    pl.when(odd == 0)(functools.partial(write, near, far))


def place_kernel(mask_in, right, screen, cross, chip, *arrays):
    field, keep, shifted = arrays[:3]
    nx, ny, nz = right.shape
    mask = mask_in[...]
    own = pl.ds(EDGE, ny)
    for x in range(nx):
        field[WIDE + x, own] = right[x] * mask
        set_weight(keep, shifted, NEAR + x, own, screen[x] * mask)
    odd = odd_on("gx")
    for target, high in ((cross, odd), (chip, 1 - odd)):
        for x in range(WIDE):
            target[x * ny : (x + 1) * ny] = right[high * (nx - WIDE) + x] * mask
        for x in range(NEAR):
            row = (WIDE + x) * ny
            target[row : row + ny] = screen[high * (nx - NEAR) + x] * mask
    groups = row_groups(field)
    pl.when(odd == 1)(functools.partial(own_powers, arrays, groups[1:-1], groups[2:-2]))


def row_groups(field):
    return range((field.shape[1] - 2 * EDGE + 2 * HEM) // 8)


def own_powers(arrays, groups, next_groups):
    field, keep, shifted, first, second, yp1, yq1, yp2, yq2 = arrays
    nx = field.shape[0] - 2 * WIDE
    advance(first, field, EDGE - HEM, keep, shifted, 0, yp1, yq1, nx, WIDE, groups)
    advance(second, first, EDGE, keep, shifted, 2, yp2, yq2, nx - 4, WIDE, next_groups)


def widen_kernel(far, near, chip_in, chip, corner):
    nx = far.shape[0] // EDGE
    base = chip.shape[0] - corner.shape[0]
    odd = odd_on("gx")

    def fill(low, high):
        for target, start, side in ((corner, 0, odd), (chip, base, 1 - odd)):
            for x in range(WIDE):
                tile = pl.ds((side * (nx - WIDE) + x) * EDGE, EDGE)
                row = start + 2 * x * EDGE
                target[row : row + EDGE] = low[tile]
                target[row + EDGE : row + 2 * EDGE] = high[tile]

    by_y(fill, far, near)


def by_y(action, far, near):
    odd = odd_on("gy")
    pl.when(odd == 1)(functools.partial(action, near, far))
    pl.when(odd == 0)(functools.partial(action, far, near))


def near_z(value):
    lane = lax.broadcasted_iota(jnp.int32, value.shape, 1)
    last = value.shape[1]

    def shifted(step):
        before = jnp.where(lane >= step, pltpu.roll(value, step, 1), 0.0)
        after = jnp.where(lane < last - step, pltpu.roll(value, last - step, 1), 0.0)
        return before + after

    return shifted(1), shifted(2)


def set_beside(field, x, keep, shifted, weight_x, tile, high):
    start = field.shape[1] - EDGE if high else 0
    field[x, start : start + EDGE] = tile
    if weight_x is not None:
        set_weight(keep, shifted, weight_x, pl.ds(start, EDGE), pltpu.roll(tile, NEAR if high else WIDE, 0))


def set_weight(keep, shifted, at, rows, weight):
    on = weight > 0.0
    keep[at, rows] = jnp.where(on, SCALE, 0.0)
    shifted[at, rows] = jnp.where(on, weight - SHIFT, 0.0)


def near_y(source, x, row, top, end):
    def part(step):
        return source[x, pl.ds(row + step, 8)]

    below, above = part(-2), part(2)
    place = lax.broadcasted_iota(jnp.int32, below.shape, 0)
    if top:
        below = jnp.where(place == 0, 0.0, jnp.where(place == 1, 2.0 * below, below))
    if end:
        above = jnp.where(place == 7, 0.0, jnp.where(place == 6, 2.0 * above, above))
    return part(0), part(-1) + part(1), below + above


def along_yz(source, x, row, top=False, end=False):
    here, one, two = near_y(source, x, row, top, end)
    heavy, stretched = mass(here, one, two), stiff(here, one, two)
    heavy_near, stretched_near = near_z(heavy), near_z(stretched)
    return mass(heavy, *heavy_near), stiff(heavy, *heavy_near) + mass(stretched, *stretched_near)


def across(window):
    p, q = zip(*window)
    return mass(q[2], q[1] + q[3], q[0] + q[4]) + stiff(p[2], p[1] + p[3], p[0] + p[4])


def power(target, source, row, keep, shifted, skip, x, group, window):
    rows, at = pl.ds(EDGE + 8 * group, 8), pl.ds(EDGE - HEM + 8 * group, 8)
    center = source[x + 2, pl.ds(row + 8 * group, 8)]
    target[x, rows] = keep[x + skip, at] * across(window) + shifted[x + skip, at] * center


def advance(target, source, row, keep, shifted, skip, yp, yq, count, first, groups):
    for group in groups:
        rows = pl.ds(8 * group, 8)
        window = []
        for x in range(first, first + count):
            p, q = along_yz(source, x, row + 8 * group)
            yp[x, rows] = p
            yq[x, rows] = q
            window = window[-4:] + [(p, q)]
            if len(window) == 5:
                power(target, source, row, keep, shifted, skip, x - 4, group, window)


def advance_side(target, source, row, keep, shifted, skip, yp, yq, high, groups):
    base = high * (target.shape[0] - WIDE)
    start = high * (source.shape[0] - WIDE)
    for group in groups:
        rows = pl.ds(8 * group, 8)
        for k in range(WIDE):
            p, q = along_yz(source, start + k, row + 8 * group)
            yp[start + k, rows] = p
            yq[start + k, rows] = q
    for group in groups:
        rows = pl.ds(8 * group, 8)
        window = [(yp[base + k, rows], yq[base + k, rows]) for k in range(WIDE + 4)]
        for k in range(WIDE):
            power(target, source, row, keep, shifted, skip, base + k, group, window[k : k + 5])


def last_rows(source, yp, yq, count, first):
    groups = yp.shape[1] // 8
    for group in range(groups):
        rows = pl.ds(8 * group, 8)
        for k in range(count):
            p, q = along_yz(source, first + k, EDGE + HEM + 8 * group, group == 0, group == groups - 1)
            yp[first + 1 + k, rows] = p
            yq[first + 1 + k, rows] = q


def fold(value):
    return jnp.sum(value.reshape(-1, 8, value.shape[1]), axis=0)


def add_each(left, right):
    return [a + b for a, b in zip(left, right)]


def add_sums(totals, arrays, count, first_x):
    field, keep, shifted, first, second, yp, yq = arrays
    parts = []
    for group in range(yp.shape[1] // 8):
        rows = pl.ds(8 * group, 8)
        mid, own = pl.ds(EDGE + 8 * group, 8), pl.ds(EDGE + HEM + 8 * group, 8)
        window = [(yp[first_x + k, rows], yq[first_x + k, rows]) for k in range(count + 4)]
        part = None
        for k in range(count):
            x = first_x + k
            v0 = field[x + WIDE, mid]
            v1 = first[x + NEAR, own]
            v2 = second[x + 1, own]
            form = v2 * (SCALE * across(window[k : k + 5]) + shifted[x + NEAR, mid] * v2)
            on = jnp.where(keep[x + NEAR, mid] > 0.0, 1.0, 0.0)
            new = (v0 * v0, v0 * v1, v1 * v1, v1 * v2, v2 * v2, form, v0, v1, v2, on)
            part = new if part is None else add_each(part, new)
        parts.append(part)
    while len(parts) > 1:
        parts = [add_each(*parts[k : k + 2]) for k in range(0, len(parts), 2)]
    return list(parts[0]) if totals is None else add_each(totals, parts[0])


def inner_kernel(far, near, *refs):
    arrays = refs[EARLY : 2 * EARLY]
    field, keep, shifted, first, second = arrays[:5]
    yp3, yq3, sums = refs[2 * EARLY :]
    nx = field.shape[0] - 2 * WIDE

    def fill(low, high):
        for x in range(nx):
            set_beside(field, WIDE + x, keep, shifted, NEAR + x, low[EDGE * x : EDGE * (x + 1)], False)
            set_beside(field, WIDE + x, keep, shifted, NEAR + x, high[EDGE * x : EDGE * (x + 1)], True)

    by_y(fill, far, near)
    odd, groups = odd_on("gx"), row_groups(field)
    rest = (groups[0], groups[-1]), (*groups[:2], *groups[-2:])
    pl.when(odd == 1)(functools.partial(own_powers, arrays, *rest))
    pl.when(odd == 0)(functools.partial(own_powers, arrays, groups, groups))
    last_rows(second, yp3, yq3, nx - 8, WIDE)
    arrays = (field, keep, shifted, first, second, yp3, yq3)
    totals = add_sums(None, arrays, nx - 12, WIDE + 1)
    for place, total in enumerate(totals):
        sums[place] = total


def place_message(message, high, held):
    field, keep, shifted = held[:3]
    nx, ny = field.shape[0] - 2 * WIDE, field.shape[1] - 2 * EDGE
    own = pl.ds(EDGE, ny)
    for x in range(WIDE):
        field[high * (nx + WIDE) + x, own] = message[x * ny : (x + 1) * ny]
    for x in range(NEAR):
        row = (WIDE + x) * ny
        set_weight(keep, shifted, high * (nx + NEAR) + x, own, message[row : row + ny])


def side_powers(held, high, groups, next_groups):
    field, keep, shifted, first, second, yp1, yq1, yp2, yq2 = held[:9]
    advance_side(first, field, EDGE - HEM, keep, shifted, 0, yp1, yq1, high, groups)
    advance_side(second, first, EDGE, keep, shifted, 2, yp2, yq2, high, next_groups)


def straight_kernel(message, *refs):
    held, high = refs[HELD:], odd_on("gx")
    groups = row_groups(held[0])
    place_message(message, high, held)
    side_powers(held, high, groups[1:-1], groups[2:-2])


def side_kernel(last, message, corner, *refs):
    sums_in = refs[HELD]
    held = refs[HELD + 1 :]
    field, keep, shifted, first, second, yp1, yq1, yp2, yq2, yp3, yq3, sums = held
    planes, wide, nz = field.shape
    nx, ny = planes - 2 * WIDE, wide - 2 * EDGE
    odd = odd_on("gx")
    high = odd if last else 1 - odd
    groups = row_groups(field)
    if not last:
        place_message(message, high, held)
    base = corner.shape[0] - 2 * WIDE * EDGE
    for x in range(WIDE):
        for up in range(2):
            row = base + (2 * x + up) * EDGE
            set_beside(field, high * (nx + WIDE) + x, keep, shifted, None, corner[row : row + EDGE], up == 1)
    for x in range(NEAR):
        place = base + (x + (1 - high) * (WIDE - NEAR)) * 2 * EDGE
        for up in range(2):
            tile = corner[pl.ds(place + up * EDGE, EDGE)]
            rows = pl.ds(up * (wide - EDGE), EDGE)
            set_weight(keep, shifted, high * (nx + NEAR) + x, rows, pltpu.roll(tile, NEAR if up else WIDE, 0))
    if last:
        side_powers(held, high, (groups[0], groups[-1]), (*groups[:2], *groups[-2:]))
    else:
        side_powers(held, high, groups, groups)
    last_rows(second, yp3, yq3, WIDE, high * (nx + 2 - WIDE))
    none = jnp.zeros((ny, nz), F32)
    yp3[high * (nx + 3)] = none
    yq3[high * (nx + 3)] = none
    totals = tuple(sums_in[place] for place in range(10))
    arrays = (field, keep, shifted, first, second, yp3, yq3)
    totals = list(add_sums(totals, arrays, WIDE + 1, high * (nx - WIDE - 1)))
    own = pl.ds(EDGE + HEM, ny)
    beside, edge, next_edge = 1 + high * (nx + 1), 2 + high * (nx - 1), 3 + high * (nx - 3)
    give = 13.0 * yq3[edge] - yp3[edge] + (yq3[next_edge] - yp3[next_edge])
    take = 13.0 * yq3[beside] - yp3[beside]
    totals[5] += SCALE * fold(second[beside - 1, own] * give - second[edge - 1, own] * take)
    if not last:
        for place, total in enumerate(totals):
            sums[place] = total
        return
    row = lax.broadcasted_iota(jnp.int32, (SUMS, nz), 0)
    lane = lax.broadcasted_iota(jnp.int32, (SUMS, nz), 1)
    lines = jnp.zeros((SUMS, nz), F32)
    for place, total in enumerate(totals):
        lines = jnp.where(row == place, jnp.sum(total, axis=0, keepdims=True), lines)
    pieces, rest = [], lines
    for _ in range(3):
        pieces.append(rest.astype(jnp.bfloat16))
        rest = rest - pieces[-1].astype(F32)
    ones = jnp.ones((nz, nz), jnp.bfloat16)
    whole_sums = jnp.dot(jnp.concatenate(pieces, axis=0), ones, preferred_element_type=F32)
    top, rest = two_sum(whole_sums[:SUMS], whole_sums[SUMS : 2 * SUMS])
    pair = two_sum(top, rest + whole_sums[2 * SUMS :])
    spot = jnp.where(lane == row, pair[0], jnp.where(lane == row + SUMS, pair[1], 0.0))
    sums[...] = jnp.sum(spot, axis=0, keepdims=True)


def two_sum(a, b):
    total = a + b
    part = total - a
    return total, (a - (total - part)) + (b - part)


def pair_add(a, b):
    total, rest = two_sum(a[0], b[0])
    return total, rest + (a[1] + b[1])


def halves(a):
    wide = 4097.0 * a
    top = wide - (wide - a)
    return top, a - top


def pair_mul(a, b):
    product = a[0] * b[0]
    a_top, a_rest = halves(a[0])
    b_top, b_rest = halves(b[0])
    rest = ((a_top * b_top - product) + a_top * b_rest + a_rest * b_top) + a_rest * b_rest
    rest = rest + (a[0] * b[1] + a[1] * b[0])
    total = product + rest
    return total, rest - (total - product)


def pair_sub(a, b):
    total, rest = two_sum(a[0], -b[0])
    rest = rest + (a[1] - b[1])
    out = total + rest
    return out, rest - (out - total)


def ratio(over, under, low, high):
    good = under > 0.0
    value = jnp.where(good, over / jnp.where(good, under, 1.0), 0.5 * (low + high))
    return jnp.minimum(jnp.maximum(value, low), high)


def coefficients(total):
    scale = 1.0 / total[0][0]
    zero = jnp.zeros_like(scale)
    g = [pair_mul(item, (scale, zero)) for item in total[:6]]
    shift = (jnp.full_like(scale, SHIFT), zero)
    h = [pair_add(g[k + 1], pair_mul(g[k], shift)) for k in range(5)]

    def minor(a, b, c, d):
        return pair_sub(pair_mul(a, b), pair_mul(c, d))

    s11 = minor(h[2], h[0], h[1], h[1])
    s12 = minor(h[3], h[0], h[1], h[2])
    s22 = minor(h[4], h[0], h[2], h[2])
    y1 = minor(g[1], h[0], h[1], g[0])
    y2 = minor(g[2], h[0], h[2], g[0])
    last = minor(s22, s11, s12, s12)
    side = minor(y2, s11, s12, y1)
    alpha = g[0][0] / h[0][0]
    l10 = h[1][0] / h[0][0]
    l20 = h[2][0] / h[0][0]
    l21 = ratio(s12[0], s11[0], l10 + (LOW - SHIFT), l10 + (HIGH - SHIFT))
    gamma1 = ratio(y1[0], s11[0], -alpha / LOW, -alpha / HIGH)
    gamma2 = ratio(side[0], last[0], -gamma1 / HIGH, -gamma1 / LOW)
    c1 = gamma1 - gamma2 * l21
    return alpha - c1 * l10 - gamma2 * l20, c1, gamma2


def sigmoid(value):
    return 1.0 / (1.0 + jnp.exp(-SHARP * value))


def finish_kernel(
    visible_hbm, parts, field, first, second, indicator_hbm, crossing_hbm,
    visible, indicator, crossing, level, weight, sem, slot_sems, result_sem,
):
    nx, ny, nz = indicator.shape
    copy = pltpu.make_async_copy(visible_hbm, visible, sem)
    copy.start()
    devices = parts.shape[0]
    tiles = [parts[pl.ds(8 * k, 8)] for k in range(devices // 8)]
    pairs = [(tile, pltpu.roll(tile, nz - SUMS, 1)) for tile in tiles]
    while len(pairs) > 1:
        pairs = [pair_add(a, b) for a, b in zip(pairs[::2], pairs[1::2])]
    total = pairs[0]
    for step in (4, 2, 1):
        total = pair_add(total, (pltpu.roll(total[0], step, 0), pltpu.roll(total[1], step, 0)))

    def spread(value, k):
        return jnp.broadcast_to(value[0:1, k : k + 1], (1, nz))

    item = [(spread(total[0], k), spread(total[1], k)) for k in range(10)]
    c0, c1, c2 = coefficients(item)
    over = c0 * (item[6][0] + item[6][1]) + c1 * (item[7][0] + item[7][1]) + c2 * (item[8][0] + item[8][1])
    iso = over / item[9][0]

    def set_level(x):
        v0 = field[x + WIDE, pl.ds(EDGE, ny + EDGE)]
        v1 = first[x + NEAR, pl.ds(EDGE + HEM, ny + HEM)]
        v2 = second[x + 1, pl.ds(EDGE + HEM, ny + HEM)]
        value = c0 * v0[: ny + HEM] + c1 * v1 + c2 * v2
        level[x, pl.ds(0, ny + HEM)] = sigmoid(value - iso)
        return value

    for x in range(nx):
        indicator[x] = set_level(x)[:ny]

    set_level(nx)
    result = pltpu.make_async_copy(indicator, indicator_hbm, result_sem)
    result.start()
    outside = sigmoid(-iso)
    lane = lax.broadcasted_iota(jnp.int32, (ny, nz), 1)

    for x in range(nx):
        here = level[x, pl.ds(0, ny)]
        above = jnp.where(lane < nz - 1, pltpu.roll(here, nz - 1, 1), outside)
        for edge, there in enumerate((level[x + 1, pl.ds(0, ny)], level[x, pl.ds(1, ny)], above)):
            value = here * (1.0 - there) + (1.0 - here) * there
            for row in range(0, ny, 8):
                turned = pltpu.roll(value[row : row + 8], 0, 1, stride=BLK, stride_axis=0)
                weight[edge, pl.ds(x * (ny + 1) + row, 8)] = turned

    chunk = lax.broadcasted_iota(jnp.int32, (8, nz), 1) // BLK
    bricks_z = nz // BLK
    per_row = nz // BLK

    copy.wait()

    def out(slot):
        return pltpu.make_async_copy(crossing.at[slot], crossing_hbm.at[slot], slot_sems.at[slot])

    for slot in range(visible.shape[0]):
        number = visible[slot]
        safe = jnp.maximum(number, 0)
        begin = (safe // bricks_z) * BLK
        column = safe % bricks_z
        spots = [chunk == lax.rem(column + row, per_row) for row in range(per_row)]
        turn = lax.rem(nz - column * BLK, nz)
        for edge in range(3):
            for half in range(2):
                for part in range(BLK // per_row):
                    at = half * 8 * (ny + 1) + begin + part * per_row
                    tile = weight[edge, pl.ds(at, 8, stride=ny + 1)]
                    for row in range(1, per_row):
                        lines = weight[edge, pl.ds(at + row, 8, stride=ny + 1)]
                        tile = jnp.where(spots[row], lines, tile)
                    tile = jnp.where(number >= 0, pltpu.roll(tile, turn, 1), 0.0)
                    crossing[slot, edge, pl.ds(half * 16 + part, 8, stride=2)] = tile
        out(slot).start()

    for slot in range(visible.shape[0]):
        out(slot).wait()
    result.wait()


def whole(*shape):
    return jax.ShapeDtypeStruct(shape, F32)


VMEM = pl.BlockSpec(memory_space=pltpu.VMEM)


HBM = pl.BlockSpec(memory_space=pltpu.HBM)


def kernel(body, inputs, outputs, scratch=(), results=VMEM, alias=None, flops=0):
    return pl.pallas_call(
        body,
        in_specs=list(inputs),
        out_specs=[results] * len(outputs),
        out_shape=list(outputs),
        scratch_shapes=list(scratch),
        input_output_aliases=alias or {},
        cost_estimate=pl.CostEstimate(flops=flops, bytes_accessed=flops // 4, transcendentals=0),
        compiler_params=pltpu.CompilerParams(vmem_limit_bytes=32 * 1024 * 1024),
    )


def in_hbm(value):
    return pltpu.with_memory_space_constraint(value, pltpu.HBM)


def swap(value, axis, first):
    count = lax.axis_size(axis)
    pairs = [(k, k + 1) for k in range(first, count - 1, 2)]
    return lax.ppermute(value, axis, pairs + [(b, a) for a, b in pairs])


def body(right_side, screening, active_blocks, visible_bricks):
    nx, ny, nz = right_side.shape
    active = active_blocks.reshape(-1)
    visible = visible_bricks.reshape(-1)
    devices = lax.axis_size("gx") * lax.axis_size("gy")
    slab = whole(nx, ny, nz)
    planes, near, third = nx + 2 * WIDE, nx + 2 * NEAR, nx + 2
    wide, rows = ny + 2 * EDGE, ny + 2 * HEM
    rim = whole(nx * EDGE, nz)
    edges = pltpu.VMEM((2, nx, EDGE, nz), F32)
    far, near_by, mask = kernel(
        pack_kernel,
        (HBM, HBM, HBM),
        (rim, rim, whole(ny, nz)),
        (pltpu.SMEM(active.shape, jnp.int32), edges, edges, pltpu.SemaphoreType.DMA((5,))),
    )(in_hbm(active), in_hbm(right_side), in_hbm(screening))
    far = swap(far, "gy", 1)
    near_by = swap(near_by, "gy", 0)
    straight, corners = (WIDE + NEAR) * ny, 2 * WIDE * EDGE
    side = whole(straight + corners, nz)
    kept = [whole(planes, wide, nz)] + [whole(near, wide, nz)] * 2
    kept += [whole(near, rows + 2 * EDGE, nz), whole(third, rows + 2 * EDGE, nz)]
    kept += [whole(planes, rows, nz)] * 2 + [whole(near, rows, nz)] * 2 + [whole(third + 2, ny, nz)] * 2
    arrays = kept[:EARLY]
    cross, chip, *held = kernel(
        place_kernel, (VMEM,) * 3, [whole(straight + EXTRA, nz), side] + arrays
    )(mask, right_side, screening)
    cross = swap(cross, "gx", 1)
    chip, corner = kernel(widen_kernel, (VMEM,) * 3, (side, whole(corners, nz)), alias={2: 0})(far, near_by, chip)
    chip = swap(chip, "gx", 0)
    corner = swap(corner, "gx", 1)
    tallies = whole(10, 8, nz)
    held = kernel(
        inner_kernel,
        (VMEM,) * (EARLY + 2),
        kept + [tallies],
        alias={2 + k: k for k in range(EARLY)},
        flops=INNER,
    )(far, near_by, *held)
    for last, messages in ((False, (chip, chip)), (True, (cross, corner))):
        if last:
            *head, tally = held
            head = kernel(
                straight_kernel,
                (VMEM,) * (HELD + 1),
                kept,
                alias={1 + k: k for k in range(HELD)},
                flops=SIDE,
            )(cross, *head)
            held = [*head, tally]
        held = kernel(
            functools.partial(side_kernel, last),
            (VMEM,) * (HELD + 3),
            kept + [whole(1, nz) if last else tallies],
            alias={2 + k: k for k in range(HELD)},
            flops=SIDE,
        )(*messages, *held)
    field, _, _, first, second = held[:5]
    devices = lax.axis_size("gx") * lax.axis_size("gy")
    parts = lax.all_to_all(jnp.broadcast_to(held[-1], (devices, 1, nz)), ("gx", "gy"), 0, 0)
    slots = visible.shape[0]
    shape = (slots, 3, BLK**3 // nz, nz)
    indicator, crossing = kernel(
        finish_kernel,
        (HBM,) + (VMEM,) * 4,
        (slab, whole(*shape)),
        (
            pltpu.SMEM(visible.shape, jnp.int32),
            pltpu.VMEM(slab.shape, F32),
            pltpu.VMEM(shape, F32),
            pltpu.VMEM((nx + 1, ny + EDGE, nz), F32),
            pltpu.VMEM((3, nx * (ny + 1), nz), F32),
            pltpu.SemaphoreType.DMA,
            pltpu.SemaphoreType.DMA((slots,)),
            pltpu.SemaphoreType.DMA,
        ),
        results=HBM,
    )(in_hbm(visible), parts.reshape(devices, nz), field, first, second)
    return indicator, crossing.reshape(slots, 1, 3, BLK**3)


def solution(mesh):
    return jax.shard_map(
        body,
        mesh=mesh,
        in_specs=(
            P("gx", "gy", None),
            P("gx", "gy", None),
            P("gx", "gy", None),
            P("gx", "gy", None),
        ),
        out_specs=(P("gx", "gy", None), P("gx", "gy", None, None)),
        check_vma=False,
    )
```

```python
import functools

import jax
import jax.numpy as jnp
from jax import lax
from jax.experimental import pallas as pl
from jax.experimental.pallas import tpu as pltpu
from jax.sharding import PartitionSpec as P

BLK = 16
WIDE = 5
NEAR = 3
HEM = 4
EDGE = 8
SHARP = 4.0
SCALE = 1.0 / 86400.0
SHIFT = 2.0
LOW, HIGH = 0.5, 7.0
SUMS = 16
EXTRA, INNER, SIDE = 96, 0, 0
HELD = 11
F32 = jnp.float32


def mass(mid, one, two):
    return 66.0 * mid + (26.0 * one + two)


def stiff(mid, one, two):
    return 6.0 * mid - (2.0 * one + two)


def block_mask(active, slots, rows, columns):
    y = lax.broadcasted_iota(jnp.int32, (rows, columns), 0)
    z = lax.broadcasted_iota(jnp.int32, (rows, columns), 1)
    number = (y // BLK) * (columns // BLK) + z // BLK
    mask = jnp.zeros((rows, columns), F32)
    for slot in range(slots):
        mask = jnp.where(number == active[slot], 1.0, mask)
    return mask


def on_odd():
    return lax.rem(lax.axis_index("gx"), 2)


def odd_on(axis):
    return lax.rem(lax.axis_index(axis), 2)


def pack_kernel(active_hbm, right_hbm, screen_hbm, far, near, mask_out, active, right, screen, sems):
    nx, ny, nz = right_hbm.shape
    copies = [pltpu.make_async_copy(active_hbm, active, sems.at[0])]
    for k, (source, target) in enumerate(((right_hbm, right), (screen_hbm, screen))):
        for high in range(2):
            rows = pl.ds(high * (ny - EDGE), EDGE)
            copies.append(pltpu.make_async_copy(source.at[:, rows], target.at[high], sems.at[1 + 2 * k + high]))
    for copy in copies:
        copy.start()
    copies[0].wait()
    mask = block_mask(active, active.shape[0], ny, nz)
    mask_out[...] = mask
    row = lax.broadcasted_iota(jnp.int32, (EDGE, nz), 0)
    for copy in copies[1:]:
        copy.wait()

    def write(high_out, low_out):
        for x in range(nx):
            rows = pl.ds(x * EDGE, EDGE)
            low_out[rows] = jnp.where(row < WIDE, right[0, x], pltpu.roll(screen[0, x], WIDE, 0)) * mask[:EDGE]
            beside = pltpu.roll(screen[1, x] * mask[ny - EDGE :], NEAR, 0)
            high_out[rows] = jnp.where(row >= NEAR, right[1, x] * mask[ny - EDGE :], beside)

    odd = odd_on("gy")
    pl.when(odd == 1)(functools.partial(write, far, near))
    pl.when(odd == 0)(functools.partial(write, near, far))


def place_kernel(mask_in, right, screen, field, weight, cross, chip):
    nx, ny, nz = right.shape
    mask = mask_in[...]
    own = pl.ds(EDGE, ny)
    for x in range(nx):
        field[WIDE + x, own] = right[x] * mask
        weight[x, own] = screen[x] * mask
    odd = odd_on("gx")
    for target, high in ((cross, odd), (chip, 1 - odd)):
        for x in range(WIDE):
            target[x * ny : (x + 1) * ny] = field[WIDE + high * (nx - WIDE) + x, own]
        for x in range(NEAR):
            row = (WIDE + x) * ny
            target[row : row + ny] = weight[high * (nx - NEAR) + x, own]


def widen_kernel(far, near, chip_in, chip, corner):
    nx = far.shape[0] // EDGE
    base = chip.shape[0] - corner.shape[0]
    odd = odd_on("gx")

    def fill(low, high):
        for target, start, side in ((corner, 0, odd), (chip, base, 1 - odd)):
            for x in range(WIDE):
                tile = pl.ds((side * (nx - WIDE) + x) * EDGE, EDGE)
                row = start + 2 * x * EDGE
                target[row : row + EDGE] = low[tile]
                target[row + EDGE : row + 2 * EDGE] = high[tile]

    by_y(fill, far, near)


def by_y(action, far, near):
    odd = odd_on("gy")
    pl.when(odd == 1)(functools.partial(action, near, far))
    pl.when(odd == 0)(functools.partial(action, far, near))


def near_z(value):
    lane = lax.broadcasted_iota(jnp.int32, value.shape, 1)
    last = value.shape[1]

    def shifted(step):
        before = jnp.where(lane >= step, pltpu.roll(value, step, 1), 0.0)
        after = jnp.where(lane < last - step, pltpu.roll(value, last - step, 1), 0.0)
        return before + after

    return shifted(1), shifted(2)


def set_beside(field, x, keep, shifted, weight_x, tile, high):
    start = field.shape[1] - EDGE if high else 0
    field[x, start : start + EDGE] = tile
    if weight_x is not None:
        set_weight(keep, shifted, weight_x, pl.ds(start, EDGE), pltpu.roll(tile, NEAR if high else WIDE, 0))


def set_weight(keep, shifted, at, rows, weight):
    on = weight > 0.0
    keep[at, rows] = jnp.where(on, SCALE, 0.0)
    shifted[at, rows] = jnp.where(on, weight - SHIFT, 0.0)


def near_y(source, x, row, top, end):
    def part(step):
        return source[x, pl.ds(row + step, 8)]

    below, above = part(-2), part(2)
    place = lax.broadcasted_iota(jnp.int32, below.shape, 0)
    if top:
        below = jnp.where(place == 0, 0.0, jnp.where(place == 1, 2.0 * below, below))
    if end:
        above = jnp.where(place == 7, 0.0, jnp.where(place == 6, 2.0 * above, above))
    return part(0), part(-1) + part(1), below + above


def along_yz(source, x, row, top=False, end=False):
    here, one, two = near_y(source, x, row, top, end)
    heavy, stretched = mass(here, one, two), stiff(here, one, two)
    heavy_near, stretched_near = near_z(heavy), near_z(stretched)
    return mass(heavy, *heavy_near), stiff(heavy, *heavy_near) + mass(stretched, *stretched_near)


def across(window):
    p, q = zip(*window)
    return mass(q[2], q[1] + q[3], q[0] + q[4]) + stiff(p[2], p[1] + p[3], p[0] + p[4])


def power(target, source, row, keep, shifted, skip, x, group, window):
    rows, at = pl.ds(EDGE + 8 * group, 8), pl.ds(EDGE - HEM + 8 * group, 8)
    center = source[x + 2, pl.ds(row + 8 * group, 8)]
    target[x, rows] = keep[x + skip, at] * across(window) + shifted[x + skip, at] * center


def advance(target, source, row, keep, shifted, skip, yp, yq, count, first):
    for group in range(target.shape[1] // 8 - 2):
        rows = pl.ds(8 * group, 8)
        window = []
        for x in range(first, first + count):
            p, q = along_yz(source, x, row + 8 * group)
            yp[x, rows] = p
            yq[x, rows] = q
            window = window[-4:] + [(p, q)]
            if len(window) == 5:
                power(target, source, row, keep, shifted, skip, x - 4, group, window)


def advance_side(target, source, row, keep, shifted, skip, yp, yq, high):
    groups = target.shape[1] // 8 - 2
    base = high * (target.shape[0] - WIDE)
    start = high * (source.shape[0] - WIDE)
    for group in range(groups):
        rows = pl.ds(8 * group, 8)
        for k in range(WIDE):
            p, q = along_yz(source, start + k, row + 8 * group)
            yp[start + k, rows] = p
            yq[start + k, rows] = q
    for group in range(groups):
        rows = pl.ds(8 * group, 8)
        window = [(yp[base + k, rows], yq[base + k, rows]) for k in range(WIDE + 4)]
        for k in range(WIDE):
            power(target, source, row, keep, shifted, skip, base + k, group, window[k : k + 5])


def last_rows(source, yp, yq, count, first):
    groups = yp.shape[1] // 8
    for group in range(groups):
        rows = pl.ds(8 * group, 8)
        for k in range(count):
            p, q = along_yz(source, first + k, EDGE + HEM + 8 * group, group == 0, group == groups - 1)
            yp[first + 1 + k, rows] = p
            yq[first + 1 + k, rows] = q


def fold(value):
    return jnp.sum(value.reshape(-1, 8, value.shape[1]), axis=0)


def add_each(left, right):
    return [a + b for a, b in zip(left, right)]


def add_sums(totals, arrays, count, first_x):
    field, keep, shifted, first, second, yp, yq = arrays
    parts = []
    for group in range(yp.shape[1] // 8):
        rows = pl.ds(8 * group, 8)
        mid, own = pl.ds(EDGE + 8 * group, 8), pl.ds(EDGE + HEM + 8 * group, 8)
        window = [(yp[first_x + k, rows], yq[first_x + k, rows]) for k in range(count + 4)]
        part = None
        for k in range(count):
            x = first_x + k
            v0 = field[x + WIDE, mid]
            v1 = first[x + NEAR, own]
            v2 = second[x + 1, own]
            form = v2 * (SCALE * across(window[k : k + 5]) + shifted[x + NEAR, mid] * v2)
            on = jnp.where(keep[x + NEAR, mid] > 0.0, 1.0, 0.0)
            new = (v0 * v0, v0 * v1, v1 * v1, v1 * v2, v2 * v2, form, v0, v1, v2, on)
            part = new if part is None else add_each(part, new)
        parts.append(part)
    while len(parts) > 1:
        parts = [add_each(*parts[k : k + 2]) for k in range(0, len(parts), 2)]
    return list(parts[0]) if totals is None else add_each(totals, parts[0])


def inner_kernel(
    far, near, field_in, weight, field, keep, shifted, first, second, yp1, yq1, yp2, yq2, yp3, yq3, sums
):
    nx, wide, nz = weight.shape
    ny = wide - 2 * EDGE

    def fill(low, high):
        for x in range(nx):
            set_beside(field, WIDE + x, keep, shifted, NEAR + x, low[EDGE * x : EDGE * (x + 1)], False)
            set_beside(field, WIDE + x, keep, shifted, NEAR + x, high[EDGE * x : EDGE * (x + 1)], True)

    by_y(fill, far, near)
    own = pl.ds(EDGE, ny)
    for x in range(nx):
        set_weight(keep, shifted, NEAR + x, own, weight[x, own])
    advance(first, field, EDGE - HEM, keep, shifted, 0, yp1, yq1, nx, WIDE)
    advance(second, first, EDGE, keep, shifted, 2, yp2, yq2, nx - 4, WIDE)
    last_rows(second, yp3, yq3, nx - 8, WIDE)
    arrays = (field, keep, shifted, first, second, yp3, yq3)
    totals = add_sums(None, arrays, nx - 12, WIDE + 1)
    for place, total in enumerate(totals):
        sums[place] = total


def side_kernel(last, message, corner, *refs):
    sums_in = refs[HELD]
    field, keep, shifted, first, second, yp1, yq1, yp2, yq2, yp3, yq3, sums = refs[HELD + 1 :]
    planes, wide, nz = field.shape
    nx, ny = planes - 2 * WIDE, wide - 2 * EDGE
    odd = odd_on("gx")
    high = odd if last else 1 - odd
    own = pl.ds(EDGE, ny)
    base = corner.shape[0] - 2 * WIDE * EDGE
    for x in range(WIDE):
        plane = high * (nx + WIDE) + x
        field[plane, own] = message[x * ny : (x + 1) * ny]
        for up in range(2):
            row = base + (2 * x + up) * EDGE
            set_beside(field, plane, keep, shifted, None, corner[row : row + EDGE], up == 1)
    for x in range(NEAR):
        plane = high * (nx + NEAR) + x
        row = (WIDE + x) * ny
        set_weight(keep, shifted, plane, own, message[row : row + ny])
        place = base + (x + (1 - high) * (WIDE - NEAR)) * 2 * EDGE
        for up in range(2):
            tile = corner[pl.ds(place + up * EDGE, EDGE)]
            rows = pl.ds(up * (wide - EDGE), EDGE)
            set_weight(keep, shifted, plane, rows, pltpu.roll(tile, NEAR if up else WIDE, 0))
    advance_side(first, field, EDGE - HEM, keep, shifted, 0, yp1, yq1, high)
    advance_side(second, first, EDGE, keep, shifted, 2, yp2, yq2, high)
    last_rows(second, yp3, yq3, WIDE, high * (nx + 2 - WIDE))
    none = jnp.zeros((ny, nz), F32)
    yp3[high * (nx + 3)] = none
    yq3[high * (nx + 3)] = none
    totals = tuple(sums_in[place] for place in range(10))
    arrays = (field, keep, shifted, first, second, yp3, yq3)
    totals = list(add_sums(totals, arrays, WIDE + 1, high * (nx - WIDE - 1)))
    own = pl.ds(EDGE + HEM, ny)
    beside, edge, next_edge = 1 + high * (nx + 1), 2 + high * (nx - 1), 3 + high * (nx - 3)
    give = 13.0 * yq3[edge] - yp3[edge] + (yq3[next_edge] - yp3[next_edge])
    take = 13.0 * yq3[beside] - yp3[beside]
    totals[5] += SCALE * fold(second[beside - 1, own] * give - second[edge - 1, own] * take)
    if not last:
        for place, total in enumerate(totals):
            sums[place] = total
        return
    row = lax.broadcasted_iota(jnp.int32, (SUMS, nz), 0)
    lane = lax.broadcasted_iota(jnp.int32, (SUMS, nz), 1)
    lines = jnp.zeros((SUMS, nz), F32)
    for place, total in enumerate(totals):
        lines = jnp.where(row == place, jnp.sum(total, axis=0, keepdims=True), lines)
    pieces, rest = [], lines
    for _ in range(3):
        pieces.append(rest.astype(jnp.bfloat16))
        rest = rest - pieces[-1].astype(F32)
    ones = jnp.ones((nz, nz), jnp.bfloat16)
    whole_sums = jnp.dot(jnp.concatenate(pieces, axis=0), ones, preferred_element_type=F32)
    top, rest = two_sum(whole_sums[:SUMS], whole_sums[SUMS : 2 * SUMS])
    pair = two_sum(top, rest + whole_sums[2 * SUMS :])
    spot = jnp.where(lane == row, pair[0], jnp.where(lane == row + SUMS, pair[1], 0.0))
    sums[...] = jnp.sum(spot, axis=0, keepdims=True)


def two_sum(a, b):
    total = a + b
    part = total - a
    return total, (a - (total - part)) + (b - part)


def pair_add(a, b):
    total, rest = two_sum(a[0], b[0])
    return total, rest + (a[1] + b[1])


def halves(a):
    wide = 4097.0 * a
    top = wide - (wide - a)
    return top, a - top


def pair_mul(a, b):
    product = a[0] * b[0]
    a_top, a_rest = halves(a[0])
    b_top, b_rest = halves(b[0])
    rest = ((a_top * b_top - product) + a_top * b_rest + a_rest * b_top) + a_rest * b_rest
    rest = rest + (a[0] * b[1] + a[1] * b[0])
    total = product + rest
    return total, rest - (total - product)


def pair_sub(a, b):
    total, rest = two_sum(a[0], -b[0])
    rest = rest + (a[1] - b[1])
    out = total + rest
    return out, rest - (out - total)


def ratio(over, under, low, high):
    good = under > 0.0
    value = jnp.where(good, over / jnp.where(good, under, 1.0), 0.5 * (low + high))
    return jnp.minimum(jnp.maximum(value, low), high)


def coefficients(total):
    scale = 1.0 / total[0][0]
    zero = jnp.zeros_like(scale)
    g = [pair_mul(item, (scale, zero)) for item in total[:6]]
    shift = (jnp.full_like(scale, SHIFT), zero)
    h = [pair_add(g[k + 1], pair_mul(g[k], shift)) for k in range(5)]

    def minor(a, b, c, d):
        return pair_sub(pair_mul(a, b), pair_mul(c, d))

    s11 = minor(h[2], h[0], h[1], h[1])
    s12 = minor(h[3], h[0], h[1], h[2])
    s22 = minor(h[4], h[0], h[2], h[2])
    y1 = minor(g[1], h[0], h[1], g[0])
    y2 = minor(g[2], h[0], h[2], g[0])
    last = minor(s22, s11, s12, s12)
    side = minor(y2, s11, s12, y1)
    alpha = g[0][0] / h[0][0]
    l10 = h[1][0] / h[0][0]
    l20 = h[2][0] / h[0][0]
    l21 = ratio(s12[0], s11[0], l10 + (LOW - SHIFT), l10 + (HIGH - SHIFT))
    gamma1 = ratio(y1[0], s11[0], -alpha / LOW, -alpha / HIGH)
    gamma2 = ratio(side[0], last[0], -gamma1 / HIGH, -gamma1 / LOW)
    c1 = gamma1 - gamma2 * l21
    return alpha - c1 * l10 - gamma2 * l20, c1, gamma2


def sigmoid(value):
    return 1.0 / (1.0 + jnp.exp(-SHARP * value))


def finish_kernel(
    visible_hbm, parts, field, first, second, indicator_hbm, crossing_hbm,
    visible, indicator, crossing, level, weight, sem, slot_sems, result_sem,
):
    nx, ny, nz = indicator.shape
    copy = pltpu.make_async_copy(visible_hbm, visible, sem)
    copy.start()
    devices = parts.shape[0]
    tiles = [parts[pl.ds(8 * k, 8)] for k in range(devices // 8)]
    pairs = [(tile, pltpu.roll(tile, nz - SUMS, 1)) for tile in tiles]
    while len(pairs) > 1:
        pairs = [pair_add(a, b) for a, b in zip(pairs[::2], pairs[1::2])]
    total = pairs[0]
    for step in (4, 2, 1):
        total = pair_add(total, (pltpu.roll(total[0], step, 0), pltpu.roll(total[1], step, 0)))

    def spread(value, k):
        return jnp.broadcast_to(value[0:1, k : k + 1], (1, nz))

    item = [(spread(total[0], k), spread(total[1], k)) for k in range(10)]
    c0, c1, c2 = coefficients(item)
    over = c0 * (item[6][0] + item[6][1]) + c1 * (item[7][0] + item[7][1]) + c2 * (item[8][0] + item[8][1])
    iso = over / item[9][0]

    def set_level(x):
        v0 = field[x + WIDE, pl.ds(EDGE, ny + EDGE)]
        v1 = first[x + NEAR, pl.ds(EDGE + HEM, ny + EDGE)]
        v2 = second[x + 1, pl.ds(EDGE + HEM, ny + EDGE)]
        value = c0 * v0 + c1 * v1 + c2 * v2
        here = sigmoid(value - iso)
        for row in range(0, ny + EDGE, 8):
            level[x, row : row + 8] = pltpu.roll(here[row : row + 8], 0, 1, stride=BLK, stride_axis=0)
        return value

    for x in range(nx):
        indicator[x] = set_level(x)[:ny]

    set_level(nx)
    result = pltpu.make_async_copy(indicator, indicator_hbm, result_sem)
    result.start()
    outside = sigmoid(-iso)
    lane = lax.broadcasted_iota(jnp.int32, (8, nz), 1)
    end = lane == lax.rem(nz - 1 + BLK * lax.broadcasted_iota(jnp.int32, (8, nz), 0), nz)

    for x in range(nx):
        for row in range(0, ny, 8):
            here = level[x, row : row + 8]
            beside = pltpu.roll(level[x, row + 1 : row + 9], nz - BLK, 1)
            above = jnp.where(end, outside, pltpu.roll(here, nz - 1, 1))
            for edge, there in enumerate((level[x + 1, row : row + 8], beside, above)):
                value = here * (1.0 - there) + (1.0 - here) * there
                weight[edge, pl.ds(x * (ny + 1) + row, 8)] = value

    chunk = lax.broadcasted_iota(jnp.int32, (8, nz), 1) // BLK
    bricks_z = nz // BLK
    per_row = nz // BLK

    copy.wait()

    def out(slot):
        return pltpu.make_async_copy(crossing.at[slot], crossing_hbm.at[slot], slot_sems.at[slot])

    for slot in range(visible.shape[0]):
        number = visible[slot]
        safe = jnp.maximum(number, 0)
        begin = (safe // bricks_z) * BLK
        column = safe % bricks_z
        spots = [chunk == lax.rem(column + row, per_row) for row in range(per_row)]
        turn = lax.rem(nz - column * BLK, nz)
        for edge in range(3):
            for half in range(2):
                for part in range(BLK // per_row):
                    at = half * 8 * (ny + 1) + begin + part * per_row
                    tile = weight[edge, pl.ds(at, 8, stride=ny + 1)]
                    for row in range(1, per_row):
                        lines = weight[edge, pl.ds(at + row, 8, stride=ny + 1)]
                        tile = jnp.where(spots[row], lines, tile)
                    tile = jnp.where(number >= 0, pltpu.roll(tile, turn, 1), 0.0)
                    crossing[slot, edge, pl.ds(half * 16 + part, 8, stride=2)] = tile
        out(slot).start()

    for slot in range(visible.shape[0]):
        out(slot).wait()
    result.wait()


def whole(*shape):
    return jax.ShapeDtypeStruct(shape, F32)


VMEM = pl.BlockSpec(memory_space=pltpu.VMEM)


HBM = pl.BlockSpec(memory_space=pltpu.HBM)


def kernel(body, inputs, outputs, scratch=(), results=VMEM, alias=None, flops=0):
    return pl.pallas_call(
        body,
        in_specs=list(inputs),
        out_specs=[results] * len(outputs),
        out_shape=list(outputs),
        scratch_shapes=list(scratch),
        input_output_aliases=alias or {},
        cost_estimate=pl.CostEstimate(flops=flops, bytes_accessed=flops // 4, transcendentals=0),
        compiler_params=pltpu.CompilerParams(vmem_limit_bytes=32 * 1024 * 1024),
    )


def in_hbm(value):
    return pltpu.with_memory_space_constraint(value, pltpu.HBM)


def swap(value, axis, first):
    count = lax.axis_size(axis)
    pairs = [(k, k + 1) for k in range(first, count - 1, 2)]
    return lax.ppermute(value, axis, pairs + [(b, a) for a, b in pairs])


def body(right_side, screening, active_blocks, visible_bricks):
    nx, ny, nz = right_side.shape
    active = active_blocks.reshape(-1)
    visible = visible_bricks.reshape(-1)
    devices = lax.axis_size("gx") * lax.axis_size("gy")
    slab = whole(nx, ny, nz)
    planes, near, third = nx + 2 * WIDE, nx + 2 * NEAR, nx + 2
    wide, rows = ny + 2 * EDGE, ny + 2 * HEM
    rim = whole(nx * EDGE, nz)
    edges = pltpu.VMEM((2, nx, EDGE, nz), F32)
    far, near_by, mask = kernel(
        pack_kernel,
        (HBM, HBM, HBM),
        (rim, rim, whole(ny, nz)),
        (pltpu.SMEM(active.shape, jnp.int32), edges, edges, pltpu.SemaphoreType.DMA((5,))),
    )(in_hbm(active), in_hbm(right_side), in_hbm(screening))
    far = swap(far, "gy", 1)
    near_by = swap(near_by, "gy", 0)
    straight, corners = (WIDE + NEAR) * ny, 2 * WIDE * EDGE
    side = whole(straight + corners, nz)
    field, weight, cross, chip = kernel(
        place_kernel,
        (VMEM,) * 3,
        (whole(planes, wide, nz), whole(nx, wide, nz), whole(straight + EXTRA, nz), side),
    )(mask, right_side, screening)
    cross = swap(cross, "gx", 1)
    chip, corner = kernel(widen_kernel, (VMEM,) * 3, (side, whole(corners, nz)), alias={2: 0})(far, near_by, chip)
    chip = swap(chip, "gx", 0)
    corner = swap(corner, "gx", 1)
    kept = [whole(planes, wide, nz)] + [whole(near, wide, nz)] * 2
    kept += [whole(near, rows + 2 * EDGE, nz), whole(third, rows + 2 * EDGE, nz)]
    kept += [whole(planes, rows, nz)] * 2 + [whole(near, rows, nz)] * 2 + [whole(third + 2, ny, nz)] * 2
    tallies = whole(10, 8, nz)
    held = kernel(inner_kernel, (VMEM,) * 4, kept + [tallies], alias={2: 0}, flops=INNER)(
        far, near_by, field, weight
    )
    for last, messages in ((False, (chip, chip)), (True, (cross, corner))):
        held = kernel(
            functools.partial(side_kernel, last),
            (VMEM,) * (HELD + 3),
            kept + [whole(1, nz) if last else tallies],
            alias={2 + k: k for k in range(HELD)},
            flops=SIDE,
        )(*messages, *held)
    field, _, _, first, second = held[:5]
    devices = lax.axis_size("gx") * lax.axis_size("gy")
    parts = lax.all_to_all(jnp.broadcast_to(held[-1], (devices, 1, nz)), ("gx", "gy"), 0, 0)
    slots = visible.shape[0]
    shape = (slots, 3, BLK**3 // nz, nz)
    indicator, crossing = kernel(
        finish_kernel,
        (HBM,) + (VMEM,) * 4,
        (slab, whole(*shape)),
        (
            pltpu.SMEM(visible.shape, jnp.int32),
            pltpu.VMEM(slab.shape, F32),
            pltpu.VMEM(shape, F32),
            pltpu.VMEM((nx + 1, ny + EDGE, nz), F32),
            pltpu.VMEM((3, nx * (ny + 1), nz), F32),
            pltpu.SemaphoreType.DMA,
            pltpu.SemaphoreType.DMA((slots,)),
            pltpu.SemaphoreType.DMA,
        ),
        results=HBM,
    )(in_hbm(visible), parts.reshape(devices, nz), field, first, second)
    return indicator, crossing.reshape(slots, 1, 3, BLK**3)


def solution(mesh):
    return jax.shard_map(
        body,
        mesh=mesh,
        in_specs=(
            P("gx", "gy", None),
            P("gx", "gy", None),
            P("gx", "gy", None),
            P("gx", "gy", None),
        ),
        out_specs=(P("gx", "gy", None), P("gx", "gy", None, None)),
        check_vma=False,
    )
```

```python
import functools

import jax
import jax.numpy as jnp
from jax import lax
from jax.experimental import pallas as pl
from jax.experimental.pallas import tpu as pltpu
from jax.sharding import PartitionSpec as P

BLK = 16
WIDE = 5
NEAR = 3
HEM = 4
EDGE = 8
SHARP = 4.0
SCALE = 1.0 / 86400.0
SHIFT = 2.0
LOW, HIGH = 0.5, 7.0
SUMS = 16
EXTRA, INNER, SIDE = 96, 0, 0
HELD = 11
F32 = jnp.float32


def mass(mid, one, two):
    return 66.0 * mid + (26.0 * one + two)


def stiff(mid, one, two):
    return 6.0 * mid - (2.0 * one + two)


def block_mask(active, slots, rows, columns):
    y = lax.broadcasted_iota(jnp.int32, (rows, columns), 0)
    z = lax.broadcasted_iota(jnp.int32, (rows, columns), 1)
    number = (y // BLK) * (columns // BLK) + z // BLK
    mask = jnp.zeros((rows, columns), F32)
    for slot in range(slots):
        mask = jnp.where(number == active[slot], 1.0, mask)
    return mask


def on_odd():
    return lax.rem(lax.axis_index("gx"), 2)


def odd_on(axis):
    return lax.rem(lax.axis_index(axis), 2)


def pack_kernel(active_hbm, right_hbm, screen_hbm, far, near, mask_out, active, right, screen, sems):
    nx, ny, nz = right_hbm.shape
    copies = [pltpu.make_async_copy(active_hbm, active, sems.at[0])]
    for k, (source, target) in enumerate(((right_hbm, right), (screen_hbm, screen))):
        for high in range(2):
            rows = pl.ds(high * (ny - EDGE), EDGE)
            copies.append(pltpu.make_async_copy(source.at[:, rows], target.at[high], sems.at[1 + 2 * k + high]))
    for copy in copies:
        copy.start()
    copies[0].wait()
    mask = block_mask(active, active.shape[0], ny, nz)
    mask_out[...] = mask
    row = lax.broadcasted_iota(jnp.int32, (EDGE, nz), 0)
    for copy in copies[1:]:
        copy.wait()

    def write(high_out, low_out):
        for x in range(nx):
            rows = pl.ds(x * EDGE, EDGE)
            low_out[rows] = jnp.where(row < WIDE, right[0, x], pltpu.roll(screen[0, x], WIDE, 0)) * mask[:EDGE]
            beside = pltpu.roll(screen[1, x] * mask[ny - EDGE :], NEAR, 0)
            high_out[rows] = jnp.where(row >= NEAR, right[1, x] * mask[ny - EDGE :], beside)

    odd = odd_on("gy")
    pl.when(odd == 1)(functools.partial(write, far, near))
    pl.when(odd == 0)(functools.partial(write, near, far))


def place_kernel(mask_in, right, screen, field, weight, cross, chip):
    nx, ny, nz = right.shape
    mask = mask_in[...]
    own = pl.ds(EDGE, ny)
    for x in range(nx):
        field[WIDE + x, own] = right[x] * mask
        weight[x, own] = screen[x] * mask
    odd = odd_on("gx")
    for target, high in ((cross, odd), (chip, 1 - odd)):
        for x in range(WIDE):
            target[x * ny : (x + 1) * ny] = field[WIDE + high * (nx - WIDE) + x, own]
        for x in range(NEAR):
            row = (WIDE + x) * ny
            target[row : row + ny] = weight[high * (nx - NEAR) + x, own]


def widen_kernel(far, near, chip_in, chip, corner):
    nx = far.shape[0] // EDGE
    base = chip.shape[0] - corner.shape[0]
    odd = odd_on("gx")

    def fill(low, high):
        for target, start, side in ((corner, 0, odd), (chip, base, 1 - odd)):
            for x in range(WIDE):
                tile = pl.ds((side * (nx - WIDE) + x) * EDGE, EDGE)
                row = start + 2 * x * EDGE
                target[row : row + EDGE] = low[tile]
                target[row + EDGE : row + 2 * EDGE] = high[tile]

    by_y(fill, far, near)


def by_y(action, far, near):
    odd = odd_on("gy")
    pl.when(odd == 1)(functools.partial(action, near, far))
    pl.when(odd == 0)(functools.partial(action, far, near))


def near_z(value):
    lane = lax.broadcasted_iota(jnp.int32, value.shape, 1)
    last = value.shape[1]

    def shifted(step):
        before = jnp.where(lane >= step, pltpu.roll(value, step, 1), 0.0)
        after = jnp.where(lane < last - step, pltpu.roll(value, last - step, 1), 0.0)
        return before + after

    return shifted(1), shifted(2)


def set_beside(field, x, keep, shifted, weight_x, tile, high):
    start = field.shape[1] - EDGE if high else 0
    field[x, start : start + EDGE] = tile
    if weight_x is not None:
        set_weight(keep, shifted, weight_x, pl.ds(start, EDGE), pltpu.roll(tile, NEAR if high else WIDE, 0))


def set_weight(keep, shifted, at, rows, weight):
    on = weight > 0.0
    keep[at, rows] = jnp.where(on, SCALE, 0.0)
    shifted[at, rows] = jnp.where(on, weight - SHIFT, 0.0)


def near_y(source, x, row, top, end):
    def part(step):
        return source[x, pl.ds(row + step, 8)]

    below, above = part(-2), part(2)
    place = lax.broadcasted_iota(jnp.int32, below.shape, 0)
    if top:
        below = jnp.where(place == 0, 0.0, jnp.where(place == 1, 2.0 * below, below))
    if end:
        above = jnp.where(place == 7, 0.0, jnp.where(place == 6, 2.0 * above, above))
    return part(0), part(-1) + part(1), below + above


def along_yz(source, x, row, top=False, end=False):
    here, one, two = near_y(source, x, row, top, end)
    heavy, stretched = mass(here, one, two), stiff(here, one, two)
    heavy_near, stretched_near = near_z(heavy), near_z(stretched)
    return mass(heavy, *heavy_near), stiff(heavy, *heavy_near) + mass(stretched, *stretched_near)


def across(window):
    p, q = zip(*window)
    return mass(q[2], q[1] + q[3], q[0] + q[4]) + stiff(p[2], p[1] + p[3], p[0] + p[4])


def power(target, source, row, keep, shifted, skip, x, group, window):
    rows, at = pl.ds(EDGE + 8 * group, 8), pl.ds(EDGE - HEM + 8 * group, 8)
    center = source[x + 2, pl.ds(row + 8 * group, 8)]
    target[x, rows] = keep[x + skip, at] * across(window) + shifted[x + skip, at] * center


def advance(target, source, row, keep, shifted, skip, yp, yq, count, first):
    for group in range(target.shape[1] // 8 - 2):
        rows = pl.ds(8 * group, 8)
        window = []
        for x in range(first, first + count):
            p, q = along_yz(source, x, row + 8 * group)
            yp[x, rows] = p
            yq[x, rows] = q
            window = window[-4:] + [(p, q)]
            if len(window) == 5:
                power(target, source, row, keep, shifted, skip, x - 4, group, window)


def advance_side(target, source, row, keep, shifted, skip, yp, yq, high):
    groups = target.shape[1] // 8 - 2
    base = high * (target.shape[0] - WIDE)
    start = high * (source.shape[0] - WIDE)
    for group in range(groups):
        rows = pl.ds(8 * group, 8)
        for k in range(WIDE):
            p, q = along_yz(source, start + k, row + 8 * group)
            yp[start + k, rows] = p
            yq[start + k, rows] = q
    for group in range(groups):
        rows = pl.ds(8 * group, 8)
        window = [(yp[base + k, rows], yq[base + k, rows]) for k in range(WIDE + 4)]
        for k in range(WIDE):
            power(target, source, row, keep, shifted, skip, base + k, group, window[k : k + 5])


def last_rows(source, yp, yq, count, first):
    groups = yp.shape[1] // 8
    for group in range(groups):
        rows = pl.ds(8 * group, 8)
        for k in range(count):
            p, q = along_yz(source, first + k, EDGE + HEM + 8 * group, group == 0, group == groups - 1)
            yp[first + 1 + k, rows] = p
            yq[first + 1 + k, rows] = q


def fold(value):
    return jnp.sum(value.reshape(-1, 8, value.shape[1]), axis=0)


def add_each(left, right):
    return [a + b for a, b in zip(left, right)]


def add_sums(totals, arrays, count, first_x):
    field, keep, shifted, first, second, yp, yq = arrays
    parts = []
    for group in range(yp.shape[1] // 8):
        rows = pl.ds(8 * group, 8)
        mid, own = pl.ds(EDGE + 8 * group, 8), pl.ds(EDGE + HEM + 8 * group, 8)
        window = [(yp[first_x + k, rows], yq[first_x + k, rows]) for k in range(count + 4)]
        part = None
        for k in range(count):
            x = first_x + k
            v0 = field[x + WIDE, mid]
            v1 = first[x + NEAR, own]
            v2 = second[x + 1, own]
            form = v2 * (SCALE * across(window[k : k + 5]) + shifted[x + NEAR, mid] * v2)
            on = jnp.where(keep[x + NEAR, mid] > 0.0, 1.0, 0.0)
            new = (v0 * v0, v0 * v1, v1 * v1, v1 * v2, v2 * v2, form, v0, v1, v2, on)
            part = new if part is None else add_each(part, new)
        parts.append(part)
    while len(parts) > 1:
        parts = [add_each(*parts[k : k + 2]) for k in range(0, len(parts), 2)]
    return list(parts[0]) if totals is None else add_each(totals, parts[0])


def inner_kernel(
    far, near, field_in, weight, field, keep, shifted, first, second, yp1, yq1, yp2, yq2, yp3, yq3, sums
):
    nx, wide, nz = weight.shape
    ny = wide - 2 * EDGE

    def fill(low, high):
        for x in range(nx):
            set_beside(field, WIDE + x, keep, shifted, NEAR + x, low[EDGE * x : EDGE * (x + 1)], False)
            set_beside(field, WIDE + x, keep, shifted, NEAR + x, high[EDGE * x : EDGE * (x + 1)], True)

    by_y(fill, far, near)
    own = pl.ds(EDGE, ny)
    for x in range(nx):
        set_weight(keep, shifted, NEAR + x, own, weight[x, own])
    advance(first, field, EDGE - HEM, keep, shifted, 0, yp1, yq1, nx, WIDE)
    advance(second, first, EDGE, keep, shifted, 2, yp2, yq2, nx - 4, WIDE)
    last_rows(second, yp3, yq3, nx - 8, WIDE)
    arrays = (field, keep, shifted, first, second, yp3, yq3)
    totals = add_sums(None, arrays, nx - 12, WIDE + 1)
    for place, total in enumerate(totals):
        sums[place] = total


def side_kernel(last, message, corner, *refs):
    sums_in = refs[HELD]
    field, keep, shifted, first, second, yp1, yq1, yp2, yq2, yp3, yq3, sums = refs[HELD + 1 :]
    planes, wide, nz = field.shape
    nx, ny = planes - 2 * WIDE, wide - 2 * EDGE
    odd = odd_on("gx")
    high = odd if last else 1 - odd
    own = pl.ds(EDGE, ny)
    base = corner.shape[0] - 2 * WIDE * EDGE
    for x in range(WIDE):
        plane = high * (nx + WIDE) + x
        field[plane, own] = message[x * ny : (x + 1) * ny]
        for up in range(2):
            row = base + (2 * x + up) * EDGE
            set_beside(field, plane, keep, shifted, None, corner[row : row + EDGE], up == 1)
    for x in range(NEAR):
        plane = high * (nx + NEAR) + x
        row = (WIDE + x) * ny
        set_weight(keep, shifted, plane, own, message[row : row + ny])
        place = base + (x + (1 - high) * (WIDE - NEAR)) * 2 * EDGE
        for up in range(2):
            tile = corner[pl.ds(place + up * EDGE, EDGE)]
            rows = pl.ds(up * (wide - EDGE), EDGE)
            set_weight(keep, shifted, plane, rows, pltpu.roll(tile, NEAR if up else WIDE, 0))
    advance_side(first, field, EDGE - HEM, keep, shifted, 0, yp1, yq1, high)
    advance_side(second, first, EDGE, keep, shifted, 2, yp2, yq2, high)
    last_rows(second, yp3, yq3, WIDE, high * (nx + 2 - WIDE))
    none = jnp.zeros((ny, nz), F32)
    yp3[high * (nx + 3)] = none
    yq3[high * (nx + 3)] = none
    totals = tuple(sums_in[place] for place in range(10))
    arrays = (field, keep, shifted, first, second, yp3, yq3)
    totals = list(add_sums(totals, arrays, WIDE + 1, high * (nx - WIDE - 1)))
    own = pl.ds(EDGE + HEM, ny)
    beside, edge, next_edge = 1 + high * (nx + 1), 2 + high * (nx - 1), 3 + high * (nx - 3)
    give = 13.0 * yq3[edge] - yp3[edge] + (yq3[next_edge] - yp3[next_edge])
    take = 13.0 * yq3[beside] - yp3[beside]
    totals[5] += SCALE * fold(second[beside - 1, own] * give - second[edge - 1, own] * take)
    if not last:
        for place, total in enumerate(totals):
            sums[place] = total
        return
    row = lax.broadcasted_iota(jnp.int32, (SUMS, nz), 0)
    lane = lax.broadcasted_iota(jnp.int32, (SUMS, nz), 1)
    lines = jnp.zeros((SUMS, nz), F32)
    for place, total in enumerate(totals):
        lines = jnp.where(row == place, jnp.sum(total, axis=0, keepdims=True), lines)
    pieces, rest = [], lines
    for _ in range(3):
        pieces.append(rest.astype(jnp.bfloat16))
        rest = rest - pieces[-1].astype(F32)
    ones = jnp.ones((nz, nz), jnp.bfloat16)
    whole_sums = jnp.dot(jnp.concatenate(pieces, axis=0), ones, preferred_element_type=F32)
    top, rest = two_sum(whole_sums[:SUMS], whole_sums[SUMS : 2 * SUMS])
    pair = two_sum(top, rest + whole_sums[2 * SUMS :])
    spot = jnp.where(lane == row, pair[0], jnp.where(lane == row + SUMS, pair[1], 0.0))
    sums[...] = jnp.sum(spot, axis=0, keepdims=True)


def two_sum(a, b):
    total = a + b
    part = total - a
    return total, (a - (total - part)) + (b - part)


def pair_add(a, b):
    total, rest = two_sum(a[0], b[0])
    return total, rest + (a[1] + b[1])


def halves(a):
    wide = 4097.0 * a
    top = wide - (wide - a)
    return top, a - top


def pair_mul(a, b):
    product = a[0] * b[0]
    a_top, a_rest = halves(a[0])
    b_top, b_rest = halves(b[0])
    rest = ((a_top * b_top - product) + a_top * b_rest + a_rest * b_top) + a_rest * b_rest
    rest = rest + (a[0] * b[1] + a[1] * b[0])
    total = product + rest
    return total, rest - (total - product)


def pair_sub(a, b):
    total, rest = two_sum(a[0], -b[0])
    rest = rest + (a[1] - b[1])
    out = total + rest
    return out, rest - (out - total)


def ratio(over, under, low, high):
    good = under > 0.0
    value = jnp.where(good, over / jnp.where(good, under, 1.0), 0.5 * (low + high))
    return jnp.minimum(jnp.maximum(value, low), high)


def coefficients(total):
    scale = 1.0 / total[0][0]
    zero = jnp.zeros_like(scale)
    g = [pair_mul(item, (scale, zero)) for item in total[:6]]
    shift = (jnp.full_like(scale, SHIFT), zero)
    h = [pair_add(g[k + 1], pair_mul(g[k], shift)) for k in range(5)]

    def minor(a, b, c, d):
        return pair_sub(pair_mul(a, b), pair_mul(c, d))

    s11 = minor(h[2], h[0], h[1], h[1])
    s12 = minor(h[3], h[0], h[1], h[2])
    s22 = minor(h[4], h[0], h[2], h[2])
    y1 = minor(g[1], h[0], h[1], g[0])
    y2 = minor(g[2], h[0], h[2], g[0])
    last = minor(s22, s11, s12, s12)
    side = minor(y2, s11, s12, y1)
    alpha = g[0][0] / h[0][0]
    l10 = h[1][0] / h[0][0]
    l20 = h[2][0] / h[0][0]
    l21 = ratio(s12[0], s11[0], l10 + (LOW - SHIFT), l10 + (HIGH - SHIFT))
    gamma1 = ratio(y1[0], s11[0], -alpha / LOW, -alpha / HIGH)
    gamma2 = ratio(side[0], last[0], -gamma1 / HIGH, -gamma1 / LOW)
    c1 = gamma1 - gamma2 * l21
    return alpha - c1 * l10 - gamma2 * l20, c1, gamma2


def sigmoid(value):
    return 1.0 / (1.0 + jnp.exp(-SHARP * value))


def finish_kernel(
    visible_hbm, parts, field, first, second, indicator_hbm, crossing_hbm,
    visible, indicator, crossing, level, weight, sem, slot_sems, result_sem,
):
    nx, ny, nz = indicator.shape
    copy = pltpu.make_async_copy(visible_hbm, visible, sem)
    copy.start()
    devices = parts.shape[0]
    tiles = [parts[pl.ds(8 * k, 8)] for k in range(devices // 8)]
    pairs = [(tile, pltpu.roll(tile, nz - SUMS, 1)) for tile in tiles]
    while len(pairs) > 1:
        pairs = [pair_add(a, b) for a, b in zip(pairs[::2], pairs[1::2])]
    total = pairs[0]
    for step in (4, 2, 1):
        total = pair_add(total, (pltpu.roll(total[0], step, 0), pltpu.roll(total[1], step, 0)))

    def spread(value, k):
        return jnp.broadcast_to(value[0:1, k : k + 1], (1, nz))

    item = [(spread(total[0], k), spread(total[1], k)) for k in range(10)]
    c0, c1, c2 = coefficients(item)
    over = c0 * (item[6][0] + item[6][1]) + c1 * (item[7][0] + item[7][1]) + c2 * (item[8][0] + item[8][1])
    iso = over / item[9][0]

    def set_level(x):
        v0 = field[x + WIDE, pl.ds(EDGE, ny + EDGE)]
        v1 = first[x + NEAR, pl.ds(EDGE + HEM, ny + EDGE)]
        v2 = second[x + 1, pl.ds(EDGE + HEM, ny + EDGE)]
        value = c0 * v0 + c1 * v1 + c2 * v2
        here = sigmoid(value - iso)
        for row in range(0, ny + EDGE, 8):
            level[x, row : row + 8] = pltpu.roll(here[row : row + 8], 0, 1, stride=BLK, stride_axis=0)
        return value

    for x in range(nx):
        indicator[x] = set_level(x)[:ny]

    set_level(nx)
    result = pltpu.make_async_copy(indicator, indicator_hbm, result_sem)
    result.start()
    outside = sigmoid(-iso)
    lane = lax.broadcasted_iota(jnp.int32, (8, nz), 1)
    end = lane == lax.rem(nz - 1 + BLK * lax.broadcasted_iota(jnp.int32, (8, nz), 0), nz)

    for x in range(nx):
        for row in range(0, ny, 8):
            here = level[x, row : row + 8]
            beside = pltpu.roll(level[x, row + 1 : row + 9], nz - BLK, 1)
            above = jnp.where(end, outside, pltpu.roll(here, nz - 1, 1))
            for edge, there in enumerate((level[x + 1, row : row + 8], beside, above)):
                value = here * (1.0 - there) + (1.0 - here) * there
                weight[edge, pl.ds(x * (ny + 1) + row, 8)] = value

    chunk = lax.broadcasted_iota(jnp.int32, (8, nz), 1) // BLK
    bricks_z = nz // BLK
    per_row = nz // BLK

    copy.wait()

    def out(slot):
        filled = crossing.at[slot, :, pl.ds(0, crossing_hbm.shape[2])]
        return pltpu.make_async_copy(filled, crossing_hbm.at[slot], slot_sems.at[slot])

    for slot in range(visible.shape[0]):
        number = visible[slot]
        safe = jnp.maximum(number, 0)
        begin = (safe // bricks_z) * BLK
        column = safe % bricks_z
        spots = [chunk == lax.rem(column + row, per_row) for row in range(per_row)]
        turn = lax.rem(nz - column * BLK, nz)
        for edge in range(3):
            for half in range(2):
                for part in range(BLK // per_row):
                    at = half * 8 * (ny + 1) + begin + part * per_row
                    tile = weight[edge, pl.ds(at, 8, stride=ny + 1)]
                    for row in range(1, per_row):
                        lines = weight[edge, pl.ds(at + row, 8, stride=ny + 1)]
                        tile = jnp.where(spots[row], lines, tile)
                    tile = jnp.where(number >= 0, pltpu.roll(tile, turn, 1), 0.0)
                    crossing[slot, edge, pl.ds(half * 16 + part, 8, stride=2)] = tile
        out(slot).start()

    for slot in range(visible.shape[0]):
        out(slot).wait()
    result.wait()


def whole(*shape):
    return jax.ShapeDtypeStruct(shape, F32)


VMEM = pl.BlockSpec(memory_space=pltpu.VMEM)


HBM = pl.BlockSpec(memory_space=pltpu.HBM)


def kernel(body, inputs, outputs, scratch=(), results=VMEM, alias=None, flops=0):
    return pl.pallas_call(
        body,
        in_specs=list(inputs),
        out_specs=[results] * len(outputs),
        out_shape=list(outputs),
        scratch_shapes=list(scratch),
        input_output_aliases=alias or {},
        cost_estimate=pl.CostEstimate(flops=flops, bytes_accessed=flops // 4, transcendentals=0),
        compiler_params=pltpu.CompilerParams(vmem_limit_bytes=32 * 1024 * 1024),
    )


def in_hbm(value):
    return pltpu.with_memory_space_constraint(value, pltpu.HBM)


def swap(value, axis, first):
    count = lax.axis_size(axis)
    pairs = [(k, k + 1) for k in range(first, count - 1, 2)]
    return lax.ppermute(value, axis, pairs + [(b, a) for a, b in pairs])


def body(right_side, screening, active_blocks, visible_bricks):
    nx, ny, nz = right_side.shape
    active = active_blocks.reshape(-1)
    visible = visible_bricks.reshape(-1)
    devices = lax.axis_size("gx") * lax.axis_size("gy")
    slab = whole(nx, ny, nz)
    planes, near, third = nx + 2 * WIDE, nx + 2 * NEAR, nx + 2
    wide, rows = ny + 2 * EDGE, ny + 2 * HEM
    rim = whole(nx * EDGE, nz)
    edges = pltpu.VMEM((2, nx, EDGE, nz), F32)
    far, near_by, mask = kernel(
        pack_kernel,
        (HBM, HBM, HBM),
        (rim, rim, whole(ny, nz)),
        (pltpu.SMEM(active.shape, jnp.int32), edges, edges, pltpu.SemaphoreType.DMA((5,))),
    )(in_hbm(active), in_hbm(right_side), in_hbm(screening))
    far = swap(far, "gy", 1)
    near_by = swap(near_by, "gy", 0)
    straight, corners = (WIDE + NEAR) * ny, 2 * WIDE * EDGE
    side = whole(straight + corners, nz)
    field, weight, cross, chip = kernel(
        place_kernel,
        (VMEM,) * 3,
        (whole(planes, wide, nz), whole(nx, wide, nz), whole(straight + EXTRA, nz), side),
    )(mask, right_side, screening)
    cross = swap(cross, "gx", 1)
    chip, corner = kernel(widen_kernel, (VMEM,) * 3, (side, whole(corners, nz)), alias={2: 0})(far, near_by, chip)
    chip = swap(chip, "gx", 0)
    corner = swap(corner, "gx", 1)
    kept = [whole(planes, wide, nz)] + [whole(near, wide, nz)] * 2
    kept += [whole(near, rows + 2 * EDGE, nz), whole(third, rows + 2 * EDGE, nz)]
    kept += [whole(planes, rows, nz)] * 2 + [whole(near, rows, nz)] * 2 + [whole(third + 2, ny, nz)] * 2
    tallies = whole(10, 8, nz)
    held = kernel(inner_kernel, (VMEM,) * 4, kept + [tallies], alias={2: 0}, flops=INNER)(
        far, near_by, field, weight
    )
    for last, messages in ((False, (chip, chip)), (True, (cross, corner))):
        held = kernel(
            functools.partial(side_kernel, last),
            (VMEM,) * (HELD + 3),
            kept + [whole(1, nz) if last else tallies],
            alias={2 + k: k for k in range(HELD)},
            flops=SIDE,
        )(*messages, *held)
    field, _, _, first, second = held[:5]
    devices = lax.axis_size("gx") * lax.axis_size("gy")
    parts = lax.all_to_all(jnp.broadcast_to(held[-1], (devices, 1, nz)), ("gx", "gy"), 0, 0)
    slots = visible.shape[0]
    shape = (slots, 3, BLK**3 // nz, nz)
    indicator, crossing = kernel(
        finish_kernel,
        (HBM,) + (VMEM,) * 4,
        (slab, whole(*shape)),
        (
            pltpu.SMEM(visible.shape, jnp.int32),
            pltpu.VMEM(slab.shape, F32),
            pltpu.VMEM((slots, 3, BLK**3 // nz + 8, nz), F32),
            pltpu.VMEM((nx + 1, ny + EDGE, nz), F32),
            pltpu.VMEM((3, (nx + 1) * (ny + 1), nz), F32),
            pltpu.SemaphoreType.DMA,
            pltpu.SemaphoreType.DMA((slots,)),
            pltpu.SemaphoreType.DMA,
        ),
        results=HBM,
    )(in_hbm(visible), parts.reshape(devices, nz), field, first, second)
    return indicator, crossing.reshape(slots, 1, 3, BLK**3)


def solution(mesh):
    return jax.shard_map(
        body,
        mesh=mesh,
        in_specs=(
            P("gx", "gy", None),
            P("gx", "gy", None),
            P("gx", "gy", None),
            P("gx", "gy", None),
        ),
        out_specs=(P("gx", "gy", None), P("gx", "gy", None, None)),
        check_vma=False,
    )
```

```python
import functools

import jax
import jax.numpy as jnp
from jax import lax
from jax.experimental import pallas as pl
from jax.experimental.pallas import tpu as pltpu
from jax.sharding import PartitionSpec as P

BLK = 16
WIDE = 5
NEAR = 3
HEM = 4
EDGE = 8
SHARP = 4.0
SCALE = 1.0 / 86400.0
SHIFT = 2.0
LOW, HIGH = 0.5, 7.0
SUMS = 16
EXTRA, INNER, SIDE = 96, 0, 0
HELD = 11
F32 = jnp.float32


def mass(mid, one, two):
    return 66.0 * mid + (26.0 * one + two)


def stiff(mid, one, two):
    return 6.0 * mid - (2.0 * one + two)


def block_mask(active, slots, rows, columns):
    y = lax.broadcasted_iota(jnp.int32, (rows, columns), 0)
    z = lax.broadcasted_iota(jnp.int32, (rows, columns), 1)
    number = (y // BLK) * (columns // BLK) + z // BLK
    mask = jnp.zeros((rows, columns), F32)
    for slot in range(slots):
        mask = jnp.where(number == active[slot], 1.0, mask)
    return mask


def on_odd():
    return lax.rem(lax.axis_index("gx"), 2)


def odd_on(axis):
    return lax.rem(lax.axis_index(axis), 2)


def pack_kernel(active_hbm, right_hbm, screen_hbm, far, near, mask_out, active, right, screen, sems):
    nx, ny, nz = right_hbm.shape
    copies = [pltpu.make_async_copy(active_hbm, active, sems.at[0])]
    for k, (source, target) in enumerate(((right_hbm, right), (screen_hbm, screen))):
        for high in range(2):
            rows = pl.ds(high * (ny - EDGE), EDGE)
            copies.append(pltpu.make_async_copy(source.at[:, rows], target.at[high], sems.at[1 + 2 * k + high]))
    for copy in copies:
        copy.start()
    copies[0].wait()
    mask = block_mask(active, active.shape[0], ny, nz)
    mask_out[...] = mask
    row = lax.broadcasted_iota(jnp.int32, (EDGE, nz), 0)
    for copy in copies[1:]:
        copy.wait()

    def write(high_out, low_out):
        for x in range(nx):
            rows = pl.ds(x * EDGE, EDGE)
            low_out[rows] = jnp.where(row < WIDE, right[0, x], pltpu.roll(screen[0, x], WIDE, 0)) * mask[:EDGE]
            beside = pltpu.roll(screen[1, x] * mask[ny - EDGE :], NEAR, 0)
            high_out[rows] = jnp.where(row >= NEAR, right[1, x] * mask[ny - EDGE :], beside)

    odd = odd_on("gy")
    pl.when(odd == 1)(functools.partial(write, far, near))
    pl.when(odd == 0)(functools.partial(write, near, far))


def place_kernel(mask_in, right, screen, field, weight, cross, chip):
    nx, ny, nz = right.shape
    mask = mask_in[...]
    own = pl.ds(EDGE, ny)
    for x in range(nx):
        field[WIDE + x, own] = right[x] * mask
        weight[x, own] = screen[x] * mask
    odd = odd_on("gx")
    for target, high in ((cross, odd), (chip, 1 - odd)):
        for x in range(WIDE):
            target[x * ny : (x + 1) * ny] = field[WIDE + high * (nx - WIDE) + x, own]
        for x in range(NEAR):
            row = (WIDE + x) * ny
            target[row : row + ny] = weight[high * (nx - NEAR) + x, own]


def widen_kernel(far, near, chip_in, chip, corner):
    nx = far.shape[0] // EDGE
    base = chip.shape[0] - corner.shape[0]
    odd = odd_on("gx")

    def fill(low, high):
        for target, start, side in ((corner, 0, odd), (chip, base, 1 - odd)):
            for x in range(WIDE):
                tile = pl.ds((side * (nx - WIDE) + x) * EDGE, EDGE)
                row = start + 2 * x * EDGE
                target[row : row + EDGE] = low[tile]
                target[row + EDGE : row + 2 * EDGE] = high[tile]

    by_y(fill, far, near)


def by_y(action, far, near):
    odd = odd_on("gy")
    pl.when(odd == 1)(functools.partial(action, near, far))
    pl.when(odd == 0)(functools.partial(action, far, near))


def near_z(value):
    lane = lax.broadcasted_iota(jnp.int32, value.shape, 1)
    last = value.shape[1]

    def shifted(step):
        before = jnp.where(lane >= step, pltpu.roll(value, step, 1), 0.0)
        after = jnp.where(lane < last - step, pltpu.roll(value, last - step, 1), 0.0)
        return before + after

    return shifted(1), shifted(2)


def set_beside(field, x, keep, shifted, weight_x, tile, high):
    start = field.shape[1] - EDGE if high else 0
    field[x, start : start + EDGE] = tile
    if weight_x is not None:
        set_weight(keep, shifted, weight_x, pl.ds(start, EDGE), pltpu.roll(tile, NEAR if high else WIDE, 0))


def set_weight(keep, shifted, at, rows, weight):
    on = weight > 0.0
    keep[at, rows] = jnp.where(on, SCALE, 0.0)
    shifted[at, rows] = jnp.where(on, weight - SHIFT, 0.0)


def near_y(source, x, row, top, end):
    def part(step):
        return source[x, pl.ds(row + step, 8)]

    below, above = part(-2), part(2)
    place = lax.broadcasted_iota(jnp.int32, below.shape, 0)
    if top:
        below = jnp.where(place == 0, 0.0, jnp.where(place == 1, 2.0 * below, below))
    if end:
        above = jnp.where(place == 7, 0.0, jnp.where(place == 6, 2.0 * above, above))
    return part(0), part(-1) + part(1), below + above


def along_yz(source, x, row, top=False, end=False):
    here, one, two = near_y(source, x, row, top, end)
    heavy, stretched = mass(here, one, two), stiff(here, one, two)
    heavy_near, stretched_near = near_z(heavy), near_z(stretched)
    return mass(heavy, *heavy_near), stiff(heavy, *heavy_near) + mass(stretched, *stretched_near)


def across(window):
    p, q = zip(*window)
    return mass(q[2], q[1] + q[3], q[0] + q[4]) + stiff(p[2], p[1] + p[3], p[0] + p[4])


def power(target, source, row, keep, shifted, skip, x, group, window):
    rows, at = pl.ds(EDGE + 8 * group, 8), pl.ds(EDGE - HEM + 8 * group, 8)
    center = source[x + 2, pl.ds(row + 8 * group, 8)]
    target[x, rows] = keep[x + skip, at] * across(window) + shifted[x + skip, at] * center


def advance(target, source, row, keep, shifted, skip, yp, yq, count, first):
    for group in range(target.shape[1] // 8 - 2):
        rows = pl.ds(8 * group, 8)
        window = []
        for x in range(first, first + count):
            p, q = along_yz(source, x, row + 8 * group)
            yp[x, rows] = p
            yq[x, rows] = q
            window = window[-4:] + [(p, q)]
            if len(window) == 5:
                power(target, source, row, keep, shifted, skip, x - 4, group, window)


def advance_side(target, source, row, keep, shifted, skip, yp, yq, high):
    groups = target.shape[1] // 8 - 2
    base = high * (target.shape[0] - WIDE)
    start = high * (source.shape[0] - WIDE)
    for group in range(groups):
        rows = pl.ds(8 * group, 8)
        for k in range(WIDE):
            p, q = along_yz(source, start + k, row + 8 * group)
            yp[start + k, rows] = p
            yq[start + k, rows] = q
    for group in range(groups):
        rows = pl.ds(8 * group, 8)
        window = [(yp[base + k, rows], yq[base + k, rows]) for k in range(WIDE + 4)]
        for k in range(WIDE):
            power(target, source, row, keep, shifted, skip, base + k, group, window[k : k + 5])


def last_rows(source, yp, yq, count, first):
    groups = yp.shape[1] // 8
    for group in range(groups):
        rows = pl.ds(8 * group, 8)
        for k in range(count):
            p, q = along_yz(source, first + k, EDGE + HEM + 8 * group, group == 0, group == groups - 1)
            yp[first + 1 + k, rows] = p
            yq[first + 1 + k, rows] = q


def fold(value):
    return jnp.sum(value.reshape(-1, 8, value.shape[1]), axis=0)


def add_each(left, right):
    return [a + b for a, b in zip(left, right)]


def add_sums(totals, arrays, count, first_x):
    field, keep, shifted, first, second, yp, yq = arrays
    parts = []
    for group in range(yp.shape[1] // 8):
        rows = pl.ds(8 * group, 8)
        mid, own = pl.ds(EDGE + 8 * group, 8), pl.ds(EDGE + HEM + 8 * group, 8)
        window = [(yp[first_x + k, rows], yq[first_x + k, rows]) for k in range(count + 4)]
        part = None
        for k in range(count):
            x = first_x + k
            v0 = field[x + WIDE, mid]
            v1 = first[x + NEAR, own]
            v2 = second[x + 1, own]
            form = v2 * (SCALE * across(window[k : k + 5]) + shifted[x + NEAR, mid] * v2)
            on = jnp.where(keep[x + NEAR, mid] > 0.0, 1.0, 0.0)
            new = (v0 * v0, v0 * v1, v1 * v1, v1 * v2, v2 * v2, form, v0, v1, v2, on)
            part = new if part is None else add_each(part, new)
        parts.append(part)
    while len(parts) > 1:
        parts = [add_each(*parts[k : k + 2]) for k in range(0, len(parts), 2)]
    return list(parts[0]) if totals is None else add_each(totals, parts[0])


def inner_kernel(
    far, near, field_in, weight, field, keep, shifted, first, second, yp1, yq1, yp2, yq2, yp3, yq3, sums
):
    nx, wide, nz = weight.shape
    ny = wide - 2 * EDGE

    def fill(low, high):
        for x in range(nx):
            set_beside(field, WIDE + x, keep, shifted, NEAR + x, low[EDGE * x : EDGE * (x + 1)], False)
            set_beside(field, WIDE + x, keep, shifted, NEAR + x, high[EDGE * x : EDGE * (x + 1)], True)

    by_y(fill, far, near)
    own = pl.ds(EDGE, ny)
    for x in range(nx):
        set_weight(keep, shifted, NEAR + x, own, weight[x, own])
    advance(first, field, EDGE - HEM, keep, shifted, 0, yp1, yq1, nx, WIDE)
    advance(second, first, EDGE, keep, shifted, 2, yp2, yq2, nx - 4, WIDE)
    last_rows(second, yp3, yq3, nx - 8, WIDE)
    arrays = (field, keep, shifted, first, second, yp3, yq3)
    totals = add_sums(None, arrays, nx - 12, WIDE + 1)
    for place, total in enumerate(totals):
        sums[place] = total


def side_kernel(last, message, corner, *refs):
    sums_in = refs[HELD]
    field, keep, shifted, first, second, yp1, yq1, yp2, yq2, yp3, yq3, sums = refs[HELD + 1 :]
    planes, wide, nz = field.shape
    nx, ny = planes - 2 * WIDE, wide - 2 * EDGE
    odd = odd_on("gx")
    high = odd if last else 1 - odd
    own = pl.ds(EDGE, ny)
    base = corner.shape[0] - 2 * WIDE * EDGE
    for x in range(WIDE):
        plane = high * (nx + WIDE) + x
        field[plane, own] = message[x * ny : (x + 1) * ny]
        for up in range(2):
            row = base + (2 * x + up) * EDGE
            set_beside(field, plane, keep, shifted, None, corner[row : row + EDGE], up == 1)
    for x in range(NEAR):
        plane = high * (nx + NEAR) + x
        row = (WIDE + x) * ny
        set_weight(keep, shifted, plane, own, message[row : row + ny])
        place = base + (x + (1 - high) * (WIDE - NEAR)) * 2 * EDGE
        for up in range(2):
            tile = corner[pl.ds(place + up * EDGE, EDGE)]
            rows = pl.ds(up * (wide - EDGE), EDGE)
            set_weight(keep, shifted, plane, rows, pltpu.roll(tile, NEAR if up else WIDE, 0))
    advance_side(first, field, EDGE - HEM, keep, shifted, 0, yp1, yq1, high)
    advance_side(second, first, EDGE, keep, shifted, 2, yp2, yq2, high)
    last_rows(second, yp3, yq3, WIDE, high * (nx + 2 - WIDE))
    none = jnp.zeros((ny, nz), F32)
    yp3[high * (nx + 3)] = none
    yq3[high * (nx + 3)] = none
    totals = tuple(sums_in[place] for place in range(10))
    arrays = (field, keep, shifted, first, second, yp3, yq3)
    totals = list(add_sums(totals, arrays, WIDE + 1, high * (nx - WIDE - 1)))
    own = pl.ds(EDGE + HEM, ny)
    beside, edge, next_edge = 1 + high * (nx + 1), 2 + high * (nx - 1), 3 + high * (nx - 3)
    give = 13.0 * yq3[edge] - yp3[edge] + (yq3[next_edge] - yp3[next_edge])
    take = 13.0 * yq3[beside] - yp3[beside]
    totals[5] += SCALE * fold(second[beside - 1, own] * give - second[edge - 1, own] * take)
    if not last:
        for place, total in enumerate(totals):
            sums[place] = total
        return
    row = lax.broadcasted_iota(jnp.int32, (SUMS, nz), 0)
    lane = lax.broadcasted_iota(jnp.int32, (SUMS, nz), 1)
    lines = jnp.zeros((SUMS, nz), F32)
    for place, total in enumerate(totals):
        lines = jnp.where(row == place, jnp.sum(total, axis=0, keepdims=True), lines)
    pieces, rest = [], lines
    for _ in range(3):
        pieces.append(rest.astype(jnp.bfloat16))
        rest = rest - pieces[-1].astype(F32)
    ones = jnp.ones((nz, nz), jnp.bfloat16)
    whole_sums = jnp.dot(jnp.concatenate(pieces, axis=0), ones, preferred_element_type=F32)
    top, rest = two_sum(whole_sums[:SUMS], whole_sums[SUMS : 2 * SUMS])
    pair = two_sum(top, rest + whole_sums[2 * SUMS :])
    spot = jnp.where(lane == row, pair[0], jnp.where(lane == row + SUMS, pair[1], 0.0))
    sums[...] = jnp.sum(spot, axis=0, keepdims=True)


def two_sum(a, b):
    total = a + b
    part = total - a
    return total, (a - (total - part)) + (b - part)


def pair_add(a, b):
    total, rest = two_sum(a[0], b[0])
    return total, rest + (a[1] + b[1])


def halves(a):
    wide = 4097.0 * a
    top = wide - (wide - a)
    return top, a - top


def pair_mul(a, b):
    product = a[0] * b[0]
    a_top, a_rest = halves(a[0])
    b_top, b_rest = halves(b[0])
    rest = ((a_top * b_top - product) + a_top * b_rest + a_rest * b_top) + a_rest * b_rest
    rest = rest + (a[0] * b[1] + a[1] * b[0])
    total = product + rest
    return total, rest - (total - product)


def pair_sub(a, b):
    total, rest = two_sum(a[0], -b[0])
    rest = rest + (a[1] - b[1])
    out = total + rest
    return out, rest - (out - total)


def ratio(over, under, low, high):
    good = under > 0.0
    value = jnp.where(good, over / jnp.where(good, under, 1.0), 0.5 * (low + high))
    return jnp.minimum(jnp.maximum(value, low), high)


def coefficients(total):
    scale = 1.0 / total[0][0]
    zero = jnp.zeros_like(scale)
    g = [pair_mul(item, (scale, zero)) for item in total[:6]]
    shift = (jnp.full_like(scale, SHIFT), zero)
    h = [pair_add(g[k + 1], pair_mul(g[k], shift)) for k in range(5)]

    def minor(a, b, c, d):
        return pair_sub(pair_mul(a, b), pair_mul(c, d))

    s11 = minor(h[2], h[0], h[1], h[1])
    s12 = minor(h[3], h[0], h[1], h[2])
    s22 = minor(h[4], h[0], h[2], h[2])
    y1 = minor(g[1], h[0], h[1], g[0])
    y2 = minor(g[2], h[0], h[2], g[0])
    last = minor(s22, s11, s12, s12)
    side = minor(y2, s11, s12, y1)
    alpha = g[0][0] / h[0][0]
    l10 = h[1][0] / h[0][0]
    l20 = h[2][0] / h[0][0]
    l21 = ratio(s12[0], s11[0], l10 + (LOW - SHIFT), l10 + (HIGH - SHIFT))
    gamma1 = ratio(y1[0], s11[0], -alpha / LOW, -alpha / HIGH)
    gamma2 = ratio(side[0], last[0], -gamma1 / HIGH, -gamma1 / LOW)
    c1 = gamma1 - gamma2 * l21
    return alpha - c1 * l10 - gamma2 * l20, c1, gamma2


def sigmoid(value):
    return 1.0 / (1.0 + jnp.exp(-SHARP * value))


def finish_kernel(
    visible_hbm, parts, field, first, second, indicator_hbm, crossing_hbm,
    visible, indicator, crossing, level, weight, sem, slot_sems, result_sem,
):
    nx, ny, nz = indicator.shape
    copy = pltpu.make_async_copy(visible_hbm, visible, sem)
    copy.start()
    devices = parts.shape[0]
    tiles = [parts[pl.ds(8 * k, 8)] for k in range(devices // 8)]
    pairs = [(tile, pltpu.roll(tile, nz - SUMS, 1)) for tile in tiles]
    while len(pairs) > 1:
        pairs = [pair_add(a, b) for a, b in zip(pairs[::2], pairs[1::2])]
    total = pairs[0]
    for step in (4, 2, 1):
        total = pair_add(total, (pltpu.roll(total[0], step, 0), pltpu.roll(total[1], step, 0)))

    def spread(value, k):
        return jnp.broadcast_to(value[0:1, k : k + 1], (1, nz))

    item = [(spread(total[0], k), spread(total[1], k)) for k in range(10)]
    c0, c1, c2 = coefficients(item)
    over = c0 * (item[6][0] + item[6][1]) + c1 * (item[7][0] + item[7][1]) + c2 * (item[8][0] + item[8][1])
    iso = over / item[9][0]

    def set_level(x):
        v0 = field[x + WIDE, pl.ds(EDGE, ny + EDGE)]
        v1 = first[x + NEAR, pl.ds(EDGE + HEM, ny + EDGE)]
        v2 = second[x + 1, pl.ds(EDGE + HEM, ny + EDGE)]
        value = c0 * v0 + c1 * v1 + c2 * v2
        here = sigmoid(value - iso)
        for row in range(0, ny + EDGE, 8):
            level[x, row : row + 8] = pltpu.roll(here[row : row + 8], 0, 1, stride=BLK, stride_axis=0)
        return value

    outside = sigmoid(-iso)
    lane = lax.broadcasted_iota(jnp.int32, (8, nz), 1)
    end = lane == lax.rem(nz - 1 + BLK * lax.broadcasted_iota(jnp.int32, (8, nz), 0), nz)

    def set_weights(x):
        for row in range(0, ny, 8):
            here = level[x, row : row + 8]
            beside = pltpu.roll(level[x, row + 1 : row + 9], nz - BLK, 1)
            above = jnp.where(end, outside, pltpu.roll(here, nz - 1, 1))
            for edge, there in enumerate((level[x + 1, row : row + 8], beside, above)):
                value = here * (1.0 - there) + (1.0 - here) * there
                weight[edge, pl.ds(x * (ny + 1) + row, 8)] = value

    for x in range(nx):
        indicator[x] = set_level(x)[:ny]
        if x > 0:
            set_weights(x - 1)
    set_level(nx)
    result = pltpu.make_async_copy(indicator, indicator_hbm, result_sem)
    result.start()
    set_weights(nx - 1)

    chunk = lax.broadcasted_iota(jnp.int32, (8, nz), 1) // BLK
    bricks_z = nz // BLK
    per_row = nz // BLK

    copy.wait()

    def out(slot):
        filled = crossing.at[slot, :, pl.ds(0, crossing_hbm.shape[2])]
        return pltpu.make_async_copy(filled, crossing_hbm.at[slot], slot_sems.at[slot])

    for slot in range(visible.shape[0]):
        number = visible[slot]
        safe = jnp.maximum(number, 0)
        begin = (safe // bricks_z) * BLK
        column = safe % bricks_z
        spots = [chunk == lax.rem(column + row, per_row) for row in range(per_row)]
        turn = lax.rem(nz - column * BLK, nz)
        for edge in range(3):
            for half in range(2):
                for part in range(BLK // per_row):
                    at = half * 8 * (ny + 1) + begin + part * per_row
                    tile = weight[edge, pl.ds(at, 8, stride=ny + 1)]
                    for row in range(1, per_row):
                        lines = weight[edge, pl.ds(at + row, 8, stride=ny + 1)]
                        tile = jnp.where(spots[row], lines, tile)
                    tile = jnp.where(number >= 0, pltpu.roll(tile, turn, 1), 0.0)
                    crossing[slot, edge, pl.ds(half * 16 + part, 8, stride=2)] = tile
        out(slot).start()

    for slot in range(visible.shape[0]):
        out(slot).wait()
    result.wait()


def whole(*shape):
    return jax.ShapeDtypeStruct(shape, F32)


VMEM = pl.BlockSpec(memory_space=pltpu.VMEM)


HBM = pl.BlockSpec(memory_space=pltpu.HBM)


def kernel(body, inputs, outputs, scratch=(), results=VMEM, alias=None, flops=0):
    return pl.pallas_call(
        body,
        in_specs=list(inputs),
        out_specs=[results] * len(outputs),
        out_shape=list(outputs),
        scratch_shapes=list(scratch),
        input_output_aliases=alias or {},
        cost_estimate=pl.CostEstimate(flops=flops, bytes_accessed=flops // 4, transcendentals=0),
        compiler_params=pltpu.CompilerParams(vmem_limit_bytes=32 * 1024 * 1024),
    )


def in_hbm(value):
    return pltpu.with_memory_space_constraint(value, pltpu.HBM)


def swap(value, axis, first):
    count = lax.axis_size(axis)
    pairs = [(k, k + 1) for k in range(first, count - 1, 2)]
    return lax.ppermute(value, axis, pairs + [(b, a) for a, b in pairs])


def body(right_side, screening, active_blocks, visible_bricks):
    nx, ny, nz = right_side.shape
    active = active_blocks.reshape(-1)
    visible = visible_bricks.reshape(-1)
    devices = lax.axis_size("gx") * lax.axis_size("gy")
    slab = whole(nx, ny, nz)
    planes, near, third = nx + 2 * WIDE, nx + 2 * NEAR, nx + 2
    wide, rows = ny + 2 * EDGE, ny + 2 * HEM
    rim = whole(nx * EDGE, nz)
    edges = pltpu.VMEM((2, nx, EDGE, nz), F32)
    far, near_by, mask = kernel(
        pack_kernel,
        (HBM, HBM, HBM),
        (rim, rim, whole(ny, nz)),
        (pltpu.SMEM(active.shape, jnp.int32), edges, edges, pltpu.SemaphoreType.DMA((5,))),
    )(in_hbm(active), in_hbm(right_side), in_hbm(screening))
    far = swap(far, "gy", 1)
    near_by = swap(near_by, "gy", 0)
    straight, corners = (WIDE + NEAR) * ny, 2 * WIDE * EDGE
    side = whole(straight + corners, nz)
    field, weight, cross, chip = kernel(
        place_kernel,
        (VMEM,) * 3,
        (whole(planes, wide, nz), whole(nx, wide, nz), whole(straight + EXTRA, nz), side),
    )(mask, right_side, screening)
    cross = swap(cross, "gx", 1)
    chip, corner = kernel(widen_kernel, (VMEM,) * 3, (side, whole(corners, nz)), alias={2: 0})(far, near_by, chip)
    chip = swap(chip, "gx", 0)
    corner = swap(corner, "gx", 1)
    kept = [whole(planes, wide, nz)] + [whole(near, wide, nz)] * 2
    kept += [whole(near, rows + 2 * EDGE, nz), whole(third, rows + 2 * EDGE, nz)]
    kept += [whole(planes, rows, nz)] * 2 + [whole(near, rows, nz)] * 2 + [whole(third + 2, ny, nz)] * 2
    tallies = whole(10, 8, nz)
    held = kernel(inner_kernel, (VMEM,) * 4, kept + [tallies], alias={2: 0}, flops=INNER)(
        far, near_by, field, weight
    )
    for last, messages in ((False, (chip, chip)), (True, (cross, corner))):
        held = kernel(
            functools.partial(side_kernel, last),
            (VMEM,) * (HELD + 3),
            kept + [whole(1, nz) if last else tallies],
            alias={2 + k: k for k in range(HELD)},
            flops=SIDE,
        )(*messages, *held)
    field, _, _, first, second = held[:5]
    devices = lax.axis_size("gx") * lax.axis_size("gy")
    parts = lax.all_to_all(jnp.broadcast_to(held[-1], (devices, 1, nz)), ("gx", "gy"), 0, 0)
    slots = visible.shape[0]
    shape = (slots, 3, BLK**3 // nz, nz)
    indicator, crossing = kernel(
        finish_kernel,
        (HBM,) + (VMEM,) * 4,
        (slab, whole(*shape)),
        (
            pltpu.SMEM(visible.shape, jnp.int32),
            pltpu.VMEM(slab.shape, F32),
            pltpu.VMEM((slots, 3, BLK**3 // nz + 8, nz), F32),
            pltpu.VMEM((nx + 1, ny + EDGE, nz), F32),
            pltpu.VMEM((3, (nx + 1) * (ny + 1), nz), F32),
            pltpu.SemaphoreType.DMA,
            pltpu.SemaphoreType.DMA((slots,)),
            pltpu.SemaphoreType.DMA,
        ),
        results=HBM,
    )(in_hbm(visible), parts.reshape(devices, nz), field, first, second)
    return indicator, crossing.reshape(slots, 1, 3, BLK**3)


def solution(mesh):
    return jax.shard_map(
        body,
        mesh=mesh,
        in_specs=(
            P("gx", "gy", None),
            P("gx", "gy", None),
            P("gx", "gy", None),
            P("gx", "gy", None),
        ),
        out_specs=(P("gx", "gy", None), P("gx", "gy", None, None)),
        check_vma=False,
    )
```
